32 devices in a mesh: rows: 4 (over y, x), seq: 8 (over z, core).
Axes of the slice: x: 2, y: 2, z: 4, core: 2. Of those that a mesh axis runs over, the one named last changes fastest.
Arguments:
- tokens: bfloat16 [4, 1024, 1024], P('rows', 'seq'), may hold values from -6 to 6
- cotangent: bfloat16 [4, 1024, 1024], P('rows', 'seq'), may hold values from -6 to 6
- doc_lengths: int32 [4, 8], P('rows'), may hold values from 1 to 512, 1024 in all within a row
- norm_gain: float32 [1024], replicated, may hold values from 0.5 to 1.5
- in_proj: bfloat16 [1024, 4096], replicated, may hold values from -0.1875 to 0.1875
- conv_weight: float32 [4, 2048], replicated, may hold values from -3 to 3
- conv_bias: float32 [2048], replicated, may hold values from -3 to 3
- x_proj: bfloat16 [2048, 96], replicated, may hold values from -0.125 to 0.125
- dt_proj: bfloat16 [64, 2048], replicated, may hold values from -0.75 to 0.75
- dt_bias: float32 [2048], replicated, may hold values from -6.5 to -2.5
- a_log: float32 [16, 2048], replicated, may hold values from 0 to 2.77
- d_skip: float32 [2048], replicated, may hold values from 0.5 to 1.5
- out_proj: bfloat16 [2048, 1024], replicated, may hold values from -0.25 to 0.25
- moment_norm_gain: float32 [1024], P('seq'), may hold values from -0.0024414062 to 0.0024414062
- moment_in_proj: float32 [1024, 4096], P('seq'), may hold values from -0.0024414062 to 0.0024414062
- moment_conv_weight: float32 [4, 2048], P(None, 'seq'), may hold values from -0.0024414062 to 0.0024414062
- moment_conv_bias: float32 [2048], P('seq'), may hold values from -0.0024414062 to 0.0024414062
- moment_x_proj: float32 [2048, 96], P('seq'), may hold values from -0.0024414062 to 0.0024414062
- moment_dt_proj: float32 [64, 2048], P(None, 'seq'), may hold values from -0.0024414062 to 0.0024414062
- moment_dt_bias: float32 [2048], P('seq'), may hold values from -0.0024414062 to 0.0024414062
- moment_a_log: float32 [16, 2048], P(None, 'seq'), may hold values from -0.0024414062 to 0.0024414062
- moment_d_skip: float32 [2048], P('seq'), may hold values from -0.0024414062 to 0.0024414062
- moment_out_proj: float32 [2048, 1024], P('seq'), may hold values from -0.0024414062 to 0.0024414062
- average_norm_gain: float32 [1024], P('seq'), may hold values from 0.5 to 1.5
- average_in_proj: float32 [1024, 4096], P('seq'), may hold values from -0.1875 to 0.1875
- average_conv_weight: float32 [4, 2048], P(None, 'seq'), may hold values from -3 to 3
- average_conv_bias: float32 [2048], P('seq'), may hold values from -3 to 3
- average_x_proj: float32 [2048, 96], P('seq'), may hold values from -0.125 to 0.125
- average_dt_proj: float32 [64, 2048], P(None, 'seq'), may hold values from -0.75 to 0.75
- average_dt_bias: float32 [2048], P('seq'), may hold values from -6.5 to 1.5
- average_a_log: float32 [16, 2048], P(None, 'seq'), may hold values from 0 to 2.77
- average_d_skip: float32 [2048], P('seq'), may hold values from 0.5 to 1.5
- average_out_proj: float32 [2048, 1024], P('seq'), may hold values from -0.25 to 0.25
Outputs:
- block_output: float32 [4, 1024, 1024], P('rows', 'seq')
- input_grad: float32 [4, 1024, 1024], P('rows', 'seq')
- grad_norm: float32 [], replicated
- new_moment_norm_gain: float32 [1024], P('seq')
- new_weight_norm_gain: float32 [1024], P('seq')
- new_average_norm_gain: float32 [1024], P('seq')
- new_moment_in_proj: float32 [1024, 4096], P('seq')
- new_weight_in_proj: float32 [1024, 4096], P('seq')
- new_average_in_proj: float32 [1024, 4096], P('seq')
- new_moment_conv_weight: float32 [4, 2048], P(None, 'seq')
- new_weight_conv_weight: float32 [4, 2048], P(None, 'seq')
- new_average_conv_weight: float32 [4, 2048], P(None, 'seq')
- new_moment_conv_bias: float32 [2048], P('seq')
- new_weight_conv_bias: float32 [2048], P('seq')
- new_average_conv_bias: float32 [2048], P('seq')
- new_moment_x_proj: float32 [2048, 96], P('seq')
- new_weight_x_proj: float32 [2048, 96], P('seq')
- new_average_x_proj: float32 [2048, 96], P('seq')
- new_moment_dt_proj: float32 [64, 2048], P(None, 'seq')
- new_weight_dt_proj: float32 [64, 2048], P(None, 'seq')
- new_average_dt_proj: float32 [64, 2048], P(None, 'seq')
- new_moment_dt_bias: float32 [2048], P('seq')
- new_weight_dt_bias: float32 [2048], P('seq')
- new_average_dt_bias: float32 [2048], P('seq')
- new_moment_a_log: float32 [16, 2048], P(None, 'seq')
- new_weight_a_log: float32 [16, 2048], P(None, 'seq')
- new_average_a_log: float32 [16, 2048], P(None, 'seq')
- new_moment_d_skip: float32 [2048], P('seq')
- new_weight_d_skip: float32 [2048], P('seq')
- new_average_d_skip: float32 [2048], P('seq')
- new_moment_out_proj: float32 [2048, 1024], P('seq')
- new_weight_out_proj: float32 [2048, 1024], P('seq')
- new_average_out_proj: float32 [2048, 1024], P('seq')
The draws below stay inside these ranges and needn't reach their ends.
All inputs are finite; a program needn't handle non-finite values.
Results may differ from the reference program's by a relative error of at most 0.008.
The reference program's roundings to bfloat16 on the way count: a program that leaves them out, or rounds other values in their place, can miss the bound.
Values may be sent and summed in bfloat16 or wider, within the bound.
A program may use at most 384 MiB of HBM per device.

```python
import math
import jax
import jax.numpy as jnp
import numpy as np
from jax import lax

D = 1024
E = 2048
N = 16
R = 64
K = 4
NDOC = 8
NROWS = 4
LENGTH = 1024
PARAMS = 6667264


def block_levels(key, extent, shards, least, high):
    factor_of = 1.0
    for axis_at, blocks in shards:
        heights = jax.random.uniform(jax.random.fold_in(jax.random.fold_in(key, 6), axis_at), (blocks,), jnp.float32, least / len(shards), high / len(shards))
        factor_of = factor_of * jnp.repeat(jnp.exp(heights), extent[axis_at] // blocks).reshape((-1,) + (1,) * (len(extent) - 1 - axis_at))
    return factor_of


def length_profile(count, total, bound, lean):
    loads = [(1 << 20) // math.isqrt(grade ** lean) + 1 for grade in range(2, count + 1)]
    spare, given = total - bound - (count - 1), [1] * (count - 1)
    while spare > 0:
        free = [i for i in range(count - 1) if given[i] < bound]
        pool, remaining = sum([loads[i] for i in free]), spare
        for i in free:
            addition = min(bound - given[i], max(1, remaining * loads[i] // pool), spare)
            given[i] = given[i] + addition
            spare = spare - addition
    return np.array([bound] + given)


def uneven_parts(key, number_of, total, most, skew):
    if number_of == 2:
        one = jax.random.randint(key, (), max(1, total - most), min(most, total - 1) + 1)
        return jnp.stack([one, total - one])
    lengths = jnp.asarray(length_profile(number_of, total, most, skew), jnp.int32)
    twos = (number_of - 1) // 2
    source_of, taker = lengths[1:1 + 2 * twos:2], lengths[2:2 + 2 * twos:2]
    room = jnp.minimum(source_of - 1, most - taker)
    shifted = jax.random.randint(jax.random.fold_in(key, 1), (twos,), 0, 1 << 20) % (room + 1)
    lengths = lengths.at[1:1 + 2 * twos:2].set(source_of - shifted).at[2:2 + 2 * twos:2].set(taker + shifted)
    return lengths[jax.random.permutation(jax.random.fold_in(key, 2), number_of)]


def bell_draw(rng, shape, spread, bound, split=(), kind=jnp.bfloat16):
    factor_of = block_levels(rng, shape, split, -0.22, 0.18) if split else 1.0
    drawn = jax.random.normal(rng, shape, jnp.float32) * spread * factor_of
    return jnp.minimum(jnp.maximum(drawn, -bound), bound).astype(kind)


def setup_inputs(seed: int = 0) -> dict:
    splits = jax.random.split(jax.random.key(seed), 34)
    tokens = bell_draw(splits[0], (NROWS, LENGTH, D), 1.0, 6.0, ((0, 4), (1, 8)))
    cotangent = bell_draw(splits[1], (NROWS, LENGTH, D), 1.0, 6.0, ((0, 4), (1, 8)))
    doc_lengths = jax.vmap(lambda own: uneven_parts(own, NDOC, LENGTH, LENGTH // 2, 2))(jax.random.split(splits[2], NROWS)).reshape((NROWS, NDOC)).astype(jnp.int32)
    norm_gain = jnp.clip(1.0 + 0.1 * jax.random.normal(splits[3], (D,), jnp.float32), 0.5, 1.5)
    in_proj = bell_draw(splits[4], (D, 2 * E), D ** -0.5, 0.1875)
    conv_weight = bell_draw(splits[5], (K, E), K ** -0.5, 3.0, (), jnp.float32)
    conv_bias = bell_draw(splits[6], (E,), 0.5, 3.0, (), jnp.float32)
    x_proj = bell_draw(splits[7], (E, R + 2 * N), E ** -0.5, 0.125)
    dt_proj = bell_draw(splits[8], (R, E), R ** -0.5, 0.75)
    dt_bias = jnp.clip(jax.random.uniform(splits[9], (E,), jnp.float32, -6.5, -2.5), -6.5, -2.5)
    a_log = jnp.clip(jax.random.uniform(splits[10], (N, E), jnp.float32, 0.0, 2.77), 0.0, 2.77)
    d_skip = jnp.clip(jax.random.uniform(splits[11], (E,), jnp.float32, 0.5, 1.5), 0.5, 1.5)
    out_proj = bell_draw(splits[12], (E, D), (E // 4) ** -0.5, 0.25)
    moment_norm_gain = bell_draw(splits[13], (D,), PARAMS ** -0.5, 0.0024414062, ((0, 8),), jnp.float32)
    moment_in_proj = bell_draw(splits[14], (D, 2 * E), PARAMS ** -0.5, 0.0024414062, ((0, 8),), jnp.float32)
    moment_conv_weight = bell_draw(splits[15], (K, E), PARAMS ** -0.5, 0.0024414062, ((1, 8),), jnp.float32)
    moment_conv_bias = bell_draw(splits[16], (E,), PARAMS ** -0.5, 0.0024414062, ((0, 8),), jnp.float32)
    moment_x_proj = bell_draw(splits[17], (E, R + 2 * N), PARAMS ** -0.5, 0.0024414062, ((0, 8),), jnp.float32)
    moment_dt_proj = bell_draw(splits[18], (R, E), PARAMS ** -0.5, 0.0024414062, ((1, 8),), jnp.float32)
    moment_dt_bias = bell_draw(splits[19], (E,), PARAMS ** -0.5, 0.0024414062, ((0, 8),), jnp.float32)
    moment_a_log = bell_draw(splits[20], (N, E), PARAMS ** -0.5, 0.0024414062, ((1, 8),), jnp.float32)
    moment_d_skip = bell_draw(splits[21], (E,), PARAMS ** -0.5, 0.0024414062, ((0, 8),), jnp.float32)
    moment_out_proj = bell_draw(splits[22], (E, D), PARAMS ** -0.5, 0.0024414062, ((0, 8),), jnp.float32)
    average_norm_gain = jnp.clip(1.0 + 0.1 * jax.random.normal(splits[23], (D,), jnp.float32), 0.5, 1.5)
    average_in_proj = bell_draw(splits[24], (D, 2 * E), D ** -0.5, 0.1875, ((0, 8),), jnp.float32)
    average_conv_weight = bell_draw(splits[25], (K, E), K ** -0.5, 3.0, ((1, 8),), jnp.float32)
    average_conv_bias = bell_draw(splits[26], (E,), 0.5, 3.0, ((0, 8),), jnp.float32)
    average_x_proj = bell_draw(splits[27], (E, R + 2 * N), E ** -0.5, 0.125, ((0, 8),), jnp.float32)
    average_dt_proj = bell_draw(splits[28], (R, E), R ** -0.5, 0.75, ((1, 8),), jnp.float32)
    average_dt_bias = jnp.clip(-6.5 + 8.0 * jax.random.uniform(splits[29], (E,), jnp.float32) ** block_levels(splits[29], (E,), ((0, 8),), -0.2, 0.2), -6.5, 1.5)
    average_a_log = jnp.clip(2.77 * jax.random.uniform(splits[30], (N, E), jnp.float32) ** block_levels(splits[30], (N, E), ((1, 8),), -0.2, 0.2), 0.0, 2.77)
    average_d_skip = jnp.clip(0.5 + 1.0 * jax.random.uniform(splits[31], (E,), jnp.float32) ** block_levels(splits[31], (E,), ((0, 8),), -0.2, 0.2), 0.5, 1.5)
    average_out_proj = bell_draw(splits[32], (E, D), (E // 4) ** -0.5, 0.25, ((0, 8),), jnp.float32)
    return {"tokens": tokens, "cotangent": cotangent, "doc_lengths": doc_lengths, "norm_gain": norm_gain, "in_proj": in_proj, "conv_weight": conv_weight, "conv_bias": conv_bias, "x_proj": x_proj, "dt_proj": dt_proj, "dt_bias": dt_bias, "a_log": a_log, "d_skip": d_skip, "out_proj": out_proj, "moment_norm_gain": moment_norm_gain, "moment_in_proj": moment_in_proj, "moment_conv_weight": moment_conv_weight, "moment_conv_bias": moment_conv_bias, "moment_x_proj": moment_x_proj, "moment_dt_proj": moment_dt_proj, "moment_dt_bias": moment_dt_bias, "moment_a_log": moment_a_log, "moment_d_skip": moment_d_skip, "moment_out_proj": moment_out_proj, "average_norm_gain": average_norm_gain, "average_in_proj": average_in_proj, "average_conv_weight": average_conv_weight, "average_conv_bias": average_conv_bias, "average_x_proj": average_x_proj, "average_dt_proj": average_dt_proj, "average_dt_bias": average_dt_bias, "average_a_log": average_a_log, "average_d_skip": average_d_skip, "average_out_proj": average_out_proj}


EPS = 1e-05
MOMENTUM = 0.9
AVERAGE = 0.9
RATES = (0.1, 0.03, 0.1, 0.1, 0.03, 0.03, 0.3, 0.3, 0.1, 0.03)
HIGHEST = lax.Precision.HIGHEST

@jax.custom_vjp
def low(v):
    return lax.optimization_barrier(v.astype(jnp.bfloat16)).astype(jnp.float32)

@jax.custom_vjp
def low_back(v):
    return v

def low_keep(v):
    return (low(v), None)

def low_pass(kept, grad):
    return (grad,)

def back_keep(v):
    return (v, None)

def back_low(kept, grad):
    return (low(grad),)
low.defvjp(low_keep, low_pass)
low_back.defvjp(back_keep, back_low)

def silu(values):
    return values * jax.nn.sigmoid(values)

def doc_tables(lengths_row, overall):
    ends = jnp.cumsum(lengths_row).astype(jnp.int32)
    starts = (ends - lengths_row).astype(jnp.int32)
    positions = jnp.arange(overall, dtype=jnp.int32)
    docid = lax.optimization_barrier(jnp.sum((positions[None, :] >= starts[:, None]).astype(jnp.int32), axis=0)).astype(jnp.int32)
    first = lax.optimization_barrier(jnp.sum((positions[None, :] == starts[:, None]).astype(jnp.float32), axis=0))
    return (docid, 1.0 - first)

def conv_masks(docid, window):
    masks = []
    for offset in range(window):
        filler = jnp.full((offset,), -1, jnp.int32)
        earlier = jnp.concatenate([filler, docid[:docid.shape[0] - offset]]).astype(jnp.int32)
        masks.append((earlier == docid).astype(jnp.float32))
    return jnp.stack(masks)

def scan_block(carry, pieces):
    carried, rates_t = carry

    def one_step(hidden, current):
        delta_now, act_now, inmat_now, outmat_now, keep_now = current
        hidden = keep_now * jnp.exp(delta_now[:, None] * rates_t) * hidden + (delta_now * act_now)[:, None] * inmat_now[None, :]
        return (hidden, lax.optimization_barrier(jnp.sum(hidden * outmat_now[None, :], axis=1)))
    carried, scanned = lax.scan(one_step, carried, pieces)
    return ((carried, rates_t), scanned)

def row_forward(weights, stream, keep, masks):
    norm_gain, in_proj, conv_weight, conv_bias, x_proj, dt_proj, dt_bias, a_log, d_skip, out_proj = weights
    length = stream.shape[0]
    inverse = lax.rsqrt(lax.optimization_barrier(jnp.mean(stream * stream, axis=1, keepdims=True)) + EPS)
    normed = low(stream * inverse * norm_gain)
    xz = low_back(low(jnp.dot(normed, in_proj, precision=HIGHEST)))
    inner = xz[:, :E]
    gates = xz[:, E:]
    pre_act = conv_bias[None, :] + jnp.zeros_like(inner)
    for offset in range(K):
        delayed = jnp.concatenate([jnp.zeros((offset, E), jnp.float32), inner[:length - offset]], axis=0)
        pre_act = pre_act + conv_weight[offset][None, :] * delayed * masks[offset][:, None]
    act = silu(pre_act)
    proj = low_back(jnp.dot(low(act), x_proj, precision=HIGHEST))
    rank_low = low(proj[:, :R])
    in_mat = proj[:, R:R + N]
    out_mat = proj[:, R + N:]
    delta_pre = low_back(jnp.dot(rank_low, dt_proj, precision=HIGHEST) + dt_bias[None, :])
    delta = jax.nn.softplus(delta_pre)
    rates = -jnp.exp(a_log).T
    block = math.gcd(length, 128)
    blocks = length // block
    pieces = (delta.reshape(blocks, block, E), act.reshape(blocks, block, E), in_mat.reshape(blocks, block, N), out_mat.reshape(blocks, block, N), keep.reshape(blocks, block))
    start_state = jnp.zeros((E, N), jnp.float32)
    carry_out, scanned = lax.scan(jax.checkpoint(scan_block), (start_state, rates), pieces)
    scanned = scanned.reshape(length, E)
    y_full = scanned + d_skip[None, :] * act
    gated = low_back(low(y_full * silu(gates)))
    return stream + jnp.dot(gated, out_proj, precision=HIGHEST)

def reference(tokens, cotangent, doc_lengths, norm_gain, in_proj, conv_weight, conv_bias, x_proj, dt_proj, dt_bias, a_log, d_skip, out_proj, moment_norm_gain, moment_in_proj, moment_conv_weight, moment_conv_bias, moment_x_proj, moment_dt_proj, moment_dt_bias, moment_a_log, moment_d_skip, moment_out_proj, average_norm_gain, average_in_proj, average_conv_weight, average_conv_bias, average_x_proj, average_dt_proj, average_dt_bias, average_a_log, average_d_skip, average_out_proj):
    weights = (norm_gain, in_proj.astype(jnp.float32), conv_weight, conv_bias, x_proj.astype(jnp.float32), dt_proj.astype(jnp.float32), dt_bias, a_log, d_skip, out_proj.astype(jnp.float32))

    def per_row(summed, current):
        row_tokens, row_cot, row_lengths = current
        docid, keep = doc_tables(row_lengths, LENGTH)
        masks = conv_masks(docid, K)
        stream = row_tokens.astype(jnp.float32)
        result, pullback = jax.vjp(lambda params, values: row_forward(params, values, keep, masks), weights, stream)
        grads, grad_stream = pullback(row_cot.astype(jnp.float32))
        summed = jax.tree.map(jnp.add, summed, grads)
        return (summed, (result, grad_stream))
    zeros = jax.tree.map(jnp.zeros_like, weights)
    grads, (outputs, input_grads) = lax.scan(per_row, zeros, (tokens, cotangent, doc_lengths))
    squares = jnp.float32(0.0)
    for member in grads:
        squares = squares + jnp.sum(member * member)
    grad_norm = jnp.sqrt(squares)
    shrink_by = 1.0 / jnp.maximum(grad_norm, 1.0)
    moments = (moment_norm_gain, moment_in_proj, moment_conv_weight, moment_conv_bias, moment_x_proj, moment_dt_proj, moment_dt_bias, moment_a_log, moment_d_skip, moment_out_proj)
    averages = (average_norm_gain, average_in_proj, average_conv_weight, average_conv_bias, average_x_proj, average_dt_proj, average_dt_bias, average_a_log, average_d_skip, average_out_proj)
    results = [outputs, input_grads, grad_norm]
    for ordinal in range(10):
        clipped = grads[ordinal] * shrink_by
        momentum_new = MOMENTUM * moments[ordinal] + clipped
        renewed = weights[ordinal] - RATES[ordinal] * math.sqrt(PARAMS) * (clipped + MOMENTUM * momentum_new)
        results += [momentum_new, renewed, AVERAGE * averages[ordinal] + (1.0 - AVERAGE) * renewed]
    return tuple(results)
```

```python
import math

import jax
import jax.numpy as jnp
from jax import lax
from jax.experimental import pallas as pl
from jax.experimental.pallas import tpu as pltpu
from jax.sharding import PartitionSpec as P

D = 1024
E = 2048
N = 16
R = 64
K = 4
PARAMS = 6667264

LANES = 128
RESET = 1e30


EPS = 1e-05
MOMENTUM = 0.9
AVERAGE = 0.9
RATES = (0.1, 0.03, 0.1, 0.1, 0.03, 0.03, 0.3, 0.3, 0.1, 0.03)


def silu(values):
    return values * jax.nn.sigmoid(values)


def silu_slope(values):
    sigmoid_of = jax.nn.sigmoid(values)
    return sigmoid_of * (1.0 + values * (1.0 - sigmoid_of))


def doc_tables(lengths_row, positions):
    ends = jnp.cumsum(lengths_row)
    starts = ends - lengths_row
    docid = jnp.sum((positions[None, :] >= starts[:, None]).astype(jnp.int32), axis=0)
    first = jnp.sum((positions[None, :] == starts[:, None]).astype(jnp.int32), axis=0)
    return (docid, first > 0)


def ends_kernel(ddec_ref, drive_ref, grady_ref, inb_ref, outb_ref, rates_ref, ends_ref):
    groups, steps = ddec_ref.shape[:2]
    columns = [pl.ds(group * LANES, LANES) for group in range(groups)]

    def step(t, carry):
        hidden, decayed, pulled = carry
        in_row, out_row = inb_ref[t], outb_ref[t]
        new = ([], [], [])
        for group in range(groups):
            here = (group, pl.ds(t, 1))
            decay = jnp.exp2(ddec_ref[here] * rates_ref[:, columns[group]])
            new[0].append(decay * hidden[group] + drive_ref[here] * in_row)
            product = decay * decayed[group]
            new[1].append(product)
            new[2].append(pulled[group] + product * (grady_ref[here] * out_row))
        return new

    zeros = [jnp.zeros((N, LANES), jnp.float32) for _ in range(groups)]
    ones = [jnp.ones((N, LANES), jnp.float32) for _ in range(groups)]
    hidden, _, pulled = lax.fori_loop(0, steps, step, (zeros, ones, zeros), unroll=4)
    for group in range(groups):
        ends_ref[:N, columns[group]] = hidden[group]
        ends_ref[N : 2 * N, columns[group]] = pulled[group]
        total = jnp.sum(ddec_ref[group], axis=0, keepdims=True)
        ends_ref[2 * N :, columns[group]] = jnp.broadcast_to(total, (8, LANES))


def scan_kernel(
    member_ref,
    ddec_ref,
    drive_ref,
    grady_ref,
    inb_ref,
    outb_ref,
    rates_ref,
    all_ref,
    scanned_ref,
    along_ref,
    decayed_ref,
    gin_ref,
    gout_ref,
    grates_ref,
    kept,
    first,
    second,
):
    groups, steps = ddec_ref.shape[:2]
    devices = all_ref.shape[0]
    member = member_ref[0]
    columns = [pl.ds(group * LANES, LANES) for group in range(groups)]
    half = N // 2

    @pl.when(pl.program_id(0) == 0)
    def _():
        gin_ref[...] = jnp.zeros_like(gin_ref)
        gout_ref[...] = jnp.zeros_like(gout_ref)

    def through(device, state, offset):
        factor = jnp.exp2(all_ref[device, 2 * N : 2 * N + 1, :] * rates_ref[...])
        return factor * state + all_ref[device, offset : offset + N, :]

    nothing = jnp.zeros(rates_ref.shape, jnp.float32)
    entering = lax.fori_loop(0, member, lambda d, s: through(d, s, 0), nothing)
    leaving = lax.fori_loop(
        0, devices - 1 - member, lambda d, s: through(devices - 1 - d, s, N), nothing
    )

    def fold(values):
        return values[:half] + values[half:]

    def forward(t, hidden):
        in_row, out_row = inb_ref[t], outb_ref[t]
        new = []
        for group in range(groups):
            here = (group, pl.ds(t, 1))
            decay = jnp.exp2(ddec_ref[here] * rates_ref[:, columns[group]])
            state = decay * hidden[group] + drive_ref[here] * in_row
            kept[t + 1, :, columns[group]] = state
            first[group, pl.ds(pl.multiple_of(t * half, half), half), :] = fold(state * out_row)
            new.append(state)
        return new

    kept[0] = entering
    begin = [entering[:, group * LANES : (group + 1) * LANES] for group in range(groups)]
    lax.fori_loop(0, steps, forward, begin, unroll=4)

    def collapse(source, target_ref):
        for group in range(groups):
            total = source[group, pl.ds(0, steps, stride=half), :]
            for place in range(1, half):
                total = total + source[group, pl.ds(place, steps, stride=half), :]
            target_ref[group] = total

    collapse(first, scanned_ref)

    def backward(back, carry):
        later, grates = carry
        t = steps - 1 - back
        in_row, out_row = inb_ref[t], outb_ref[t]
        gin, gout = gin_ref[t], gout_ref[t]
        new = ([], [])
        rows = pl.ds(pl.multiple_of(t * half, half), half)
        for group in range(groups):
            here = (group, pl.ds(t, 1))
            grady = grady_ref[here]
            delta = ddec_ref[here]
            rates = rates_ref[:, columns[group]]
            adjoint = grady * out_row + later[group]
            gout = gout + grady * kept[t + 1, :, columns[group]]
            gin = gin + adjoint * drive_ref[here]
            first[group, rows, :] = fold(adjoint * in_row)
            passed = jnp.exp2(delta * rates) * adjoint
            pulled = passed * kept[t, :, columns[group]]
            second[group, rows, :] = fold(pulled * rates)
            new[0].append(passed)
            new[1].append(grates[group] + pulled * delta)
        gin_ref[t] = gin
        gout_ref[t] = gout
        return new

    end = [leaving[:, group * LANES : (group + 1) * LANES] for group in range(groups)]
    zeros = [jnp.zeros((N, LANES), jnp.float32) for _ in range(groups)]
    _, grates = lax.fori_loop(0, steps, backward, (end, zeros), unroll=4)
    collapse(first, along_ref)
    collapse(second, decayed_ref)
    for group in range(groups):
        grates_ref[:, columns[group]] = grates[group]


def ends_of(ddec, drive, grady, inb, outb, rates, block):
    steps = ddec.shape[1]
    wide = pl.BlockSpec((block // LANES, steps, LANES), lambda b: (b, 0, 0))
    whole = pl.BlockSpec((steps, N, LANES), lambda b: (0, 0, 0))
    return pl.pallas_call(
        ends_kernel,
        grid=(E // block,),
        in_specs=[wide, wide, wide, whole, whole, pl.BlockSpec((N, block), lambda b: (0, b))],
        out_specs=pl.BlockSpec((2 * N + 8, block), lambda b: (0, b)),
        out_shape=jax.ShapeDtypeStruct((2 * N + 8, E), jnp.float32),
        compiler_params=pltpu.CompilerParams(vmem_limit_bytes=48 * 2**20),
        name="ends",
    )(ddec, drive, grady, inb, outb, rates)


def scan_of(member, ddec, drive, grady, inb, outb, rates, everyone, block):
    steps = ddec.shape[1]
    devices = everyone.shape[0]
    groups = block // LANES
    wide = pl.BlockSpec((block // LANES, steps, LANES), lambda b: (b, 0, 0))
    whole = pl.BlockSpec((steps, N, LANES), lambda b: (0, 0, 0))
    narrow = pl.BlockSpec((N, block), lambda b: (0, b))
    full = jax.ShapeDtypeStruct((E // LANES, steps, LANES), jnp.float32)
    spread = jax.ShapeDtypeStruct((steps, N, LANES), jnp.float32)
    return pl.pallas_call(
        scan_kernel,
        grid=(E // block,),
        in_specs=[
            pl.BlockSpec(memory_space=pltpu.SMEM),
            wide,
            wide,
            wide,
            whole,
            whole,
            narrow,
            pl.BlockSpec((devices, 2 * N + 8, block), lambda b: (0, 0, b)),
        ],
        out_specs=[wide, wide, wide, whole, whole, narrow],
        out_shape=[full, full, full, spread, spread, jax.ShapeDtypeStruct((N, E), jnp.float32)],
        scratch_shapes=[
            pltpu.VMEM((steps + 1, N, block), jnp.float32),
            pltpu.VMEM((groups, steps * N // 2, LANES), jnp.float32),
            pltpu.VMEM((groups, steps * N // 2, LANES), jnp.float32),
        ],
        compiler_params=pltpu.CompilerParams(vmem_limit_bytes=48 * 2**20),
        name="scan",
    )(member, ddec, drive, grady, inb, outb, rates, everyone)


def local(
    tokens,
    cotangent,
    doc_lengths,
    norm_gain,
    in_proj,
    conv_weight,
    conv_bias,
    x_proj,
    dt_proj,
    dt_bias,
    a_log,
    d_skip,
    out_proj,
    moment_norm_gain,
    moment_in_proj,
    moment_conv_weight,
    moment_conv_bias,
    moment_x_proj,
    moment_dt_proj,
    moment_dt_bias,
    moment_a_log,
    moment_d_skip,
    moment_out_proj,
    average_norm_gain,
    average_in_proj,
    average_conv_weight,
    average_conv_bias,
    average_x_proj,
    average_dt_proj,
    average_dt_bias,
    average_a_log,
    average_d_skip,
    average_out_proj,
):
    devices = lax.axis_size("seq")
    member_id = lax.axis_index("seq")
    channels = E // devices
    begin = member_id * channels
    stream = tokens[0].astype(jnp.float32)
    steps = stream.shape[0]
    length = steps * devices
    cot_low = cotangent[0]
    inverse = lax.rsqrt(jnp.mean(stream * stream, axis=1, keepdims=True) + EPS)
    normed = (stream * inverse * norm_gain[None, :]).astype(jnp.bfloat16)
    normed_all = lax.all_gather(normed, "seq", axis=0, tiled=True)
    cot_all = lax.all_gather(cot_low, "seq", axis=0, tiled=True)
    xz = jnp.dot(normed, in_proj, preferred_element_type=jnp.float32).astype(jnp.bfloat16)
    halo = lax.ppermute(
        xz[steps - 8 :, :E], "seq", [(i, i + 1) for i in range(devices - 1)]
    )
    back_gated = lax.dot_general(
        cot_low, out_proj, (((1,), (1,)), ((), ())), preferred_element_type=jnp.float32
    ).astype(jnp.bfloat16)
    positions = member_id * steps + jnp.arange(-8, steps + 8, dtype=jnp.int32)
    docid, starting = doc_tables(doc_lengths[0], positions)
    reset = starting[8 : 8 + steps, None]
    masks = []
    for offset in range(K):
        linked = (docid[8:] == docid[8 - offset : steps + 16 - offset]) & (
            positions[8 - offset : steps + 16 - offset] >= 0
        )
        masks.append((linked & (positions[8:] < length)).astype(jnp.float32)[:, None])
    padded = jnp.concatenate([halo, xz[:, :E]], axis=0).astype(jnp.float32)
    gates = xz[:, E:].astype(jnp.float32)
    pre_act = jnp.broadcast_to(conv_bias[None, :], (steps, E))
    for offset in range(K):
        pre_act = (
            pre_act
            + conv_weight[offset][None, :]
            * padded[8 - offset : 8 - offset + steps]
            * masks[offset][:steps]
        )
    act = silu(pre_act)
    act_low = act.astype(jnp.bfloat16)
    proj = jnp.dot(act_low, x_proj, preferred_element_type=jnp.float32)
    rank_low = proj[:, :R].astype(jnp.bfloat16)
    in_mat = proj[:, R : R + N]
    out_mat = proj[:, R + N :]
    delta_pre = (
        jnp.dot(rank_low, dt_proj, preferred_element_type=jnp.float32) + dt_bias[None, :]
    )
    delta = jax.nn.softplus(delta_pre)
    rates = -jnp.exp(a_log)
    scaled_rates = rates * (1.0 / math.log(2.0))
    ddec = jnp.where(reset, RESET, delta)
    drive = delta * act
    silu_gate = silu(gates)
    chan_back = back_gated.astype(jnp.float32)
    grad_y = chan_back * silu_gate
    inb = jnp.broadcast_to(in_mat[:, :, None], (steps, N, LANES))
    outb = jnp.broadcast_to(out_mat[:, :, None], (steps, N, LANES))
    def grouped(values):
        return jnp.transpose(values.reshape(steps, E // LANES, LANES), (1, 0, 2))

    def flat(values):
        return jnp.transpose(values, (1, 0, 2)).reshape(steps, E)

    ddec, drive, grady_rows = grouped(ddec), grouped(drive), grouped(grad_y)
    ends = ends_of(ddec, drive, grady_rows, inb, outb, scaled_rates, 512)
    everyone = lax.all_gather(ends, "seq", axis=0)
    member_word = jnp.reshape(member_id, (1,)).astype(jnp.int32)
    scanned, along_in, pulled_sum, gin, gout, grad_rates = scan_of(
        member_word, ddec, drive, grady_rows, inb, outb, scaled_rates, everyone, 512
    )
    scanned, along_in, pulled_sum = flat(scanned), flat(along_in), flat(pulled_sum)
    y_full = scanned + d_skip[None, :] * act
    gated = (y_full * silu_gate).astype(jnp.bfloat16)
    block_output = (
        stream + jnp.dot(gated, out_proj, preferred_element_type=jnp.float32)
    )[None]
    gated_mine = lax.all_to_all(gated, "seq", split_axis=1, concat_axis=0, tiled=True)
    grad_out_proj = lax.dot_general(
        gated_mine, cot_all, (((0,), (0,)), ((), ())), preferred_element_type=jnp.float32
    )
    grad_gates = chan_back * y_full * silu_slope(gates)
    grad_dskip = jnp.sum(grad_y * act, axis=0)
    grad_in_mat = jnp.sum(gin, axis=2)
    grad_out_mat = jnp.sum(gout, axis=2)
    grad_delta = along_in * act + pulled_sum * math.log(2.0)
    grad_alog = grad_rates * rates
    grad_pre = (grad_delta * jax.nn.sigmoid(delta_pre)).astype(jnp.bfloat16)
    grad_dtbias = jnp.sum(grad_pre.astype(jnp.float32), axis=0)
    grad_dtproj = lax.dot_general(
        rank_low, grad_pre, (((0,), (0,)), ((), ())), preferred_element_type=jnp.float32
    )
    rank_back = lax.dot_general(
        grad_pre, dt_proj, (((1,), (1,)), ((), ())), preferred_element_type=jnp.float32
    )
    proj_back = jnp.concatenate([rank_back, grad_in_mat, grad_out_mat], axis=1).astype(jnp.bfloat16)
    grad_xproj = lax.dot_general(
        act_low, proj_back, (((0,), (0,)), ((), ())), preferred_element_type=jnp.float32
    )
    grad_act = (
        grad_y * d_skip[None, :]
        + along_in * delta
        + lax.dot_general(
            proj_back, x_proj, (((1,), (1,)), ((), ())), preferred_element_type=jnp.float32
        )
    )
    grad_pre_act = grad_act * silu_slope(pre_act)
    ahead = lax.ppermute(
        grad_pre_act[:8], "seq", [(i + 1, i) for i in range(devices - 1)]
    )
    extended = jnp.concatenate([grad_pre_act, ahead], axis=0)
    grad_conv_bias = jnp.sum(grad_pre_act, axis=0)
    grad_inner = jnp.zeros_like(gates)
    conv_rows = []
    for offset in range(K):
        masked = extended * masks[offset]
        conv_rows.append(
            jnp.sum(masked[:steps] * padded[8 - offset : 8 - offset + steps], axis=0)
        )
        grad_inner = grad_inner + conv_weight[offset][None, :] * masked[offset : offset + steps]
    grad_convw = jnp.stack(conv_rows)
    back_xz = jnp.stack([grad_inner, grad_gates]).astype(jnp.bfloat16)
    back_mine = lax.all_to_all(back_xz, "seq", split_axis=2, concat_axis=1, tiled=True)
    grad_normed = lax.dot_general(
        back_xz[0], in_proj[:, :E], (((1,), (1,)), ((), ())), preferred_element_type=jnp.float32
    ) + lax.dot_general(
        back_xz[1], in_proj[:, E:], (((1,), (1,)), ((), ())), preferred_element_type=jnp.float32
    )
    grad_in_proj = jnp.einsum(
        "td,ktc->dkc", normed_all, back_mine, preferred_element_type=jnp.float32
    )
    grad_gain = jnp.sum(grad_normed * stream * inverse, axis=0)
    scaled = grad_normed * norm_gain[None, :]
    input_grad = (
        cot_low.astype(jnp.float32)
        + inverse * scaled
        - stream * inverse * inverse * inverse * jnp.mean(scaled * stream, axis=1, keepdims=True)
    )
    summed = lax.psum((grad_in_proj, grad_out_proj), "rows")
    in_share = lax.all_to_all(summed[0], "seq", split_axis=0, concat_axis=2, tiled=True)
    small = jnp.concatenate(
        [
            grad_xproj.T,
            grad_dtproj,
            grad_alog,
            grad_convw,
            grad_conv_bias[None],
            grad_dtbias[None],
            grad_dskip[None],
            jnp.pad(
                grad_gain.reshape(devices, D // devices),
                ((0, 0), (0, channels - D // devices)),
            ).reshape(1, E),
        ],
        axis=0,
    )
    small = lax.psum(small, "rows")
    small = lax.psum_scatter(small, "seq", scatter_dimension=1, tiled=True)
    parts = []
    at = 0
    for count in (R + 2 * N, R, N, K, 1, 1, 1, 1):
        parts.append(small[at : at + count])
        at += count
    owner_grads = (
        parts[7][0, : D // devices],
        in_share.reshape(D // devices, 2 * E),
        parts[3],
        parts[4][0],
        parts[0].T,
        parts[1],
        parts[5][0],
        parts[2],
        parts[6][0],
        summed[1],
    )
    conv_mine = lax.dynamic_slice_in_dim(conv_weight, begin, channels, 1)
    cbias_mine = lax.dynamic_slice_in_dim(conv_bias, begin, channels, 0)
    xproj_mine = lax.dynamic_slice_in_dim(x_proj, begin, channels, 0)
    dtproj_mine = lax.dynamic_slice_in_dim(dt_proj, begin, channels, 1)
    dtbias_mine = lax.dynamic_slice_in_dim(dt_bias, begin, channels, 0)
    alog_mine = lax.dynamic_slice_in_dim(a_log, begin, channels, 1)
    dskip_mine = lax.dynamic_slice_in_dim(d_skip, begin, channels, 0)
    squares = jnp.float32(0.0)
    for member in owner_grads:
        squares = squares + jnp.sum(member * member)
    squares_all = lax.psum(squares, "seq")
    grad_norm = jnp.sqrt(squares_all)
    shrink_by = 1.0 / jnp.maximum(grad_norm, 1.0)
    gain_rows = D // devices
    outer_rows = E // devices
    mine_weights = (
        lax.dynamic_slice_in_dim(norm_gain, member_id * gain_rows, gain_rows, 0),
        lax.dynamic_slice_in_dim(in_proj, member_id * gain_rows, gain_rows, 0).astype(jnp.float32),
        conv_mine,
        cbias_mine,
        xproj_mine.astype(jnp.float32),
        dtproj_mine.astype(jnp.float32),
        dtbias_mine,
        alog_mine,
        dskip_mine,
        lax.dynamic_slice_in_dim(out_proj, member_id * outer_rows, outer_rows, 0).astype(
            jnp.float32
        ),
    )
    moments = (
        moment_norm_gain,
        moment_in_proj,
        moment_conv_weight,
        moment_conv_bias,
        moment_x_proj,
        moment_dt_proj,
        moment_dt_bias,
        moment_a_log,
        moment_d_skip,
        moment_out_proj,
    )
    averages = (
        average_norm_gain,
        average_in_proj,
        average_conv_weight,
        average_conv_bias,
        average_x_proj,
        average_dt_proj,
        average_dt_bias,
        average_a_log,
        average_d_skip,
        average_out_proj,
    )
    results = [block_output, input_grad[None], grad_norm]
    for ordinal in range(10):
        clipped = owner_grads[ordinal] * shrink_by
        momentum_new = MOMENTUM * moments[ordinal] + clipped
        renewed = mine_weights[ordinal] - RATES[ordinal] * math.sqrt(PARAMS) * (
            clipped + MOMENTUM * momentum_new
        )
        results += [momentum_new, renewed, AVERAGE * averages[ordinal] + (1.0 - AVERAGE) * renewed]
    return tuple(results)


def solution(mesh):
    return jax.shard_map(
        local,
        mesh=mesh,
        in_specs=(
            P("rows", "seq", None),
            P("rows", "seq", None),
            P("rows", None),
            P(),
            P(),
            P(),
            P(),
            P(),
            P(),
            P(),
            P(),
            P(),
            P(),
            P("seq"),
            P("seq", None),
            P(None, "seq"),
            P("seq"),
            P("seq", None),
            P(None, "seq"),
            P("seq"),
            P(None, "seq"),
            P("seq"),
            P("seq", None),
            P("seq"),
            P("seq", None),
            P(None, "seq"),
            P("seq"),
            P("seq", None),
            P(None, "seq"),
            P("seq"),
            P(None, "seq"),
            P("seq"),
            P("seq", None),
        ),
        out_specs=(
            P("rows", "seq", None),
            P("rows", "seq", None),
            P(),
            P("seq"),
            P("seq"),
            P("seq"),
            P("seq", None),
            P("seq", None),
            P("seq", None),
            P(None, "seq"),
            P(None, "seq"),
            P(None, "seq"),
            P("seq"),
            P("seq"),
            P("seq"),
            P("seq", None),
            P("seq", None),
            P("seq", None),
            P(None, "seq"),
            P(None, "seq"),
            P(None, "seq"),
            P("seq"),
            P("seq"),
            P("seq"),
            P(None, "seq"),
            P(None, "seq"),
            P(None, "seq"),
            P("seq"),
            P("seq"),
            P("seq"),
            P("seq", None),
            P("seq", None),
            P("seq", None),
        ),
        check_vma=False,
    )
```

```python
import functools
import math

import jax
import jax.numpy as jnp
from jax import lax
from jax.experimental import pallas as pl
from jax.experimental.pallas import tpu as pltpu
from jax.sharding import PartitionSpec as P

D = 1024
E = 2048
N = 16
R = 64
K = 4
PARAMS = 6667264

LANES = 128
RESET = 1e30
MESH = pl.DeviceIdType.MESH


EPS = 1e-05
MOMENTUM = 0.9
AVERAGE = 0.9
RATES = (0.1, 0.03, 0.1, 0.1, 0.03, 0.03, 0.3, 0.3, 0.1, 0.03)


def silu(values):
    return values * jax.nn.sigmoid(values)


def silu_slope(values):
    sigmoid_of = jax.nn.sigmoid(values)
    return sigmoid_of * (1.0 + values * (1.0 - sigmoid_of))


def doc_tables(lengths_row, positions):
    ends = jnp.cumsum(lengths_row)
    starts = ends - lengths_row
    docid = jnp.sum((positions[None, :] >= starts[:, None]).astype(jnp.int32), axis=0)
    first = jnp.sum((positions[None, :] == starts[:, None]).astype(jnp.int32), axis=0)
    return (docid, first > 0)


def ends_kernel(ddec_ref, drive_ref, grady_ref, inb_ref, outb_ref, rates_ref, ends_ref, sums_ref):
    groups, steps = ddec_ref.shape[:2]
    columns = [pl.ds(group * LANES, LANES) for group in range(groups)]

    def step(t, carry):
        hidden, decayed, pulled = carry
        in_row, out_row = inb_ref[t], outb_ref[t]
        new = ([], [], [])
        for group in range(groups):
            here = (group, pl.ds(t, 1))
            decay = jnp.exp2(ddec_ref[here] * rates_ref[:, columns[group]])
            new[0].append(decay * hidden[group] + drive_ref[here] * in_row)
            product = decay * decayed[group]
            new[1].append(product)
            new[2].append(pulled[group] + product * (grady_ref[here] * out_row))
        return new

    zeros = [jnp.zeros((N, LANES), jnp.float32) for _ in range(groups)]
    ones = [jnp.ones((N, LANES), jnp.float32) for _ in range(groups)]
    hidden, _, pulled = lax.fori_loop(0, steps, step, (zeros, ones, zeros), unroll=4)
    for group in range(groups):
        ends_ref[0, :, columns[group]] = hidden[group].astype(ends_ref.dtype)
        ends_ref[1, :, columns[group]] = pulled[group].astype(ends_ref.dtype)
        sums_ref[pl.ds(pl.program_id(0) * groups + group, 1), :] = jnp.sum(
            ddec_ref[group], axis=0, keepdims=True
        )


def scan_kernel(
    member_ref,
    ddec_ref,
    drive_ref,
    grady_ref,
    inb_ref,
    outb_ref,
    rates_ref,
    all_ref,
    sums_ref,
    scanned_ref,
    along_ref,
    decayed_ref,
    gin_ref,
    gout_ref,
    grates_ref,
    kept,
    first,
    second,
):
    groups, steps = ddec_ref.shape[:2]
    devices = all_ref.shape[0]
    base = pl.program_id(0) * groups
    member = member_ref[0]
    columns = [pl.ds(group * LANES, LANES) for group in range(groups)]
    half = N // 2

    @pl.when(pl.program_id(0) == 0)
    def _():
        gin_ref[...] = jnp.zeros_like(gin_ref)
        gout_ref[...] = jnp.zeros_like(gout_ref)

    def through(device, states):
        new = []
        for group in range(groups):
            total = sums_ref[device, pl.ds(base + group, 1), :]
            factor = jnp.exp2(total * rates_ref[:, columns[group]])
            new.append(
                factor * states[group]
                + all_ref[device, :, columns[group]].astype(jnp.float32)
            )
        return new

    zeros = [jnp.zeros((N, LANES), jnp.float32) for _ in range(groups)]
    entering = lax.fori_loop(0, member, through, zeros)
    leaving = lax.fori_loop(
        0, devices - 1 - member, lambda d, s: through(devices - 1 - d, s), zeros
    )

    def fold(values):
        return values[:half] + values[half:]

    def forward(t, hidden):
        in_row, out_row = inb_ref[t], outb_ref[t]
        new = []
        for group in range(groups):
            here = (group, pl.ds(t, 1))
            decay = jnp.exp2(ddec_ref[here] * rates_ref[:, columns[group]])
            state = decay * hidden[group] + drive_ref[here] * in_row
            kept[t + 1, :, columns[group]] = state
            first[group, pl.ds(pl.multiple_of(t * half, half), half), :] = fold(state * out_row)
            new.append(state)
        return new

    for group in range(groups):
        kept[0, :, columns[group]] = entering[group]
    lax.fori_loop(0, steps, forward, entering, unroll=4)

    def collapse(source, target_ref):
        for group in range(groups):
            total = source[group, pl.ds(0, steps, stride=half), :]
            for place in range(1, half):
                total = total + source[group, pl.ds(place, steps, stride=half), :]
            target_ref[group] = total

    collapse(first, scanned_ref)

    def backward(back, carry):
        later, grates = carry
        t = steps - 1 - back
        in_row, out_row = inb_ref[t], outb_ref[t]
        gin, gout = gin_ref[t], gout_ref[t]
        new = ([], [])
        rows = pl.ds(pl.multiple_of(t * half, half), half)
        for group in range(groups):
            here = (group, pl.ds(t, 1))
            grady = grady_ref[here]
            delta = ddec_ref[here]
            rates = rates_ref[:, columns[group]]
            adjoint = grady * out_row + later[group]
            gout = gout + grady * kept[t + 1, :, columns[group]]
            gin = gin + adjoint * drive_ref[here]
            first[group, rows, :] = fold(adjoint * in_row)
            passed = jnp.exp2(delta * rates) * adjoint
            pulled = passed * kept[t, :, columns[group]]
            second[group, rows, :] = fold(pulled * rates)
            new[0].append(passed)
            new[1].append(grates[group] + pulled * delta)
        gin_ref[t] = gin
        gout_ref[t] = gout
        return new

    _, grates = lax.fori_loop(0, steps, backward, (leaving, zeros), unroll=4)
    collapse(first, along_ref)
    collapse(second, decayed_ref)
    for group in range(groups):
        grates_ref[:, columns[group]] = grates[group]


def ends_of(ddec, drive, grady, inb, outb, rates, block):
    steps = ddec.shape[1]
    wide = pl.BlockSpec((block // LANES, steps, LANES), lambda b: (b, 0, 0))
    whole = pl.BlockSpec((steps, N, LANES), lambda b: (0, 0, 0))
    return pl.pallas_call(
        ends_kernel,
        grid=(E // block,),
        in_specs=[wide, wide, wide, whole, whole, pl.BlockSpec((N, block), lambda b: (0, b))],
        out_specs=[
            pl.BlockSpec((2, N, block), lambda b: (0, 0, b)),
            pl.BlockSpec((E // LANES, LANES), lambda b: (0, 0)),
        ],
        out_shape=[
            jax.ShapeDtypeStruct((2, N, E), jnp.bfloat16),
            jax.ShapeDtypeStruct((E // LANES, LANES), jnp.float32),
        ],
        compiler_params=pltpu.CompilerParams(vmem_limit_bytes=48 * 2**20),
        name="ends",
    )(ddec, drive, grady, inb, outb, rates)


def scan_of(member, ddec, drive, grady, inb, outb, rates, everyone, sums, block):
    steps = ddec.shape[1]
    devices = everyone.shape[0]
    groups = block // LANES
    wide = pl.BlockSpec((block // LANES, steps, LANES), lambda b: (b, 0, 0))
    whole = pl.BlockSpec((steps, N, LANES), lambda b: (0, 0, 0))
    narrow = pl.BlockSpec((N, block), lambda b: (0, b))
    full = jax.ShapeDtypeStruct((E // LANES, steps, LANES), jnp.float32)
    spread = jax.ShapeDtypeStruct((steps, N, LANES), jnp.float32)
    return pl.pallas_call(
        scan_kernel,
        grid=(E // block,),
        in_specs=[
            pl.BlockSpec(memory_space=pltpu.SMEM),
            wide,
            wide,
            wide,
            whole,
            whole,
            narrow,
            pl.BlockSpec((devices, N, block), lambda b: (0, 0, b)),
            pl.BlockSpec(sums.shape, lambda b: (0, 0, 0)),
        ],
        out_specs=[wide, wide, wide, whole, whole, narrow],
        out_shape=[full, full, full, spread, spread, jax.ShapeDtypeStruct((N, E), jnp.float32)],
        scratch_shapes=[
            pltpu.VMEM((steps + 1, N, block), jnp.float32),
            pltpu.VMEM((groups, steps * N // 2, LANES), jnp.float32),
            pltpu.VMEM((groups, steps * N // 2, LANES), jnp.float32),
        ],
        compiler_params=pltpu.CompilerParams(vmem_limit_bytes=48 * 2**20),
        name="scan",
    )(member, ddec, drive, grady, inb, outb, rates, everyone, sums)


def partner(axis, offset):
    size = lax.axis_size(axis)
    return lax.rem(lax.axis_index(axis) + offset, size)


def greet(counts):
    barrier = pltpu.get_barrier_semaphore()
    total = 0
    for axis, count in counts:
        for offset in range(1, count):
            pl.semaphore_signal(
                barrier, inc=1, device_id={axis: partner(axis, offset)}, device_id_type=MESH
            )
        total += count - 1
    pl.semaphore_wait(barrier, total)


def push(source, target, semaphores, at, axis, offset):
    copy = pltpu.make_async_remote_copy(
        src_ref=source,
        dst_ref=target,
        send_sem=semaphores.at[0, at],
        recv_sem=semaphores.at[1, at],
        device_id={axis: partner(axis, offset)},
        device_id_type=MESH,
    )
    copy.start()
    return copy


def states_kernel(devices, ends_ref, sums_ref, ends_out, sums_out, wires, sum_wires):
    member = lax.axis_index("seq")
    greet((("seq", devices),))
    copies = []
    for offset in range(1, devices):
        wrapped = (member + offset) // devices
        copies.append(
            push(ends_ref.at[wrapped], ends_out.at[member], wires, offset - 1, "seq", offset)
        )
        copies.append(push(sums_ref, sums_out.at[member], sum_wires, offset - 1, "seq", offset))
    ends_out[member] = ends_ref[0]
    sums_out[member] = sums_ref[...]
    for copy in copies:
        copy.wait()


def states_of(ends, sums, devices):
    return pl.pallas_call(
        functools.partial(states_kernel, devices),
        in_specs=[pl.BlockSpec(memory_space=pltpu.VMEM)] * 2,
        out_specs=[pl.BlockSpec(memory_space=pltpu.VMEM)] * 2,
        out_shape=[
            jax.ShapeDtypeStruct((devices,) + ends.shape[1:], ends.dtype),
            jax.ShapeDtypeStruct((devices,) + sums.shape, sums.dtype),
        ],
        scratch_shapes=[
            pltpu.SemaphoreType.DMA((2, devices - 1)),
            pltpu.SemaphoreType.DMA((2, devices - 1)),
        ],
        compiler_params=pltpu.CompilerParams(
            collective_id=0, has_side_effects=True, vmem_limit_bytes=48 * 2**20
        ),
        name="states",
    )(ends, sums)


def trade_kernel(devices, gated_ref, back_ref, gated_out, back_out, wires, back_wires, local):
    member = lax.axis_index("seq")
    steps = gated_ref.shape[0]
    channels = gated_ref.shape[1] // devices
    rows = pl.ds(pl.multiple_of(member * steps, steps), steps)
    greet((("seq", devices),))
    copies = []
    for offset in range(1, devices):
        columns = pl.ds(pl.multiple_of(partner("seq", offset) * channels, channels), channels)
        copies.append(
            push(
                back_ref.at[:, :, columns],
                back_out.at[:, rows, :],
                back_wires,
                offset - 1,
                "seq",
                offset,
            )
        )
        copies.append(
            push(
                gated_ref.at[:, columns], gated_out.at[rows, :], wires, offset - 1, "seq", offset
            )
        )
    columns = pl.ds(pl.multiple_of(member * channels, channels), channels)
    own = pltpu.make_async_copy(back_ref.at[:, :, columns], back_out.at[:, rows, :], local.at[0])
    own_gated = pltpu.make_async_copy(
        gated_ref.at[:, columns], gated_out.at[rows, :], local.at[1]
    )
    own.start()
    own_gated.start()
    own.wait()
    own_gated.wait()
    for copy in copies:
        copy.wait()


def trade(gated, back, devices):
    steps = gated.shape[0]
    channels = gated.shape[1] // devices
    return pl.pallas_call(
        functools.partial(trade_kernel, devices),
        in_specs=[pl.BlockSpec(memory_space=pltpu.VMEM)] * 2,
        out_specs=[pl.BlockSpec(memory_space=pltpu.VMEM)] * 2,
        out_shape=[
            jax.ShapeDtypeStruct((steps * devices, channels), gated.dtype),
            jax.ShapeDtypeStruct((2, steps * devices, channels), back.dtype),
        ],
        scratch_shapes=[
            pltpu.SemaphoreType.DMA((2, devices - 1)),
            pltpu.SemaphoreType.DMA((2, devices - 1)),
            pltpu.SemaphoreType.DMA((2,)),
        ],
        compiler_params=pltpu.CompilerParams(
            collective_id=1, has_side_effects=True, vmem_limit_bytes=48 * 2**20
        ),
        name="trade",
    )(gated, back)


def grads_kernel(
    nrows,
    devices,
    normed_ref,
    back_ref,
    gated_ref,
    cot_ref,
    small_ref,
    gin_out,
    gout_out,
    small_out,
    norm_out,
    small_got,
    small_part,
    small_seq,
    gout_sum,
    gout_low,
    gout_got,
    gin_sum,
    gin_low,
    gin_got,
    gin_part,
    norm_seq,
    norm_rows,
    row_wires,
    seq_wires,
):
    row = lax.axis_index("rows")
    member = lax.axis_index("seq")
    few = small_ref.shape[0] // nrows
    outer = gout_out.shape[0] // nrows
    inner = gin_part.shape[0] // devices
    channels = small_out.shape[1]
    greet((("rows", nrows), ("seq", devices)))

    def share(index, size):
        return pl.ds(pl.multiple_of(index * size, size), size)

    def to_rows(kind, make):
        return [
            push(*make(partner("rows", offset), offset - 1), row_wires.at[kind], offset - 1, "rows", offset)
            for offset in range(1, nrows)
        ]

    def to_seq(kind, make):
        return [
            push(*make(partner("seq", offset), offset - 1), seq_wires.at[kind], offset - 1, "seq", offset)
            for offset in range(1, devices)
        ]

    def settle(copies):
        for copy in copies:
            copy.wait()

    def squares(values):
        return jnp.sum(values * values, axis=0, keepdims=True)

    small_moves = to_rows(
        0, lambda other, at: (small_ref.at[share(other, few)], small_got.at[at])
    )
    gout_sum[...] = lax.dot_general(
        gated_ref[...], cot_ref[...], (((0,), (0,)), ((), ())), preferred_element_type=jnp.float32
    )
    gout_low[...] = gout_sum[...].astype(jnp.bfloat16)
    gout_moves = to_rows(
        1, lambda other, at: (gout_low.at[share(other, outer)], gout_got.at[at])
    )
    for half in range(2):
        result = lax.dot_general(
            normed_ref[...],
            back_ref[half],
            (((0,), (0,)), ((), ())),
            preferred_element_type=jnp.float32,
        )
        wide = gin_sum.shape[2]
        for place in range(nrows // 2):
            piece = result[:, place * wide : (place + 1) * wide]
            gin_sum[half * (nrows // 2) + place] = piece
            gin_low[half * (nrows // 2) + place] = piece.astype(jnp.bfloat16)
    gin_moves = to_rows(2, lambda other, at: (gin_low.at[other], gin_got.at[at]))

    settle(small_moves)
    total = small_ref[share(row, few), :].astype(jnp.float32)
    for at in range(nrows - 1):
        total = total + small_got[at].astype(jnp.float32)
    small_part[...] = total.astype(jnp.bfloat16)
    small_moves = to_seq(
        0, lambda other, at: (small_part.at[:, share(other, channels)], small_seq.at[at])
    )

    settle(gout_moves)
    total = gout_sum[share(row, outer), :]
    for at in range(nrows - 1):
        total = total + gout_got[at].astype(jnp.float32)
    gout_out[share(row, outer), :] = total.astype(jnp.bfloat16)
    gout_moves = to_rows(
        3,
        lambda other, at: (gout_out.at[share(row, outer)], gout_out.at[share(row, outer)]),
    )
    norm = jnp.sum(squares(total), axis=1, keepdims=True)

    settle(gin_moves)
    total = gin_sum[row]
    for at in range(nrows - 1):
        total = total + gin_got[at].astype(jnp.float32)
    gin_part[...] = total.astype(jnp.bfloat16)
    gin_moves = to_seq(
        1, lambda other, at: (gin_part.at[share(other, inner)], gin_out.at[row, member])
    )
    gin_out[row, member] = gin_part[share(member, inner), :]
    norm = norm + jnp.sum(squares(total), axis=1, keepdims=True)

    settle(small_moves)
    total = small_part[:, share(member, channels)].astype(jnp.float32)
    for at in range(devices - 1):
        total = total + small_seq[at].astype(jnp.float32)
    small_out[share(row, few), :] = total.astype(jnp.bfloat16)
    small_moves = to_rows(
        4, lambda other, at: (small_out.at[share(row, few)], small_out.at[share(row, few)])
    )
    norm = norm + jnp.sum(squares(total), axis=1, keepdims=True)
    norm_seq[member] = jnp.broadcast_to(norm, (8, LANES))
    norm_moves = to_seq(2, lambda other, at: (norm_seq.at[member], norm_seq.at[member]))

    settle(gin_moves)
    gin_moves = to_rows(5, lambda other, at: (gin_out.at[row], gin_out.at[row]))
    settle(norm_moves)
    norm_rows[row] = jnp.sum(norm_seq[...], axis=0)
    norm_moves = to_rows(6, lambda other, at: (norm_rows.at[row], norm_rows.at[row]))
    settle(norm_moves)
    norm_out[...] = jnp.sqrt(jnp.sum(norm_rows[...], axis=0))
    settle(small_moves)
    settle(gout_moves)
    settle(gin_moves)


def grads_of(normed_all, back_mine, gated_mine, cot_all, small, nrows, devices):
    depth = normed_all.shape[1]
    channels = gated_mine.shape[1]
    wide = 2 * channels // nrows
    few = small.shape[0] // nrows
    low = jnp.bfloat16
    return pl.pallas_call(
        functools.partial(grads_kernel, nrows, devices),
        in_specs=[pl.BlockSpec(memory_space=pltpu.VMEM)] * 5,
        out_specs=[pl.BlockSpec(memory_space=pltpu.VMEM)] * 4,
        out_shape=[
            jax.ShapeDtypeStruct((nrows, devices, depth // devices, wide), low),
            jax.ShapeDtypeStruct((channels, depth), low),
            jax.ShapeDtypeStruct((small.shape[0], channels), low),
            jax.ShapeDtypeStruct((8, LANES), jnp.float32),
        ],
        scratch_shapes=[
            pltpu.VMEM((nrows - 1, few, E), low),
            pltpu.VMEM((few, E), low),
            pltpu.VMEM((devices - 1, few, channels), low),
            pltpu.VMEM((channels, depth), jnp.float32),
            pltpu.VMEM((channels, depth), low),
            pltpu.VMEM((nrows - 1, channels // nrows, depth), low),
            pltpu.VMEM((nrows, depth, wide), jnp.float32),
            pltpu.VMEM((nrows, depth, wide), low),
            pltpu.VMEM((nrows - 1, depth, wide), low),
            pltpu.VMEM((depth, wide), low),
            pltpu.VMEM((devices, 8, LANES), jnp.float32),
            pltpu.VMEM((nrows, 8, LANES), jnp.float32),
            pltpu.SemaphoreType.DMA((7, 2, nrows - 1)),
            pltpu.SemaphoreType.DMA((3, 2, devices - 1)),
        ],
        compiler_params=pltpu.CompilerParams(
            collective_id=2, has_side_effects=True, vmem_limit_bytes=56 * 2**20
        ),
        name="grads",
    )(normed_all, back_mine, gated_mine, cot_all, small)


def local(
    tokens,
    cotangent,
    doc_lengths,
    norm_gain,
    in_proj,
    conv_weight,
    conv_bias,
    x_proj,
    dt_proj,
    dt_bias,
    a_log,
    d_skip,
    out_proj,
    moment_norm_gain,
    moment_in_proj,
    moment_conv_weight,
    moment_conv_bias,
    moment_x_proj,
    moment_dt_proj,
    moment_dt_bias,
    moment_a_log,
    moment_d_skip,
    moment_out_proj,
    average_norm_gain,
    average_in_proj,
    average_conv_weight,
    average_conv_bias,
    average_x_proj,
    average_dt_proj,
    average_dt_bias,
    average_a_log,
    average_d_skip,
    average_out_proj,
):
    devices = lax.axis_size("seq")
    member_id = lax.axis_index("seq")
    channels = E // devices
    begin = member_id * channels
    stream = tokens[0].astype(jnp.float32)
    steps = stream.shape[0]
    length = steps * devices
    cot_low = cotangent[0]
    inverse = lax.rsqrt(jnp.mean(stream * stream, axis=1, keepdims=True) + EPS)
    normed = (stream * inverse * norm_gain[None, :]).astype(jnp.bfloat16)
    normed_all = lax.all_gather(normed, "seq", axis=0, tiled=True)
    cot_all = lax.all_gather(cot_low, "seq", axis=0, tiled=True)
    xz = jnp.dot(normed, in_proj, preferred_element_type=jnp.float32).astype(jnp.bfloat16)
    halo = lax.ppermute(
        xz[steps - 8 :, :E], "seq", [(i, i + 1) for i in range(devices - 1)]
    )
    back_gated = lax.dot_general(
        cot_low, out_proj, (((1,), (1,)), ((), ())), preferred_element_type=jnp.float32
    ).astype(jnp.bfloat16)
    positions = member_id * steps + jnp.arange(-8, steps + 8, dtype=jnp.int32)
    docid, starting = doc_tables(doc_lengths[0], positions)
    reset = starting[8 : 8 + steps, None]
    masks = []
    for offset in range(K):
        linked = (docid[8:] == docid[8 - offset : steps + 16 - offset]) & (
            positions[8 - offset : steps + 16 - offset] >= 0
        )
        masks.append((linked & (positions[8:] < length)).astype(jnp.float32)[:, None])
    padded = jnp.concatenate([halo, xz[:, :E]], axis=0).astype(jnp.float32)
    gates = xz[:, E:].astype(jnp.float32)
    pre_act = jnp.broadcast_to(conv_bias[None, :], (steps, E))
    for offset in range(K):
        pre_act = (
            pre_act
            + conv_weight[offset][None, :]
            * padded[8 - offset : 8 - offset + steps]
            * masks[offset][:steps]
        )
    act = silu(pre_act)
    act_low = act.astype(jnp.bfloat16)
    proj = jnp.dot(act_low, x_proj, preferred_element_type=jnp.float32)
    rank_low = proj[:, :R].astype(jnp.bfloat16)
    in_mat = proj[:, R : R + N]
    out_mat = proj[:, R + N :]
    delta_pre = (
        jnp.dot(rank_low, dt_proj, preferred_element_type=jnp.float32) + dt_bias[None, :]
    )
    delta = jax.nn.softplus(delta_pre)
    rates = -jnp.exp(a_log)
    scaled_rates = rates * (1.0 / math.log(2.0))
    ddec = jnp.where(reset, RESET, delta)
    drive = delta * act
    silu_gate = silu(gates)
    chan_back = back_gated.astype(jnp.float32)
    grad_y = chan_back * silu_gate
    inb = jnp.broadcast_to(in_mat[:, :, None], (steps, N, LANES))
    outb = jnp.broadcast_to(out_mat[:, :, None], (steps, N, LANES))
    def grouped(values):
        return jnp.transpose(values.reshape(steps, E // LANES, LANES), (1, 0, 2))

    def flat(values):
        return jnp.transpose(values, (1, 0, 2)).reshape(steps, E)

    ddec, drive, grady_rows = grouped(ddec), grouped(drive), grouped(grad_y)
    ends, sums = ends_of(ddec, drive, grady_rows, inb, outb, scaled_rates, 512)
    everyone, all_sums = states_of(ends, sums, devices)
    member_word = jnp.reshape(member_id, (1,)).astype(jnp.int32)
    scanned, along_in, pulled_sum, gin, gout, grad_rates = scan_of(
        member_word, ddec, drive, grady_rows, inb, outb, scaled_rates, everyone, all_sums, 512
    )
    scanned, along_in, pulled_sum = flat(scanned), flat(along_in), flat(pulled_sum)
    y_full = scanned + d_skip[None, :] * act
    gated = (y_full * silu_gate).astype(jnp.bfloat16)
    block_output = (
        stream + jnp.dot(gated, out_proj, preferred_element_type=jnp.float32)
    )[None]
    grad_gates = chan_back * y_full * silu_slope(gates)
    grad_dskip = jnp.sum(grad_y * act, axis=0)
    grad_in_mat = jnp.sum(gin, axis=2)
    grad_out_mat = jnp.sum(gout, axis=2)
    grad_delta = along_in * act + pulled_sum * math.log(2.0)
    grad_alog = grad_rates * rates
    grad_pre = (grad_delta * jax.nn.sigmoid(delta_pre)).astype(jnp.bfloat16)
    grad_dtbias = jnp.sum(grad_pre.astype(jnp.float32), axis=0)
    grad_dtproj = lax.dot_general(
        rank_low, grad_pre, (((0,), (0,)), ((), ())), preferred_element_type=jnp.float32
    )
    rank_back = lax.dot_general(
        grad_pre, dt_proj, (((1,), (1,)), ((), ())), preferred_element_type=jnp.float32
    )
    proj_back = jnp.concatenate([rank_back, grad_in_mat, grad_out_mat], axis=1).astype(jnp.bfloat16)
    grad_xproj = lax.dot_general(
        act_low, proj_back, (((0,), (0,)), ((), ())), preferred_element_type=jnp.float32
    )
    grad_act = (
        grad_y * d_skip[None, :]
        + along_in * delta
        + lax.dot_general(
            proj_back, x_proj, (((1,), (1,)), ((), ())), preferred_element_type=jnp.float32
        )
    )
    grad_pre_act = grad_act * silu_slope(pre_act)
    ahead = lax.ppermute(
        grad_pre_act[:8], "seq", [(i + 1, i) for i in range(devices - 1)]
    )
    extended = jnp.concatenate([grad_pre_act, ahead], axis=0)
    grad_conv_bias = jnp.sum(grad_pre_act, axis=0)
    grad_inner = jnp.zeros_like(gates)
    conv_rows = []
    for offset in range(K):
        masked = extended * masks[offset]
        conv_rows.append(
            jnp.sum(masked[:steps] * padded[8 - offset : 8 - offset + steps], axis=0)
        )
        grad_inner = grad_inner + conv_weight[offset][None, :] * masked[offset : offset + steps]
    grad_convw = jnp.stack(conv_rows)
    back_xz = jnp.stack([grad_inner, grad_gates]).astype(jnp.bfloat16)
    grad_normed = lax.dot_general(
        back_xz[0], in_proj[:, :E], (((1,), (1,)), ((), ())), preferred_element_type=jnp.float32
    ) + lax.dot_general(
        back_xz[1], in_proj[:, E:], (((1,), (1,)), ((), ())), preferred_element_type=jnp.float32
    )
    grad_gain = jnp.sum(grad_normed * stream * inverse, axis=0)
    scaled = grad_normed * norm_gain[None, :]
    input_grad = (
        cot_low.astype(jnp.float32)
        + inverse * scaled
        - stream * inverse * inverse * inverse * jnp.mean(scaled * stream, axis=1, keepdims=True)
    )
    small = jnp.concatenate(
        [
            grad_xproj.T,
            grad_dtproj,
            grad_alog,
            grad_convw,
            grad_conv_bias[None],
            grad_dtbias[None],
            grad_dskip[None],
            jnp.pad(
                grad_gain.reshape(devices, D // devices),
                ((0, 0), (0, channels - D // devices)),
            ).reshape(1, E),
            jnp.zeros((8, E), jnp.float32),
        ],
        axis=0,
    )
    nrows = lax.axis_size("rows")
    if channels % LANES == 0 and 2 * channels == nrows * LANES:
        gated_mine, back_mine = trade(gated, back_xz, devices)
        gin_parts, gout_share, small, norm_tile = grads_of(
            normed_all, back_mine, gated_mine, cot_all, small.astype(jnp.bfloat16), nrows, devices
        )
        gin_share = jnp.transpose(
            gin_parts.reshape(2, nrows // 2, devices, D // devices, LANES), (3, 0, 2, 1, 4)
        ).reshape(D // devices, 2 * E)
        grad_norm = norm_tile[0, 0]
    else:
        gated_mine = lax.all_to_all(gated, "seq", split_axis=1, concat_axis=0, tiled=True)
        back_mine = lax.all_to_all(back_xz, "seq", split_axis=2, concat_axis=1, tiled=True)
        gout_share = lax.psum(
            lax.dot_general(
                gated_mine, cot_all, (((0,), (0,)), ((), ())), preferred_element_type=jnp.float32
            ),
            "rows",
        )
        gin_share = lax.psum(
            jnp.einsum("td,ktc->dkc", normed_all, back_mine, preferred_element_type=jnp.float32),
            "rows",
        )
        gin_share = lax.all_to_all(
            gin_share, "seq", split_axis=0, concat_axis=2, tiled=True
        ).reshape(D // devices, 2 * E)
        small = lax.psum(small, "rows")
        small = lax.psum_scatter(small, "seq", scatter_dimension=1, tiled=True)
        squares = jnp.sum(gin_share * gin_share) + jnp.sum(gout_share * gout_share)
        grad_norm = jnp.sqrt(lax.psum(squares + jnp.sum(small * small), "seq"))
    small = small.astype(jnp.float32)
    parts = []
    at = 0
    for count in (R + 2 * N, R, N, K, 1, 1, 1, 1):
        parts.append(small[at : at + count])
        at += count
    owner_grads = (
        parts[7][0, : D // devices],
        gin_share.astype(jnp.float32),
        parts[3],
        parts[4][0],
        parts[0].T,
        parts[1],
        parts[5][0],
        parts[2],
        parts[6][0],
        gout_share.astype(jnp.float32),
    )
    conv_mine = lax.dynamic_slice_in_dim(conv_weight, begin, channels, 1)
    cbias_mine = lax.dynamic_slice_in_dim(conv_bias, begin, channels, 0)
    xproj_mine = lax.dynamic_slice_in_dim(x_proj, begin, channels, 0)
    dtproj_mine = lax.dynamic_slice_in_dim(dt_proj, begin, channels, 1)
    dtbias_mine = lax.dynamic_slice_in_dim(dt_bias, begin, channels, 0)
    alog_mine = lax.dynamic_slice_in_dim(a_log, begin, channels, 1)
    dskip_mine = lax.dynamic_slice_in_dim(d_skip, begin, channels, 0)
    shrink_by = 1.0 / jnp.maximum(grad_norm, 1.0)
    gain_rows = D // devices
    outer_rows = E // devices
    mine_weights = (
        lax.dynamic_slice_in_dim(norm_gain, member_id * gain_rows, gain_rows, 0),
        lax.dynamic_slice_in_dim(in_proj, member_id * gain_rows, gain_rows, 0).astype(jnp.float32),
        conv_mine,
        cbias_mine,
        xproj_mine.astype(jnp.float32),
        dtproj_mine.astype(jnp.float32),
        dtbias_mine,
        alog_mine,
        dskip_mine,
        lax.dynamic_slice_in_dim(out_proj, member_id * outer_rows, outer_rows, 0).astype(
            jnp.float32
        ),
    )
    moments = (
        moment_norm_gain,
        moment_in_proj,
        moment_conv_weight,
        moment_conv_bias,
        moment_x_proj,
        moment_dt_proj,
        moment_dt_bias,
        moment_a_log,
        moment_d_skip,
        moment_out_proj,
    )
    averages = (
        average_norm_gain,
        average_in_proj,
        average_conv_weight,
        average_conv_bias,
        average_x_proj,
        average_dt_proj,
        average_dt_bias,
        average_a_log,
        average_d_skip,
        average_out_proj,
    )
    results = [block_output, input_grad[None], grad_norm]
    for ordinal in range(10):
        clipped = owner_grads[ordinal] * shrink_by
        momentum_new = MOMENTUM * moments[ordinal] + clipped
        renewed = mine_weights[ordinal] - RATES[ordinal] * math.sqrt(PARAMS) * (
            clipped + MOMENTUM * momentum_new
        )
        results += [momentum_new, renewed, AVERAGE * averages[ordinal] + (1.0 - AVERAGE) * renewed]
    return tuple(results)


def solution(mesh):
    return jax.shard_map(
        local,
        mesh=mesh,
        in_specs=(
            P("rows", "seq", None),
            P("rows", "seq", None),
            P("rows", None),
            P(),
            P(),
            P(),
            P(),
            P(),
            P(),
            P(),
            P(),
            P(),
            P(),
            P("seq"),
            P("seq", None),
            P(None, "seq"),
            P("seq"),
            P("seq", None),
            P(None, "seq"),
            P("seq"),
            P(None, "seq"),
            P("seq"),
            P("seq", None),
            P("seq"),
            P("seq", None),
            P(None, "seq"),
            P("seq"),
            P("seq", None),
            P(None, "seq"),
            P("seq"),
            P(None, "seq"),
            P("seq"),
            P("seq", None),
        ),
        out_specs=(
            P("rows", "seq", None),
            P("rows", "seq", None),
            P(),
            P("seq"),
            P("seq"),
            P("seq"),
            P("seq", None),
            P("seq", None),
            P("seq", None),
            P(None, "seq"),
            P(None, "seq"),
            P(None, "seq"),
            P("seq"),
            P("seq"),
            P("seq"),
            P("seq", None),
            P("seq", None),
            P("seq", None),
            P(None, "seq"),
            P(None, "seq"),
            P(None, "seq"),
            P("seq"),
            P("seq"),
            P("seq"),
            P(None, "seq"),
            P(None, "seq"),
            P(None, "seq"),
            P("seq"),
            P("seq"),
            P("seq"),
            P("seq", None),
            P("seq", None),
            P("seq", None),
        ),
        check_vma=False,
    )
```

```python
import functools
import math

import jax
import jax.numpy as jnp
from jax import lax
from jax.experimental import pallas as pl
from jax.experimental.pallas import tpu as pltpu
from jax.sharding import PartitionSpec as P

D = 1024
E = 2048
N = 16
R = 64
K = 4
PARAMS = 6667264

LANES = 128
RESET = 1e30
MESH = pl.DeviceIdType.MESH


EPS = 1e-05
MOMENTUM = 0.9
AVERAGE = 0.9
RATES = (0.1, 0.03, 0.1, 0.1, 0.03, 0.03, 0.3, 0.3, 0.1, 0.03)


def silu(values):
    return values * jax.nn.sigmoid(values)


def silu_slope(values):
    sigmoid_of = jax.nn.sigmoid(values)
    return sigmoid_of * (1.0 + values * (1.0 - sigmoid_of))


def doc_tables(lengths_row, positions):
    ends = jnp.cumsum(lengths_row)
    starts = ends - lengths_row
    docid = jnp.sum((positions[None, :] >= starts[:, None]).astype(jnp.int32), axis=0)
    first = jnp.sum((positions[None, :] == starts[:, None]).astype(jnp.int32), axis=0)
    return (docid, first > 0)


def scan_kernel(
    member_ref,
    ddec_ref,
    drive_ref,
    grady_ref,
    inb_ref,
    outb_ref,
    rates_ref,
    all_ref,
    sums_ref,
    scanned_ref,
    along_ref,
    decayed_ref,
    gin_ref,
    gout_ref,
    grates_ref,
    kept,
    first,
    second,
):
    groups, steps = ddec_ref.shape[:2]
    devices = all_ref.shape[0]
    base = pl.program_id(0) * groups
    member = member_ref[0]
    columns = [pl.ds(group * LANES, LANES) for group in range(groups)]
    half = N // 2

    @pl.when(pl.program_id(0) == 0)
    def _():
        gin_ref[...] = jnp.zeros_like(gin_ref)
        gout_ref[...] = jnp.zeros_like(gout_ref)

    def through(device, states):
        new = []
        for group in range(groups):
            total = sums_ref[device, pl.ds(base + group, 1), :]
            factor = jnp.exp2(total * rates_ref[:, columns[group]])
            new.append(
                factor * states[group]
                + all_ref[device, 0, :, columns[group]].astype(jnp.float32)
            )
        return new

    zeros = [jnp.zeros((N, LANES), jnp.float32) for _ in range(groups)]
    reach = devices // 2
    entering = lax.fori_loop(jnp.maximum(member - reach, 0), member, through, zeros)
    last = jnp.minimum(member + reach, devices - 1)
    leaving = lax.fori_loop(0, last - member, lambda d, s: through(last - d, s), zeros)

    def fold(values):
        return values[:half] + values[half:]

    def forward(t, hidden):
        in_row, out_row = inb_ref[t], outb_ref[t]
        new = []
        for group in range(groups):
            here = (group, pl.ds(t, 1))
            decay = jnp.exp2(ddec_ref[here] * rates_ref[:, columns[group]])
            state = decay * hidden[group] + drive_ref[here] * in_row
            kept[t + 1, :, columns[group]] = state
            first[group, pl.ds(pl.multiple_of(t * half, half), half), :] = fold(state * out_row)
            new.append(state)
        return new

    for group in range(groups):
        kept[0, :, columns[group]] = entering[group]
    lax.fori_loop(0, steps, forward, entering, unroll=4)

    def collapse(source, target_ref):
        for group in range(groups):
            total = source[group, pl.ds(0, steps, stride=half), :]
            for place in range(1, half):
                total = total + source[group, pl.ds(place, steps, stride=half), :]
            target_ref[group] = total

    collapse(first, scanned_ref)

    def backward(back, carry):
        later, grates = carry
        t = steps - 1 - back
        in_row, out_row = inb_ref[t], outb_ref[t]
        gin, gout = gin_ref[t], gout_ref[t]
        new = ([], [])
        rows = pl.ds(pl.multiple_of(t * half, half), half)
        for group in range(groups):
            here = (group, pl.ds(t, 1))
            grady = grady_ref[here]
            delta = ddec_ref[here]
            rates = rates_ref[:, columns[group]]
            adjoint = grady * out_row + later[group]
            gout = gout + grady * kept[t + 1, :, columns[group]]
            gin = gin + adjoint * drive_ref[here]
            first[group, rows, :] = fold(adjoint * in_row)
            passed = jnp.exp2(delta * rates) * adjoint
            pulled = passed * kept[t, :, columns[group]]
            second[group, rows, :] = fold(pulled * rates)
            new[0].append(passed)
            new[1].append(grates[group] + pulled * delta)
        gin_ref[t] = gin
        gout_ref[t] = gout
        return new

    _, grates = lax.fori_loop(0, steps, backward, (leaving, zeros), unroll=4)
    collapse(first, along_ref)
    collapse(second, decayed_ref)
    for group in range(groups):
        grates_ref[:, columns[group]] = grates[group]


def scan_of(member, ddec, drive, grady, inb, outb, rates, everyone, sums, block):
    steps = ddec.shape[1]
    devices = everyone.shape[0]
    groups = block // LANES
    wide = pl.BlockSpec((block // LANES, steps, LANES), lambda b: (b, 0, 0))
    whole = pl.BlockSpec((steps, N, LANES), lambda b: (0, 0, 0))
    narrow = pl.BlockSpec((N, block), lambda b: (0, b))
    full = jax.ShapeDtypeStruct((E // LANES, steps, LANES), jnp.float32)
    spread = jax.ShapeDtypeStruct((steps, N, LANES), jnp.float32)
    return pl.pallas_call(
        scan_kernel,
        grid=(E // block,),
        in_specs=[
            pl.BlockSpec(memory_space=pltpu.SMEM),
            wide,
            wide,
            wide,
            whole,
            whole,
            narrow,
            pl.BlockSpec((devices, 1, N, block), lambda b: (0, b, 0, 0)),
            pl.BlockSpec(sums.shape, lambda b: (0, 0, 0)),
        ],
        out_specs=[wide, wide, wide, whole, whole, narrow],
        out_shape=[full, full, full, spread, spread, jax.ShapeDtypeStruct((N, E), jnp.float32)],
        scratch_shapes=[
            pltpu.VMEM((steps + 1, N, block), jnp.float32),
            pltpu.VMEM((groups, steps * N // 2, LANES), jnp.float32),
            pltpu.VMEM((groups, steps * N // 2, LANES), jnp.float32),
        ],
        compiler_params=pltpu.CompilerParams(vmem_limit_bytes=48 * 2**20),
        name="scan",
    )(member, ddec, drive, grady, inb, outb, rates, everyone, sums)


def partner(axis, offset):
    size = lax.axis_size(axis)
    return lax.rem(lax.axis_index(axis) + offset, size)


def greet(counts):
    barrier = pltpu.get_barrier_semaphore()
    total = 0
    for axis, count in counts:
        for offset in range(1, count):
            pl.semaphore_signal(
                barrier, inc=1, device_id={axis: partner(axis, offset)}, device_id_type=MESH
            )
        total += count - 1
    pl.semaphore_wait(barrier, total)


def push(source, target, semaphores, at, axis, offset):
    copy = pltpu.make_async_remote_copy(
        src_ref=source,
        dst_ref=target,
        send_sem=semaphores.at[0, at],
        recv_sem=semaphores.at[1, at],
        device_id={axis: partner(axis, offset)},
        device_id_type=MESH,
    )
    copy.start()
    return copy


def span(index, size):
    return pl.ds(index * size, size)


def softplus(values):
    return jnp.maximum(values, 0.0) + jnp.log1p(jnp.exp(-jnp.abs(values)))


def front_kernel(
    devices,
    starts_ref,
    tokens_ref,
    cot_ref,
    gain_ref,
    in_proj_ref,
    out_proj_ref,
    conv_ref,
    cbias_ref,
    x_proj_ref,
    dt_proj_ref,
    dtbias_ref,
    rates_ref,
    normed_ref,
    inner_ref,
    gates_ref,
    back_ref,
    pre_act_ref,
    delta_pre_ref,
    ddec_ref,
    drive_ref,
    grady_ref,
    rank_ref,
    inb_ref,
    outb_ref,
    ends_out,
    sums_out,
    in_proj_buf,
    out_proj_buf,
    padded,
    docid,
    masks,
    proj,
    ends,
    loads,
    halo_wires,
    wires,
    sum_wires,
):
    member = lax.axis_index("seq")
    steps = tokens_ref.shape[0]
    groups = E // LANES
    chunk = 4 * LANES
    chunks = E // chunk
    reach = devices // 2
    halo = inner_ref.shape[0] - steps
    in_loads = [
        pltpu.make_async_copy(
            in_proj_ref.at[:, span(at, chunk)], in_proj_buf.at[at], loads.at[at]
        )
        for at in range(2 * chunks)
    ]
    out_loads = [
        pltpu.make_async_copy(
            out_proj_ref.at[span(at, chunk), :], out_proj_buf.at[at], loads.at[2 * chunks + at]
        )
        for at in range(chunks)
    ]
    for load in in_loads + out_loads:
        load.start()
    barrier = pltpu.get_barrier_semaphore()
    for offset in range(1, devices):
        pl.semaphore_signal(
            barrier, inc=1, device_id={"seq": partner("seq", offset)}, device_id_type=MESH
        )

    stream = tokens_ref[...].astype(jnp.float32)
    inverse = lax.rsqrt(jnp.mean(stream * stream, axis=1, keepdims=True) + EPS)
    normed_ref[...] = (stream * inverse * gain_ref[...]).astype(jnp.bfloat16)

    places = member * steps - 8 + lax.broadcasted_iota(jnp.int32, docid.shape, 0)
    count = jnp.zeros(docid.shape, jnp.int32)
    first = jnp.zeros(docid.shape, jnp.float32)
    for index in range(starts_ref.shape[0]):
        count = count + jnp.where(places >= starts_ref[index], 1, 0)
        first = jnp.where(places == starts_ref[index], 1.0, first)
    docid[...] = count
    masks[0] = first[8 : 8 + steps]
    for offset in range(1, K):
        masks[offset] = jnp.where(
            docid[8 - offset : 8 - offset + steps, :] == docid[8 : 8 + steps, :], 1.0, 0.0
        )

    def project(at):
        in_loads[at].wait()
        return jnp.dot(
            normed_ref[...], in_proj_buf[at], preferred_element_type=jnp.float32
        ).astype(jnp.bfloat16)

    for at in range(chunks):
        inner_ref[halo:, span(at, chunk)] = project(at)
    pl.semaphore_wait(barrier, devices - 1)
    halo_copy = pltpu.make_async_remote_copy(
        src_ref=inner_ref.at[steps : steps + halo, :],
        dst_ref=inner_ref.at[0:halo, :],
        send_sem=halo_wires.at[0],
        recv_sem=halo_wires.at[1],
        device_id={"seq": partner("seq", 1)},
        device_id_type=MESH,
    )

    @pl.when(member < devices - 1)
    def _():
        halo_copy.start()

    @pl.when(member == 0)
    def _():
        inner_ref[0:halo, :] = jnp.zeros((halo, E), jnp.bfloat16)

    for at in range(chunks):
        gates_ref[:, span(at, chunk)] = project(chunks + at)
    for at in range(chunks):
        out_loads[at].wait()
        back_ref[:, span(at, chunk)] = lax.dot_general(
            cot_ref[...],
            out_proj_buf[at],
            (((1,), (1,)), ((), ())),
            preferred_element_type=jnp.float32,
        ).astype(jnp.bfloat16)

    @pl.when(member < devices - 1)
    def _():
        halo_copy.wait_send()

    @pl.when(member > 0)
    def _():
        halo_copy.wait_recv()

    proj[...] = jnp.zeros_like(proj)
    for at in range(chunks):
        lows = []
        for group in range(4 * at, 4 * at + 4):
            columns = span(group, LANES)
            padded[...] = inner_ref[halo - 8 :, columns].astype(jnp.float32)
            value = cbias_ref[:, columns] + conv_ref[0:1, columns] * padded[8:, :]
            for offset in range(1, K):
                value = (
                    value
                    + conv_ref[offset : offset + 1, columns]
                    * padded[8 - offset : 8 - offset + steps, :]
                    * masks[offset]
                )
            pre_act_ref[group] = value
            act = silu(value)
            drive_ref[group] = act
            lows.append(act.astype(jnp.bfloat16))
        proj[...] += jnp.dot(
            jnp.concatenate(lows, axis=1),
            x_proj_ref[span(at, chunk), :],
            preferred_element_type=jnp.float32,
        )
    rank_ref[...] = proj[:, :R].astype(jnp.bfloat16)
    inb_ref[...] = jnp.broadcast_to(proj[:, R : R + N][:, :, None], inb_ref.shape)
    outb_ref[...] = jnp.broadcast_to(proj[:, R + N :][:, :, None], outb_ref.shape)

    def later(distance, at):
        return pltpu.make_async_remote_copy(
            src_ref=ends.at[0, at],
            dst_ref=ends_out.at[member, at],
            send_sem=wires.at[0, 0, at, distance - 1],
            recv_sem=wires.at[0, 1, at, distance - 1],
            device_id={"seq": partner("seq", distance)},
            device_id_type=MESH,
        )

    def earlier(distance, at):
        return pltpu.make_async_remote_copy(
            src_ref=ends.at[1, at],
            dst_ref=ends_out.at[member, at],
            send_sem=wires.at[1, 0, at, distance - 1],
            recv_sem=wires.at[1, 1, at, distance - 1],
            device_id={"seq": partner("seq", devices - distance)},
            device_id_type=MESH,
        )

    def sums_to(distance, side):
        offset = distance if side == 0 else devices - distance
        return pltpu.make_async_remote_copy(
            src_ref=sums_out.at[member],
            dst_ref=sums_out.at[member],
            send_sem=sum_wires.at[side, 0, distance - 1],
            recv_sem=sum_wires.at[side, 1, distance - 1],
            device_id={"seq": partner("seq", offset)},
            device_id_type=MESH,
        )

    for at in range(chunks):
        delta_pre = (
            jnp.dot(
                rank_ref[...], dt_proj_ref[:, span(at, chunk)], preferred_element_type=jnp.float32
            )
            + dtbias_ref[:, span(at, chunk)]
        )
        for place in range(4):
            group = 4 * at + place
            columns = span(group, LANES)
            here = delta_pre[:, place * LANES : (place + 1) * LANES]
            delta = softplus(here)
            delta_pre_ref[group] = here
            drive_ref[group] = drive_ref[group] * delta
            ddec = jnp.where(masks[0] > 0.0, RESET, delta)
            ddec_ref[group] = ddec
            sums_out[member, group : group + 1, :] = jnp.sum(ddec, axis=0, keepdims=True)
            grady_ref[group] = back_ref[:, columns].astype(jnp.float32) * silu(
                gates_ref[:, columns].astype(jnp.float32)
            )

        def step(t, carry):
            hidden, decayed, pulled = carry
            in_row, out_row = inb_ref[t], outb_ref[t]
            new = ([], [], [])
            for place in range(4):
                here = (4 * at + place, pl.ds(t, 1))
                decay = jnp.exp2(ddec_ref[here] * rates_ref[:, span(4 * at + place, LANES)])
                new[0].append(decay * hidden[place] + drive_ref[here] * in_row)
                product = decay * decayed[place]
                new[1].append(product)
                new[2].append(pulled[place] + product * (grady_ref[here] * out_row))
            return new

        zeros = [jnp.zeros((N, LANES), jnp.float32) for _ in range(4)]
        ones = [jnp.ones((N, LANES), jnp.float32) for _ in range(4)]
        hidden, _, pulled = lax.fori_loop(0, steps, step, (zeros, ones, zeros), unroll=4)
        ends[0, at] = jnp.concatenate(hidden, axis=1).astype(jnp.bfloat16)
        ends[1, at] = jnp.concatenate(pulled, axis=1).astype(jnp.bfloat16)
        for distance in range(1, reach + 1):

            @pl.when(member + distance < devices)
            def _():
                later(distance, at).start()

            @pl.when(member >= distance)
            def _():
                earlier(distance, at).start()

    for distance in range(1, reach + 1):

        @pl.when(member + distance < devices)
        def _():
            sums_to(distance, 0).start()

        @pl.when(member >= distance)
        def _():
            sums_to(distance, 1).start()

    for distance in range(1, reach + 1):

        @pl.when(member + distance < devices)
        def _():
            for at in range(chunks):
                later(distance, at).wait_send()
                earlier(distance, at).wait_recv()
            sums_to(distance, 0).wait_send()
            sums_to(distance, 1).wait_recv()

        @pl.when(member >= distance)
        def _():
            for at in range(chunks):
                earlier(distance, at).wait_send()
                later(distance, at).wait_recv()
            sums_to(distance, 1).wait_send()
            sums_to(distance, 0).wait_recv()


def front_of(starts, tokens, cot, gain, in_proj, out_proj, conv, cbias, x_proj, dt_proj, dtbias, rates, devices):
    steps = tokens.shape[0]
    groups = E // LANES
    chunk = 4 * LANES
    chunks = E // chunk
    reach = devices // 2
    halo = 16
    low = jnp.bfloat16
    vmem = pl.BlockSpec(memory_space=pltpu.VMEM)
    grouped = jax.ShapeDtypeStruct((groups, steps, LANES), jnp.float32)
    spread = jax.ShapeDtypeStruct((steps, N, LANES), jnp.float32)
    return pl.pallas_call(
        functools.partial(front_kernel, devices),
        in_specs=[pl.BlockSpec(memory_space=pltpu.SMEM)]
        + [vmem] * 3
        + [pl.BlockSpec(memory_space=pl.ANY)] * 2
        + [vmem] * 6,
        out_specs=[vmem] * 14,
        out_shape=[
            jax.ShapeDtypeStruct((steps, D), low),
            jax.ShapeDtypeStruct((steps + halo, E), low),
            jax.ShapeDtypeStruct((steps, E), low),
            jax.ShapeDtypeStruct((steps, E), low),
            grouped,
            grouped,
            grouped,
            grouped,
            grouped,
            jax.ShapeDtypeStruct((steps, R), low),
            spread,
            spread,
            jax.ShapeDtypeStruct((devices, chunks, N, chunk), low),
            jax.ShapeDtypeStruct((devices, groups, LANES), jnp.float32),
        ],
        scratch_shapes=[
            pltpu.VMEM((2 * chunks, D, chunk), low),
            pltpu.VMEM((chunks, chunk, D), low),
            pltpu.VMEM((steps + 8, LANES), jnp.float32),
            pltpu.VMEM((steps + 16, LANES), jnp.int32),
            pltpu.VMEM((K, steps, LANES), jnp.float32),
            pltpu.VMEM((steps, R + 2 * N), jnp.float32),
            pltpu.VMEM((2, chunks, N, chunk), low),
            pltpu.SemaphoreType.DMA((3 * chunks,)),
            pltpu.SemaphoreType.DMA((2,)),
            pltpu.SemaphoreType.DMA((2, 2, chunks, reach)),
            pltpu.SemaphoreType.DMA((2, 2, reach)),
        ],
        compiler_params=pltpu.CompilerParams(
            collective_id=0, has_side_effects=True, vmem_limit_bytes=60 * 2**20
        ),
        name="front",
    )(starts, tokens, cot, gain, in_proj, out_proj, conv, cbias, x_proj, dt_proj, dtbias, rates)


def trade_kernel(devices, gated_ref, back_ref, gated_out, back_out, wires, back_wires, local):
    member = lax.axis_index("seq")
    steps = gated_ref.shape[0]
    channels = gated_ref.shape[1] // devices
    rows = pl.ds(pl.multiple_of(member * steps, steps), steps)
    greet((("seq", devices),))
    copies = []
    for offset in range(1, devices):
        columns = pl.ds(pl.multiple_of(partner("seq", offset) * channels, channels), channels)
        copies.append(
            push(
                back_ref.at[:, :, columns],
                back_out.at[:, rows, :],
                back_wires,
                offset - 1,
                "seq",
                offset,
            )
        )
        copies.append(
            push(
                gated_ref.at[:, columns], gated_out.at[rows, :], wires, offset - 1, "seq", offset
            )
        )
    columns = pl.ds(pl.multiple_of(member * channels, channels), channels)
    own = pltpu.make_async_copy(back_ref.at[:, :, columns], back_out.at[:, rows, :], local.at[0])
    own_gated = pltpu.make_async_copy(
        gated_ref.at[:, columns], gated_out.at[rows, :], local.at[1]
    )
    own.start()
    own_gated.start()
    own.wait()
    own_gated.wait()
    for copy in copies:
        copy.wait()


def trade(gated, back, devices):
    steps = gated.shape[0]
    channels = gated.shape[1] // devices
    return pl.pallas_call(
        functools.partial(trade_kernel, devices),
        in_specs=[pl.BlockSpec(memory_space=pltpu.VMEM)] * 2,
        out_specs=[pl.BlockSpec(memory_space=pltpu.VMEM)] * 2,
        out_shape=[
            jax.ShapeDtypeStruct((steps * devices, channels), gated.dtype),
            jax.ShapeDtypeStruct((2, steps * devices, channels), back.dtype),
        ],
        scratch_shapes=[
            pltpu.SemaphoreType.DMA((2, devices - 1)),
            pltpu.SemaphoreType.DMA((2, devices - 1)),
            pltpu.SemaphoreType.DMA((2,)),
        ],
        compiler_params=pltpu.CompilerParams(
            collective_id=1, has_side_effects=True, vmem_limit_bytes=48 * 2**20
        ),
        name="trade",
    )(gated, back)


def grads_kernel(
    nrows,
    devices,
    normed_ref,
    back_ref,
    gated_ref,
    cot_ref,
    small_ref,
    gin_out,
    gout_out,
    small_out,
    norm_out,
    small_got,
    small_part,
    small_seq,
    gout_sum,
    gout_low,
    gout_got,
    gin_sum,
    gin_low,
    gin_got,
    gin_part,
    norm_seq,
    norm_rows,
    row_wires,
    seq_wires,
):
    row = lax.axis_index("rows")
    member = lax.axis_index("seq")
    few = small_ref.shape[0] // nrows
    outer = gout_out.shape[0] // nrows
    inner = gin_part.shape[0] // devices
    channels = small_out.shape[1]
    greet((("rows", nrows), ("seq", devices)))

    def share(index, size):
        return pl.ds(pl.multiple_of(index * size, size), size)

    def to_rows(kind, make):
        return [
            push(*make(partner("rows", offset), offset - 1), row_wires.at[kind], offset - 1, "rows", offset)
            for offset in range(1, nrows)
        ]

    def to_seq(kind, make):
        return [
            push(*make(partner("seq", offset), offset - 1), seq_wires.at[kind], offset - 1, "seq", offset)
            for offset in range(1, devices)
        ]

    def settle(copies):
        for copy in copies:
            copy.wait()

    def squares(values):
        return jnp.sum(values * values, axis=0, keepdims=True)

    small_moves = to_rows(
        0, lambda other, at: (small_ref.at[share(other, few)], small_got.at[at])
    )
    gout_sum[...] = lax.dot_general(
        gated_ref[...], cot_ref[...], (((0,), (0,)), ((), ())), preferred_element_type=jnp.float32
    )
    gout_low[...] = gout_sum[...].astype(jnp.bfloat16)
    gout_moves = to_rows(
        1, lambda other, at: (gout_low.at[share(other, outer)], gout_got.at[at])
    )
    for half in range(2):
        result = lax.dot_general(
            normed_ref[...],
            back_ref[half],
            (((0,), (0,)), ((), ())),
            preferred_element_type=jnp.float32,
        )
        wide = gin_sum.shape[2]
        for place in range(nrows // 2):
            piece = result[:, place * wide : (place + 1) * wide]
            gin_sum[half * (nrows // 2) + place] = piece
            gin_low[half * (nrows // 2) + place] = piece.astype(jnp.bfloat16)
    gin_moves = to_rows(2, lambda other, at: (gin_low.at[other], gin_got.at[at]))

    settle(small_moves)
    total = small_ref[share(row, few), :].astype(jnp.float32)
    for at in range(nrows - 1):
        total = total + small_got[at].astype(jnp.float32)
    small_part[...] = total.astype(jnp.bfloat16)
    small_moves = to_seq(
        0, lambda other, at: (small_part.at[:, share(other, channels)], small_seq.at[at])
    )

    settle(gout_moves)
    total = gout_sum[share(row, outer), :]
    for at in range(nrows - 1):
        total = total + gout_got[at].astype(jnp.float32)
    gout_out[share(row, outer), :] = total.astype(jnp.bfloat16)
    gout_moves = to_rows(
        3,
        lambda other, at: (gout_out.at[share(row, outer)], gout_out.at[share(row, outer)]),
    )
    norm = jnp.sum(squares(total), axis=1, keepdims=True)

    settle(gin_moves)
    total = gin_sum[row]
    for at in range(nrows - 1):
        total = total + gin_got[at].astype(jnp.float32)
    gin_part[...] = total.astype(jnp.bfloat16)
    gin_moves = to_seq(
        1, lambda other, at: (gin_part.at[share(other, inner)], gin_out.at[row, member])
    )
    gin_out[row, member] = gin_part[share(member, inner), :]
    norm = norm + jnp.sum(squares(total), axis=1, keepdims=True)

    settle(small_moves)
    total = small_part[:, share(member, channels)].astype(jnp.float32)
    for at in range(devices - 1):
        total = total + small_seq[at].astype(jnp.float32)
    small_out[share(row, few), :] = total.astype(jnp.bfloat16)
    small_moves = to_rows(
        4, lambda other, at: (small_out.at[share(row, few)], small_out.at[share(row, few)])
    )
    norm = norm + jnp.sum(squares(total), axis=1, keepdims=True)
    norm_seq[member] = jnp.broadcast_to(norm, (8, LANES))
    norm_moves = to_seq(2, lambda other, at: (norm_seq.at[member], norm_seq.at[member]))

    settle(gin_moves)
    gin_moves = to_rows(5, lambda other, at: (gin_out.at[row], gin_out.at[row]))
    settle(norm_moves)
    norm_rows[row] = jnp.sum(norm_seq[...], axis=0)
    norm_moves = to_rows(6, lambda other, at: (norm_rows.at[row], norm_rows.at[row]))
    settle(norm_moves)
    norm_out[...] = jnp.sqrt(jnp.sum(norm_rows[...], axis=0))
    settle(small_moves)
    settle(gout_moves)
    settle(gin_moves)


def grads_of(normed_all, back_mine, gated_mine, cot_all, small, nrows, devices):
    depth = normed_all.shape[1]
    channels = gated_mine.shape[1]
    wide = 2 * channels // nrows
    few = small.shape[0] // nrows
    low = jnp.bfloat16
    return pl.pallas_call(
        functools.partial(grads_kernel, nrows, devices),
        in_specs=[pl.BlockSpec(memory_space=pltpu.VMEM)] * 5,
        out_specs=[pl.BlockSpec(memory_space=pltpu.VMEM)] * 4,
        out_shape=[
            jax.ShapeDtypeStruct((nrows, devices, depth // devices, wide), low),
            jax.ShapeDtypeStruct((channels, depth), low),
            jax.ShapeDtypeStruct((small.shape[0], channels), low),
            jax.ShapeDtypeStruct((8, LANES), jnp.float32),
        ],
        scratch_shapes=[
            pltpu.VMEM((nrows - 1, few, E), low),
            pltpu.VMEM((few, E), low),
            pltpu.VMEM((devices - 1, few, channels), low),
            pltpu.VMEM((channels, depth), jnp.float32),
            pltpu.VMEM((channels, depth), low),
            pltpu.VMEM((nrows - 1, channels // nrows, depth), low),
            pltpu.VMEM((nrows, depth, wide), jnp.float32),
            pltpu.VMEM((nrows, depth, wide), low),
            pltpu.VMEM((nrows - 1, depth, wide), low),
            pltpu.VMEM((depth, wide), low),
            pltpu.VMEM((devices, 8, LANES), jnp.float32),
            pltpu.VMEM((nrows, 8, LANES), jnp.float32),
            pltpu.SemaphoreType.DMA((7, 2, nrows - 1)),
            pltpu.SemaphoreType.DMA((3, 2, devices - 1)),
        ],
        compiler_params=pltpu.CompilerParams(
            collective_id=2, has_side_effects=True, vmem_limit_bytes=56 * 2**20
        ),
        name="grads",
    )(normed_all, back_mine, gated_mine, cot_all, small)


PACKED = (R + 2 * N, R, N, K, 1, 1, 1, 1)
PACKED_ROWS = 192


def packed_rows():
    spans = []
    at = 0
    for count in PACKED:
        spans.append((at, at + count))
        at += count
    return spans


def update_kernel(member_ref, norm_ref, gin_ref, gout_ref, small_ref, *refs):
    weights, moments, averages, outs = refs[:10], refs[10:20], refs[20:30], refs[30:]
    shrink_by = 1.0 / jnp.maximum(norm_ref[0:1, 0:1], 1.0)

    def renew(ordinal, grad, at=Ellipsis):
        clipped = grad * shrink_by
        momentum_new = MOMENTUM * moments[ordinal][at] + clipped
        renewed = weights[ordinal][at].astype(jnp.float32) - RATES[ordinal] * math.sqrt(PARAMS) * (
            clipped + MOMENTUM * momentum_new
        )
        outs[3 * ordinal][at] = momentum_new
        outs[3 * ordinal + 1][at] = renewed
        outs[3 * ordinal + 2][at] = AVERAGE * averages[ordinal][at] + (1.0 - AVERAGE) * renewed

    places, members = gin_ref.shape[:2]
    for column in range(members):
        for place in range(places):
            columns = pl.ds((column * places + place) * LANES, LANES)
            renew(1, gin_ref[place, column].astype(jnp.float32), (slice(None), columns))
    renew(9, gout_ref[...].astype(jnp.float32))

    @pl.when(pl.program_id(0) == 0)
    def _():
        spans = packed_rows()

        def part(index):
            return small_ref[spans[index][0] : spans[index][1], :].astype(jnp.float32)

        small = small_ref[...].astype(jnp.float32)
        renew(4, jnp.transpose(part(0)))
        renew(5, part(1))
        renew(7, part(2))
        renew(2, part(3))
        for ordinal, index in ((3, 4), (6, 5), (8, 6)):
            renew(ordinal, small[spans[index][0] : spans[index][1]])
        gain = small[spans[7][0] : spans[7][1], : weights[0].shape[1]]
        renew(0, gain)


def update_of(member, norm_tile, gin_parts, gout, small, weights, moments, averages):
    nrows, devices, inner, wide = gin_parts.shape
    channels = gout.shape[0]
    blocks = 8
    outer = channels // blocks
    half = blocks // 2
    pair = devices // half
    block = nrows // 2 * pair * wide
    flat = (0, 3, 6, 8)

    def rows_of(array, ordinal):
        return array.reshape(1, -1) if ordinal in flat else array

    def shard(shape, ordinal):
        if ordinal == 1:
            return pl.BlockSpec((inner, block), lambda j, m: (0, j))
        if ordinal == 9:
            return pl.BlockSpec((outer, shape[1]), lambda j, m: (j, 0))
        return pl.BlockSpec(shape, lambda j, m: (0, 0))

    def weight(shape, ordinal):
        if ordinal == 1:
            return pl.BlockSpec((inner, block), lambda j, m: (m[0], j))
        if ordinal == 9:
            return pl.BlockSpec((outer, shape[1]), lambda j, m: (m[0] * blocks + j, 0))
        if ordinal == 4:
            return pl.BlockSpec(shape, lambda j, m: (m[0], 0))
        return pl.BlockSpec(shape, lambda j, m: (0, m[0]))

    weights = [rows_of(array, ordinal) for ordinal, array in enumerate(weights)]
    moments = [rows_of(array, ordinal) for ordinal, array in enumerate(moments)]
    averages = [rows_of(array, ordinal) for ordinal, array in enumerate(averages)]
    shapes = [array.shape for array in moments]
    shards = [shard(shape, ordinal) for ordinal, shape in enumerate(shapes)]
    outs = pl.pallas_call(
        update_kernel,
        grid_spec=pltpu.PrefetchScalarGridSpec(
            num_scalar_prefetch=1,
            grid=(blocks,),
            in_specs=[
                pl.BlockSpec(norm_tile.shape, lambda j, m: (0, 0)),
                pl.BlockSpec(
                    (nrows // 2, pair, inner, wide), lambda j, m: (j // half, j % half, 0, 0)
                ),
                pl.BlockSpec((outer, gout.shape[1]), lambda j, m: (j, 0)),
                pl.BlockSpec(small.shape, lambda j, m: (0, 0)),
            ]
            + [weight(shape, ordinal) for ordinal, shape in enumerate(shapes)]
            + shards
            + shards,
            out_specs=[shards[ordinal] for ordinal in range(10) for _ in range(3)],
        ),
        out_shape=[
            jax.ShapeDtypeStruct(shapes[ordinal], jnp.float32)
            for ordinal in range(10)
            for _ in range(3)
        ],
        compiler_params=pltpu.CompilerParams(vmem_limit_bytes=48 * 2**20),
        name="update",
    )(member, norm_tile, gin_parts, gout, small, *weights, *moments, *averages)
    return [
        out.reshape(-1) if index // 3 in flat else out for index, out in enumerate(outs)
    ]


def local(
    tokens,
    cotangent,
    doc_lengths,
    norm_gain,
    in_proj,
    conv_weight,
    conv_bias,
    x_proj,
    dt_proj,
    dt_bias,
    a_log,
    d_skip,
    out_proj,
    moment_norm_gain,
    moment_in_proj,
    moment_conv_weight,
    moment_conv_bias,
    moment_x_proj,
    moment_dt_proj,
    moment_dt_bias,
    moment_a_log,
    moment_d_skip,
    moment_out_proj,
    average_norm_gain,
    average_in_proj,
    average_conv_weight,
    average_conv_bias,
    average_x_proj,
    average_dt_proj,
    average_dt_bias,
    average_a_log,
    average_d_skip,
    average_out_proj,
):
    devices = lax.axis_size("seq")
    member_id = lax.axis_index("seq")
    channels = E // devices
    begin = member_id * channels
    stream = tokens[0].astype(jnp.float32)
    steps = stream.shape[0]
    length = steps * devices
    cot_low = cotangent[0]
    inverse = lax.rsqrt(jnp.mean(stream * stream, axis=1, keepdims=True) + EPS)
    rates = -jnp.exp(a_log)
    scaled_rates = rates * (1.0 / math.log(2.0))
    lengths = doc_lengths[0]
    starts = (jnp.cumsum(lengths) - lengths).astype(jnp.int32)
    (
        normed,
        inner_low,
        gates_low,
        back_gated,
        pre_act,
        delta_pre,
        ddec,
        drive,
        grady_rows,
        rank_low,
        inb,
        outb,
        everyone,
        all_sums,
    ) = front_of(
        starts,
        tokens[0],
        cot_low,
        norm_gain[None],
        in_proj,
        out_proj,
        conv_weight,
        conv_bias[None],
        x_proj,
        dt_proj,
        dt_bias[None],
        scaled_rates,
        devices,
    )
    normed_all = lax.all_gather(normed, "seq", axis=0, tiled=True)
    cot_all = lax.all_gather(cot_low, "seq", axis=0, tiled=True)
    positions = member_id * steps + jnp.arange(-8, steps + 8, dtype=jnp.int32)
    docid, starting = doc_tables(doc_lengths[0], positions)
    masks = []
    for offset in range(K):
        linked = (docid[8:] == docid[8 - offset : steps + 16 - offset]) & (
            positions[8 - offset : steps + 16 - offset] >= 0
        )
        masks.append((linked & (positions[8:] < length)).astype(jnp.float32)[:, None])

    def flat(values):
        return jnp.transpose(values, (1, 0, 2)).reshape(steps, E)

    pre_act, delta_pre = flat(pre_act), flat(delta_pre)
    padded = inner_low[8:].astype(jnp.float32)
    gates = gates_low.astype(jnp.float32)
    act = silu(pre_act)
    act_low = act.astype(jnp.bfloat16)
    delta = jax.nn.softplus(delta_pre)
    silu_gate = silu(gates)
    chan_back = back_gated.astype(jnp.float32)
    grad_y = chan_back * silu_gate
    member_word = jnp.reshape(member_id, (1,)).astype(jnp.int32)
    scanned, along_in, pulled_sum, gin, gout, grad_rates = scan_of(
        member_word, ddec, drive, grady_rows, inb, outb, scaled_rates, everyone, all_sums, 512
    )
    scanned, along_in, pulled_sum = flat(scanned), flat(along_in), flat(pulled_sum)
    y_full = scanned + d_skip[None, :] * act
    gated = (y_full * silu_gate).astype(jnp.bfloat16)
    block_output = (
        stream + jnp.dot(gated, out_proj, preferred_element_type=jnp.float32)
    )[None]
    grad_gates = chan_back * y_full * silu_slope(gates)
    grad_dskip = jnp.sum(grad_y * act, axis=0)
    grad_in_mat = jnp.sum(gin, axis=2)
    grad_out_mat = jnp.sum(gout, axis=2)
    grad_delta = along_in * act + pulled_sum * math.log(2.0)
    grad_alog = grad_rates * rates
    grad_pre = (grad_delta * jax.nn.sigmoid(delta_pre)).astype(jnp.bfloat16)
    grad_dtbias = jnp.sum(grad_pre.astype(jnp.float32), axis=0)
    grad_dtproj = lax.dot_general(
        rank_low, grad_pre, (((0,), (0,)), ((), ())), preferred_element_type=jnp.float32
    )
    rank_back = lax.dot_general(
        grad_pre, dt_proj, (((1,), (1,)), ((), ())), preferred_element_type=jnp.float32
    )
    proj_back = jnp.concatenate([rank_back, grad_in_mat, grad_out_mat], axis=1).astype(jnp.bfloat16)
    grad_xproj = lax.dot_general(
        act_low, proj_back, (((0,), (0,)), ((), ())), preferred_element_type=jnp.float32
    )
    grad_act = (
        grad_y * d_skip[None, :]
        + along_in * delta
        + lax.dot_general(
            proj_back, x_proj, (((1,), (1,)), ((), ())), preferred_element_type=jnp.float32
        )
    )
    grad_pre_act = grad_act * silu_slope(pre_act)
    ahead = lax.ppermute(
        grad_pre_act[:8], "seq", [(i + 1, i) for i in range(devices - 1)]
    )
    extended = jnp.concatenate([grad_pre_act, ahead], axis=0)
    grad_conv_bias = jnp.sum(grad_pre_act, axis=0)
    grad_inner = jnp.zeros_like(gates)
    conv_rows = []
    for offset in range(K):
        masked = extended * masks[offset]
        conv_rows.append(
            jnp.sum(masked[:steps] * padded[8 - offset : 8 - offset + steps], axis=0)
        )
        grad_inner = grad_inner + conv_weight[offset][None, :] * masked[offset : offset + steps]
    grad_convw = jnp.stack(conv_rows)
    back_xz = jnp.stack([grad_inner, grad_gates]).astype(jnp.bfloat16)
    grad_normed = lax.dot_general(
        back_xz[0], in_proj[:, :E], (((1,), (1,)), ((), ())), preferred_element_type=jnp.float32
    ) + lax.dot_general(
        back_xz[1], in_proj[:, E:], (((1,), (1,)), ((), ())), preferred_element_type=jnp.float32
    )
    grad_gain = jnp.sum(grad_normed * stream * inverse, axis=0)
    scaled = grad_normed * norm_gain[None, :]
    input_grad = (
        cot_low.astype(jnp.float32)
        + inverse * scaled
        - stream * inverse * inverse * inverse * jnp.mean(scaled * stream, axis=1, keepdims=True)
    )
    small = jnp.concatenate(
        [
            grad_xproj.T,
            grad_dtproj,
            grad_alog,
            grad_convw,
            grad_conv_bias[None],
            grad_dtbias[None],
            grad_dskip[None],
            jnp.pad(
                grad_gain.reshape(devices, D // devices),
                ((0, 0), (0, channels - D // devices)),
            ).reshape(1, E),
            jnp.zeros((PACKED_ROWS - sum(PACKED), E), jnp.float32),
        ],
        axis=0,
    )
    nrows = lax.axis_size("rows")
    direct = channels % LANES == 0 and 2 * channels == nrows * LANES
    if direct:
        gated_mine, back_mine = trade(gated, back_xz, devices)
        gin_parts, gout_share, small, norm_tile = grads_of(
            normed_all, back_mine, gated_mine, cot_all, small.astype(jnp.bfloat16), nrows, devices
        )
        grad_norm = norm_tile[0, 0]
    else:
        gated_mine = lax.all_to_all(gated, "seq", split_axis=1, concat_axis=0, tiled=True)
        back_mine = lax.all_to_all(back_xz, "seq", split_axis=2, concat_axis=1, tiled=True)
        gout_share = lax.psum(
            lax.dot_general(
                gated_mine, cot_all, (((0,), (0,)), ((), ())), preferred_element_type=jnp.float32
            ),
            "rows",
        )
        gin_share = lax.psum(
            jnp.einsum("td,ktc->dkc", normed_all, back_mine, preferred_element_type=jnp.float32),
            "rows",
        )
        gin_share = lax.all_to_all(
            gin_share, "seq", split_axis=0, concat_axis=2, tiled=True
        ).reshape(D // devices, 2 * E)
        small = lax.psum(small, "rows")
        small = lax.psum_scatter(small, "seq", scatter_dimension=1, tiled=True)
        squares = jnp.sum(gin_share * gin_share) + jnp.sum(gout_share * gout_share)
        grad_norm = jnp.sqrt(lax.psum(squares + jnp.sum(small * small), "seq"))
    moments = (
        moment_norm_gain,
        moment_in_proj,
        moment_conv_weight,
        moment_conv_bias,
        moment_x_proj,
        moment_dt_proj,
        moment_dt_bias,
        moment_a_log,
        moment_d_skip,
        moment_out_proj,
    )
    averages = (
        average_norm_gain,
        average_in_proj,
        average_conv_weight,
        average_conv_bias,
        average_x_proj,
        average_dt_proj,
        average_dt_bias,
        average_a_log,
        average_d_skip,
        average_out_proj,
    )
    results = [block_output, input_grad[None], grad_norm]
    if direct:
        weights = (
            norm_gain,
            in_proj,
            conv_weight,
            conv_bias,
            x_proj,
            dt_proj,
            dt_bias,
            a_log,
            d_skip,
            out_proj,
        )
        results += update_of(
            member_word, norm_tile, gin_parts, gout_share, small, weights, moments, averages
        )
        return tuple(results)
    parts = [small[low:high] for low, high in packed_rows()]
    owner_grads = (
        parts[7][0, : D // devices],
        gin_share.astype(jnp.float32),
        parts[3],
        parts[4][0],
        parts[0].T,
        parts[1],
        parts[5][0],
        parts[2],
        parts[6][0],
        gout_share.astype(jnp.float32),
    )
    conv_mine = lax.dynamic_slice_in_dim(conv_weight, begin, channels, 1)
    cbias_mine = lax.dynamic_slice_in_dim(conv_bias, begin, channels, 0)
    xproj_mine = lax.dynamic_slice_in_dim(x_proj, begin, channels, 0)
    dtproj_mine = lax.dynamic_slice_in_dim(dt_proj, begin, channels, 1)
    dtbias_mine = lax.dynamic_slice_in_dim(dt_bias, begin, channels, 0)
    alog_mine = lax.dynamic_slice_in_dim(a_log, begin, channels, 1)
    dskip_mine = lax.dynamic_slice_in_dim(d_skip, begin, channels, 0)
    shrink_by = 1.0 / jnp.maximum(grad_norm, 1.0)
    gain_rows = D // devices
    outer_rows = E // devices
    mine_weights = (
        lax.dynamic_slice_in_dim(norm_gain, member_id * gain_rows, gain_rows, 0),
        lax.dynamic_slice_in_dim(in_proj, member_id * gain_rows, gain_rows, 0).astype(jnp.float32),
        conv_mine,
        cbias_mine,
        xproj_mine.astype(jnp.float32),
        dtproj_mine.astype(jnp.float32),
        dtbias_mine,
        alog_mine,
        dskip_mine,
        lax.dynamic_slice_in_dim(out_proj, member_id * outer_rows, outer_rows, 0).astype(
            jnp.float32
        ),
    )
    for ordinal in range(10):
        clipped = owner_grads[ordinal] * shrink_by
        momentum_new = MOMENTUM * moments[ordinal] + clipped
        renewed = mine_weights[ordinal] - RATES[ordinal] * math.sqrt(PARAMS) * (
            clipped + MOMENTUM * momentum_new
        )
        results += [momentum_new, renewed, AVERAGE * averages[ordinal] + (1.0 - AVERAGE) * renewed]
    return tuple(results)


def solution(mesh):
    return jax.shard_map(
        local,
        mesh=mesh,
        in_specs=(
            P("rows", "seq", None),
            P("rows", "seq", None),
            P("rows", None),
            P(),
            P(),
            P(),
            P(),
            P(),
            P(),
            P(),
            P(),
            P(),
            P(),
            P("seq"),
            P("seq", None),
            P(None, "seq"),
            P("seq"),
            P("seq", None),
            P(None, "seq"),
            P("seq"),
            P(None, "seq"),
            P("seq"),
            P("seq", None),
            P("seq"),
            P("seq", None),
            P(None, "seq"),
            P("seq"),
            P("seq", None),
            P(None, "seq"),
            P("seq"),
            P(None, "seq"),
            P("seq"),
            P("seq", None),
        ),
        out_specs=(
            P("rows", "seq", None),
            P("rows", "seq", None),
            P(),
            P("seq"),
            P("seq"),
            P("seq"),
            P("seq", None),
            P("seq", None),
            P("seq", None),
            P(None, "seq"),
            P(None, "seq"),
            P(None, "seq"),
            P("seq"),
            P("seq"),
            P("seq"),
            P("seq", None),
            P("seq", None),
            P("seq", None),
            P(None, "seq"),
            P(None, "seq"),
            P(None, "seq"),
            P("seq"),
            P("seq"),
            P("seq"),
            P(None, "seq"),
            P(None, "seq"),
            P(None, "seq"),
            P("seq"),
            P("seq"),
            P("seq"),
            P("seq", None),
            P("seq", None),
            P("seq", None),
        ),
        check_vma=False,
    )
```

```python
import functools
import math

import jax
import jax.numpy as jnp
from jax import lax
from jax.experimental import pallas as pl
from jax.experimental.pallas import tpu as pltpu
from jax.sharding import PartitionSpec as P

D = 1024
E = 2048
N = 16
R = 64
K = 4
PARAMS = 6667264

LANES = 128
RESET = 1e30
MESH = pl.DeviceIdType.MESH


EPS = 1e-05
MOMENTUM = 0.9
AVERAGE = 0.9
RATES = (0.1, 0.03, 0.1, 0.1, 0.03, 0.03, 0.3, 0.3, 0.1, 0.03)


def silu(values):
    return values * jax.nn.sigmoid(values)


def silu_slope(values):
    sigmoid_of = jax.nn.sigmoid(values)
    return sigmoid_of * (1.0 + values * (1.0 - sigmoid_of))


def doc_tables(lengths_row, positions):
    ends = jnp.cumsum(lengths_row)
    starts = ends - lengths_row
    docid = jnp.sum((positions[None, :] >= starts[:, None]).astype(jnp.int32), axis=0)
    first = jnp.sum((positions[None, :] == starts[:, None]).astype(jnp.int32), axis=0)
    return (docid, first > 0)


def scan_kernel(
    member_ref,
    ddec_ref,
    drive_ref,
    grady_ref,
    inb_ref,
    outb_ref,
    rates_ref,
    all_ref,
    sums_ref,
    scanned_ref,
    along_ref,
    decayed_ref,
    gin_ref,
    gout_ref,
    grates_ref,
    kept,
    first,
    second,
):
    groups, steps = ddec_ref.shape[:2]
    devices = all_ref.shape[0]
    base = pl.program_id(0) * groups
    member = member_ref[0]
    columns = [pl.ds(group * LANES, LANES) for group in range(groups)]
    half = N // 2

    @pl.when(pl.program_id(0) == 0)
    def _():
        gin_ref[...] = jnp.zeros_like(gin_ref)
        gout_ref[...] = jnp.zeros_like(gout_ref)

    def through(device, states):
        new = []
        for group in range(groups):
            total = sums_ref[device, pl.ds(base + group, 1), :]
            factor = jnp.exp2(total * rates_ref[:, columns[group]])
            new.append(
                factor * states[group]
                + all_ref[device, 0, :, columns[group]].astype(jnp.float32)
            )
        return new

    zeros = [jnp.zeros((N, LANES), jnp.float32) for _ in range(groups)]
    reach = devices // 2
    entering = lax.fori_loop(jnp.maximum(member - reach, 0), member, through, zeros)
    last = jnp.minimum(member + reach, devices - 1)
    leaving = lax.fori_loop(0, last - member, lambda d, s: through(last - d, s), zeros)

    def fold(values):
        return values[:half] + values[half:]

    def forward(t, hidden):
        in_row, out_row = inb_ref[t], outb_ref[t]
        new = []
        for group in range(groups):
            here = (group, pl.ds(t, 1))
            decay = jnp.exp2(ddec_ref[here] * rates_ref[:, columns[group]])
            state = decay * hidden[group] + drive_ref[here] * in_row
            kept[t + 1, :, columns[group]] = state
            first[group, pl.ds(pl.multiple_of(t * half, half), half), :] = fold(state * out_row)
            new.append(state)
        return new

    for group in range(groups):
        kept[0, :, columns[group]] = entering[group]
    lax.fori_loop(0, steps, forward, entering, unroll=4)

    def collapse(source, target_ref):
        for group in range(groups):
            total = source[group, pl.ds(0, steps, stride=half), :]
            for place in range(1, half):
                total = total + source[group, pl.ds(place, steps, stride=half), :]
            target_ref[group] = total

    collapse(first, scanned_ref)

    def backward(back, carry):
        later, grates = carry
        t = steps - 1 - back
        in_row, out_row = inb_ref[t], outb_ref[t]
        gin, gout = gin_ref[t], gout_ref[t]
        new = ([], [])
        rows = pl.ds(pl.multiple_of(t * half, half), half)
        for group in range(groups):
            here = (group, pl.ds(t, 1))
            grady = grady_ref[here]
            delta = ddec_ref[here]
            rates = rates_ref[:, columns[group]]
            adjoint = grady * out_row + later[group]
            gout = gout + grady * kept[t + 1, :, columns[group]]
            gin = gin + adjoint * drive_ref[here]
            first[group, rows, :] = fold(adjoint * in_row)
            passed = jnp.exp2(delta * rates) * adjoint
            pulled = passed * kept[t, :, columns[group]]
            second[group, rows, :] = fold(pulled * rates)
            new[0].append(passed)
            new[1].append(grates[group] + pulled * delta)
        gin_ref[t] = gin
        gout_ref[t] = gout
        return new

    _, grates = lax.fori_loop(0, steps, backward, (leaving, zeros), unroll=4)
    collapse(first, along_ref)
    collapse(second, decayed_ref)
    for group in range(groups):
        grates_ref[:, columns[group]] = grates[group]


def scan_of(member, ddec, drive, grady, inb, outb, rates, everyone, sums, block):
    steps = ddec.shape[1]
    devices = everyone.shape[0]
    groups = block // LANES
    wide = pl.BlockSpec((block // LANES, steps, LANES), lambda b: (b, 0, 0))
    whole = pl.BlockSpec((steps, N, LANES), lambda b: (0, 0, 0))
    narrow = pl.BlockSpec((N, block), lambda b: (0, b))
    full = jax.ShapeDtypeStruct((E // LANES, steps, LANES), jnp.float32)
    spread = jax.ShapeDtypeStruct((steps, N, LANES), jnp.float32)
    return pl.pallas_call(
        scan_kernel,
        grid=(E // block,),
        in_specs=[
            pl.BlockSpec(memory_space=pltpu.SMEM),
            wide,
            wide,
            wide,
            whole,
            whole,
            narrow,
            pl.BlockSpec((devices, 1, N, block), lambda b: (0, b, 0, 0)),
            pl.BlockSpec(sums.shape, lambda b: (0, 0, 0)),
        ],
        out_specs=[wide, wide, wide, whole, whole, narrow],
        out_shape=[full, full, full, spread, spread, jax.ShapeDtypeStruct((N, E), jnp.float32)],
        scratch_shapes=[
            pltpu.VMEM((steps + 1, N, block), jnp.float32),
            pltpu.VMEM((groups, steps * N // 2, LANES), jnp.float32),
            pltpu.VMEM((groups, steps * N // 2, LANES), jnp.float32),
        ],
        compiler_params=pltpu.CompilerParams(vmem_limit_bytes=48 * 2**20),
        name="scan",
    )(member, ddec, drive, grady, inb, outb, rates, everyone, sums)


def partner(axis, offset):
    size = lax.axis_size(axis)
    return lax.rem(lax.axis_index(axis) + offset, size)


def greet(counts):
    barrier = pltpu.get_barrier_semaphore()
    total = 0
    for axis, count in counts:
        for offset in range(1, count):
            pl.semaphore_signal(
                barrier, inc=1, device_id={axis: partner(axis, offset)}, device_id_type=MESH
            )
        total += count - 1
    pl.semaphore_wait(barrier, total)


def push(source, target, semaphores, at, axis, offset):
    copy = pltpu.make_async_remote_copy(
        src_ref=source,
        dst_ref=target,
        send_sem=semaphores.at[0, at],
        recv_sem=semaphores.at[1, at],
        device_id={axis: partner(axis, offset)},
        device_id_type=MESH,
    )
    copy.start()
    return copy


def span(index, size):
    return pl.ds(index * size, size)


def softplus(values):
    return jnp.maximum(values, 0.0) + jnp.log1p(jnp.exp(-jnp.abs(values)))


def front_kernel(
    devices,
    nrows,
    starts_ref,
    tokens_ref,
    cot_ref,
    gain_ref,
    in_proj_ref,
    out_proj_ref,
    conv_ref,
    cbias_ref,
    x_proj_ref,
    dt_proj_ref,
    dtbias_ref,
    rates_ref,
    normed_ref,
    inner_ref,
    gates_ref,
    back_ref,
    pre_act_ref,
    delta_pre_ref,
    ddec_ref,
    drive_ref,
    grady_ref,
    rank_ref,
    inb_ref,
    outb_ref,
    ends_out,
    sums_out,
    in_proj_buf,
    out_proj_buf,
    padded,
    docid,
    masks,
    proj,
    ends,
    loads,
    halo_wires,
    wires,
    sum_wires,
    row_wires,
):
    member = lax.axis_index("seq")
    own = lax.axis_index("rows") if nrows > 1 else 0
    steps = tokens_ref.shape[0]
    groups = E // LANES
    chunk = 4 * LANES
    chunks = E // chunk
    reach = devices // 2
    halo = inner_ref.shape[0] - steps
    in_loads = [
        pltpu.make_async_copy(
            in_proj_ref.at[:, span(at, chunk)], in_proj_buf.at[at], loads.at[at]
        )
        for at in range(2 * chunks)
    ]
    out_loads = [
        pltpu.make_async_copy(
            out_proj_ref.at[span(at, chunk), :], out_proj_buf.at[at], loads.at[2 * chunks + at]
        )
        for at in range(chunks)
    ]
    for load in in_loads + out_loads:
        load.start()
    barrier = pltpu.get_barrier_semaphore()
    for axis, count in (("seq", devices), ("rows", nrows)):
        for offset in range(1, count):
            pl.semaphore_signal(
                barrier, inc=1, device_id={axis: partner(axis, offset)}, device_id_type=MESH
            )

    stream = tokens_ref[...].astype(jnp.float32)
    inverse = lax.rsqrt(jnp.mean(stream * stream, axis=1, keepdims=True) + EPS)
    normed_ref[own] = (stream * inverse * gain_ref[...]).astype(jnp.bfloat16)

    places = member * steps - 8 + lax.broadcasted_iota(jnp.int32, docid.shape, 0)
    count = jnp.zeros(docid.shape, jnp.int32)
    first = jnp.zeros(docid.shape, jnp.float32)
    for index in range(starts_ref.shape[0]):
        count = count + jnp.where(places >= starts_ref[index], 1, 0)
        first = jnp.where(places == starts_ref[index], 1.0, first)
    docid[...] = count
    masks[0] = first[8 : 8 + steps]
    for offset in range(1, K):
        masks[offset] = jnp.where(
            docid[8 - offset : 8 - offset + steps, :] == docid[8 : 8 + steps, :], 1.0, 0.0
        )

    def project(at):
        in_loads[at].wait()
        return jnp.dot(
            normed_ref[own], in_proj_buf[at], preferred_element_type=jnp.float32
        ).astype(jnp.bfloat16)

    for at in range(chunks):
        inner_ref[halo:, span(at, chunk)] = project(at)
    pl.semaphore_wait(barrier, devices + nrows - 2)
    halo_copy = pltpu.make_async_remote_copy(
        src_ref=inner_ref.at[steps : steps + halo, :],
        dst_ref=inner_ref.at[0:halo, :],
        send_sem=halo_wires.at[0],
        recv_sem=halo_wires.at[1],
        device_id={"seq": partner("seq", 1)},
        device_id_type=MESH,
    )

    @pl.when(member < devices - 1)
    def _():
        halo_copy.start()

    row_copies = [
        push(normed_ref.at[own], normed_ref.at[own], row_wires, offset - 1, "rows", offset)
        for offset in range(1, nrows)
    ]

    @pl.when(member == 0)
    def _():
        inner_ref[0:halo, :] = jnp.zeros((halo, E), jnp.bfloat16)

    for at in range(chunks):
        gates_ref[:, span(at, chunk)] = project(chunks + at)
    for at in range(chunks):
        out_loads[at].wait()
        back_ref[:, span(at, chunk)] = lax.dot_general(
            cot_ref[...],
            out_proj_buf[at],
            (((1,), (1,)), ((), ())),
            preferred_element_type=jnp.float32,
        ).astype(jnp.bfloat16)

    @pl.when(member < devices - 1)
    def _():
        halo_copy.wait_send()

    @pl.when(member > 0)
    def _():
        halo_copy.wait_recv()

    proj[...] = jnp.zeros_like(proj)
    for at in range(chunks):
        lows = []
        for group in range(4 * at, 4 * at + 4):
            columns = span(group, LANES)
            padded[...] = inner_ref[halo - 8 :, columns].astype(jnp.float32)
            value = cbias_ref[:, columns] + conv_ref[0:1, columns] * padded[8:, :]
            for offset in range(1, K):
                value = (
                    value
                    + conv_ref[offset : offset + 1, columns]
                    * padded[8 - offset : 8 - offset + steps, :]
                    * masks[offset]
                )
            pre_act_ref[group] = value
            act = silu(value)
            drive_ref[group] = act
            lows.append(act.astype(jnp.bfloat16))
        proj[...] += lax.dot_general(
            jnp.concatenate(lows, axis=1),
            x_proj_ref[:, span(at, chunk)],
            (((1,), (1,)), ((), ())),
            preferred_element_type=jnp.float32,
        )
    rank_ref[...] = proj[:, :R].astype(jnp.bfloat16)
    inb_ref[...] = jnp.broadcast_to(proj[:, R : R + N][:, :, None], inb_ref.shape)
    outb_ref[...] = jnp.broadcast_to(proj[:, R + N :][:, :, None], outb_ref.shape)

    def later(distance, at):
        return pltpu.make_async_remote_copy(
            src_ref=ends.at[0, at],
            dst_ref=ends_out.at[member, at],
            send_sem=wires.at[0, 0, at, distance - 1],
            recv_sem=wires.at[0, 1, at, distance - 1],
            device_id={"seq": partner("seq", distance)},
            device_id_type=MESH,
        )

    def earlier(distance, at):
        return pltpu.make_async_remote_copy(
            src_ref=ends.at[1, at],
            dst_ref=ends_out.at[member, at],
            send_sem=wires.at[1, 0, at, distance - 1],
            recv_sem=wires.at[1, 1, at, distance - 1],
            device_id={"seq": partner("seq", devices - distance)},
            device_id_type=MESH,
        )

    def sums_to(distance, side):
        offset = distance if side == 0 else devices - distance
        return pltpu.make_async_remote_copy(
            src_ref=sums_out.at[member],
            dst_ref=sums_out.at[member],
            send_sem=sum_wires.at[side, 0, distance - 1],
            recv_sem=sum_wires.at[side, 1, distance - 1],
            device_id={"seq": partner("seq", offset)},
            device_id_type=MESH,
        )

    for at in range(chunks):
        delta_pre = (
            jnp.dot(
                rank_ref[...], dt_proj_ref[:, span(at, chunk)], preferred_element_type=jnp.float32
            )
            + dtbias_ref[:, span(at, chunk)]
        )
        for place in range(4):
            group = 4 * at + place
            columns = span(group, LANES)
            here = delta_pre[:, place * LANES : (place + 1) * LANES]
            delta = softplus(here)
            delta_pre_ref[group] = here
            drive_ref[group] = drive_ref[group] * delta
            ddec = jnp.where(masks[0] > 0.0, RESET, delta)
            ddec_ref[group] = ddec
            sums_out[member, group : group + 1, :] = jnp.sum(ddec, axis=0, keepdims=True)
            grady_ref[group] = back_ref[:, columns].astype(jnp.float32) * silu(
                gates_ref[:, columns].astype(jnp.float32)
            )

        def step(t, carry):
            hidden, decayed, pulled = carry
            in_row, out_row = inb_ref[t], outb_ref[t]
            new = ([], [], [])
            for place in range(4):
                here = (4 * at + place, pl.ds(t, 1))
                decay = jnp.exp2(ddec_ref[here] * rates_ref[:, span(4 * at + place, LANES)])
                new[0].append(decay * hidden[place] + drive_ref[here] * in_row)
                product = decay * decayed[place]
                new[1].append(product)
                new[2].append(pulled[place] + product * (grady_ref[here] * out_row))
            return new

        zeros = [jnp.zeros((N, LANES), jnp.float32) for _ in range(4)]
        ones = [jnp.ones((N, LANES), jnp.float32) for _ in range(4)]
        hidden, _, pulled = lax.fori_loop(0, steps, step, (zeros, ones, zeros), unroll=4)
        ends[0, at] = jnp.concatenate(hidden, axis=1).astype(jnp.bfloat16)
        ends[1, at] = jnp.concatenate(pulled, axis=1).astype(jnp.bfloat16)
        for distance in range(1, reach + 1):

            @pl.when(member + distance < devices)
            def _():
                later(distance, at).start()

            @pl.when(member >= distance)
            def _():
                earlier(distance, at).start()

    for distance in range(1, reach + 1):

        @pl.when(member + distance < devices)
        def _():
            sums_to(distance, 0).start()

        @pl.when(member >= distance)
        def _():
            sums_to(distance, 1).start()

    for distance in range(1, reach + 1):

        @pl.when(member + distance < devices)
        def _():
            for at in range(chunks):
                later(distance, at).wait_send()
                earlier(distance, at).wait_recv()
            sums_to(distance, 0).wait_send()
            sums_to(distance, 1).wait_recv()

        @pl.when(member >= distance)
        def _():
            for at in range(chunks):
                earlier(distance, at).wait_send()
                later(distance, at).wait_recv()
            sums_to(distance, 1).wait_send()
            sums_to(distance, 0).wait_recv()
    for copy in row_copies:
        copy.wait()


def front_of(starts, tokens, cot, gain, in_proj, out_proj, conv, cbias, x_proj, dt_proj, dtbias, rates, devices, nrows):
    steps = tokens.shape[0]
    groups = E // LANES
    chunk = 4 * LANES
    chunks = E // chunk
    reach = devices // 2
    halo = 16
    low = jnp.bfloat16
    vmem = pl.BlockSpec(memory_space=pltpu.VMEM)
    grouped = jax.ShapeDtypeStruct((groups, steps, LANES), jnp.float32)
    spread = jax.ShapeDtypeStruct((steps, N, LANES), jnp.float32)
    return pl.pallas_call(
        functools.partial(front_kernel, devices, nrows),
        in_specs=[pl.BlockSpec(memory_space=pltpu.SMEM)]
        + [vmem] * 3
        + [pl.BlockSpec(memory_space=pl.ANY)] * 2
        + [vmem] * 6,
        out_specs=[vmem] * 14,
        out_shape=[
            jax.ShapeDtypeStruct((nrows, steps, D), low),
            jax.ShapeDtypeStruct((steps + halo, E), low),
            jax.ShapeDtypeStruct((steps, E), low),
            jax.ShapeDtypeStruct((steps, E), low),
            grouped,
            grouped,
            grouped,
            grouped,
            grouped,
            jax.ShapeDtypeStruct((steps, R), low),
            spread,
            spread,
            jax.ShapeDtypeStruct((devices, chunks, N, chunk), low),
            jax.ShapeDtypeStruct((devices, groups, LANES), jnp.float32),
        ],
        scratch_shapes=[
            pltpu.VMEM((2 * chunks, D, chunk), low),
            pltpu.VMEM((chunks, chunk, D), low),
            pltpu.VMEM((steps + 8, LANES), jnp.float32),
            pltpu.VMEM((steps + 16, LANES), jnp.int32),
            pltpu.VMEM((K, steps, LANES), jnp.float32),
            pltpu.VMEM((steps, R + 2 * N), jnp.float32),
            pltpu.VMEM((2, chunks, N, chunk), low),
            pltpu.SemaphoreType.DMA((3 * chunks,)),
            pltpu.SemaphoreType.DMA((2,)),
            pltpu.SemaphoreType.DMA((2, 2, chunks, reach)),
            pltpu.SemaphoreType.DMA((2, 2, reach)),
            pltpu.SemaphoreType.DMA((2, max(nrows - 1, 1))),
        ],
        compiler_params=pltpu.CompilerParams(
            collective_id=0, has_side_effects=True, vmem_limit_bytes=60 * 2**20
        ),
        name="front",
    )(starts, tokens, cot, gain, in_proj, out_proj, conv, cbias, x_proj, dt_proj, dtbias, rates)


PACKED = (R + 2 * N, R, N, K, 1, 1, 1, 1)
PACKED_ROWS = 192


def packed_rows():
    spans = []
    at = 0
    for count in PACKED:
        spans.append((at, at + count))
        at += count
    return spans


def silu_pair(values):
    sigmoid_of = jax.nn.sigmoid(values)
    return values * sigmoid_of, sigmoid_of * (1.0 + values * (1.0 - sigmoid_of))


def core_kernel(
    nrows,
    devices,
    starts_ref,
    tokens_ref,
    cot_ref,
    gain_ref,
    in_proj_ref,
    out_proj_ref,
    conv_ref,
    x_proj_ref,
    dt_proj_ref,
    dskip_ref,
    rates_ref,
    normed_ref,
    inner_ref,
    gates_ref,
    back_ref,
    pre_act_ref,
    delta_pre_ref,
    ddec_ref,
    drive_ref,
    grady_ref,
    rank_ref,
    inb_ref,
    outb_ref,
    all_ref,
    sums_ref,
    cot_all_ref,
    output_ref,
    grad_ref,
    gin_out,
    gout_out,
    small_out,
    norm_out,
    in_proj_buf,
    out_proj_buf,
    docid,
    masks,
    kept,
    first,
    second,
    gin,
    gout,
    gated,
    back_gates,
    back_inner,
    grad_act,
    grad_conv,
    padded,
    rank_back,
    proj_back,
    normed_sib,
    gated_got,
    back_got,
    gout_sum,
    gout_low,
    gout_got,
    gin_sum,
    gin_low,
    gin_got,
    gin_pub,
    small,
    small_low,
    small_got,
    small_part,
    small_seq,
    norm_seq,
    norm_rows,
    loads,
    sib_wires,
    halo_wires,
    gated_wires,
    back_wires,
    line_wires,
    plane_wires,
    row_wires,
    seq_wires,
    local,
):
    row = lax.axis_index("rows")
    member = lax.axis_index("seq")
    level, side = member // 2, lax.rem(member, 2)
    levels = devices // 2
    steps = tokens_ref.shape[0]
    groups = E // LANES
    chunk = 4 * LANES
    chunks = E // chunk
    shard = E // devices
    halo = inner_ref.shape[0] - steps
    reach = devices // 2
    half = N // 2
    low = jnp.bfloat16
    wide = jnp.float32
    spans = packed_rows()

    in_loads = [
        pltpu.make_async_copy(
            in_proj_ref.at[:, span(at, chunk)], in_proj_buf.at[at], loads.at[at]
        )
        for at in range(2 * chunks)
    ]
    out_load = pltpu.make_async_copy(out_proj_ref, out_proj_buf, loads.at[2 * chunks])
    for load in in_loads + [out_load]:
        load.start()

    def share(index, size):
        return pl.ds(pl.multiple_of(index * size, size), size)

    def plane(turn, other):
        return {
            "rows": lax.rem(row + turn, nrows),
            "seq": 2 * level + lax.rem(side + other, 2),
        }

    def line(turn):
        return {"seq": 2 * lax.rem(level + turn, levels) + side}

    def remote(source, target, send, recv, device):
        return pltpu.make_async_remote_copy(
            src_ref=source,
            dst_ref=target,
            send_sem=send,
            recv_sem=recv,
            device_id=device,
            device_id_type=MESH,
        )

    def begin(copies):
        for copy in copies:
            copy.start()
        return copies

    def settle(copies):
        for copy in copies:
            copy.wait()

    barrier = pltpu.get_barrier_semaphore()
    greeted = [{"seq": partner("seq", offset)} for offset in range(1, devices)]
    greeted += [plane(turn, other) for turn in range(1, nrows) for other in range(2)]
    for device in greeted:
        pl.semaphore_signal(barrier, inc=1, device_id=device, device_id_type=MESH)

    places = member * steps - 8 + lax.broadcasted_iota(jnp.int32, docid.shape, 0)
    count = jnp.zeros(docid.shape, jnp.int32)
    for index in range(starts_ref.shape[0]):
        count = count + jnp.where(places >= starts_ref[index], 1, 0)
    docid[...] = count
    for offset in range(1, K):
        masks[offset] = jnp.where(
            docid[8 - offset : 16 - offset + steps, :] == docid[8:, :], 1.0, 0.0
        )
    gin[...] = jnp.zeros_like(gin)
    gout[...] = jnp.zeros_like(gout)
    rank_back[...] = jnp.zeros_like(rank_back)
    small[...] = jnp.zeros_like(small)
    pl.semaphore_wait(barrier, len(greeted))

    normed_copy = remote(
        normed_ref, normed_sib, sib_wires.at[0], sib_wires.at[1], {"seq": 2 * level + 1 - side}
    )
    normed_copy.start()

    def fold(values):
        return values[:half] + values[half:]

    def collapse(source, place):
        total = source[place, pl.ds(0, steps, stride=half), :]
        for index in range(1, half):
            total = total + source[place, pl.ds(index, steps, stride=half), :]
        return total

    def lanes(at, place):
        return share(4 * at + place, LANES)

    def column_sum(values):
        return jnp.sum(values, axis=0, keepdims=True)

    def trade(kind, source, at, turn):
        copies = []
        for other in range(2):
            columns = share(2 * at + lax.rem(side + other, 2), shard)
            target = back_got.at[kind, other, row]
            if turn == 0 and other == 0:
                copies.append(
                    pltpu.make_async_copy(source.at[:, columns], target, local.at[kind])
                )
            else:
                copies.append(
                    remote(
                        source.at[:, columns],
                        target,
                        back_wires.at[kind, 0, 2 * turn + other],
                        back_wires.at[kind, 1, 2 * turn + other],
                        plane(turn, other),
                    )
                )
        return begin(copies)

    def gated_copy(target_member):
        return remote(
            gated.at[:, share(target_member, shard)],
            gated_got.at[share(member, steps), :],
            gated_wires.at[0, target_member],
            gated_wires.at[1, member],
            {"seq": target_member},
        )

    gate_moves = []
    order = [(turn, lax.rem(row + turn, nrows)) for turn in [*range(1, nrows), 0]]
    for turn, at in order:

        def through(device, states):
            new = []
            for place in range(4):
                total = sums_ref[device, pl.ds(4 * at + place, 1), :]
                factor = jnp.exp2(total * rates_ref[:, lanes(at, place)])
                new.append(
                    factor * states[place]
                    + all_ref[device, at, :, place * LANES : (place + 1) * LANES].astype(wide)
                )
            return new

        def forward(t, hidden):
            in_row, out_row = inb_ref[t], outb_ref[t]
            new = []
            for place in range(4):
                here = (4 * at + place, pl.ds(t, 1))
                decay = jnp.exp2(ddec_ref[here] * rates_ref[:, lanes(at, place)])
                state = decay * hidden[place] + drive_ref[here] * in_row
                kept[t + 1, place] = state
                first[place, share(t, half), :] = fold(state * out_row)
                new.append(state)
            return new

        def backward(back, carry):
            later, grates = carry
            t = steps - 1 - back
            in_row, out_row = inb_ref[t], outb_ref[t]
            gin_row, gout_row = gin[t], gout[t]
            new = ([], [])
            for place in range(4):
                here = (4 * at + place, pl.ds(t, 1))
                grady = grady_ref[here]
                delta = ddec_ref[here]
                rates = rates_ref[:, lanes(at, place)]
                adjoint = grady * out_row + later[place]
                gout_row = gout_row + grady * kept[t + 1, place]
                gin_row = gin_row + adjoint * drive_ref[here]
                first[place, share(t, half), :] = fold(adjoint * in_row)
                passed = jnp.exp2(delta * rates) * adjoint
                pulled = passed * kept[t, place]
                second[place, share(t, half), :] = fold(pulled * rates)
                new[0].append(passed)
                new[1].append(grates[place] + pulled * delta)
            gin[t] = gin_row
            gout[t] = gout_row
            return new

        zeros = [jnp.zeros((N, LANES), wide) for _ in range(4)]
        entering = lax.fori_loop(jnp.maximum(member - reach, 0), member, through, zeros)
        last = jnp.minimum(member + reach, devices - 1)
        leaving = lax.fori_loop(0, last - member, lambda d, s: through(last - d, s), zeros)
        for place in range(4):
            kept[0, place] = entering[place]
        lax.fori_loop(0, steps, forward, entering, unroll=4)
        for place in range(4):
            group, columns = 4 * at + place, lanes(at, place)
            act = silu(pre_act_ref[group])
            y_full = collapse(first, place) + dskip_ref[:, columns] * act
            gate, slope = silu_pair(gates_ref[:, columns].astype(wide))
            gated[:, columns] = (y_full * gate).astype(low)
            back_gates[:, columns] = (
                back_ref[:, columns].astype(wide) * y_full * slope
            ).astype(low)
            small[spans[6][0] : spans[6][1], columns] = column_sum(grady_ref[group] * act)
        gate_moves += trade(1, back_gates, at, turn)
        for core in range(2):

            @pl.when(2 * at + core != member)
            def _():
                gated_copy(2 * at + core).start()

        _, grates = lax.fori_loop(0, steps, backward, (leaving, zeros), unroll=4)
        lows = []
        for place in range(4):
            group, columns = 4 * at + place, lanes(at, place)
            along = collapse(first, place)
            delta_pre = delta_pre_ref[group]
            act = silu(pre_act_ref[group])
            grad_delta = along * act + collapse(second, place) * math.log(2.0)
            pre_low = (grad_delta * jax.nn.sigmoid(delta_pre)).astype(low)
            lows.append(pre_low)
            grad_act[group] = grady_ref[group] * dskip_ref[:, columns] + along * softplus(delta_pre)
            small[spans[5][0] : spans[5][1], columns] = column_sum(pre_low.astype(wide))
            small[spans[2][0] : spans[2][1], columns] = (
                grates[place] * rates_ref[:, columns] * math.log(2.0)
            )
        lows = jnp.concatenate(lows, axis=1)
        rank_back[...] += lax.dot_general(
            lows,
            dt_proj_ref[:, share(at, chunk)],
            (((1,), (1,)), ((), ())),
            preferred_element_type=wide,
        )
        small[spans[1][0] : spans[1][1], share(at, chunk)] = lax.dot_general(
            rank_ref[...], lows, (((0,), (0,)), ((), ())), preferred_element_type=wide
        )

    gated_got[share(member, steps), :] = gated[:, share(member, shard)]
    for offset in range(1, devices):
        gated_copy(partner("seq", offset)).wait_send()
        source = partner("seq", offset)
        remote(
            gated.at[:, share(member, shard)],
            gated_got.at[share(source, steps), :],
            gated_wires.at[0, member],
            gated_wires.at[1, source],
            {"seq": source},
        ).wait_recv()

    def to_rows(kind, make):
        return begin(
            [
                remote(
                    *make(partner("rows", offset), offset - 1),
                    row_wires.at[kind, 0, offset - 1],
                    row_wires.at[kind, 1, offset - 1],
                    {"rows": partner("rows", offset)},
                )
                for offset in range(1, nrows)
            ]
        )

    def to_seq(kind, make):
        return begin(
            [
                remote(
                    *make(partner("seq", offset), offset - 1),
                    seq_wires.at[kind, 0, offset - 1],
                    seq_wires.at[kind, 1, offset - 1],
                    {"seq": partner("seq", offset)},
                )
                for offset in range(1, devices)
            ]
        )

    def squares(values):
        return jnp.sum(jnp.sum(values * values, axis=0, keepdims=True), axis=1, keepdims=True)

    def in_grads(kind):
        total = jnp.zeros((D, shard), wide)
        for other, normed in ((0, normed_ref), (1, normed_sib)):
            for source in range(nrows):
                total = total + lax.dot_general(
                    normed[source],
                    back_got[kind, other, source],
                    (((0,), (0,)), ((), ())),
                    preferred_element_type=wide,
                )
        gin_sum[kind] = total
        gin_low[kind] = total.astype(low)
        return begin(
            [
                remote(
                    gin_low.at[kind, share(lax.rem(level + turn, levels), D // levels), :],
                    gin_got.at[kind, turn - 1],
                    line_wires.at[kind, 0, turn - 1],
                    line_wires.at[kind, 1, turn - 1],
                    line(turn),
                )
                for turn in range(1, levels)
            ]
        )

    def in_share(kind):
        total = gin_sum[kind, share(level, D // levels), :]
        for turn in range(levels - 1):
            total = total + gin_got[kind, turn].astype(wide)
        gin_pub[kind] = total.astype(low)
        owned = D // devices
        columns = share(kind * devices + 2 * row + side, shard)
        gin_out[:, columns] = gin_pub[kind, share(side, owned), :]
        copies = [
            remote(
                gin_pub.at[kind, share(lax.rem(side + other, 2), owned), :],
                gin_out.at[:, columns],
                plane_wires.at[kind, 0, 2 * turn + other],
                plane_wires.at[kind, 1, 2 * turn + other],
                plane(turn, other),
            )
            for turn in range(nrows)
            for other in range(2)
            if turn + other > 0
        ]
        return begin(copies), squares(total)

    outer = gout_out.shape[0] // nrows
    gout_sum[...] = lax.dot_general(
        gated_got[...], cot_all_ref[...], (((0,), (0,)), ((), ())), preferred_element_type=wide
    )
    gout_low[...] = gout_sum[...].astype(low)
    gout_moves = to_rows(
        0, lambda other, at: (gout_low.at[share(other, outer), :], gout_got.at[at])
    )
    normed_copy.wait()
    settle(gate_moves)
    gate_moves = in_grads(1)

    proj_back[:, :R] = rank_back[...].astype(low)
    proj_back[:, R : R + N] = jnp.sum(gin[...], axis=2).astype(low)
    proj_back[:, R + N :] = jnp.sum(gout[...], axis=2).astype(low)
    for at in range(chunks):
        pulled = jnp.dot(
            proj_back[...], x_proj_ref[:, span(at, chunk)], preferred_element_type=wide
        )
        lows = []
        for place in range(4):
            group = 4 * at + place
            act, slope = silu_pair(pre_act_ref[group])
            lows.append(act.astype(low))
            grad_conv[group, :steps, :] = (
                grad_act[group] + pulled[:, place * LANES : (place + 1) * LANES]
            ) * slope
        small[spans[0][0] : spans[0][1], span(at, chunk)] = lax.dot_general(
            proj_back[...],
            jnp.concatenate(lows, axis=1),
            (((0,), (0,)), ((), ())),
            preferred_element_type=wide,
        )
    halo_copy = remote(
        grad_conv.at[:, 0:8, :],
        grad_conv.at[:, steps : steps + 8, :],
        halo_wires.at[0],
        halo_wires.at[1],
        {"seq": partner("seq", devices - 1)},
    )

    @pl.when(member > 0)
    def _():
        halo_copy.start()

    @pl.when(member == devices - 1)
    def _():
        grad_conv[:, steps : steps + 8, :] = jnp.zeros((groups, 8, LANES), wide)

    out_load.wait()
    stream = tokens_ref[...].astype(wide)
    output_ref[...] = stream + jnp.dot(
        gated[...], out_proj_buf[...], preferred_element_type=wide
    )
    for load in in_loads:
        load.wait()
    grad_normed = jnp.zeros((steps, D), wide)
    for at in range(chunks):
        grad_normed = grad_normed + lax.dot_general(
            back_gates[:, span(at, chunk)],
            in_proj_buf[chunks + at],
            (((1,), (1,)), ((), ())),
            preferred_element_type=wide,
        )

    @pl.when(member > 0)
    def _():
        halo_copy.wait_send()

    @pl.when(member < devices - 1)
    def _():
        halo_copy.wait_recv()

    inner_moves = []
    for turn, at in order:
        for place in range(4):
            group, columns = 4 * at + place, lanes(at, place)
            padded[...] = inner_ref[halo - 8 :, columns].astype(wide)
            here = grad_conv[group, :steps, :]
            pulled = conv_ref[0:1, columns] * here
            small[spans[4][0] : spans[4][1], columns] = column_sum(here)
            at_row = spans[3][0]
            small[at_row : at_row + 1, columns] = column_sum(here * padded[8:, :])
            for offset in range(1, K):
                small[at_row + offset : at_row + offset + 1, columns] = column_sum(
                    here * masks[offset, :steps, :] * padded[8 - offset : 8 - offset + steps, :]
                )
                pulled = pulled + conv_ref[offset : offset + 1, columns] * (
                    grad_conv[group, offset : offset + steps, :]
                    * masks[offset, offset : offset + steps, :]
                )
            back_inner[:, columns] = pulled.astype(low)
        inner_moves += trade(0, back_inner, at, turn)

    for at in range(chunks):
        grad_normed = grad_normed + lax.dot_general(
            back_inner[:, span(at, chunk)],
            in_proj_buf[at],
            (((1,), (1,)), ((), ())),
            preferred_element_type=wide,
        )
    inverse = lax.rsqrt(jnp.mean(stream * stream, axis=1, keepdims=True) + EPS)
    grad_gain = column_sum(grad_normed * stream * inverse)
    owned = D // devices
    for index in range(devices):
        small[spans[7][0] : spans[7][1], index * shard : index * shard + owned] = grad_gain[
            :, index * owned : (index + 1) * owned
        ]
    scaled = grad_normed * gain_ref[...]
    grad_ref[...] = (
        cot_ref[...].astype(wide)
        + inverse * scaled
        - stream
        * inverse
        * inverse
        * inverse
        * jnp.mean(scaled * stream, axis=1, keepdims=True)
    )
    few = small_low.shape[0] // nrows
    small_low[...] = small[...].astype(low)
    small_moves = to_rows(
        1, lambda other, at: (small_low.at[share(other, few), :], small_got.at[at])
    )

    settle(gout_moves)
    total = gout_sum[share(row, outer), :]
    for at in range(nrows - 1):
        total = total + gout_got[at].astype(wide)
    gout_out[share(row, outer), :] = total.astype(low)
    gout_moves = to_rows(
        2,
        lambda other, at: (
            gout_out.at[share(row, outer), :],
            gout_out.at[share(row, outer), :],
        ),
    )
    norm = squares(total)

    settle(inner_moves)
    inner_moves = in_grads(0)

    settle(small_moves)
    total = small[share(row, few), :]
    for at in range(nrows - 1):
        total = total + small_got[at].astype(wide)
    small_part[...] = total.astype(low)
    small_moves = to_seq(
        0, lambda other, at: (small_part.at[:, share(other, shard)], small_seq.at[at])
    )

    settle(gate_moves)
    gate_moves, part = in_share(1)
    norm = norm + part

    settle(small_moves)
    total = small_part[:, share(member, shard)].astype(wide)
    for at in range(devices - 1):
        total = total + small_seq[at].astype(wide)
    small_out[share(row, few), :] = total.astype(low)
    small_moves = to_rows(
        3,
        lambda other, at: (
            small_out.at[share(row, few), :],
            small_out.at[share(row, few), :],
        ),
    )
    norm = norm + squares(total)

    settle(inner_moves)
    inner_moves, part = in_share(0)
    norm_seq[member] = jnp.broadcast_to(norm + part, (8, LANES))
    settle(to_seq(1, lambda other, at: (norm_seq.at[member], norm_seq.at[member])))
    norm_rows[row] = jnp.sum(norm_seq[...], axis=0)
    settle(to_rows(4, lambda other, at: (norm_rows.at[row], norm_rows.at[row])))
    norm_out[...] = jnp.sqrt(jnp.sum(norm_rows[...], axis=0))
    settle(gout_moves)
    settle(gate_moves)
    settle(small_moves)
    settle(inner_moves)


def core_of(operands, nrows, devices):
    steps = operands[1].shape[0]
    groups = E // LANES
    chunk = 4 * LANES
    chunks = E // chunk
    levels = devices // 2
    shard = E // devices
    low, wide = jnp.bfloat16, jnp.float32
    few = PACKED_ROWS // nrows
    vmem = pl.BlockSpec(memory_space=pltpu.VMEM)
    specs = [vmem] * len(operands)
    specs[0] = pl.BlockSpec(memory_space=pltpu.SMEM)
    specs[4] = specs[5] = pl.BlockSpec(memory_space=pl.ANY)
    dma = pltpu.SemaphoreType.DMA
    return pl.pallas_call(
        functools.partial(core_kernel, nrows, devices),
        in_specs=specs,
        out_specs=[vmem] * 6,
        out_shape=[
            jax.ShapeDtypeStruct((steps, D), wide),
            jax.ShapeDtypeStruct((steps, D), wide),
            jax.ShapeDtypeStruct((D // devices, 2 * E), low),
            jax.ShapeDtypeStruct((shard, D), low),
            jax.ShapeDtypeStruct((PACKED_ROWS, shard), low),
            jax.ShapeDtypeStruct((8, LANES), wide),
        ],
        scratch_shapes=[
            pltpu.VMEM((2 * chunks, D, chunk), low),
            pltpu.VMEM((E, D), low),
            pltpu.VMEM((steps + 16, LANES), jnp.int32),
            pltpu.VMEM((K, steps + 8, LANES), wide),
            pltpu.VMEM((steps + 1, 4, N, LANES), wide),
            pltpu.VMEM((4, steps * N // 2, LANES), wide),
            pltpu.VMEM((4, steps * N // 2, LANES), wide),
            pltpu.VMEM((steps, N, LANES), wide),
            pltpu.VMEM((steps, N, LANES), wide),
            pltpu.VMEM((steps, E), low),
            pltpu.VMEM((steps, E), low),
            pltpu.VMEM((steps, E), low),
            pltpu.VMEM((groups, steps, LANES), wide),
            pltpu.VMEM((groups, steps + 8, LANES), wide),
            pltpu.VMEM((steps + 8, LANES), wide),
            pltpu.VMEM((steps, R), wide),
            pltpu.VMEM((steps, R + 2 * N), low),
            pltpu.VMEM((nrows, steps, D), low),
            pltpu.VMEM((steps * devices, shard), low),
            pltpu.VMEM((2, 2, nrows, steps, shard), low),
            pltpu.VMEM((shard, D), wide),
            pltpu.VMEM((shard, D), low),
            pltpu.VMEM((nrows - 1, shard // nrows, D), low),
            pltpu.VMEM((2, D, shard), wide),
            pltpu.VMEM((2, D, shard), low),
            pltpu.VMEM((2, levels - 1, D // levels, shard), low),
            pltpu.VMEM((2, D // levels, shard), low),
            pltpu.VMEM((PACKED_ROWS, E), wide),
            pltpu.VMEM((PACKED_ROWS, E), low),
            pltpu.VMEM((nrows - 1, few, E), low),
            pltpu.VMEM((few, E), low),
            pltpu.VMEM((devices - 1, few, shard), low),
            pltpu.VMEM((devices, 8, LANES), wide),
            pltpu.VMEM((nrows, 8, LANES), wide),
            dma((2 * chunks + 1,)),
            dma((2,)),
            dma((2,)),
            dma((2, devices)),
            dma((2, 2, 2 * nrows)),
            dma((2, 2, levels - 1)),
            dma((2, 2, 2 * nrows)),
            dma((5, 2, nrows - 1)),
            dma((2, 2, devices - 1)),
            dma((2,)),
        ],
        compiler_params=pltpu.CompilerParams(
            collective_id=1, has_side_effects=True, vmem_limit_bytes=62 * 2**20
        ),
        name="core",
    )(*operands)


def update_kernel(member_ref, norm_ref, gin_ref, gout_ref, small_ref, *refs):
    weights, moments, averages, outs = refs[:10], refs[10:20], refs[20:30], refs[30:]
    shrink_by = 1.0 / jnp.maximum(norm_ref[0:1, 0:1], 1.0)

    def renew(ordinal, grad, at=Ellipsis):
        clipped = grad * shrink_by
        momentum_new = MOMENTUM * moments[ordinal][at] + clipped
        renewed = weights[ordinal][at].astype(jnp.float32) - RATES[ordinal] * math.sqrt(PARAMS) * (
            clipped + MOMENTUM * momentum_new
        )
        outs[3 * ordinal][at] = momentum_new
        outs[3 * ordinal + 1][at] = renewed
        outs[3 * ordinal + 2][at] = AVERAGE * averages[ordinal][at] + (1.0 - AVERAGE) * renewed

    renew(1, gin_ref[...].astype(jnp.float32))
    renew(9, gout_ref[...].astype(jnp.float32))

    @pl.when(pl.program_id(0) == 0)
    def _():
        spans = packed_rows()

        def part(index):
            return small_ref[spans[index][0] : spans[index][1], :].astype(jnp.float32)

        small = small_ref[...].astype(jnp.float32)
        renew(4, part(0))
        renew(5, part(1))
        renew(7, part(2))
        renew(2, part(3))
        for ordinal, index in ((3, 4), (6, 5), (8, 6)):
            renew(ordinal, small[spans[index][0] : spans[index][1]])
        gain = small[spans[7][0] : spans[7][1], : weights[0].shape[1]]
        renew(0, gain)


def update_of(member, norm_tile, gin, gout, small, weights, moments, averages):
    inner = gin.shape[0]
    channels = gout.shape[0]
    blocks = 8
    outer = channels // blocks
    block = gin.shape[1] // blocks
    flat = (0, 3, 6, 8)

    def rows_of(array, ordinal):
        return array.reshape(1, -1) if ordinal in flat else array.T if ordinal == 4 else array

    def shard(shape, ordinal):
        if ordinal == 1:
            return pl.BlockSpec((inner, block), lambda j, m: (0, j))
        if ordinal == 9:
            return pl.BlockSpec((outer, shape[1]), lambda j, m: (j, 0))
        return pl.BlockSpec(shape, lambda j, m: (0, 0))

    def weight(shape, ordinal):
        if ordinal == 1:
            return pl.BlockSpec((inner, block), lambda j, m: (m[0], j))
        if ordinal == 9:
            return pl.BlockSpec((outer, shape[1]), lambda j, m: (m[0] * blocks + j, 0))
        return pl.BlockSpec(shape, lambda j, m: (0, m[0]))

    weights = [rows_of(array, ordinal) for ordinal, array in enumerate(weights)]
    moments = [rows_of(array, ordinal) for ordinal, array in enumerate(moments)]
    averages = [rows_of(array, ordinal) for ordinal, array in enumerate(averages)]
    shapes = [array.shape for array in moments]
    shards = [shard(shape, ordinal) for ordinal, shape in enumerate(shapes)]
    outs = pl.pallas_call(
        update_kernel,
        grid_spec=pltpu.PrefetchScalarGridSpec(
            num_scalar_prefetch=1,
            grid=(blocks,),
            in_specs=[
                pl.BlockSpec(norm_tile.shape, lambda j, m: (0, 0)),
                pl.BlockSpec((inner, block), lambda j, m: (0, j)),
                pl.BlockSpec((outer, gout.shape[1]), lambda j, m: (j, 0)),
                pl.BlockSpec(small.shape, lambda j, m: (0, 0)),
            ]
            + [weight(shape, ordinal) for ordinal, shape in enumerate(shapes)]
            + shards
            + shards,
            out_specs=[shards[ordinal] for ordinal in range(10) for _ in range(3)],
        ),
        out_shape=[
            jax.ShapeDtypeStruct(shapes[ordinal], jnp.float32)
            for ordinal in range(10)
            for _ in range(3)
        ],
        compiler_params=pltpu.CompilerParams(vmem_limit_bytes=63 * 2**20),
        name="update",
    )(member, norm_tile, gin, gout, small, *weights, *moments, *averages)
    return [
        out.reshape(-1) if index // 3 in flat else out.T if index // 3 == 4 else out
        for index, out in enumerate(outs)
    ]


def local(
    tokens,
    cotangent,
    doc_lengths,
    norm_gain,
    in_proj,
    conv_weight,
    conv_bias,
    x_proj,
    dt_proj,
    dt_bias,
    a_log,
    d_skip,
    out_proj,
    moment_norm_gain,
    moment_in_proj,
    moment_conv_weight,
    moment_conv_bias,
    moment_x_proj,
    moment_dt_proj,
    moment_dt_bias,
    moment_a_log,
    moment_d_skip,
    moment_out_proj,
    average_norm_gain,
    average_in_proj,
    average_conv_weight,
    average_conv_bias,
    average_x_proj,
    average_dt_proj,
    average_dt_bias,
    average_a_log,
    average_d_skip,
    average_out_proj,
):
    devices = lax.axis_size("seq")
    member_id = lax.axis_index("seq")
    channels = E // devices
    begin = member_id * channels
    stream = tokens[0].astype(jnp.float32)
    steps = stream.shape[0]
    length = steps * devices
    cot_low = cotangent[0]
    inverse = lax.rsqrt(jnp.mean(stream * stream, axis=1, keepdims=True) + EPS)
    rates = -jnp.exp(a_log)
    scaled_rates = rates * (1.0 / math.log(2.0))
    lengths = doc_lengths[0]
    starts = (jnp.cumsum(lengths) - lengths).astype(jnp.int32)
    nrows = lax.axis_size("rows")
    direct = devices == 2 * nrows and E % (2 * nrows * LANES) == 0 and E == nrows * 4 * LANES
    (
        normed,
        inner_low,
        gates_low,
        back_gated,
        pre_act,
        delta_pre,
        ddec,
        drive,
        grady_rows,
        rank_low,
        inb,
        outb,
        everyone,
        all_sums,
    ) = front_of(
        starts,
        tokens[0],
        cot_low,
        norm_gain[None],
        in_proj,
        out_proj,
        conv_weight,
        conv_bias[None],
        x_proj.T,
        dt_proj,
        dt_bias[None],
        scaled_rates,
        devices,
        nrows if direct else 1,
    )
    cot_all = lax.all_gather(cot_low, "seq", axis=0, tiled=True)
    member_word = jnp.reshape(member_id, (1,)).astype(jnp.int32)
    moments = (
        moment_norm_gain,
        moment_in_proj,
        moment_conv_weight,
        moment_conv_bias,
        moment_x_proj,
        moment_dt_proj,
        moment_dt_bias,
        moment_a_log,
        moment_d_skip,
        moment_out_proj,
    )
    averages = (
        average_norm_gain,
        average_in_proj,
        average_conv_weight,
        average_conv_bias,
        average_x_proj,
        average_dt_proj,
        average_dt_bias,
        average_a_log,
        average_d_skip,
        average_out_proj,
    )
    if direct:
        weights = (
            norm_gain,
            in_proj,
            conv_weight,
            conv_bias,
            x_proj,
            dt_proj,
            dt_bias,
            a_log,
            d_skip,
            out_proj,
        )
        block_output, input_grad, gin_share, gout_share, small, norm_tile = core_of(
            (
                starts,
                tokens[0],
                cot_low,
                norm_gain[None],
                in_proj,
                out_proj,
                conv_weight,
                x_proj.T,
                dt_proj,
                d_skip[None],
                scaled_rates,
                normed,
                inner_low,
                gates_low,
                back_gated,
                pre_act,
                delta_pre,
                ddec,
                drive,
                grady_rows,
                rank_low,
                inb,
                outb,
                everyone,
                all_sums,
                cot_all,
            ),
            nrows,
            devices,
        )
        updated = update_of(
            member_word, norm_tile, gin_share, gout_share, small, weights, moments, averages
        )
        return (block_output[None], input_grad[None], norm_tile[0, 0], *updated)
    normed_all = lax.all_gather(normed[0], "seq", axis=0, tiled=True)
    positions = member_id * steps + jnp.arange(-8, steps + 8, dtype=jnp.int32)
    docid, starting = doc_tables(doc_lengths[0], positions)
    masks = []
    for offset in range(K):
        linked = (docid[8:] == docid[8 - offset : steps + 16 - offset]) & (
            positions[8 - offset : steps + 16 - offset] >= 0
        )
        masks.append((linked & (positions[8:] < length)).astype(jnp.float32)[:, None])

    def flat(values):
        return jnp.transpose(values, (1, 0, 2)).reshape(steps, E)

    pre_act, delta_pre = flat(pre_act), flat(delta_pre)
    padded = inner_low[8:].astype(jnp.float32)
    gates = gates_low.astype(jnp.float32)
    act = silu(pre_act)
    act_low = act.astype(jnp.bfloat16)
    delta = jax.nn.softplus(delta_pre)
    silu_gate = silu(gates)
    chan_back = back_gated.astype(jnp.float32)
    grad_y = chan_back * silu_gate
    scanned, along_in, pulled_sum, gin, gout, grad_rates = scan_of(
        member_word, ddec, drive, grady_rows, inb, outb, scaled_rates, everyone, all_sums, 512
    )
    scanned, along_in, pulled_sum = flat(scanned), flat(along_in), flat(pulled_sum)
    y_full = scanned + d_skip[None, :] * act
    gated = (y_full * silu_gate).astype(jnp.bfloat16)
    block_output = (
        stream + jnp.dot(gated, out_proj, preferred_element_type=jnp.float32)
    )[None]
    grad_gates = chan_back * y_full * silu_slope(gates)
    grad_dskip = jnp.sum(grad_y * act, axis=0)
    grad_in_mat = jnp.sum(gin, axis=2)
    grad_out_mat = jnp.sum(gout, axis=2)
    grad_delta = along_in * act + pulled_sum * math.log(2.0)
    grad_alog = grad_rates * rates
    grad_pre = (grad_delta * jax.nn.sigmoid(delta_pre)).astype(jnp.bfloat16)
    grad_dtbias = jnp.sum(grad_pre.astype(jnp.float32), axis=0)
    grad_dtproj = lax.dot_general(
        rank_low, grad_pre, (((0,), (0,)), ((), ())), preferred_element_type=jnp.float32
    )
    rank_back = lax.dot_general(
        grad_pre, dt_proj, (((1,), (1,)), ((), ())), preferred_element_type=jnp.float32
    )
    proj_back = jnp.concatenate([rank_back, grad_in_mat, grad_out_mat], axis=1).astype(jnp.bfloat16)
    grad_xproj = lax.dot_general(
        act_low, proj_back, (((0,), (0,)), ((), ())), preferred_element_type=jnp.float32
    )
    grad_act = (
        grad_y * d_skip[None, :]
        + along_in * delta
        + lax.dot_general(
            proj_back, x_proj, (((1,), (1,)), ((), ())), preferred_element_type=jnp.float32
        )
    )
    grad_pre_act = grad_act * silu_slope(pre_act)
    ahead = lax.ppermute(
        grad_pre_act[:8], "seq", [(i + 1, i) for i in range(devices - 1)]
    )
    extended = jnp.concatenate([grad_pre_act, ahead], axis=0)
    grad_conv_bias = jnp.sum(grad_pre_act, axis=0)
    grad_inner = jnp.zeros_like(gates)
    conv_rows = []
    for offset in range(K):
        masked = extended * masks[offset]
        conv_rows.append(
            jnp.sum(masked[:steps] * padded[8 - offset : 8 - offset + steps], axis=0)
        )
        grad_inner = grad_inner + conv_weight[offset][None, :] * masked[offset : offset + steps]
    grad_convw = jnp.stack(conv_rows)
    back_xz = jnp.stack([grad_inner, grad_gates]).astype(jnp.bfloat16)
    grad_normed = lax.dot_general(
        back_xz[0], in_proj[:, :E], (((1,), (1,)), ((), ())), preferred_element_type=jnp.float32
    ) + lax.dot_general(
        back_xz[1], in_proj[:, E:], (((1,), (1,)), ((), ())), preferred_element_type=jnp.float32
    )
    grad_gain = jnp.sum(grad_normed * stream * inverse, axis=0)
    scaled = grad_normed * norm_gain[None, :]
    input_grad = (
        cot_low.astype(jnp.float32)
        + inverse * scaled
        - stream * inverse * inverse * inverse * jnp.mean(scaled * stream, axis=1, keepdims=True)
    )
    small = jnp.concatenate(
        [
            grad_xproj.T,
            grad_dtproj,
            grad_alog,
            grad_convw,
            grad_conv_bias[None],
            grad_dtbias[None],
            grad_dskip[None],
            jnp.pad(
                grad_gain.reshape(devices, D // devices),
                ((0, 0), (0, channels - D // devices)),
            ).reshape(1, E),
            jnp.zeros((PACKED_ROWS - sum(PACKED), E), jnp.float32),
        ],
        axis=0,
    )
    gated_mine = lax.all_to_all(gated, "seq", split_axis=1, concat_axis=0, tiled=True)
    back_mine = lax.all_to_all(back_xz, "seq", split_axis=2, concat_axis=1, tiled=True)
    gout_share = lax.psum(
        lax.dot_general(
            gated_mine, cot_all, (((0,), (0,)), ((), ())), preferred_element_type=jnp.float32
        ),
        "rows",
    )
    gin_share = lax.psum(
        jnp.einsum("td,ktc->dkc", normed_all, back_mine, preferred_element_type=jnp.float32),
        "rows",
    )
    gin_share = lax.all_to_all(
        gin_share, "seq", split_axis=0, concat_axis=2, tiled=True
    ).reshape(D // devices, 2 * E)
    small = lax.psum(small, "rows")
    small = lax.psum_scatter(small, "seq", scatter_dimension=1, tiled=True)
    squares = jnp.sum(gin_share * gin_share) + jnp.sum(gout_share * gout_share)
    grad_norm = jnp.sqrt(lax.psum(squares + jnp.sum(small * small), "seq"))
    results = [block_output, input_grad[None], grad_norm]
    parts = [small[low:high] for low, high in packed_rows()]
    owner_grads = (
        parts[7][0, : D // devices],
        gin_share.astype(jnp.float32),
        parts[3],
        parts[4][0],
        parts[0].T,
        parts[1],
        parts[5][0],
        parts[2],
        parts[6][0],
        gout_share.astype(jnp.float32),
    )
    conv_mine = lax.dynamic_slice_in_dim(conv_weight, begin, channels, 1)
    cbias_mine = lax.dynamic_slice_in_dim(conv_bias, begin, channels, 0)
    xproj_mine = lax.dynamic_slice_in_dim(x_proj, begin, channels, 0)
    dtproj_mine = lax.dynamic_slice_in_dim(dt_proj, begin, channels, 1)
    dtbias_mine = lax.dynamic_slice_in_dim(dt_bias, begin, channels, 0)
    alog_mine = lax.dynamic_slice_in_dim(a_log, begin, channels, 1)
    dskip_mine = lax.dynamic_slice_in_dim(d_skip, begin, channels, 0)
    shrink_by = 1.0 / jnp.maximum(grad_norm, 1.0)
    gain_rows = D // devices
    outer_rows = E // devices
    mine_weights = (
        lax.dynamic_slice_in_dim(norm_gain, member_id * gain_rows, gain_rows, 0),
        lax.dynamic_slice_in_dim(in_proj, member_id * gain_rows, gain_rows, 0).astype(jnp.float32),
        conv_mine,
        cbias_mine,
        xproj_mine.astype(jnp.float32),
        dtproj_mine.astype(jnp.float32),
        dtbias_mine,
        alog_mine,
        dskip_mine,
        lax.dynamic_slice_in_dim(out_proj, member_id * outer_rows, outer_rows, 0).astype(
            jnp.float32
        ),
    )
    for ordinal in range(10):
        clipped = owner_grads[ordinal] * shrink_by
        momentum_new = MOMENTUM * moments[ordinal] + clipped
        renewed = mine_weights[ordinal] - RATES[ordinal] * math.sqrt(PARAMS) * (
            clipped + MOMENTUM * momentum_new
        )
        results += [momentum_new, renewed, AVERAGE * averages[ordinal] + (1.0 - AVERAGE) * renewed]
    return tuple(results)


def solution(mesh):
    return jax.shard_map(
        local,
        mesh=mesh,
        in_specs=(
            P("rows", "seq", None),
            P("rows", "seq", None),
            P("rows", None),
            P(),
            P(),
            P(),
            P(),
            P(),
            P(),
            P(),
            P(),
            P(),
            P(),
            P("seq"),
            P("seq", None),
            P(None, "seq"),
            P("seq"),
            P("seq", None),
            P(None, "seq"),
            P("seq"),
            P(None, "seq"),
            P("seq"),
            P("seq", None),
            P("seq"),
            P("seq", None),
            P(None, "seq"),
            P("seq"),
            P("seq", None),
            P(None, "seq"),
            P("seq"),
            P(None, "seq"),
            P("seq"),
            P("seq", None),
        ),
        out_specs=(
            P("rows", "seq", None),
            P("rows", "seq", None),
            P(),
            P("seq"),
            P("seq"),
            P("seq"),
            P("seq", None),
            P("seq", None),
            P("seq", None),
            P(None, "seq"),
            P(None, "seq"),
            P(None, "seq"),
            P("seq"),
            P("seq"),
            P("seq"),
            P("seq", None),
            P("seq", None),
            P("seq", None),
            P(None, "seq"),
            P(None, "seq"),
            P(None, "seq"),
            P("seq"),
            P("seq"),
            P("seq"),
            P(None, "seq"),
            P(None, "seq"),
            P(None, "seq"),
            P("seq"),
            P("seq"),
            P("seq"),
            P("seq", None),
            P("seq", None),
            P("seq", None),
        ),
        check_vma=False,
    )
```

```python
import functools
import math

import jax
import jax.numpy as jnp
from jax import lax
from jax.experimental import pallas as pl
from jax.experimental.pallas import tpu as pltpu
from jax.sharding import PartitionSpec as P

D = 1024
E = 2048
N = 16
R = 64
K = 4
PARAMS = 6667264

LANES = 128
RESET = 1e30
MESH = pl.DeviceIdType.MESH


EPS = 1e-05
MOMENTUM = 0.9
AVERAGE = 0.9
RATES = (0.1, 0.03, 0.1, 0.1, 0.03, 0.03, 0.3, 0.3, 0.1, 0.03)


def silu(values):
    return values * jax.nn.sigmoid(values)


def silu_slope(values):
    sigmoid_of = jax.nn.sigmoid(values)
    return sigmoid_of * (1.0 + values * (1.0 - sigmoid_of))


def doc_tables(lengths_row, positions):
    ends = jnp.cumsum(lengths_row)
    starts = ends - lengths_row
    docid = jnp.sum((positions[None, :] >= starts[:, None]).astype(jnp.int32), axis=0)
    first = jnp.sum((positions[None, :] == starts[:, None]).astype(jnp.int32), axis=0)
    return (docid, first > 0)


def scan_kernel(
    member_ref,
    ddec_ref,
    drive_ref,
    grady_ref,
    inb_ref,
    outb_ref,
    rates_ref,
    all_ref,
    sums_ref,
    scanned_ref,
    along_ref,
    decayed_ref,
    gin_ref,
    gout_ref,
    grates_ref,
    kept,
    first,
    second,
):
    groups, steps = ddec_ref.shape[:2]
    devices = all_ref.shape[0]
    base = pl.program_id(0) * groups
    member = member_ref[0]
    columns = [pl.ds(group * LANES, LANES) for group in range(groups)]
    half = N // 2

    @pl.when(pl.program_id(0) == 0)
    def _():
        gin_ref[...] = jnp.zeros_like(gin_ref)
        gout_ref[...] = jnp.zeros_like(gout_ref)

    def through(device, states):
        new = []
        for group in range(groups):
            total = sums_ref[device, pl.ds(base + group, 1), :]
            factor = jnp.exp2(total * rates_ref[:, columns[group]])
            new.append(
                factor * states[group]
                + all_ref[device, 0, :, columns[group]].astype(jnp.float32)
            )
        return new

    zeros = [jnp.zeros((N, LANES), jnp.float32) for _ in range(groups)]
    reach = devices // 2
    entering = lax.fori_loop(jnp.maximum(member - reach, 0), member, through, zeros)
    last = jnp.minimum(member + reach, devices - 1)
    leaving = lax.fori_loop(0, last - member, lambda d, s: through(last - d, s), zeros)

    def fold(values):
        return values[:half] + values[half:]

    def forward(t, hidden):
        in_row, out_row = inb_ref[t], outb_ref[t]
        new = []
        for group in range(groups):
            here = (group, pl.ds(t, 1))
            decay = jnp.exp2(ddec_ref[here] * rates_ref[:, columns[group]])
            state = decay * hidden[group] + drive_ref[here] * in_row
            kept[t + 1, :, columns[group]] = state
            first[group, pl.ds(pl.multiple_of(t * half, half), half), :] = fold(state * out_row)
            new.append(state)
        return new

    for group in range(groups):
        kept[0, :, columns[group]] = entering[group]
    lax.fori_loop(0, steps, forward, entering, unroll=4)

    def collapse(source, target_ref):
        for group in range(groups):
            total = source[group, pl.ds(0, steps, stride=half), :]
            for place in range(1, half):
                total = total + source[group, pl.ds(place, steps, stride=half), :]
            target_ref[group] = total

    collapse(first, scanned_ref)

    def backward(back, carry):
        later, grates = carry
        t = steps - 1 - back
        in_row, out_row = inb_ref[t], outb_ref[t]
        gin, gout = gin_ref[t], gout_ref[t]
        new = ([], [])
        rows = pl.ds(pl.multiple_of(t * half, half), half)
        for group in range(groups):
            here = (group, pl.ds(t, 1))
            grady = grady_ref[here]
            delta = ddec_ref[here]
            rates = rates_ref[:, columns[group]]
            adjoint = grady * out_row + later[group]
            gout = gout + grady * kept[t + 1, :, columns[group]]
            gin = gin + adjoint * drive_ref[here]
            first[group, rows, :] = fold(adjoint * in_row)
            passed = jnp.exp2(delta * rates) * adjoint
            pulled = passed * kept[t, :, columns[group]]
            second[group, rows, :] = fold(pulled * rates)
            new[0].append(passed)
            new[1].append(grates[group] + pulled * delta)
        gin_ref[t] = gin
        gout_ref[t] = gout
        return new

    _, grates = lax.fori_loop(0, steps, backward, (leaving, zeros), unroll=4)
    collapse(first, along_ref)
    collapse(second, decayed_ref)
    for group in range(groups):
        grates_ref[:, columns[group]] = grates[group]


def scan_of(member, ddec, drive, grady, inb, outb, rates, everyone, sums, block):
    steps = ddec.shape[1]
    devices = everyone.shape[0]
    groups = block // LANES
    wide = pl.BlockSpec((block // LANES, steps, LANES), lambda b: (b, 0, 0))
    whole = pl.BlockSpec((steps, N, LANES), lambda b: (0, 0, 0))
    narrow = pl.BlockSpec((N, block), lambda b: (0, b))
    full = jax.ShapeDtypeStruct((E // LANES, steps, LANES), jnp.float32)
    spread = jax.ShapeDtypeStruct((steps, N, LANES), jnp.float32)
    return pl.pallas_call(
        scan_kernel,
        grid=(E // block,),
        in_specs=[
            pl.BlockSpec(memory_space=pltpu.SMEM),
            wide,
            wide,
            wide,
            whole,
            whole,
            narrow,
            pl.BlockSpec((devices, 1, N, block), lambda b: (0, b, 0, 0)),
            pl.BlockSpec(sums.shape, lambda b: (0, 0, 0)),
        ],
        out_specs=[wide, wide, wide, whole, whole, narrow],
        out_shape=[full, full, full, spread, spread, jax.ShapeDtypeStruct((N, E), jnp.float32)],
        scratch_shapes=[
            pltpu.VMEM((steps + 1, N, block), jnp.float32),
            pltpu.VMEM((groups, steps * N // 2, LANES), jnp.float32),
            pltpu.VMEM((groups, steps * N // 2, LANES), jnp.float32),
        ],
        compiler_params=pltpu.CompilerParams(vmem_limit_bytes=48 * 2**20),
        name="scan",
    )(member, ddec, drive, grady, inb, outb, rates, everyone, sums)


def partner(axis, offset):
    size = lax.axis_size(axis)
    return lax.rem(lax.axis_index(axis) + offset, size)


def greet(counts):
    barrier = pltpu.get_barrier_semaphore()
    total = 0
    for axis, count in counts:
        for offset in range(1, count):
            pl.semaphore_signal(
                barrier, inc=1, device_id={axis: partner(axis, offset)}, device_id_type=MESH
            )
        total += count - 1
    pl.semaphore_wait(barrier, total)


def push(source, target, semaphores, at, axis, offset):
    copy = pltpu.make_async_remote_copy(
        src_ref=source,
        dst_ref=target,
        send_sem=semaphores.at[0, at],
        recv_sem=semaphores.at[1, at],
        device_id={axis: partner(axis, offset)},
        device_id_type=MESH,
    )
    copy.start()
    return copy


def span(index, size):
    return pl.ds(index * size, size)


def softplus(values):
    return jnp.maximum(values, 0.0) + jnp.log1p(jnp.exp(-jnp.abs(values)))


def front_kernel(
    devices,
    nrows,
    starts_ref,
    tokens_ref,
    cot_ref,
    gain_ref,
    in_proj_ref,
    out_proj_ref,
    conv_ref,
    cbias_ref,
    x_proj_ref,
    dt_proj_ref,
    dtbias_ref,
    rates_ref,
    normed_ref,
    inner_ref,
    gates_ref,
    back_ref,
    pre_act_ref,
    delta_pre_ref,
    ddec_ref,
    drive_ref,
    grady_ref,
    rank_ref,
    inb_ref,
    outb_ref,
    ends_out,
    sums_out,
    in_proj_buf,
    out_proj_buf,
    padded,
    docid,
    masks,
    proj,
    ends,
    loads,
    halo_wires,
    wires,
    sum_wires,
    row_wires,
):
    member = lax.axis_index("seq")
    own = lax.axis_index("rows") if nrows > 1 else 0
    steps = tokens_ref.shape[0]
    groups = E // LANES
    chunk = 4 * LANES
    chunks = E // chunk
    reach = devices // 2
    halo = inner_ref.shape[0] - steps
    in_loads = [
        pltpu.make_async_copy(
            in_proj_ref.at[:, span(at, chunk)], in_proj_buf.at[at], loads.at[at]
        )
        for at in range(2 * chunks)
    ]
    out_loads = [
        pltpu.make_async_copy(
            out_proj_ref.at[span(at, chunk), :], out_proj_buf.at[at], loads.at[2 * chunks + at]
        )
        for at in range(chunks)
    ]
    for load in in_loads + out_loads:
        load.start()
    barrier = pltpu.get_barrier_semaphore()
    for axis, count in (("seq", devices), ("rows", nrows)):
        for offset in range(1, count):
            pl.semaphore_signal(
                barrier, inc=1, device_id={axis: partner(axis, offset)}, device_id_type=MESH
            )

    stream = tokens_ref[...].astype(jnp.float32)
    inverse = lax.rsqrt(jnp.mean(stream * stream, axis=1, keepdims=True) + EPS)
    normed_ref[own] = (stream * inverse * gain_ref[...]).astype(jnp.bfloat16)

    places = member * steps - 8 + lax.broadcasted_iota(jnp.int32, docid.shape, 0)
    count = jnp.zeros(docid.shape, jnp.int32)
    first = jnp.zeros(docid.shape, jnp.float32)
    for index in range(starts_ref.shape[0]):
        count = count + jnp.where(places >= starts_ref[index], 1, 0)
        first = jnp.where(places == starts_ref[index], 1.0, first)
    docid[...] = count
    masks[0] = first[8 : 8 + steps]
    for offset in range(1, K):
        masks[offset] = jnp.where(
            docid[8 - offset : 8 - offset + steps, :] == docid[8 : 8 + steps, :], 1.0, 0.0
        )

    def project(at):
        in_loads[at].wait()
        return jnp.dot(
            normed_ref[own], in_proj_buf[at], preferred_element_type=jnp.float32
        ).astype(jnp.bfloat16)

    for at in range(chunks):
        inner_ref[halo:, span(at, chunk)] = project(at)
    pl.semaphore_wait(barrier, devices + nrows - 2)
    halo_copy = pltpu.make_async_remote_copy(
        src_ref=inner_ref.at[steps : steps + halo, :],
        dst_ref=inner_ref.at[0:halo, :],
        send_sem=halo_wires.at[0],
        recv_sem=halo_wires.at[1],
        device_id={"seq": partner("seq", 1)},
        device_id_type=MESH,
    )

    @pl.when(member < devices - 1)
    def _():
        halo_copy.start()

    row_copies = [
        push(normed_ref.at[own], normed_ref.at[own], row_wires, offset - 1, "rows", offset)
        for offset in range(1, nrows)
    ]

    @pl.when(member == 0)
    def _():
        inner_ref[0:halo, :] = jnp.zeros((halo, E), jnp.bfloat16)

    for at in range(chunks):
        gates_ref[:, span(at, chunk)] = project(chunks + at)
    for at in range(chunks):
        out_loads[at].wait()
        back_ref[:, span(at, chunk)] = lax.dot_general(
            cot_ref[...],
            out_proj_buf[at],
            (((1,), (1,)), ((), ())),
            preferred_element_type=jnp.float32,
        ).astype(jnp.bfloat16)

    @pl.when(member < devices - 1)
    def _():
        halo_copy.wait_send()

    @pl.when(member > 0)
    def _():
        halo_copy.wait_recv()

    proj[...] = jnp.zeros_like(proj)
    for at in range(chunks):
        lows = []
        for group in range(4 * at, 4 * at + 4):
            columns = span(group, LANES)
            padded[...] = inner_ref[halo - 8 :, columns].astype(jnp.float32)
            value = cbias_ref[:, columns] + conv_ref[0:1, columns] * padded[8:, :]
            for offset in range(1, K):
                value = (
                    value
                    + conv_ref[offset : offset + 1, columns]
                    * padded[8 - offset : 8 - offset + steps, :]
                    * masks[offset]
                )
            pre_act_ref[group] = value
            act = silu(value)
            drive_ref[group] = act
            lows.append(act.astype(jnp.bfloat16))
        proj[...] += lax.dot_general(
            jnp.concatenate(lows, axis=1),
            x_proj_ref[:, span(at, chunk)],
            (((1,), (1,)), ((), ())),
            preferred_element_type=jnp.float32,
        )
    rank_ref[...] = proj[:, :R].astype(jnp.bfloat16)
    inb_ref[...] = jnp.broadcast_to(proj[:, R : R + N][:, :, None], inb_ref.shape)
    outb_ref[...] = jnp.broadcast_to(proj[:, R + N :][:, :, None], outb_ref.shape)

    def later(distance, at):
        return pltpu.make_async_remote_copy(
            src_ref=ends.at[0, at],
            dst_ref=ends_out.at[member, at],
            send_sem=wires.at[0, 0, at, distance - 1],
            recv_sem=wires.at[0, 1, at, distance - 1],
            device_id={"seq": partner("seq", distance)},
            device_id_type=MESH,
        )

    def earlier(distance, at):
        return pltpu.make_async_remote_copy(
            src_ref=ends.at[1, at],
            dst_ref=ends_out.at[member, at],
            send_sem=wires.at[1, 0, at, distance - 1],
            recv_sem=wires.at[1, 1, at, distance - 1],
            device_id={"seq": partner("seq", devices - distance)},
            device_id_type=MESH,
        )

    def sums_to(distance, side):
        offset = distance if side == 0 else devices - distance
        return pltpu.make_async_remote_copy(
            src_ref=sums_out.at[member],
            dst_ref=sums_out.at[member],
            send_sem=sum_wires.at[side, 0, distance - 1],
            recv_sem=sum_wires.at[side, 1, distance - 1],
            device_id={"seq": partner("seq", offset)},
            device_id_type=MESH,
        )

    for at in range(chunks):
        delta_pre = (
            jnp.dot(
                rank_ref[...], dt_proj_ref[:, span(at, chunk)], preferred_element_type=jnp.float32
            )
            + dtbias_ref[:, span(at, chunk)]
        )
        for place in range(4):
            group = 4 * at + place
            columns = span(group, LANES)
            here = delta_pre[:, place * LANES : (place + 1) * LANES]
            delta = softplus(here)
            delta_pre_ref[group] = here
            drive_ref[group] = drive_ref[group] * delta
            ddec = jnp.where(masks[0] > 0.0, RESET, delta)
            ddec_ref[group] = ddec
            sums_out[member, group : group + 1, :] = jnp.sum(ddec, axis=0, keepdims=True)
            grady_ref[group] = back_ref[:, columns].astype(jnp.float32) * silu(
                gates_ref[:, columns].astype(jnp.float32)
            )

        def step(t, carry):
            hidden, decayed, pulled = carry
            in_row, out_row = inb_ref[t], outb_ref[t]
            new = ([], [], [])
            for place in range(4):
                here = (4 * at + place, pl.ds(t, 1))
                decay = jnp.exp2(ddec_ref[here] * rates_ref[:, span(4 * at + place, LANES)])
                new[0].append(decay * hidden[place] + drive_ref[here] * in_row)
                product = decay * decayed[place]
                new[1].append(product)
                new[2].append(pulled[place] + product * (grady_ref[here] * out_row))
            return new

        zeros = [jnp.zeros((N, LANES), jnp.float32) for _ in range(4)]
        ones = [jnp.ones((N, LANES), jnp.float32) for _ in range(4)]
        hidden, _, pulled = lax.fori_loop(0, steps, step, (zeros, ones, zeros), unroll=4)
        ends[0, at] = jnp.concatenate(hidden, axis=1).astype(jnp.bfloat16)
        ends[1, at] = jnp.concatenate(pulled, axis=1).astype(jnp.bfloat16)
        for distance in range(1, reach + 1):

            @pl.when(member + distance < devices)
            def _():
                later(distance, at).start()

            @pl.when(member >= distance)
            def _():
                earlier(distance, at).start()

    for distance in range(1, reach + 1):

        @pl.when(member + distance < devices)
        def _():
            sums_to(distance, 0).start()

        @pl.when(member >= distance)
        def _():
            sums_to(distance, 1).start()

    for distance in range(1, reach + 1):

        @pl.when(member + distance < devices)
        def _():
            for at in range(chunks):
                later(distance, at).wait_send()
                earlier(distance, at).wait_recv()
            sums_to(distance, 0).wait_send()
            sums_to(distance, 1).wait_recv()

        @pl.when(member >= distance)
        def _():
            for at in range(chunks):
                earlier(distance, at).wait_send()
                later(distance, at).wait_recv()
            sums_to(distance, 1).wait_send()
            sums_to(distance, 0).wait_recv()
    for copy in row_copies:
        copy.wait()


def front_of(starts, tokens, cot, gain, in_proj, out_proj, conv, cbias, x_proj, dt_proj, dtbias, rates, devices, nrows):
    steps = tokens.shape[0]
    groups = E // LANES
    chunk = 4 * LANES
    chunks = E // chunk
    reach = devices // 2
    halo = 16
    low = jnp.bfloat16
    vmem = pl.BlockSpec(memory_space=pltpu.VMEM)
    grouped = jax.ShapeDtypeStruct((groups, steps, LANES), jnp.float32)
    spread = jax.ShapeDtypeStruct((steps, N, LANES), jnp.float32)
    return pl.pallas_call(
        functools.partial(front_kernel, devices, nrows),
        in_specs=[pl.BlockSpec(memory_space=pltpu.SMEM)]
        + [vmem] * 3
        + [pl.BlockSpec(memory_space=pl.ANY)] * 2
        + [vmem] * 6,
        out_specs=[vmem] * 14,
        out_shape=[
            jax.ShapeDtypeStruct((nrows, steps, D), low),
            jax.ShapeDtypeStruct((steps + halo, E), low),
            jax.ShapeDtypeStruct((steps, E), low),
            jax.ShapeDtypeStruct((steps, E), low),
            grouped,
            grouped,
            grouped,
            grouped,
            grouped,
            jax.ShapeDtypeStruct((steps, R), low),
            spread,
            spread,
            jax.ShapeDtypeStruct((devices, chunks, N, chunk), low),
            jax.ShapeDtypeStruct((devices, groups, LANES), jnp.float32),
        ],
        scratch_shapes=[
            pltpu.VMEM((2 * chunks, D, chunk), low),
            pltpu.VMEM((chunks, chunk, D), low),
            pltpu.VMEM((steps + 8, LANES), jnp.float32),
            pltpu.VMEM((steps + 16, LANES), jnp.int32),
            pltpu.VMEM((K, steps, LANES), jnp.float32),
            pltpu.VMEM((steps, R + 2 * N), jnp.float32),
            pltpu.VMEM((2, chunks, N, chunk), low),
            pltpu.SemaphoreType.DMA((3 * chunks,)),
            pltpu.SemaphoreType.DMA((2,)),
            pltpu.SemaphoreType.DMA((2, 2, chunks, reach)),
            pltpu.SemaphoreType.DMA((2, 2, reach)),
            pltpu.SemaphoreType.DMA((2, max(nrows - 1, 1))),
        ],
        compiler_params=pltpu.CompilerParams(
            collective_id=0, has_side_effects=True, vmem_limit_bytes=60 * 2**20
        ),
        name="front",
    )(starts, tokens, cot, gain, in_proj, out_proj, conv, cbias, x_proj, dt_proj, dtbias, rates)


PACKED = (R + 2 * N, R, N, K, 1, 1, 1, 1)
PACKED_ROWS = 192


def packed_rows():
    spans = []
    at = 0
    for count in PACKED:
        spans.append((at, at + count))
        at += count
    return spans


def silu_pair(values):
    sigmoid_of = jax.nn.sigmoid(values)
    return values * sigmoid_of, sigmoid_of * (1.0 + values * (1.0 - sigmoid_of))


def block_kernel(
    nrows,
    devices,
    lengths_ref,
    tokens_ref,
    cot_ref,
    gain_ref,
    in_proj_ref,
    out_proj_ref,
    conv_ref,
    cbias_ref,
    x_proj_ref,
    dt_proj_ref,
    dtbias_ref,
    alog_ref,
    dskip_ref,
    output_ref,
    grad_ref,
    gin_out,
    gout_out,
    small_out,
    norm_out,
    in_proj_buf,
    out_proj_buf,
    rates_ref,
    normed_rows,
    normed_sib,
    cot_rows,
    cot_sib,
    inner,
    gates,
    back,
    pre_act,
    delta_pre,
    ddec,
    drive,
    grady,
    proj,
    rank_low,
    inb,
    outb,
    ends,
    ends_all,
    sums_all,
    docid,
    masks,
    padded,
    kept,
    first,
    second,
    gin,
    gout,
    gated,
    back_gates,
    back_inner,
    grad_conv,
    rank_back,
    proj_back,
    gated_got,
    back_got,
    gout_sum,
    gout_low,
    gout_got,
    gin_sum,
    gin_low,
    gin_got,
    gin_pub,
    small,
    small_low,
    small_got,
    small_part,
    small_seq,
    norm_part,
    norm_all,
    loads,
    halo_wires,
    state_wires,
    sum_wires,
    gather_wires,
    sib_wires,
    gated_wires,
    back_wires,
    gout_wires,
    line_wires,
    plane_wires,
    row_wires,
    seq_wires,
    norm_wires,
    local,
):
    row = lax.axis_index("rows")
    member = lax.axis_index("seq")
    level, side = member // 2, lax.rem(member, 2)
    levels = devices // 2
    steps = tokens_ref.shape[0]
    groups = E // LANES
    chunk = 4 * LANES
    chunks = E // chunk
    shard = E // devices
    halo = inner.shape[0] - steps
    reach = devices // 2
    half = N // 2
    low = jnp.bfloat16
    wide = jnp.float32
    spans = packed_rows()
    everyone = nrows * devices

    in_loads = [
        pltpu.make_async_copy(
            in_proj_ref.at[:, span(at, chunk)], in_proj_buf.at[at], loads.at[at]
        )
        for at in range(2 * chunks)
    ]
    out_load = pltpu.make_async_copy(out_proj_ref, out_proj_buf, loads.at[2 * chunks])
    for load in in_loads + [out_load]:
        load.start()

    def share(index, size):
        return pl.ds(pl.multiple_of(index * size, size), size)

    def plane(turn, other):
        return {
            "rows": lax.rem(row + turn, nrows),
            "seq": 2 * level + lax.rem(side + other, 2),
        }

    def line(turn):
        return {"seq": 2 * lax.rem(level + turn, levels) + side}

    def remote(source, target, send, recv, device):
        return pltpu.make_async_remote_copy(
            src_ref=source,
            dst_ref=target,
            send_sem=send,
            recv_sem=recv,
            device_id=device,
            device_id_type=MESH,
        )

    def begin(copies):
        for copy in copies:
            copy.start()
        return copies

    def settle(copies):
        for copy in copies:
            copy.wait()

    def other_device(offset):
        return {
            "rows": lax.rem(row + offset // devices, nrows),
            "seq": lax.rem(member + offset % devices, devices),
        }

    barrier = pltpu.get_barrier_semaphore()
    for offset in range(1, everyone):
        pl.semaphore_signal(
            barrier, inc=1, device_id=other_device(offset), device_id_type=MESH
        )

    def column_sum(values):
        return jnp.sum(values, axis=0, keepdims=True)

    stream = tokens_ref[...].astype(wide)
    inverse = lax.rsqrt(jnp.mean(stream * stream, axis=1, keepdims=True) + EPS)
    normed_rows[row] = (stream * inverse * gain_ref[...]).astype(low)
    cot_rows[row] = cot_ref[...]
    rates_ref[...] = jnp.exp(alog_ref[...]) * (-1.0 / math.log(2.0))

    places = member * steps - 8 + lax.broadcasted_iota(jnp.int32, docid.shape, 0)
    count = jnp.zeros(docid.shape, jnp.int32)
    starting = jnp.zeros(docid.shape, wide)
    start = 0
    for index in range(lengths_ref.shape[1]):
        count = count + jnp.where(places >= start, 1, 0)
        starting = jnp.where(places == start, 1.0, starting)
        start = start + lengths_ref[0, index]
    docid[...] = count
    masks[0] = starting[8:]
    for offset in range(1, K):
        masks[offset] = jnp.where(
            docid[8 - offset : 16 - offset + steps, :] == docid[8:, :], 1.0, 0.0
        )

    def project(at):
        in_loads[at].wait()
        return jnp.dot(
            normed_rows[row], in_proj_buf[at], preferred_element_type=wide
        ).astype(low)

    for at in range(chunks):
        inner[halo:, span(at, chunk)] = project(at)
    pl.semaphore_wait(barrier, everyone - 1)
    halo_copy = remote(
        inner.at[steps : steps + halo, :],
        inner.at[0:halo, :],
        halo_wires.at[0, 0],
        halo_wires.at[0, 1],
        {"seq": partner("seq", 1)},
    )

    @pl.when(member < devices - 1)
    def _():
        halo_copy.start()

    @pl.when(member == 0)
    def _():
        inner[0:halo, :] = jnp.zeros((halo, E), low)

    row_copies = begin(
        [
            remote(
                source.at[row],
                source.at[row],
                gather_wires.at[kind, 0, offset - 1],
                gather_wires.at[kind, 1, offset - 1],
                {"rows": partner("rows", offset)},
            )
            for kind, source in ((0, normed_rows), (1, cot_rows))
            for offset in range(1, nrows)
        ]
    )
    for at in range(chunks):
        gates[:, span(at, chunk)] = project(chunks + at)
    out_load.wait()
    for at in range(chunks):
        back[:, span(at, chunk)] = lax.dot_general(
            cot_ref[...],
            out_proj_buf[span(at, chunk), :],
            (((1,), (1,)), ((), ())),
            preferred_element_type=wide,
        ).astype(low)

    gin[...] = jnp.zeros_like(gin)
    gout[...] = jnp.zeros_like(gout)
    rank_back[...] = jnp.zeros_like(rank_back)
    small[...] = jnp.zeros_like(small)
    norm_part[...] = jnp.zeros_like(norm_part)
    proj[...] = jnp.zeros_like(proj)

    @pl.when(member < devices - 1)
    def _():
        halo_copy.wait_send()

    @pl.when(member > 0)
    def _():
        halo_copy.wait_recv()

    for at in range(chunks):
        lows = []
        for group in range(4 * at, 4 * at + 4):
            columns = span(group, LANES)
            padded[...] = inner[halo - 8 :, columns].astype(wide)
            value = cbias_ref[:, columns] + conv_ref[0:1, columns] * padded[8:, :]
            for offset in range(1, K):
                value = (
                    value
                    + conv_ref[offset : offset + 1, columns]
                    * padded[8 - offset : 8 - offset + steps, :]
                    * masks[offset, :steps, :]
                )
            pre_act[group] = value
            act = silu(value)
            drive[group] = act
            lows.append(act.astype(low))
        proj[...] += lax.dot_general(
            jnp.concatenate(lows, axis=1),
            x_proj_ref[:, span(at, chunk)],
            (((1,), (1,)), ((), ())),
            preferred_element_type=wide,
        )
    rank_low[...] = proj[:, :R].astype(low)
    inb[...] = jnp.broadcast_to(proj[:, R : R + N][:, :, None], inb.shape)
    outb[...] = jnp.broadcast_to(proj[:, R + N :][:, :, None], outb.shape)

    def state_copy(direction, distance, at):
        offset = distance if direction == 0 else devices - distance
        return remote(
            ends.at[direction, at],
            ends_all.at[member, at],
            state_wires.at[direction, 0, at, distance - 1],
            state_wires.at[direction, 1, at, distance - 1],
            {"seq": partner("seq", offset)},
        )

    def sum_copy(direction, distance):
        offset = distance if direction == 0 else devices - distance
        return remote(
            sums_all.at[member],
            sums_all.at[member],
            sum_wires.at[direction, 0, distance - 1],
            sum_wires.at[direction, 1, distance - 1],
            {"seq": partner("seq", offset)},
        )

    def to_neighbours(make):
        for distance in range(1, reach + 1):

            @pl.when(member + distance < devices)
            def _():
                make(0, distance).start()

            @pl.when(member >= distance)
            def _():
                make(1, distance).start()

    def from_neighbours(make):
        for distance in range(1, reach + 1):

            @pl.when(member + distance < devices)
            def _():
                make(0, distance).wait_send()
                make(1, distance).wait_recv()

            @pl.when(member >= distance)
            def _():
                make(1, distance).wait_send()
                make(0, distance).wait_recv()

    for at in range(chunks):
        pre = (
            jnp.dot(rank_low[...], dt_proj_ref[:, span(at, chunk)], preferred_element_type=wide)
            + dtbias_ref[:, span(at, chunk)]
        )
        for place in range(4):
            group = 4 * at + place
            columns = span(group, LANES)
            here = pre[:, place * LANES : (place + 1) * LANES]
            delta = softplus(here)
            delta_pre[group] = here
            drive[group] = drive[group] * delta
            decaying = jnp.where(masks[0, :steps, :] > 0.0, RESET, delta)
            ddec[group] = decaying
            sums_all[member, group : group + 1, :] = column_sum(decaying)
            grady[group] = back[:, columns].astype(wide) * silu(gates[:, columns].astype(wide))
    to_neighbours(sum_copy)
    zeros = [jnp.zeros((N, LANES), wide) for _ in range(4)]
    ones = [jnp.ones((N, LANES), wide) for _ in range(4)]
    for at in range(chunks):

        def step(t, carry):
            hidden, decayed, pulled = carry
            in_row, out_row = inb[t], outb[t]
            new = ([], [], [])
            for place in range(4):
                here = (4 * at + place, pl.ds(t, 1))
                decay = jnp.exp2(ddec[here] * rates_ref[:, span(4 * at + place, LANES)])
                new[0].append(decay * hidden[place] + drive[here] * in_row)
                product = decay * decayed[place]
                new[1].append(product)
                new[2].append(pulled[place] + product * (grady[here] * out_row))
            return new

        hidden, _, pulled = lax.fori_loop(0, steps, step, (zeros, ones, zeros), unroll=4)
        ends[0, at] = jnp.concatenate(hidden, axis=1).astype(low)
        ends[1, at] = jnp.concatenate(pulled, axis=1).astype(low)
        to_neighbours(lambda direction, distance: state_copy(direction, distance, at))
    from_neighbours(sum_copy)
    for at in range(chunks):
        from_neighbours(lambda direction, distance: state_copy(direction, distance, at))

    def fold(values):
        return values[:half] + values[half:]

    def collapse(source, place):
        total = source[place, pl.ds(0, steps, stride=half), :]
        for index in range(1, half):
            total = total + source[place, pl.ds(index, steps, stride=half), :]
        return total

    def lanes(at, place):
        return share(4 * at + place, LANES)

    def trade(kind, source, at, turn):
        copies = []
        for other in range(2):
            columns = share(2 * at + lax.rem(side + other, 2), shard)
            target = back_got.at[kind, other, row]
            if turn == 0 and other == 0:
                copies.append(
                    pltpu.make_async_copy(source.at[:, columns], target, local.at[kind])
                )
            else:
                copies.append(
                    remote(
                        source.at[:, columns],
                        target,
                        back_wires.at[kind, 0, 2 * turn + other],
                        back_wires.at[kind, 1, 2 * turn + other],
                        plane(turn, other),
                    )
                )
        return begin(copies)

    def trade_gated(at, turn):
        copies = []
        for jump in (turn % 2, turn % 2 + 2):
            for other in range(2):
                receiver = lax.rem(row + jump, nrows)
                columns = share(
                    4 * at + 2 * lax.rem(side + other, 2) + receiver // 2, LANES
                )
                target = gated_got.at[at // 2, other, row]
                if jump == 0 and other == 0:
                    copies.append(
                        pltpu.make_async_copy(
                            gated.at[:, columns], target, local.at[2 + turn // 2]
                        )
                    )
                else:
                    copies.append(
                        remote(
                            gated.at[:, columns],
                            target,
                            gated_wires.at[0, at // 2, 2 * jump + other],
                            gated_wires.at[1, at // 2, 2 * jump + other],
                            plane(jump, other),
                        )
                    )
        return begin(copies)

    gate_moves, gated_moves = [], []
    order = [(turn, lax.rem(row + turn, nrows)) for turn in [*range(1, nrows), 0]]
    leavings = []
    for slot, (turn, at) in enumerate(order):

        def through(device, states):
            new = []
            for place in range(4):
                total = sums_all[device, pl.ds(4 * at + place, 1), :]
                factor = jnp.exp2(total * rates_ref[:, lanes(at, place)])
                new.append(
                    factor * states[place]
                    + ends_all[device, at, :, place * LANES : (place + 1) * LANES].astype(wide)
                )
            return new

        def forward(t, hidden):
            in_row, out_row = inb[t], outb[t]
            new = []
            for place in range(4):
                here = (4 * at + place, pl.ds(t, 1))
                decay = jnp.exp2(ddec[here] * rates_ref[:, lanes(at, place)])
                state = decay * hidden[place] + drive[here] * in_row
                kept[slot, t + 1, place] = state.astype(low)
                first[place, share(t, half), :] = fold(state * out_row)
                new.append(state)
            return new

        entering = lax.fori_loop(jnp.maximum(member - reach, 0), member, through, zeros)
        last = jnp.minimum(member + reach, devices - 1)
        leavings.append(lax.fori_loop(0, last - member, lambda d, s: through(last - d, s), zeros))
        for place in range(4):
            kept[slot, 0, place] = entering[place].astype(low)
        lax.fori_loop(0, steps, forward, entering, unroll=4)
        for place in range(4):
            group, columns = 4 * at + place, lanes(at, place)
            act = silu(pre_act[group])
            y_full = collapse(first, place) + dskip_ref[:, columns] * act
            gate, slope = silu_pair(gates[:, columns].astype(wide))
            gated[:, columns] = (y_full * gate).astype(low)
            back_gates[:, columns] = (back[:, columns].astype(wide) * y_full * slope).astype(low)
            small[spans[6][0] : spans[6][1], columns] = column_sum(grady[group] * act)
        gate_moves += trade(1, back_gates, at, turn)
        gated_moves += trade_gated(at, turn)

    settle(row_copies)
    sib_moves = begin(
        [
            remote(
                source,
                target,
                sib_wires.at[kind, 0],
                sib_wires.at[kind, 1],
                {"seq": 2 * level + 1 - side},
            )
            for kind, source, target in ((0, normed_rows, normed_sib), (1, cot_rows, cot_sib))
        ]
    )

    def in_grads(kind):
        total = None
        for other, normed in ((0, normed_rows), (1, normed_sib)):
            part = lax.dot_general(
                normed[...].reshape(nrows * steps, D),
                back_got[kind, other].reshape(nrows * steps, shard),
                (((0,), (0,)), ((), ())),
                preferred_element_type=wide,
            )
            total = part if total is None else total + part
        gin_sum[kind] = total
        gin_low[kind] = total.astype(low)
        return begin(
            [
                remote(
                    gin_low.at[kind, share(lax.rem(level + turn, levels), D // levels), :],
                    gin_got.at[kind, turn - 1],
                    line_wires.at[kind, 0, turn - 1],
                    line_wires.at[kind, 1, turn - 1],
                    line(turn),
                )
                for turn in range(1, levels)
            ]
        )

    def squares(values):
        return jnp.sum(jnp.sum(values * values, axis=0, keepdims=True), axis=1, keepdims=True)

    def in_share(kind):
        total = gin_sum[kind, share(level, D // levels), :]
        for turn in range(levels - 1):
            total = total + gin_got[kind, turn].astype(wide)
        gin_pub[kind] = total.astype(low)
        owned = D // devices
        columns = share(kind * devices + 2 * row + side, shard)
        gin_out[:, columns] = gin_pub[kind, share(side, owned), :]
        copies = begin(
            [
                remote(
                    gin_pub.at[kind, share(lax.rem(side + other, 2), owned), :],
                    gin_out.at[:, columns],
                    plane_wires.at[kind, 0, 2 * turn + other],
                    plane_wires.at[kind, 1, 2 * turn + other],
                    plane(turn, other),
                )
                for turn in range(nrows)
                for other in range(2)
                if turn + other > 0
            ]
        )
        norm_part[...] += squares(total)
        return copies

    summing = lax.rem(level, 2) == lax.rem(row, 2)
    idle = lax.rem(level, 2) != lax.rem(row, 2)

    def gout_copy(turn):
        return remote(
            gout_low.at[lax.rem(level + turn, levels) // 2],
            gout_got.at[turn - 1],
            gout_wires.at[0, turn - 1],
            gout_wires.at[1, turn - 1],
            line(turn),
        )

    def gout_share_copy(turn):
        rows_of = gout_out.at[share(row // 2, LANES), :]
        return remote(
            rows_of,
            rows_of,
            row_wires.at[2, 0, turn - 1],
            row_wires.at[2, 1, turn - 1],
            {"rows": partner("rows", turn)},
        )

    def out_grads():
        for piece in range(2):
            total = None
            for other, cots in ((0, cot_rows), (1, cot_sib)):
                part = lax.dot_general(
                    gated_got[piece, other].reshape(nrows * steps, LANES),
                    cots[...].reshape(nrows * steps, D),
                    (((0,), (0,)), ((), ())),
                    preferred_element_type=wide,
                )
                total = part if total is None else total + part
            gout_sum[piece] = total
            gout_low[piece] = total.astype(low)

        @pl.when(summing)
        def _():
            gout_copy(2).start()

        @pl.when(idle)
        def _():
            gout_copy(1).start()
            gout_copy(3).start()

    def out_share():
        @pl.when(idle)
        def _():
            gout_copy(1).wait_send()
            gout_copy(3).wait_send()

        @pl.when(summing)
        def _():
            gout_copy(2).wait_send()
            for turn in range(1, levels):
                gout_copy(turn).wait_recv()
            total = gout_sum[level // 2]
            for turn in range(levels - 1):
                total = total + gout_got[turn].astype(wide)
            gout_out[share(row // 2, LANES), :] = total.astype(low)
            norm_part[...] += squares(total)
            for turn in range(1, nrows):
                gout_share_copy(turn).start()

    def out_end():
        @pl.when(summing)
        def _():
            for turn in range(1, nrows):
                gout_share_copy(turn).wait_send()
            gout_share_copy(2).wait_recv()

        @pl.when(idle)
        def _():
            gout_share_copy(1).wait_recv()
            gout_share_copy(3).wait_recv()

    for slot, (turn, at) in enumerate(order):

        def backward(back_step, carry):
            later, grates, states = carry
            t = steps - 1 - back_step
            in_row, out_row = inb[t], outb[t]
            gin_row, gout_row = gin[t], gout[t]
            new = ([], [], [])
            for place in range(4):
                here = (4 * at + place, pl.ds(t, 1))
                grad_y = grady[here]
                delta = ddec[here]
                rates = rates_ref[:, lanes(at, place)]
                before = kept[slot, t, place].astype(wide)
                adjoint = grad_y * out_row + later[place]
                gout_row = gout_row + grad_y * states[place]
                gin_row = gin_row + adjoint * drive[here]
                first[place, share(t, half), :] = fold(adjoint * in_row)
                passed = jnp.exp2(delta * rates) * adjoint
                pulled = passed * before
                second[place, share(t, half), :] = fold(pulled * rates)
                new[0].append(passed)
                new[1].append(grates[place] + pulled * delta)
                new[2].append(before)
            gin[t] = gin_row
            gout[t] = gout_row
            return new

        ending = [kept[slot, steps, place].astype(wide) for place in range(4)]
        _, grates, _ = lax.fori_loop(
            0, steps, backward, (leavings[slot], zeros, ending), unroll=4
        )
        lows = []
        for place in range(4):
            group, columns = 4 * at + place, lanes(at, place)
            along = collapse(first, place)
            here = delta_pre[group]
            act = silu(pre_act[group])
            grad_delta = along * act + collapse(second, place) * math.log(2.0)
            pre_low = (grad_delta * jax.nn.sigmoid(here)).astype(low)
            lows.append(pre_low)
            drive[group] = grady[group] * dskip_ref[:, columns] + along * softplus(here)
            small[spans[5][0] : spans[5][1], columns] = column_sum(pre_low.astype(wide))
            small[spans[2][0] : spans[2][1], columns] = (
                grates[place] * rates_ref[:, columns] * math.log(2.0)
            )
        lows = jnp.concatenate(lows, axis=1)
        rank_back[...] += lax.dot_general(
            lows,
            dt_proj_ref[:, share(at, chunk)],
            (((1,), (1,)), ((), ())),
            preferred_element_type=wide,
        )
        small[spans[1][0] : spans[1][1], share(at, chunk)] = lax.dot_general(
            rank_low[...], lows, (((0,), (0,)), ((), ())), preferred_element_type=wide
        )
        if slot == chunks - 2:
            settle(gate_moves)
            settle(sib_moves)
            gate_moves = in_grads(1)
            settle(gated_moves)
            out_grads()

    def to_rows(kind, make):
        return begin(
            [
                remote(
                    *make(partner("rows", offset), offset - 1),
                    row_wires.at[kind, 0, offset - 1],
                    row_wires.at[kind, 1, offset - 1],
                    {"rows": partner("rows", offset)},
                )
                for offset in range(1, nrows)
            ]
        )

    def to_seq(kind, make):
        return begin(
            [
                remote(
                    *make(partner("seq", offset), offset - 1),
                    seq_wires.at[kind, 0, offset - 1],
                    seq_wires.at[kind, 1, offset - 1],
                    {"seq": partner("seq", offset)},
                )
                for offset in range(1, devices)
            ]
        )

    proj_back[:, :R] = rank_back[...].astype(low)
    proj_back[:, R : R + N] = jnp.sum(gin[...], axis=2).astype(low)
    proj_back[:, R + N :] = jnp.sum(gout[...], axis=2).astype(low)
    for at in range(chunks):
        pulled = jnp.dot(
            proj_back[...], x_proj_ref[:, span(at, chunk)], preferred_element_type=wide
        )
        lows = []
        for place in range(4):
            group = 4 * at + place
            act, slope = silu_pair(pre_act[group])
            lows.append(act.astype(low))
            grad_conv[group, :steps, :] = (
                drive[group] + pulled[:, place * LANES : (place + 1) * LANES]
            ) * slope
        small[spans[0][0] : spans[0][1], span(at, chunk)] = lax.dot_general(
            proj_back[...],
            jnp.concatenate(lows, axis=1),
            (((0,), (0,)), ((), ())),
            preferred_element_type=wide,
        )
    halo_back = remote(
        grad_conv.at[:, 0:8, :],
        grad_conv.at[:, steps : steps + 8, :],
        halo_wires.at[1, 0],
        halo_wires.at[1, 1],
        {"seq": partner("seq", devices - 1)},
    )

    @pl.when(member > 0)
    def _():
        halo_back.start()

    @pl.when(member == devices - 1)
    def _():
        grad_conv[:, steps : steps + 8, :] = jnp.zeros((groups, 8, LANES), wide)

    output_ref[...] = stream + jnp.dot(
        gated[...], out_proj_buf[...], preferred_element_type=wide
    )
    grad_normed = jnp.zeros((steps, D), wide)
    for at in range(chunks):
        grad_normed = grad_normed + lax.dot_general(
            back_gates[:, span(at, chunk)],
            in_proj_buf[chunks + at],
            (((1,), (1,)), ((), ())),
            preferred_element_type=wide,
        )

    @pl.when(member > 0)
    def _():
        halo_back.wait_send()

    @pl.when(member < devices - 1)
    def _():
        halo_back.wait_recv()

    inner_moves = []
    for turn, at in order:
        for place in range(4):
            group, columns = 4 * at + place, lanes(at, place)
            padded[...] = inner[halo - 8 :, columns].astype(wide)
            here = grad_conv[group, :steps, :]
            pulled = conv_ref[0:1, columns] * here
            small[spans[4][0] : spans[4][1], columns] = column_sum(here)
            at_row = spans[3][0]
            small[at_row : at_row + 1, columns] = column_sum(here * padded[8:, :])
            for offset in range(1, K):
                small[at_row + offset : at_row + offset + 1, columns] = column_sum(
                    here * masks[offset, :steps, :] * padded[8 - offset : 8 - offset + steps, :]
                )
                pulled = pulled + conv_ref[offset : offset + 1, columns] * (
                    grad_conv[group, offset : offset + steps, :]
                    * masks[offset, offset : offset + steps, :]
                )
            back_inner[:, columns] = pulled.astype(low)
        inner_moves += trade(0, back_inner, at, turn)

    for at in range(chunks):
        grad_normed = grad_normed + lax.dot_general(
            back_inner[:, span(at, chunk)],
            in_proj_buf[at],
            (((1,), (1,)), ((), ())),
            preferred_element_type=wide,
        )
    inverse = lax.rsqrt(jnp.mean(stream * stream, axis=1, keepdims=True) + EPS)
    grad_gain = column_sum(grad_normed * stream * inverse)
    owned = D // devices
    for index in range(devices):
        small[spans[7][0] : spans[7][1], index * shard : index * shard + owned] = grad_gain[
            :, index * owned : (index + 1) * owned
        ]
    few = small_low.shape[0] // nrows
    small_low[...] = small[...].astype(low)
    small_moves = to_rows(
        0, lambda other, at: (small_low.at[share(other, few), :], small_got.at[at])
    )
    scaled = grad_normed * gain_ref[...]
    grad_ref[...] = (
        cot_ref[...].astype(wide)
        + inverse * scaled
        - stream
        * inverse
        * inverse
        * inverse
        * jnp.mean(scaled * stream, axis=1, keepdims=True)
    )

    settle(inner_moves)
    inner_moves = in_grads(0)

    settle(small_moves)
    total = small[share(row, few), :]
    for at in range(nrows - 1):
        total = total + small_got[at].astype(wide)
    small_part[...] = total.astype(low)
    small_moves = to_seq(
        0, lambda other, at: (small_part.at[:, share(other, shard)], small_seq.at[at])
    )
    out_share()
    settle(gate_moves)
    gate_moves = in_share(1)

    settle(small_moves)
    total = small_part[:, share(member, shard)].astype(wide)
    for at in range(devices - 1):
        total = total + small_seq[at].astype(wide)
    small_out[share(row, few), :] = total.astype(low)
    small_moves = to_rows(
        1,
        lambda other, at: (
            small_out.at[share(row, few), :],
            small_out.at[share(row, few), :],
        ),
    )
    norm_part[...] += squares(total)

    settle(inner_moves)
    inner_moves = in_share(0)
    here = row * devices + member
    norm_all[here] = jnp.broadcast_to(norm_part[...], (8, LANES))
    norm_moves = begin(
        [
            remote(
                norm_all.at[here],
                norm_all.at[here],
                norm_wires.at[0, offset - 1],
                norm_wires.at[1, offset - 1],
                other_device(offset),
            )
            for offset in range(1, everyone)
        ]
    )
    settle(norm_moves)
    norm_out[...] = jnp.sqrt(jnp.sum(norm_all[...], axis=0))
    out_end()
    settle(gate_moves)
    settle(small_moves)
    settle(inner_moves)


def block_of(operands, nrows, devices):
    steps = operands[1].shape[0]
    groups = E // LANES
    chunk = 4 * LANES
    chunks = E // chunk
    levels = devices // 2
    reach = devices // 2
    shard = E // devices
    halo = 16
    low, wide = jnp.bfloat16, jnp.float32
    few = PACKED_ROWS // nrows
    vmem = pl.BlockSpec(memory_space=pltpu.VMEM)
    specs = [vmem] * len(operands)
    specs[0] = pl.BlockSpec(memory_space=pltpu.SMEM)
    specs[4] = specs[5] = pl.BlockSpec(memory_space=pl.ANY)
    dma = pltpu.SemaphoreType.DMA
    grouped = pltpu.VMEM((groups, steps, LANES), wide)
    flat = pltpu.VMEM((steps, E), low)
    spread = pltpu.VMEM((steps, N, LANES), wide)
    gathered = pltpu.VMEM((nrows, steps, D), low)
    folded = pltpu.VMEM((4, steps * N // 2, LANES), wide)
    return pl.pallas_call(
        functools.partial(block_kernel, nrows, devices),
        in_specs=specs,
        out_specs=[vmem] * 6,
        out_shape=[
            jax.ShapeDtypeStruct((steps, D), wide),
            jax.ShapeDtypeStruct((steps, D), wide),
            jax.ShapeDtypeStruct((D // devices, 2 * E), low),
            jax.ShapeDtypeStruct((shard, D), low),
            jax.ShapeDtypeStruct((PACKED_ROWS, shard), low),
            jax.ShapeDtypeStruct((8, LANES), wide),
        ],
        scratch_shapes=[
            pltpu.VMEM((2 * chunks, D, chunk), low),
            pltpu.VMEM((E, D), low),
            pltpu.VMEM((N, E), wide),
            gathered,
            gathered,
            gathered,
            gathered,
            pltpu.VMEM((steps + halo, E), low),
            flat,
            flat,
            grouped,
            grouped,
            grouped,
            grouped,
            grouped,
            pltpu.VMEM((steps, R + 2 * N), wide),
            pltpu.VMEM((steps, R), low),
            spread,
            spread,
            pltpu.VMEM((2, chunks, N, chunk), low),
            pltpu.VMEM((devices, chunks, N, chunk), low),
            pltpu.VMEM((devices, groups, LANES), wide),
            pltpu.VMEM((steps + 16, LANES), jnp.int32),
            pltpu.VMEM((K, steps + 8, LANES), wide),
            pltpu.VMEM((steps + 8, LANES), wide),
            pltpu.VMEM((chunks, steps + 1, 4, N, LANES), low),
            folded,
            folded,
            spread,
            spread,
            flat,
            flat,
            flat,
            pltpu.VMEM((groups, steps + 8, LANES), wide),
            pltpu.VMEM((steps, R), wide),
            pltpu.VMEM((steps, R + 2 * N), low),
            pltpu.VMEM((2, 2, nrows, steps, LANES), low),
            pltpu.VMEM((2, 2, nrows, steps, shard), low),
            pltpu.VMEM((2, LANES, D), wide),
            pltpu.VMEM((2, LANES, D), low),
            pltpu.VMEM((levels - 1, LANES, D), low),
            pltpu.VMEM((2, D, shard), wide),
            pltpu.VMEM((2, D, shard), low),
            pltpu.VMEM((2, levels - 1, D // levels, shard), low),
            pltpu.VMEM((2, D // levels, shard), low),
            pltpu.VMEM((PACKED_ROWS, E), wide),
            pltpu.VMEM((PACKED_ROWS, E), low),
            pltpu.VMEM((nrows - 1, few, E), low),
            pltpu.VMEM((few, E), low),
            pltpu.VMEM((devices - 1, few, shard), low),
            pltpu.VMEM((1, 1), wide),
            pltpu.VMEM((nrows * devices, 8, LANES), wide),
            dma((2 * chunks + 1,)),
            dma((2, 2)),
            dma((2, 2, chunks, reach)),
            dma((2, 2, reach)),
            dma((2, 2, nrows - 1)),
            dma((2, 2)),
            dma((2, 2, 2 * nrows)),
            dma((2, 2, 2 * nrows)),
            dma((2, levels - 1)),
            dma((2, 2, levels - 1)),
            dma((2, 2, 2 * nrows)),
            dma((3, 2, nrows - 1)),
            dma((1, 2, devices - 1)),
            dma((2, nrows * devices - 1)),
            dma((4,)),
        ],
        compiler_params=pltpu.CompilerParams(
            collective_id=1, has_side_effects=True, vmem_limit_bytes=63 * 2**20
        ),
        name="block",
    )(*operands)


def update_kernel(member_ref, norm_ref, gin_ref, gout_ref, small_ref, *refs):
    weights, moments, averages, outs = refs[:10], refs[10:20], refs[20:30], refs[30:]
    shrink_by = 1.0 / jnp.maximum(norm_ref[0:1, 0:1], 1.0)

    def renew(ordinal, grad, at=Ellipsis):
        clipped = grad * shrink_by
        momentum_new = MOMENTUM * moments[ordinal][at] + clipped
        renewed = weights[ordinal][at].astype(jnp.float32) - RATES[ordinal] * math.sqrt(PARAMS) * (
            clipped + MOMENTUM * momentum_new
        )
        outs[3 * ordinal][at] = momentum_new
        outs[3 * ordinal + 1][at] = renewed
        outs[3 * ordinal + 2][at] = AVERAGE * averages[ordinal][at] + (1.0 - AVERAGE) * renewed

    renew(1, gin_ref[...].astype(jnp.float32))
    renew(9, gout_ref[...].astype(jnp.float32))

    @pl.when(pl.program_id(0) == 0)
    def _():
        spans = packed_rows()

        def part(index):
            return small_ref[spans[index][0] : spans[index][1], :].astype(jnp.float32)

        small = small_ref[...].astype(jnp.float32)
        renew(4, part(0))
        renew(5, part(1))
        renew(7, part(2))
        renew(2, part(3))
        for ordinal, index in ((3, 4), (6, 5), (8, 6)):
            renew(ordinal, small[spans[index][0] : spans[index][1]])
        gain = small[spans[7][0] : spans[7][1], : weights[0].shape[1]]
        renew(0, gain)


def update_of(member, norm_tile, gin, gout, small, weights, moments, averages):
    inner = gin.shape[0]
    channels = gout.shape[0]
    blocks = 8
    outer = channels // blocks
    block = gin.shape[1] // blocks
    flat = (0, 3, 6, 8)

    def rows_of(array, ordinal):
        return array.reshape(1, -1) if ordinal in flat else array.T if ordinal == 4 else array

    def shard(shape, ordinal):
        if ordinal == 1:
            return pl.BlockSpec((inner, block), lambda j, m: (0, j))
        if ordinal == 9:
            return pl.BlockSpec((outer, shape[1]), lambda j, m: (j, 0))
        return pl.BlockSpec(shape, lambda j, m: (0, 0))

    def weight(shape, ordinal):
        if ordinal == 1:
            return pl.BlockSpec((inner, block), lambda j, m: (m[0], j))
        if ordinal == 9:
            return pl.BlockSpec((outer, shape[1]), lambda j, m: (m[0] * blocks + j, 0))
        return pl.BlockSpec(shape, lambda j, m: (0, m[0]))

    weights = [rows_of(array, ordinal) for ordinal, array in enumerate(weights)]
    moments = [rows_of(array, ordinal) for ordinal, array in enumerate(moments)]
    averages = [rows_of(array, ordinal) for ordinal, array in enumerate(averages)]
    shapes = [array.shape for array in moments]
    shards = [shard(shape, ordinal) for ordinal, shape in enumerate(shapes)]
    outs = pl.pallas_call(
        update_kernel,
        grid_spec=pltpu.PrefetchScalarGridSpec(
            num_scalar_prefetch=1,
            grid=(blocks,),
            in_specs=[
                pl.BlockSpec(norm_tile.shape, lambda j, m: (0, 0)),
                pl.BlockSpec((inner, block), lambda j, m: (0, j)),
                pl.BlockSpec((outer, gout.shape[1]), lambda j, m: (j, 0)),
                pl.BlockSpec(small.shape, lambda j, m: (0, 0)),
            ]
            + [weight(shape, ordinal) for ordinal, shape in enumerate(shapes)]
            + shards
            + shards,
            out_specs=[shards[ordinal] for ordinal in range(10) for _ in range(3)],
        ),
        out_shape=[
            jax.ShapeDtypeStruct(shapes[ordinal], jnp.float32)
            for ordinal in range(10)
            for _ in range(3)
        ],
        compiler_params=pltpu.CompilerParams(vmem_limit_bytes=63 * 2**20),
        name="update",
    )(member, norm_tile, gin, gout, small, *weights, *moments, *averages)
    return [
        out.reshape(-1) if index // 3 in flat else out.T if index // 3 == 4 else out
        for index, out in enumerate(outs)
    ]


def local(
    tokens,
    cotangent,
    doc_lengths,
    norm_gain,
    in_proj,
    conv_weight,
    conv_bias,
    x_proj,
    dt_proj,
    dt_bias,
    a_log,
    d_skip,
    out_proj,
    moment_norm_gain,
    moment_in_proj,
    moment_conv_weight,
    moment_conv_bias,
    moment_x_proj,
    moment_dt_proj,
    moment_dt_bias,
    moment_a_log,
    moment_d_skip,
    moment_out_proj,
    average_norm_gain,
    average_in_proj,
    average_conv_weight,
    average_conv_bias,
    average_x_proj,
    average_dt_proj,
    average_dt_bias,
    average_a_log,
    average_d_skip,
    average_out_proj,
):
    devices = lax.axis_size("seq")
    member_id = lax.axis_index("seq")
    channels = E // devices
    begin = member_id * channels
    stream = tokens[0].astype(jnp.float32)
    steps = stream.shape[0]
    length = steps * devices
    cot_low = cotangent[0]
    nrows = lax.axis_size("rows")
    direct = devices == 2 * nrows and nrows == 4 and E == nrows * 4 * LANES
    member_word = jnp.reshape(member_id, (1,)).astype(jnp.int32)
    moments = (
        moment_norm_gain,
        moment_in_proj,
        moment_conv_weight,
        moment_conv_bias,
        moment_x_proj,
        moment_dt_proj,
        moment_dt_bias,
        moment_a_log,
        moment_d_skip,
        moment_out_proj,
    )
    averages = (
        average_norm_gain,
        average_in_proj,
        average_conv_weight,
        average_conv_bias,
        average_x_proj,
        average_dt_proj,
        average_dt_bias,
        average_a_log,
        average_d_skip,
        average_out_proj,
    )
    if direct:
        weights = (
            norm_gain,
            in_proj,
            conv_weight,
            conv_bias,
            x_proj,
            dt_proj,
            dt_bias,
            a_log,
            d_skip,
            out_proj,
        )
        block_output, input_grad, gin_share, gout_share, small, norm_tile = block_of(
            (
                doc_lengths,
                tokens[0],
                cot_low,
                norm_gain[None],
                in_proj,
                out_proj,
                conv_weight,
                conv_bias[None],
                x_proj.T,
                dt_proj,
                dt_bias[None],
                a_log,
                d_skip[None],
            ),
            nrows,
            devices,
        )
        updated = update_of(
            member_word, norm_tile, gin_share, gout_share, small, weights, moments, averages
        )
        return (block_output[None], input_grad[None], norm_tile[0, 0], *updated)
    inverse = lax.rsqrt(jnp.mean(stream * stream, axis=1, keepdims=True) + EPS)
    rates = -jnp.exp(a_log)
    scaled_rates = rates * (1.0 / math.log(2.0))
    lengths = doc_lengths[0]
    starts = (jnp.cumsum(lengths) - lengths).astype(jnp.int32)
    (
        normed,
        inner_low,
        gates_low,
        back_gated,
        pre_act,
        delta_pre,
        ddec,
        drive,
        grady_rows,
        rank_low,
        inb,
        outb,
        everyone,
        all_sums,
    ) = front_of(
        starts,
        tokens[0],
        cot_low,
        norm_gain[None],
        in_proj,
        out_proj,
        conv_weight,
        conv_bias[None],
        x_proj.T,
        dt_proj,
        dt_bias[None],
        scaled_rates,
        devices,
        1,
    )
    cot_all = lax.all_gather(cot_low, "seq", axis=0, tiled=True)
    normed_all = lax.all_gather(normed[0], "seq", axis=0, tiled=True)
    positions = member_id * steps + jnp.arange(-8, steps + 8, dtype=jnp.int32)
    docid, starting = doc_tables(doc_lengths[0], positions)
    masks = []
    for offset in range(K):
        linked = (docid[8:] == docid[8 - offset : steps + 16 - offset]) & (
            positions[8 - offset : steps + 16 - offset] >= 0
        )
        masks.append((linked & (positions[8:] < length)).astype(jnp.float32)[:, None])

    def flat(values):
        return jnp.transpose(values, (1, 0, 2)).reshape(steps, E)

    pre_act, delta_pre = flat(pre_act), flat(delta_pre)
    padded = inner_low[8:].astype(jnp.float32)
    gates = gates_low.astype(jnp.float32)
    act = silu(pre_act)
    act_low = act.astype(jnp.bfloat16)
    delta = jax.nn.softplus(delta_pre)
    silu_gate = silu(gates)
    chan_back = back_gated.astype(jnp.float32)
    grad_y = chan_back * silu_gate
    scanned, along_in, pulled_sum, gin, gout, grad_rates = scan_of(
        member_word, ddec, drive, grady_rows, inb, outb, scaled_rates, everyone, all_sums, 512
    )
    scanned, along_in, pulled_sum = flat(scanned), flat(along_in), flat(pulled_sum)
    y_full = scanned + d_skip[None, :] * act
    gated = (y_full * silu_gate).astype(jnp.bfloat16)
    block_output = (
        stream + jnp.dot(gated, out_proj, preferred_element_type=jnp.float32)
    )[None]
    grad_gates = chan_back * y_full * silu_slope(gates)
    grad_dskip = jnp.sum(grad_y * act, axis=0)
    grad_in_mat = jnp.sum(gin, axis=2)
    grad_out_mat = jnp.sum(gout, axis=2)
    grad_delta = along_in * act + pulled_sum * math.log(2.0)
    grad_alog = grad_rates * rates
    grad_pre = (grad_delta * jax.nn.sigmoid(delta_pre)).astype(jnp.bfloat16)
    grad_dtbias = jnp.sum(grad_pre.astype(jnp.float32), axis=0)
    grad_dtproj = lax.dot_general(
        rank_low, grad_pre, (((0,), (0,)), ((), ())), preferred_element_type=jnp.float32
    )
    rank_back = lax.dot_general(
        grad_pre, dt_proj, (((1,), (1,)), ((), ())), preferred_element_type=jnp.float32
    )
    proj_back = jnp.concatenate([rank_back, grad_in_mat, grad_out_mat], axis=1).astype(jnp.bfloat16)
    grad_xproj = lax.dot_general(
        act_low, proj_back, (((0,), (0,)), ((), ())), preferred_element_type=jnp.float32
    )
    grad_act = (
        grad_y * d_skip[None, :]
        + along_in * delta
        + lax.dot_general(
            proj_back, x_proj, (((1,), (1,)), ((), ())), preferred_element_type=jnp.float32
        )
    )
    grad_pre_act = grad_act * silu_slope(pre_act)
    ahead = lax.ppermute(
        grad_pre_act[:8], "seq", [(i + 1, i) for i in range(devices - 1)]
    )
    extended = jnp.concatenate([grad_pre_act, ahead], axis=0)
    grad_conv_bias = jnp.sum(grad_pre_act, axis=0)
    grad_inner = jnp.zeros_like(gates)
    conv_rows = []
    for offset in range(K):
        masked = extended * masks[offset]
        conv_rows.append(
            jnp.sum(masked[:steps] * padded[8 - offset : 8 - offset + steps], axis=0)
        )
        grad_inner = grad_inner + conv_weight[offset][None, :] * masked[offset : offset + steps]
    grad_convw = jnp.stack(conv_rows)
    back_xz = jnp.stack([grad_inner, grad_gates]).astype(jnp.bfloat16)
    grad_normed = lax.dot_general(
        back_xz[0], in_proj[:, :E], (((1,), (1,)), ((), ())), preferred_element_type=jnp.float32
    ) + lax.dot_general(
        back_xz[1], in_proj[:, E:], (((1,), (1,)), ((), ())), preferred_element_type=jnp.float32
    )
    grad_gain = jnp.sum(grad_normed * stream * inverse, axis=0)
    scaled = grad_normed * norm_gain[None, :]
    input_grad = (
        cot_low.astype(jnp.float32)
        + inverse * scaled
        - stream * inverse * inverse * inverse * jnp.mean(scaled * stream, axis=1, keepdims=True)
    )
    small = jnp.concatenate(
        [
            grad_xproj.T,
            grad_dtproj,
            grad_alog,
            grad_convw,
            grad_conv_bias[None],
            grad_dtbias[None],
            grad_dskip[None],
            jnp.pad(
                grad_gain.reshape(devices, D // devices),
                ((0, 0), (0, channels - D // devices)),
            ).reshape(1, E),
            jnp.zeros((PACKED_ROWS - sum(PACKED), E), jnp.float32),
        ],
        axis=0,
    )
    gated_mine = lax.all_to_all(gated, "seq", split_axis=1, concat_axis=0, tiled=True)
    back_mine = lax.all_to_all(back_xz, "seq", split_axis=2, concat_axis=1, tiled=True)
    gout_share = lax.psum(
        lax.dot_general(
            gated_mine, cot_all, (((0,), (0,)), ((), ())), preferred_element_type=jnp.float32
        ),
        "rows",
    )
    gin_share = lax.psum(
        jnp.einsum("td,ktc->dkc", normed_all, back_mine, preferred_element_type=jnp.float32),
        "rows",
    )
    gin_share = lax.all_to_all(
        gin_share, "seq", split_axis=0, concat_axis=2, tiled=True
    ).reshape(D // devices, 2 * E)
    small = lax.psum(small, "rows")
    small = lax.psum_scatter(small, "seq", scatter_dimension=1, tiled=True)
    squares = jnp.sum(gin_share * gin_share) + jnp.sum(gout_share * gout_share)
    grad_norm = jnp.sqrt(lax.psum(squares + jnp.sum(small * small), "seq"))
    results = [block_output, input_grad[None], grad_norm]
    parts = [small[low:high] for low, high in packed_rows()]
    owner_grads = (
        parts[7][0, : D // devices],
        gin_share.astype(jnp.float32),
        parts[3],
        parts[4][0],
        parts[0].T,
        parts[1],
        parts[5][0],
        parts[2],
        parts[6][0],
        gout_share.astype(jnp.float32),
    )
    conv_mine = lax.dynamic_slice_in_dim(conv_weight, begin, channels, 1)
    cbias_mine = lax.dynamic_slice_in_dim(conv_bias, begin, channels, 0)
    xproj_mine = lax.dynamic_slice_in_dim(x_proj, begin, channels, 0)
    dtproj_mine = lax.dynamic_slice_in_dim(dt_proj, begin, channels, 1)
    dtbias_mine = lax.dynamic_slice_in_dim(dt_bias, begin, channels, 0)
    alog_mine = lax.dynamic_slice_in_dim(a_log, begin, channels, 1)
    dskip_mine = lax.dynamic_slice_in_dim(d_skip, begin, channels, 0)
    shrink_by = 1.0 / jnp.maximum(grad_norm, 1.0)
    gain_rows = D // devices
    outer_rows = E // devices
    mine_weights = (
        lax.dynamic_slice_in_dim(norm_gain, member_id * gain_rows, gain_rows, 0),
        lax.dynamic_slice_in_dim(in_proj, member_id * gain_rows, gain_rows, 0).astype(jnp.float32),
        conv_mine,
        cbias_mine,
        xproj_mine.astype(jnp.float32),
        dtproj_mine.astype(jnp.float32),
        dtbias_mine,
        alog_mine,
        dskip_mine,
        lax.dynamic_slice_in_dim(out_proj, member_id * outer_rows, outer_rows, 0).astype(
            jnp.float32
        ),
    )
    for ordinal in range(10):
        clipped = owner_grads[ordinal] * shrink_by
        momentum_new = MOMENTUM * moments[ordinal] + clipped
        renewed = mine_weights[ordinal] - RATES[ordinal] * math.sqrt(PARAMS) * (
            clipped + MOMENTUM * momentum_new
        )
        results += [momentum_new, renewed, AVERAGE * averages[ordinal] + (1.0 - AVERAGE) * renewed]
    return tuple(results)


def solution(mesh):
    return jax.shard_map(
        local,
        mesh=mesh,
        in_specs=(
            P("rows", "seq", None),
            P("rows", "seq", None),
            P("rows", None),
            P(),
            P(),
            P(),
            P(),
            P(),
            P(),
            P(),
            P(),
            P(),
            P(),
            P("seq"),
            P("seq", None),
            P(None, "seq"),
            P("seq"),
            P("seq", None),
            P(None, "seq"),
            P("seq"),
            P(None, "seq"),
            P("seq"),
            P("seq", None),
            P("seq"),
            P("seq", None),
            P(None, "seq"),
            P("seq"),
            P("seq", None),
            P(None, "seq"),
            P("seq"),
            P(None, "seq"),
            P("seq"),
            P("seq", None),
        ),
        out_specs=(
            P("rows", "seq", None),
            P("rows", "seq", None),
            P(),
            P("seq"),
            P("seq"),
            P("seq"),
            P("seq", None),
            P("seq", None),
            P("seq", None),
            P(None, "seq"),
            P(None, "seq"),
            P(None, "seq"),
            P("seq"),
            P("seq"),
            P("seq"),
            P("seq", None),
            P("seq", None),
            P("seq", None),
            P(None, "seq"),
            P(None, "seq"),
            P(None, "seq"),
            P("seq"),
            P("seq"),
            P("seq"),
            P(None, "seq"),
            P(None, "seq"),
            P(None, "seq"),
            P("seq"),
            P("seq"),
            P("seq"),
            P("seq", None),
            P("seq", None),
            P("seq", None),
        ),
        check_vma=False,
    )
```

```python
import functools
import math

import jax
import jax.numpy as jnp
from jax import lax
from jax.experimental import pallas as pl
from jax.experimental.pallas import tpu as pltpu
from jax.sharding import PartitionSpec as P

D = 1024
E = 2048
N = 16
R = 64
K = 4
PARAMS = 6667264

LANES = 128
RESET = 1e30
MESH = pl.DeviceIdType.MESH


EPS = 1e-05
MOMENTUM = 0.9
AVERAGE = 0.9
RATES = (0.1, 0.03, 0.1, 0.1, 0.03, 0.03, 0.3, 0.3, 0.1, 0.03)


def silu(values):
    return values * jax.nn.sigmoid(values)


def silu_slope(values):
    sigmoid_of = jax.nn.sigmoid(values)
    return sigmoid_of * (1.0 + values * (1.0 - sigmoid_of))


def doc_tables(lengths_row, positions):
    ends = jnp.cumsum(lengths_row)
    starts = ends - lengths_row
    docid = jnp.sum((positions[None, :] >= starts[:, None]).astype(jnp.int32), axis=0)
    first = jnp.sum((positions[None, :] == starts[:, None]).astype(jnp.int32), axis=0)
    return (docid, first > 0)


def scan_kernel(
    member_ref,
    ddec_ref,
    drive_ref,
    grady_ref,
    inb_ref,
    outb_ref,
    rates_ref,
    all_ref,
    sums_ref,
    scanned_ref,
    along_ref,
    decayed_ref,
    gin_ref,
    gout_ref,
    grates_ref,
    kept,
    first,
    second,
):
    groups, steps = ddec_ref.shape[:2]
    devices = all_ref.shape[0]
    base = pl.program_id(0) * groups
    member = member_ref[0]
    columns = [pl.ds(group * LANES, LANES) for group in range(groups)]
    half = N // 2

    @pl.when(pl.program_id(0) == 0)
    def _():
        gin_ref[...] = jnp.zeros_like(gin_ref)
        gout_ref[...] = jnp.zeros_like(gout_ref)

    def through(device, states):
        new = []
        for group in range(groups):
            total = sums_ref[device, pl.ds(base + group, 1), :]
            factor = jnp.exp2(total * rates_ref[:, columns[group]])
            new.append(
                factor * states[group]
                + all_ref[device, 0, :, columns[group]].astype(jnp.float32)
            )
        return new

    zeros = [jnp.zeros((N, LANES), jnp.float32) for _ in range(groups)]
    reach = devices // 2
    entering = lax.fori_loop(jnp.maximum(member - reach, 0), member, through, zeros)
    last = jnp.minimum(member + reach, devices - 1)
    leaving = lax.fori_loop(0, last - member, lambda d, s: through(last - d, s), zeros)

    def fold(values):
        return values[:half] + values[half:]

    def forward(t, hidden):
        in_row, out_row = inb_ref[t], outb_ref[t]
        new = []
        for group in range(groups):
            here = (group, pl.ds(t, 1))
            decay = jnp.exp2(ddec_ref[here] * rates_ref[:, columns[group]])
            state = decay * hidden[group] + drive_ref[here] * in_row
            kept[t + 1, :, columns[group]] = state
            first[group, pl.ds(pl.multiple_of(t * half, half), half), :] = fold(state * out_row)
            new.append(state)
        return new

    for group in range(groups):
        kept[0, :, columns[group]] = entering[group]
    lax.fori_loop(0, steps, forward, entering, unroll=4)

    def collapse(source, target_ref):
        for group in range(groups):
            total = source[group, pl.ds(0, steps, stride=half), :]
            for place in range(1, half):
                total = total + source[group, pl.ds(place, steps, stride=half), :]
            target_ref[group] = total

    collapse(first, scanned_ref)

    def backward(back, carry):
        later, grates = carry
        t = steps - 1 - back
        in_row, out_row = inb_ref[t], outb_ref[t]
        gin, gout = gin_ref[t], gout_ref[t]
        new = ([], [])
        rows = pl.ds(pl.multiple_of(t * half, half), half)
        for group in range(groups):
            here = (group, pl.ds(t, 1))
            grady = grady_ref[here]
            delta = ddec_ref[here]
            rates = rates_ref[:, columns[group]]
            adjoint = grady * out_row + later[group]
            gout = gout + grady * kept[t + 1, :, columns[group]]
            gin = gin + adjoint * drive_ref[here]
            first[group, rows, :] = fold(adjoint * in_row)
            passed = jnp.exp2(delta * rates) * adjoint
            pulled = passed * kept[t, :, columns[group]]
            second[group, rows, :] = fold(pulled * rates)
            new[0].append(passed)
            new[1].append(grates[group] + pulled * delta)
        gin_ref[t] = gin
        gout_ref[t] = gout
        return new

    _, grates = lax.fori_loop(0, steps, backward, (leaving, zeros), unroll=4)
    collapse(first, along_ref)
    collapse(second, decayed_ref)
    for group in range(groups):
        grates_ref[:, columns[group]] = grates[group]


def scan_of(member, ddec, drive, grady, inb, outb, rates, everyone, sums, block):
    steps = ddec.shape[1]
    devices = everyone.shape[0]
    groups = block // LANES
    wide = pl.BlockSpec((block // LANES, steps, LANES), lambda b: (b, 0, 0))
    whole = pl.BlockSpec((steps, N, LANES), lambda b: (0, 0, 0))
    narrow = pl.BlockSpec((N, block), lambda b: (0, b))
    full = jax.ShapeDtypeStruct((E // LANES, steps, LANES), jnp.float32)
    spread = jax.ShapeDtypeStruct((steps, N, LANES), jnp.float32)
    return pl.pallas_call(
        scan_kernel,
        grid=(E // block,),
        in_specs=[
            pl.BlockSpec(memory_space=pltpu.SMEM),
            wide,
            wide,
            wide,
            whole,
            whole,
            narrow,
            pl.BlockSpec((devices, 1, N, block), lambda b: (0, b, 0, 0)),
            pl.BlockSpec(sums.shape, lambda b: (0, 0, 0)),
        ],
        out_specs=[wide, wide, wide, whole, whole, narrow],
        out_shape=[full, full, full, spread, spread, jax.ShapeDtypeStruct((N, E), jnp.float32)],
        scratch_shapes=[
            pltpu.VMEM((steps + 1, N, block), jnp.float32),
            pltpu.VMEM((groups, steps * N // 2, LANES), jnp.float32),
            pltpu.VMEM((groups, steps * N // 2, LANES), jnp.float32),
        ],
        compiler_params=pltpu.CompilerParams(vmem_limit_bytes=48 * 2**20),
        name="scan",
    )(member, ddec, drive, grady, inb, outb, rates, everyone, sums)


def partner(axis, offset):
    size = lax.axis_size(axis)
    return lax.rem(lax.axis_index(axis) + offset, size)


def greet(counts):
    barrier = pltpu.get_barrier_semaphore()
    total = 0
    for axis, count in counts:
        for offset in range(1, count):
            pl.semaphore_signal(
                barrier, inc=1, device_id={axis: partner(axis, offset)}, device_id_type=MESH
            )
        total += count - 1
    pl.semaphore_wait(barrier, total)


def push(source, target, semaphores, at, axis, offset):
    copy = pltpu.make_async_remote_copy(
        src_ref=source,
        dst_ref=target,
        send_sem=semaphores.at[0, at],
        recv_sem=semaphores.at[1, at],
        device_id={axis: partner(axis, offset)},
        device_id_type=MESH,
    )
    copy.start()
    return copy


def span(index, size):
    return pl.ds(index * size, size)


def softplus(values):
    return jnp.maximum(values, 0.0) + jnp.log1p(jnp.exp(-jnp.abs(values)))


def front_kernel(
    devices,
    nrows,
    starts_ref,
    tokens_ref,
    cot_ref,
    gain_ref,
    in_proj_ref,
    out_proj_ref,
    conv_ref,
    cbias_ref,
    x_proj_ref,
    dt_proj_ref,
    dtbias_ref,
    rates_ref,
    normed_ref,
    inner_ref,
    gates_ref,
    back_ref,
    pre_act_ref,
    delta_pre_ref,
    ddec_ref,
    drive_ref,
    grady_ref,
    rank_ref,
    inb_ref,
    outb_ref,
    ends_out,
    sums_out,
    in_proj_buf,
    out_proj_buf,
    padded,
    docid,
    masks,
    proj,
    ends,
    loads,
    halo_wires,
    wires,
    sum_wires,
    row_wires,
):
    member = lax.axis_index("seq")
    own = lax.axis_index("rows") if nrows > 1 else 0
    steps = tokens_ref.shape[0]
    groups = E // LANES
    chunk = 4 * LANES
    chunks = E // chunk
    reach = devices // 2
    halo = inner_ref.shape[0] - steps
    in_loads = [
        pltpu.make_async_copy(
            in_proj_ref.at[:, span(at, chunk)], in_proj_buf.at[at], loads.at[at]
        )
        for at in range(2 * chunks)
    ]
    out_loads = [
        pltpu.make_async_copy(
            out_proj_ref.at[span(at, chunk), :], out_proj_buf.at[at], loads.at[2 * chunks + at]
        )
        for at in range(chunks)
    ]
    for load in in_loads + out_loads:
        load.start()
    barrier = pltpu.get_barrier_semaphore()
    for axis, count in (("seq", devices), ("rows", nrows)):
        for offset in range(1, count):
            pl.semaphore_signal(
                barrier, inc=1, device_id={axis: partner(axis, offset)}, device_id_type=MESH
            )

    stream = tokens_ref[...].astype(jnp.float32)
    inverse = lax.rsqrt(jnp.mean(stream * stream, axis=1, keepdims=True) + EPS)
    normed_ref[own] = (stream * inverse * gain_ref[...]).astype(jnp.bfloat16)

    places = member * steps - 8 + lax.broadcasted_iota(jnp.int32, docid.shape, 0)
    count = jnp.zeros(docid.shape, jnp.int32)
    first = jnp.zeros(docid.shape, jnp.float32)
    for index in range(starts_ref.shape[0]):
        count = count + jnp.where(places >= starts_ref[index], 1, 0)
        first = jnp.where(places == starts_ref[index], 1.0, first)
    docid[...] = count
    masks[0] = first[8 : 8 + steps]
    for offset in range(1, K):
        masks[offset] = jnp.where(
            docid[8 - offset : 8 - offset + steps, :] == docid[8 : 8 + steps, :], 1.0, 0.0
        )

    def project(at):
        in_loads[at].wait()
        return jnp.dot(
            normed_ref[own], in_proj_buf[at], preferred_element_type=jnp.float32
        ).astype(jnp.bfloat16)

    for at in range(chunks):
        inner_ref[halo:, span(at, chunk)] = project(at)
    pl.semaphore_wait(barrier, devices + nrows - 2)
    halo_copy = pltpu.make_async_remote_copy(
        src_ref=inner_ref.at[steps : steps + halo, :],
        dst_ref=inner_ref.at[0:halo, :],
        send_sem=halo_wires.at[0],
        recv_sem=halo_wires.at[1],
        device_id={"seq": partner("seq", 1)},
        device_id_type=MESH,
    )

    @pl.when(member < devices - 1)
    def _():
        halo_copy.start()

    row_copies = [
        push(normed_ref.at[own], normed_ref.at[own], row_wires, offset - 1, "rows", offset)
        for offset in range(1, nrows)
    ]

    @pl.when(member == 0)
    def _():
        inner_ref[0:halo, :] = jnp.zeros((halo, E), jnp.bfloat16)

    for at in range(chunks):
        gates_ref[:, span(at, chunk)] = project(chunks + at)
    for at in range(chunks):
        out_loads[at].wait()
        back_ref[:, span(at, chunk)] = lax.dot_general(
            cot_ref[...],
            out_proj_buf[at],
            (((1,), (1,)), ((), ())),
            preferred_element_type=jnp.float32,
        ).astype(jnp.bfloat16)

    @pl.when(member < devices - 1)
    def _():
        halo_copy.wait_send()

    @pl.when(member > 0)
    def _():
        halo_copy.wait_recv()

    proj[...] = jnp.zeros_like(proj)
    for at in range(chunks):
        lows = []
        for group in range(4 * at, 4 * at + 4):
            columns = span(group, LANES)
            padded[...] = inner_ref[halo - 8 :, columns].astype(jnp.float32)
            value = cbias_ref[:, columns] + conv_ref[0:1, columns] * padded[8:, :]
            for offset in range(1, K):
                value = (
                    value
                    + conv_ref[offset : offset + 1, columns]
                    * padded[8 - offset : 8 - offset + steps, :]
                    * masks[offset]
                )
            pre_act_ref[group] = value
            act = silu(value)
            drive_ref[group] = act
            lows.append(act.astype(jnp.bfloat16))
        proj[...] += lax.dot_general(
            jnp.concatenate(lows, axis=1),
            x_proj_ref[:, span(at, chunk)],
            (((1,), (1,)), ((), ())),
            preferred_element_type=jnp.float32,
        )
    rank_ref[...] = proj[:, :R].astype(jnp.bfloat16)
    inb_ref[...] = jnp.broadcast_to(proj[:, R : R + N][:, :, None], inb_ref.shape)
    outb_ref[...] = jnp.broadcast_to(proj[:, R + N :][:, :, None], outb_ref.shape)

    def later(distance, at):
        return pltpu.make_async_remote_copy(
            src_ref=ends.at[0, at],
            dst_ref=ends_out.at[member, at],
            send_sem=wires.at[0, 0, at, distance - 1],
            recv_sem=wires.at[0, 1, at, distance - 1],
            device_id={"seq": partner("seq", distance)},
            device_id_type=MESH,
        )

    def earlier(distance, at):
        return pltpu.make_async_remote_copy(
            src_ref=ends.at[1, at],
            dst_ref=ends_out.at[member, at],
            send_sem=wires.at[1, 0, at, distance - 1],
            recv_sem=wires.at[1, 1, at, distance - 1],
            device_id={"seq": partner("seq", devices - distance)},
            device_id_type=MESH,
        )

    def sums_to(distance, side):
        offset = distance if side == 0 else devices - distance
        return pltpu.make_async_remote_copy(
            src_ref=sums_out.at[member],
            dst_ref=sums_out.at[member],
            send_sem=sum_wires.at[side, 0, distance - 1],
            recv_sem=sum_wires.at[side, 1, distance - 1],
            device_id={"seq": partner("seq", offset)},
            device_id_type=MESH,
        )

    for at in range(chunks):
        delta_pre = (
            jnp.dot(
                rank_ref[...], dt_proj_ref[:, span(at, chunk)], preferred_element_type=jnp.float32
            )
            + dtbias_ref[:, span(at, chunk)]
        )
        for place in range(4):
            group = 4 * at + place
            columns = span(group, LANES)
            here = delta_pre[:, place * LANES : (place + 1) * LANES]
            delta = softplus(here)
            delta_pre_ref[group] = here
            drive_ref[group] = drive_ref[group] * delta
            ddec = jnp.where(masks[0] > 0.0, RESET, delta)
            ddec_ref[group] = ddec
            sums_out[member, group : group + 1, :] = jnp.sum(ddec, axis=0, keepdims=True)
            grady_ref[group] = back_ref[:, columns].astype(jnp.float32) * silu(
                gates_ref[:, columns].astype(jnp.float32)
            )

        def step(t, carry):
            hidden, decayed, pulled = carry
            in_row, out_row = inb_ref[t], outb_ref[t]
            new = ([], [], [])
            for place in range(4):
                here = (4 * at + place, pl.ds(t, 1))
                decay = jnp.exp2(ddec_ref[here] * rates_ref[:, span(4 * at + place, LANES)])
                new[0].append(decay * hidden[place] + drive_ref[here] * in_row)
                product = decay * decayed[place]
                new[1].append(product)
                new[2].append(pulled[place] + product * (grady_ref[here] * out_row))
            return new

        zeros = [jnp.zeros((N, LANES), jnp.float32) for _ in range(4)]
        ones = [jnp.ones((N, LANES), jnp.float32) for _ in range(4)]
        hidden, _, pulled = lax.fori_loop(0, steps, step, (zeros, ones, zeros), unroll=4)
        ends[0, at] = jnp.concatenate(hidden, axis=1).astype(jnp.bfloat16)
        ends[1, at] = jnp.concatenate(pulled, axis=1).astype(jnp.bfloat16)
        for distance in range(1, reach + 1):

            @pl.when(member + distance < devices)
            def _():
                later(distance, at).start()

            @pl.when(member >= distance)
            def _():
                earlier(distance, at).start()

    for distance in range(1, reach + 1):

        @pl.when(member + distance < devices)
        def _():
            sums_to(distance, 0).start()

        @pl.when(member >= distance)
        def _():
            sums_to(distance, 1).start()

    for distance in range(1, reach + 1):

        @pl.when(member + distance < devices)
        def _():
            for at in range(chunks):
                later(distance, at).wait_send()
                earlier(distance, at).wait_recv()
            sums_to(distance, 0).wait_send()
            sums_to(distance, 1).wait_recv()

        @pl.when(member >= distance)
        def _():
            for at in range(chunks):
                earlier(distance, at).wait_send()
                later(distance, at).wait_recv()
            sums_to(distance, 1).wait_send()
            sums_to(distance, 0).wait_recv()
    for copy in row_copies:
        copy.wait()


def front_of(starts, tokens, cot, gain, in_proj, out_proj, conv, cbias, x_proj, dt_proj, dtbias, rates, devices, nrows):
    steps = tokens.shape[0]
    groups = E // LANES
    chunk = 4 * LANES
    chunks = E // chunk
    reach = devices // 2
    halo = 16
    low = jnp.bfloat16
    vmem = pl.BlockSpec(memory_space=pltpu.VMEM)
    grouped = jax.ShapeDtypeStruct((groups, steps, LANES), jnp.float32)
    spread = jax.ShapeDtypeStruct((steps, N, LANES), jnp.float32)
    return pl.pallas_call(
        functools.partial(front_kernel, devices, nrows),
        in_specs=[pl.BlockSpec(memory_space=pltpu.SMEM)]
        + [vmem] * 3
        + [pl.BlockSpec(memory_space=pl.ANY)] * 2
        + [vmem] * 6,
        out_specs=[vmem] * 14,
        out_shape=[
            jax.ShapeDtypeStruct((nrows, steps, D), low),
            jax.ShapeDtypeStruct((steps + halo, E), low),
            jax.ShapeDtypeStruct((steps, E), low),
            jax.ShapeDtypeStruct((steps, E), low),
            grouped,
            grouped,
            grouped,
            grouped,
            grouped,
            jax.ShapeDtypeStruct((steps, R), low),
            spread,
            spread,
            jax.ShapeDtypeStruct((devices, chunks, N, chunk), low),
            jax.ShapeDtypeStruct((devices, groups, LANES), jnp.float32),
        ],
        scratch_shapes=[
            pltpu.VMEM((2 * chunks, D, chunk), low),
            pltpu.VMEM((chunks, chunk, D), low),
            pltpu.VMEM((steps + 8, LANES), jnp.float32),
            pltpu.VMEM((steps + 16, LANES), jnp.int32),
            pltpu.VMEM((K, steps, LANES), jnp.float32),
            pltpu.VMEM((steps, R + 2 * N), jnp.float32),
            pltpu.VMEM((2, chunks, N, chunk), low),
            pltpu.SemaphoreType.DMA((3 * chunks,)),
            pltpu.SemaphoreType.DMA((2,)),
            pltpu.SemaphoreType.DMA((2, 2, chunks, reach)),
            pltpu.SemaphoreType.DMA((2, 2, reach)),
            pltpu.SemaphoreType.DMA((2, max(nrows - 1, 1))),
        ],
        compiler_params=pltpu.CompilerParams(
            collective_id=0, has_side_effects=True, vmem_limit_bytes=60 * 2**20
        ),
        name="front",
    )(starts, tokens, cot, gain, in_proj, out_proj, conv, cbias, x_proj, dt_proj, dtbias, rates)


PACKED = (R, R + 2 * N, N, K, 1, 1, 1, 1)
PACKED_ROWS = 192


def packed_rows():
    spans = []
    at = 0
    for count in PACKED:
        spans.append((at, at + count))
        at += count
    return spans


def silu_pair(values):
    sigmoid_of = jax.nn.sigmoid(values)
    return values * sigmoid_of, sigmoid_of * (1.0 + values * (1.0 - sigmoid_of))


def block_kernel(
    nrows,
    devices,
    lengths_ref,
    tokens_ref,
    cot_ref,
    gain_ref,
    in_proj_ref,
    out_proj_ref,
    conv_ref,
    cbias_ref,
    x_proj_ref,
    dt_proj_ref,
    dtbias_ref,
    alog_ref,
    dskip_ref,
    output_ref,
    grad_ref,
    gin_out,
    gout_out,
    small_out,
    norm_out,
    in_proj_buf,
    out_proj_buf,
    rates_ref,
    normed_rows,
    normed_sib,
    cot_half,
    cot_sib,
    inner,
    gates,
    back,
    pre_act,
    delta_pre,
    ddec,
    drive,
    grady,
    proj,
    rank_low,
    inb,
    outb,
    ends,
    ends_all,
    sums_all,
    docid,
    masks,
    padded,
    kept,
    first,
    second,
    gin,
    gout,
    gated,
    back_gates,
    back_inner,
    grad_conv,
    rank_back,
    proj_back,
    gated_got,
    back_got,
    gout_sum,
    gout_low,
    gout_got,
    gin_sum,
    gin_low,
    gin_got,
    gin_pub,
    small,
    small_low,
    small_got,
    small_part,
    small_seq,
    norm_part,
    norm_all,
    loads,
    halo_wires,
    state_wires,
    sum_wires,
    gather_wires,
    sib_wires,
    gated_wires,
    back_wires,
    gout_wires,
    line_wires,
    plane_wires,
    row_wires,
    seq_wires,
    norm_wires,
    local,
):
    row = lax.axis_index("rows")
    member = lax.axis_index("seq")
    level, side = member // 2, lax.rem(member, 2)
    levels = devices // 2
    steps = tokens_ref.shape[0]
    groups = E // LANES
    chunk = 4 * LANES
    chunks = E // chunk
    shard = E // devices
    halo = inner.shape[0] - steps
    reach = devices // 2
    half = N // 2
    low = jnp.bfloat16
    wide = jnp.float32
    spans = packed_rows()
    everyone = nrows * devices

    in_loads = [
        pltpu.make_async_copy(
            in_proj_ref.at[:, span(at, chunk)], in_proj_buf.at[at], loads.at[at]
        )
        for at in range(2 * chunks)
    ]
    out_load = pltpu.make_async_copy(out_proj_ref, out_proj_buf, loads.at[2 * chunks])
    for load in in_loads + [out_load]:
        load.start()

    def share(index, size):
        return pl.ds(pl.multiple_of(index * size, size), size)

    def plane(turn, other):
        return {
            "rows": lax.rem(row + turn, nrows),
            "seq": 2 * level + lax.rem(side + other, 2),
        }

    across = [levels - 1 - level, lax.rem(level + 2, levels), level + 1 - 2 * lax.rem(level, 2)]

    def line(turn):
        return {"seq": 2 * across[turn - 1] + side}

    def remote(source, target, send, recv, device):
        return pltpu.make_async_remote_copy(
            src_ref=source,
            dst_ref=target,
            send_sem=send,
            recv_sem=recv,
            device_id=device,
            device_id_type=MESH,
        )

    def begin(copies):
        for copy in copies:
            copy.start()
        return copies

    def settle(copies):
        for copy in copies:
            copy.wait()

    def other_device(offset):
        return {
            "rows": lax.rem(row + offset // devices, nrows),
            "seq": lax.rem(member + offset % devices, devices),
        }

    barrier = pltpu.get_barrier_semaphore()
    for offset in range(1, everyone):
        pl.semaphore_signal(
            barrier, inc=1, device_id=other_device(offset), device_id_type=MESH
        )

    def column_sum(values):
        return jnp.sum(values, axis=0, keepdims=True)

    stream = tokens_ref[...].astype(wide)
    inverse = lax.rsqrt(jnp.mean(stream * stream, axis=1, keepdims=True) + EPS)
    normed_rows[row] = (stream * inverse * gain_ref[...]).astype(low)
    cot_half[row] = cot_ref[:, share(lax.rem(row, 2), D // 2)]
    rates_ref[...] = jnp.exp(alog_ref[...]) * (-1.0 / math.log(2.0))

    places = member * steps - 8 + lax.broadcasted_iota(jnp.int32, docid.shape, 0)
    count = jnp.zeros(docid.shape, jnp.int32)
    starting = jnp.zeros(docid.shape, wide)
    start = 0
    for index in range(lengths_ref.shape[1]):
        count = count + jnp.where(places >= start, 1, 0)
        starting = jnp.where(places == start, 1.0, starting)
        start = start + lengths_ref[0, index]
    docid[...] = count
    masks[0] = starting[8:]
    for offset in range(1, K):
        masks[offset] = jnp.where(
            docid[8 - offset : 16 - offset + steps, :] == docid[8:, :], 1.0, 0.0
        )

    def project(at):
        in_loads[at].wait()
        return jnp.dot(
            normed_rows[row], in_proj_buf[at], preferred_element_type=wide
        ).astype(low)

    for at in range(chunks):
        inner[halo:, span(at, chunk)] = project(at)
    pl.semaphore_wait(barrier, everyone - 1)
    halo_copy = remote(
        inner.at[steps : steps + halo, :],
        inner.at[0:halo, :],
        halo_wires.at[0, 0],
        halo_wires.at[0, 1],
        {"seq": partner("seq", 1)},
    )

    @pl.when(member < devices - 1)
    def _():
        halo_copy.start()

    @pl.when(member == 0)
    def _():
        inner[0:halo, :] = jnp.zeros((halo, E), low)

    def gather_rows(kind, make, target):
        return begin(
            [
                remote(
                    make(partner("rows", offset)),
                    target.at[row],
                    gather_wires.at[kind, 0, offset - 1],
                    gather_wires.at[kind, 1, offset - 1],
                    {"rows": partner("rows", offset)},
                )
                for offset in range(1, nrows)
            ]
        )

    def to_sibling(kind, source, target):
        return begin(
            [
                remote(
                    source,
                    target,
                    sib_wires.at[kind, 0],
                    sib_wires.at[kind, 1],
                    {"seq": 2 * level + 1 - side},
                )
            ]
        )

    normed_moves = gather_rows(0, lambda other: normed_rows.at[row], normed_rows)
    cot_moves = gather_rows(
        1, lambda other: cot_ref.at[:, share(lax.rem(other, 2), D // 2)], cot_half
    )
    for at in range(chunks):
        gates[:, span(at, chunk)] = project(chunks + at)
    out_load.wait()
    for at in range(chunks):
        back[:, span(at, chunk)] = lax.dot_general(
            cot_ref[...],
            out_proj_buf[span(at, chunk), :],
            (((1,), (1,)), ((), ())),
            preferred_element_type=wide,
        ).astype(low)

    gin[...] = jnp.zeros_like(gin)
    gout[...] = jnp.zeros_like(gout)
    rank_back[...] = jnp.zeros_like(rank_back)
    small[...] = jnp.zeros_like(small)
    norm_part[...] = jnp.zeros_like(norm_part)
    proj[...] = jnp.zeros_like(proj)

    @pl.when(member < devices - 1)
    def _():
        halo_copy.wait_send()

    @pl.when(member > 0)
    def _():
        halo_copy.wait_recv()

    for at in range(chunks):
        lows = []
        for group in range(4 * at, 4 * at + 4):
            columns = span(group, LANES)
            padded[...] = inner[halo - 8 :, columns].astype(wide)
            value = cbias_ref[:, columns] + conv_ref[0:1, columns] * padded[8:, :]
            for offset in range(1, K):
                value = (
                    value
                    + conv_ref[offset : offset + 1, columns]
                    * padded[8 - offset : 8 - offset + steps, :]
                    * masks[offset, :steps, :]
                )
            pre_act[group] = value
            act = silu(value)
            drive[group] = act
            lows.append(act.astype(low))
        proj[...] += lax.dot_general(
            jnp.concatenate(lows, axis=1),
            x_proj_ref[:, span(at, chunk)],
            (((1,), (1,)), ((), ())),
            preferred_element_type=wide,
        )
    rank_low[...] = proj[:, :R].astype(low)
    inb[...] = jnp.broadcast_to(proj[:, R : R + N][:, :, None], inb.shape)
    outb[...] = jnp.broadcast_to(proj[:, R + N :][:, :, None], outb.shape)

    def lanes(at, place):
        return share(4 * at + place, LANES)

    def state_copy(direction, distance, at):
        offset = distance if direction == 0 else devices - distance
        return remote(
            ends.at[direction, at],
            ends_all.at[member, at],
            state_wires.at[direction, 0, at, distance - 1],
            state_wires.at[direction, 1, at, distance - 1],
            {"seq": partner("seq", offset)},
        )

    def sum_copy(direction, distance):
        offset = distance if direction == 0 else devices - distance
        return remote(
            sums_all.at[member],
            sums_all.at[member],
            sum_wires.at[direction, 0, distance - 1],
            sum_wires.at[direction, 1, distance - 1],
            {"seq": partner("seq", offset)},
        )

    def to_neighbours(make):
        for distance in range(reach, 0, -1):

            @pl.when(member + distance < devices)
            def _():
                make(0, distance).start()

            @pl.when(member >= distance)
            def _():
                make(1, distance).start()

    def from_neighbours(make):
        for distance in range(1, reach + 1):

            @pl.when(member + distance < devices)
            def _():
                make(0, distance).wait_send()
                make(1, distance).wait_recv()

            @pl.when(member >= distance)
            def _():
                make(1, distance).wait_send()
                make(0, distance).wait_recv()

    for at in range(chunks):
        pre = (
            jnp.dot(rank_low[...], dt_proj_ref[:, span(at, chunk)], preferred_element_type=wide)
            + dtbias_ref[:, span(at, chunk)]
        )
        for place in range(4):
            group = 4 * at + place
            columns = span(group, LANES)
            here = pre[:, place * LANES : (place + 1) * LANES]
            delta = softplus(here)
            delta_pre[group] = here
            drive[group] = drive[group] * delta
            decaying = jnp.where(masks[0, :steps, :] > 0.0, RESET, delta)
            ddec[group] = decaying
            sums_all[member, group : group + 1, :] = column_sum(decaying)
            grady[group] = back[:, columns].astype(wide) * silu(gates[:, columns].astype(wide))
    to_neighbours(sum_copy)
    zeros = [jnp.zeros((N, LANES), wide) for _ in range(4)]
    ones = [jnp.ones((N, LANES), wide) for _ in range(4)]
    order = [(turn, lax.rem(row + turn, nrows)) for turn in [*range(1, nrows), 0]]
    for _, at in order:

        def step(t, carry):
            hidden, decayed, pulled = carry
            in_row, out_row = inb[t], outb[t]
            new = ([], [], [])
            for place in range(4):
                here = (4 * at + place, pl.ds(t, 1))
                decay = jnp.exp2(ddec[here] * rates_ref[:, lanes(at, place)])
                new[0].append(decay * hidden[place] + drive[here] * in_row)
                product = decay * decayed[place]
                new[1].append(product)
                new[2].append(pulled[place] + product * (grady[here] * out_row))
            return new

        hidden, _, pulled = lax.fori_loop(0, steps, step, (zeros, ones, zeros), unroll=4)
        ends[0, at] = jnp.concatenate(hidden, axis=1).astype(low)
        ends[1, at] = jnp.concatenate(pulled, axis=1).astype(low)
        to_neighbours(lambda direction, distance: state_copy(direction, distance, at))
    from_neighbours(sum_copy)

    def fold(values):
        return values[:half] + values[half:]

    def collapse(source, place):
        total = source[place, pl.ds(0, steps, stride=half), :]
        for index in range(1, half):
            total = total + source[place, pl.ds(index, steps, stride=half), :]
        return total

    def trade(kind, source, at, turn):
        copies = []
        for other in range(2):
            columns = share(2 * at + lax.rem(side + other, 2), shard)
            target = back_got.at[kind, other, row]
            if turn == 0 and other == 0:
                copies.append(
                    pltpu.make_async_copy(source.at[:, columns], target, local.at[kind])
                )
            else:
                copies.append(
                    remote(
                        source.at[:, columns],
                        target,
                        back_wires.at[kind, 0, 2 * turn + other],
                        back_wires.at[kind, 1, 2 * turn + other],
                        plane(turn, other),
                    )
                )
        return begin(copies)

    def trade_gated(at):
        copies = []
        for turn in range(nrows):
            for other in range(2):
                columns = share(
                    4 * at + 2 * lax.rem(side + other, 2) + partner("rows", turn) // 2, LANES
                )
                target = gated_got.at[at, other, row]
                if turn == 0 and other == 0:
                    copies.append(
                        pltpu.make_async_copy(gated.at[:, columns], target, local.at[2 + at])
                    )
                else:
                    copies.append(
                        remote(
                            gated.at[:, columns],
                            target,
                            gated_wires.at[0, at, 2 * turn + other],
                            gated_wires.at[1, at, 2 * turn + other],
                            plane(turn, other),
                        )
                    )
        return begin(copies)

    gate_moves, gated_moves = [], []
    leavings = []
    for slot, (turn, at) in enumerate(order):
        from_neighbours(lambda direction, distance: state_copy(direction, distance, at))

        def through(device, states):
            new = []
            for place in range(4):
                total = sums_all[device, pl.ds(4 * at + place, 1), :]
                factor = jnp.exp2(total * rates_ref[:, lanes(at, place)])
                new.append(
                    factor * states[place]
                    + ends_all[device, at, :, place * LANES : (place + 1) * LANES].astype(wide)
                )
            return new

        def forward(t, hidden):
            in_row, out_row = inb[t], outb[t]
            new = []
            for place in range(4):
                here = (4 * at + place, pl.ds(t, 1))
                decay = jnp.exp2(ddec[here] * rates_ref[:, lanes(at, place)])
                state = decay * hidden[place] + drive[here] * in_row
                kept[slot, t + 1, place] = state.astype(low)
                first[place, share(t, half), :] = fold(state * out_row)
                new.append(state)
            return new

        entering = lax.fori_loop(jnp.maximum(member - reach, 0), member, through, zeros)
        last = jnp.minimum(member + reach, devices - 1)
        leavings.append(lax.fori_loop(0, last - member, lambda d, s: through(last - d, s), zeros))
        for place in range(4):
            kept[slot, 0, place] = entering[place].astype(low)
        lax.fori_loop(0, steps, forward, entering, unroll=4)
        for place in range(4):
            group, columns = 4 * at + place, lanes(at, place)
            act = silu(pre_act[group])
            y_full = collapse(first, place) + dskip_ref[:, columns] * act
            gate, slope = silu_pair(gates[:, columns].astype(wide))
            gated[:, columns] = (y_full * gate).astype(low)
            back_gates[:, columns] = (back[:, columns].astype(wide) * y_full * slope).astype(low)
            small[spans[6][0] : spans[6][1], columns] = column_sum(grady[group] * act)
        gate_moves += trade(1, back_gates, at, turn)


    def in_grads(kind):
        total = None
        for other, normed in ((0, normed_rows), (1, normed_sib)):
            part = lax.dot_general(
                normed[...].reshape(nrows * steps, D),
                back_got[kind, other].reshape(nrows * steps, shard),
                (((0,), (0,)), ((), ())),
                preferred_element_type=wide,
            )
            total = part if total is None else total + part
        gin_sum[kind] = total
        gin_low[kind] = total.astype(low)
        return begin(
            [
                remote(
                    gin_low.at[kind, share(across[turn - 1], D // levels), :],
                    gin_got.at[kind, turn - 1],
                    line_wires.at[kind, 0, turn - 1],
                    line_wires.at[kind, 1, turn - 1],
                    line(turn),
                )
                for turn in range(1, levels)
            ]
        )

    def squares(values):
        return jnp.sum(jnp.sum(values * values, axis=0, keepdims=True), axis=1, keepdims=True)

    def in_share(kind, before=None):
        total = gin_sum[kind, share(level, D // levels), :]
        for turn in range(levels - 1):
            total = total + gin_got[kind, turn].astype(wide)
        gin_pub[kind] = total.astype(low)
        owned = D // devices
        columns = share(kind * devices + 2 * row + side, shard)
        gin_out[:, columns] = gin_pub[kind, share(side, owned), :]
        norm_part[...] += squares(total)
        copies = [] if before is None else before()
        copies += begin(
            [
                remote(
                    gin_pub.at[kind, share(lax.rem(side + other, 2), owned), :],
                    gin_out.at[:, columns],
                    plane_wires.at[kind, 0, 2 * turn + other],
                    plane_wires.at[kind, 1, 2 * turn + other],
                    plane(turn, other),
                )
                for turn in range(nrows)
                for other in range(2)
                if turn + other > 0
            ]
        )
        return copies

    def gout_copy(turn):
        return remote(
            gout_low.at[across[turn - 1]],
            gout_got.at[turn - 1],
            gout_wires.at[0, turn - 1],
            gout_wires.at[1, turn - 1],
            line(turn),
        )

    def out_grads():
        for piece in range(levels):
            total = None
            for other, cots in ((0, cot_half), (1, cot_sib)):
                part = lax.dot_general(
                    gated_got[piece, other].reshape(nrows * steps, LANES),
                    cots[...].reshape(nrows * steps, D // 2),
                    (((0,), (0,)), ((), ())),
                    preferred_element_type=wide,
                )
                total = part if total is None else total + part
            gout_sum[piece] = total
            gout_low[piece] = total.astype(low)

    def out_share():
        total = gout_sum[level]
        for turn in range(levels - 1):
            total = total + gout_got[turn].astype(wide)
        mine = gout_out.at[share(row // 2, LANES), share(lax.rem(row, 2), D // 2)]
        mine[...] = total.astype(low)
        norm_part[...] += squares(total)
        return begin(
            [
                remote(
                    mine,
                    mine,
                    row_wires.at[2, 0, turn - 1],
                    row_wires.at[2, 1, turn - 1],
                    {"rows": partner("rows", turn)},
                )
                for turn in range(1, nrows)
            ]
        )

    for slot, (turn, at) in enumerate(order):

        def backward(back_step, carry):
            later, grates, states = carry
            t = steps - 1 - back_step
            in_row, out_row = inb[t], outb[t]
            gin_row, gout_row = gin[t], gout[t]
            new = ([], [], [])
            for place in range(4):
                here = (4 * at + place, pl.ds(t, 1))
                grad_y = grady[here]
                delta = ddec[here]
                rates = rates_ref[:, lanes(at, place)]
                before = kept[slot, t, place].astype(wide)
                adjoint = grad_y * out_row + later[place]
                gout_row = gout_row + grad_y * states[place]
                gin_row = gin_row + adjoint * drive[here]
                first[place, share(t, half), :] = fold(adjoint * in_row)
                passed = jnp.exp2(delta * rates) * adjoint
                pulled = passed * before
                second[place, share(t, half), :] = fold(pulled * rates)
                new[0].append(passed)
                new[1].append(grates[place] + pulled * delta)
                new[2].append(before)
            gin[t] = gin_row
            gout[t] = gout_row
            return new

        ending = [kept[slot, steps, place].astype(wide) for place in range(4)]
        _, grates, _ = lax.fori_loop(
            0, steps, backward, (leavings[slot], zeros, ending), unroll=4
        )
        lows = []
        for place in range(4):
            group, columns = 4 * at + place, lanes(at, place)
            along = collapse(first, place)
            here = delta_pre[group]
            act = silu(pre_act[group])
            grad_delta = along * act + collapse(second, place) * math.log(2.0)
            pre_low = (grad_delta * jax.nn.sigmoid(here)).astype(low)
            lows.append(pre_low)
            drive[group] = grady[group] * dskip_ref[:, columns] + along * softplus(here)
            small[spans[5][0] : spans[5][1], columns] = column_sum(pre_low.astype(wide))
            small[spans[2][0] : spans[2][1], columns] = (
                grates[place] * rates_ref[:, columns] * math.log(2.0)
            )
        lows = jnp.concatenate(lows, axis=1)
        rank_back[...] += lax.dot_general(
            lows,
            dt_proj_ref[:, share(at, chunk)],
            (((1,), (1,)), ((), ())),
            preferred_element_type=wide,
        )
        small[spans[0][0] : spans[0][1], share(at, chunk)] = lax.dot_general(
            rank_low[...], lows, (((0,), (0,)), ((), ())), preferred_element_type=wide
        )
        if slot == 0:
            settle(normed_moves)
            normed_moves = to_sibling(0, normed_rows, normed_sib)
            settle(cot_moves)
            cot_moves = to_sibling(1, cot_half, cot_sib)
            for _, chunk_at in order:
                gated_moves += trade_gated(chunk_at)
        if slot == chunks - 3:
            settle(normed_moves)
            settle(gate_moves)
            gate_moves = in_grads(1)

    parts = [(0, R // nrows), (R, (PACKED_ROWS - R) // nrows)]

    def scatter_small(part):
        begin_row, few = parts[part]
        rows = pl.ds(begin_row, few * nrows)
        small_low[rows, :] = small[rows, :].astype(low)
        return begin(
            [
                remote(
                    small_low.at[pl.ds(begin_row + partner("rows", turn) * few, few), :],
                    small_got.at[turn - 1, pl.ds(begin_row // nrows, few), :],
                    row_wires.at[part, 0, turn - 1],
                    row_wires.at[part, 1, turn - 1],
                    {"rows": partner("rows", turn)},
                )
                for turn in range(1, nrows)
            ]
        )

    def trade_small(part):
        begin_row, few = parts[part]
        rows = pl.ds(begin_row // nrows, few)
        total = small[pl.ds(pl.multiple_of(begin_row + row * few, few), few), :]
        for turn in range(nrows - 1):
            total = total + small_got[turn, rows, :].astype(wide)
        small_part[rows, :] = total.astype(low)
        return begin(
            [
                remote(
                    small_part.at[rows, share(partner("seq", offset), shard)],
                    small_seq.at[offset - 1, rows, :],
                    seq_wires.at[part, 0, offset - 1],
                    seq_wires.at[part, 1, offset - 1],
                    {"seq": partner("seq", offset)},
                )
                for offset in (4, 3, 5, 2, 6, 1, 7)
            ]
        )

    def share_small(part):
        begin_row, few = parts[part]
        rows = pl.ds(begin_row // nrows, few)
        total = small_part[rows, share(member, shard)].astype(wide)
        for offset in range(devices - 1):
            total = total + small_seq[offset, rows, :].astype(wide)
        mine = pl.ds(pl.multiple_of(begin_row + row * few, few), few)
        small_out[mine, :] = total.astype(low)
        norm_part[...] += squares(total)
        return begin(
            [
                remote(
                    small_out.at[mine, :],
                    small_out.at[mine, :],
                    row_wires.at[3 + part, 0, turn - 1],
                    row_wires.at[3 + part, 1, turn - 1],
                    {"rows": partner("rows", turn)},
                )
                for turn in range(1, nrows)
            ]
        )

    dt_moves = scatter_small(0)
    proj_back[:, :R] = rank_back[...].astype(low)
    proj_back[:, R : R + N] = jnp.sum(gin[...], axis=2).astype(low)
    proj_back[:, R + N :] = jnp.sum(gout[...], axis=2).astype(low)
    for at in range(chunks):
        pulled = jnp.dot(
            proj_back[...], x_proj_ref[:, span(at, chunk)], preferred_element_type=wide
        )
        lows = []
        for place in range(4):
            group = 4 * at + place
            act, slope = silu_pair(pre_act[group])
            lows.append(act.astype(low))
            grad_conv[group, :steps, :] = (
                drive[group] + pulled[:, place * LANES : (place + 1) * LANES]
            ) * slope
        small[spans[1][0] : spans[1][1], span(at, chunk)] = lax.dot_general(
            proj_back[...],
            jnp.concatenate(lows, axis=1),
            (((0,), (0,)), ((), ())),
            preferred_element_type=wide,
        )
    halo_back = remote(
        grad_conv.at[:, 0:8, :],
        grad_conv.at[:, steps : steps + 8, :],
        halo_wires.at[1, 0],
        halo_wires.at[1, 1],
        {"seq": partner("seq", devices - 1)},
    )

    @pl.when(member > 0)
    def _():
        halo_back.start()

    @pl.when(member == devices - 1)
    def _():
        grad_conv[:, steps : steps + 8, :] = jnp.zeros((groups, 8, LANES), wide)

    settle(cot_moves)
    settle(gated_moves)
    out_grads()
    output_ref[...] = stream + jnp.dot(
        gated[...], out_proj_buf[...], preferred_element_type=wide
    )
    grad_normed = jnp.zeros((steps, D), wide)
    for at in range(chunks):
        grad_normed = grad_normed + lax.dot_general(
            back_gates[:, span(at, chunk)],
            in_proj_buf[chunks + at],
            (((1,), (1,)), ((), ())),
            preferred_element_type=wide,
        )

    @pl.when(member > 0)
    def _():
        halo_back.wait_send()

    @pl.when(member < devices - 1)
    def _():
        halo_back.wait_recv()

    gout_moves = begin([gout_copy(turn) for turn in range(1, levels)])
    inner_moves = []
    for turn, at in order:
        for place in range(4):
            group, columns = 4 * at + place, lanes(at, place)
            padded[...] = inner[halo - 8 :, columns].astype(wide)
            here = grad_conv[group, :steps, :]
            pulled = conv_ref[0:1, columns] * here
            small[spans[4][0] : spans[4][1], columns] = column_sum(here)
            at_row = spans[3][0]
            small[at_row : at_row + 1, columns] = column_sum(here * padded[8:, :])
            for offset in range(1, K):
                small[at_row + offset : at_row + offset + 1, columns] = column_sum(
                    here * masks[offset, :steps, :] * padded[8 - offset : 8 - offset + steps, :]
                )
                pulled = pulled + conv_ref[offset : offset + 1, columns] * (
                    grad_conv[group, offset : offset + steps, :]
                    * masks[offset, offset : offset + steps, :]
                )
            back_inner[:, columns] = pulled.astype(low)
        inner_moves += trade(0, back_inner, at, turn)

    for at in range(chunks):
        grad_normed = grad_normed + lax.dot_general(
            back_inner[:, span(at, chunk)],
            in_proj_buf[at],
            (((1,), (1,)), ((), ())),
            preferred_element_type=wide,
        )
    settle(dt_moves)
    dt_moves = trade_small(0)
    inverse = lax.rsqrt(jnp.mean(stream * stream, axis=1, keepdims=True) + EPS)
    grad_gain = column_sum(grad_normed * stream * inverse)
    owned = D // devices
    for index in range(devices):
        small[spans[7][0] : spans[7][1], index * shard : index * shard + owned] = grad_gain[
            :, index * owned : (index + 1) * owned
        ]
    small_moves = scatter_small(1)
    scaled = grad_normed * gain_ref[...]
    grad_ref[...] = (
        cot_ref[...].astype(wide)
        + inverse * scaled
        - stream
        * inverse
        * inverse
        * inverse
        * jnp.mean(scaled * stream, axis=1, keepdims=True)
    )

    settle(gate_moves)
    gate_moves = in_share(1)
    settle(inner_moves)
    inner_moves = in_grads(0)
    settle(small_moves)
    small_moves = trade_small(1)
    settle(gout_moves)
    gout_moves = out_share()
    settle(dt_moves)
    dt_moves = share_small(0)
    settle(small_moves)
    small_moves = share_small(1)

    def spread_norm():
        here = row * devices + member
        norm_all[here] = jnp.broadcast_to(norm_part[...], (8, LANES))
        return begin(
            [
                remote(
                    norm_all.at[here],
                    norm_all.at[here],
                    norm_wires.at[0, offset - 1],
                    norm_wires.at[1, offset - 1],
                    other_device(offset),
                )
                for offset in range(1, everyone)
            ]
        )

    settle(inner_moves)
    inner_moves = in_share(0, spread_norm)
    norm_moves, inner_moves = inner_moves[: everyone - 1], inner_moves[everyone - 1 :]
    settle(norm_moves)
    norm_out[...] = jnp.sqrt(jnp.sum(norm_all[...], axis=0))
    settle(gout_moves)
    settle(gate_moves)
    settle(dt_moves)
    settle(small_moves)
    settle(inner_moves)


def block_of(operands, nrows, devices):
    steps = operands[1].shape[0]
    groups = E // LANES
    chunk = 4 * LANES
    chunks = E // chunk
    levels = devices // 2
    reach = devices // 2
    shard = E // devices
    halo = 16
    low, wide = jnp.bfloat16, jnp.float32
    few = PACKED_ROWS // nrows
    vmem = pl.BlockSpec(memory_space=pltpu.VMEM)
    specs = [vmem] * len(operands)
    specs[0] = pl.BlockSpec(memory_space=pltpu.SMEM)
    specs[4] = specs[5] = pl.BlockSpec(memory_space=pl.ANY)
    dma = pltpu.SemaphoreType.DMA
    grouped = pltpu.VMEM((groups, steps, LANES), wide)
    flat = pltpu.VMEM((steps, E), low)
    spread = pltpu.VMEM((steps, N, LANES), wide)
    gathered = pltpu.VMEM((nrows, steps, D), low)
    folded = pltpu.VMEM((4, steps * N // 2, LANES), wide)
    return pl.pallas_call(
        functools.partial(block_kernel, nrows, devices),
        in_specs=specs,
        out_specs=[vmem] * 6,
        out_shape=[
            jax.ShapeDtypeStruct((steps, D), wide),
            jax.ShapeDtypeStruct((steps, D), wide),
            jax.ShapeDtypeStruct((D // devices, 2 * E), low),
            jax.ShapeDtypeStruct((shard, D), low),
            jax.ShapeDtypeStruct((PACKED_ROWS, shard), low),
            jax.ShapeDtypeStruct((8, LANES), wide),
        ],
        scratch_shapes=[
            pltpu.VMEM((2 * chunks, D, chunk), low),
            pltpu.VMEM((E, D), low),
            pltpu.VMEM((N, E), wide),
            gathered,
            gathered,
            pltpu.VMEM((nrows, steps, D // 2), low),
            pltpu.VMEM((nrows, steps, D // 2), low),
            pltpu.VMEM((steps + halo, E), low),
            flat,
            flat,
            grouped,
            grouped,
            grouped,
            grouped,
            grouped,
            pltpu.VMEM((steps, R + 2 * N), wide),
            pltpu.VMEM((steps, R), low),
            spread,
            spread,
            pltpu.VMEM((2, chunks, N, chunk), low),
            pltpu.VMEM((devices, chunks, N, chunk), low),
            pltpu.VMEM((devices, groups, LANES), wide),
            pltpu.VMEM((steps + 16, LANES), jnp.int32),
            pltpu.VMEM((K, steps + 8, LANES), wide),
            pltpu.VMEM((steps + 8, LANES), wide),
            pltpu.VMEM((chunks, steps + 1, 4, N, LANES), low),
            folded,
            folded,
            spread,
            spread,
            flat,
            flat,
            flat,
            pltpu.VMEM((groups, steps + 8, LANES), wide),
            pltpu.VMEM((steps, R), wide),
            pltpu.VMEM((steps, R + 2 * N), low),
            pltpu.VMEM((levels, 2, nrows, steps, LANES), low),
            pltpu.VMEM((2, 2, nrows, steps, shard), low),
            pltpu.VMEM((levels, LANES, D // 2), wide),
            pltpu.VMEM((levels, LANES, D // 2), low),
            pltpu.VMEM((levels - 1, LANES, D // 2), low),
            pltpu.VMEM((2, D, shard), wide),
            pltpu.VMEM((2, D, shard), low),
            pltpu.VMEM((2, levels - 1, D // levels, shard), low),
            pltpu.VMEM((2, D // levels, shard), low),
            pltpu.VMEM((PACKED_ROWS, E), wide),
            pltpu.VMEM((PACKED_ROWS, E), low),
            pltpu.VMEM((nrows - 1, few, E), low),
            pltpu.VMEM((few, E), low),
            pltpu.VMEM((devices - 1, few, shard), low),
            pltpu.VMEM((1, 1), wide),
            pltpu.VMEM((nrows * devices, 8, LANES), wide),
            dma((2 * chunks + 1,)),
            dma((2, 2)),
            dma((2, 2, chunks, reach)),
            dma((2, 2, reach)),
            dma((2, 2, nrows - 1)),
            dma((2, 2)),
            dma((2, levels, 2 * nrows)),
            dma((2, 2, 2 * nrows)),
            dma((2, levels - 1)),
            dma((2, 2, levels - 1)),
            dma((2, 2, 2 * nrows)),
            dma((5, 2, nrows - 1)),
            dma((2, 2, devices - 1)),
            dma((2, nrows * devices - 1)),
            dma((2 + levels,)),
        ],
        compiler_params=pltpu.CompilerParams(
            collective_id=1, has_side_effects=True, vmem_limit_bytes=63 * 2**20
        ),
        name="block",
    )(*operands)


def update_kernel(member_ref, norm_ref, gin_ref, gout_ref, small_ref, *refs):
    passed, weights, moments, averages, outs = (
        refs[:2],
        refs[2:12],
        refs[12:22],
        refs[22:32],
        refs[32:],
    )
    outs[30][...] = passed[0][...]
    outs[31][...] = passed[1][...]
    outs[32][...] = norm_ref[0:1, 0:1]
    shrink_by = 1.0 / jnp.maximum(norm_ref[0:1, 0:1], 1.0)

    def renew(ordinal, grad, at=Ellipsis):
        clipped = grad * shrink_by
        momentum_new = MOMENTUM * moments[ordinal][at] + clipped
        renewed = weights[ordinal][at].astype(jnp.float32) - RATES[ordinal] * math.sqrt(PARAMS) * (
            clipped + MOMENTUM * momentum_new
        )
        outs[3 * ordinal][at] = momentum_new
        outs[3 * ordinal + 1][at] = renewed
        outs[3 * ordinal + 2][at] = AVERAGE * averages[ordinal][at] + (1.0 - AVERAGE) * renewed

    renew(1, gin_ref[...].astype(jnp.float32))
    renew(9, gout_ref[...].astype(jnp.float32))

    @pl.when(pl.program_id(0) == 0)
    def _():
        spans = packed_rows()

        def part(index):
            return small_ref[spans[index][0] : spans[index][1], :].astype(jnp.float32)

        small = small_ref[...].astype(jnp.float32)
        renew(5, part(0))
        renew(4, part(1))
        renew(7, part(2))
        renew(2, part(3))
        for ordinal, index in ((3, 4), (6, 5), (8, 6)):
            renew(ordinal, small[spans[index][0] : spans[index][1]])
        gain = small[spans[7][0] : spans[7][1], : weights[0].shape[1]]
        renew(0, gain)


def update_of(member, norm_tile, gin, gout, small, passed, weights, moments, averages):
    inner = gin.shape[0]
    channels = gout.shape[0]
    blocks = 2
    outer = channels // blocks
    block = gin.shape[1] // blocks
    flat = (0, 3, 6, 8)

    def rows_of(array, ordinal):
        return array.reshape(1, -1) if ordinal in flat else array.T if ordinal == 4 else array

    def shard(shape, ordinal):
        if ordinal == 1:
            return pl.BlockSpec((inner, block), lambda j, m: (0, j))
        if ordinal == 9:
            return pl.BlockSpec((outer, shape[1]), lambda j, m: (j, 0))
        return pl.BlockSpec(shape, lambda j, m: (0, 0))

    def weight(shape, ordinal):
        if ordinal == 1:
            return pl.BlockSpec((inner, block), lambda j, m: (m[0], j))
        if ordinal == 9:
            return pl.BlockSpec((outer, shape[1]), lambda j, m: (m[0] * blocks + j, 0))
        return pl.BlockSpec(shape, lambda j, m: (0, m[0]))

    weights = [rows_of(array, ordinal) for ordinal, array in enumerate(weights)]
    moments = [rows_of(array, ordinal) for ordinal, array in enumerate(moments)]
    averages = [rows_of(array, ordinal) for ordinal, array in enumerate(averages)]
    shapes = [array.shape for array in moments]
    shards = [shard(shape, ordinal) for ordinal, shape in enumerate(shapes)]
    steps, depth = passed[0].shape
    through = pl.BlockSpec((steps // blocks, depth), lambda j, m: (j, 0))
    outs = pl.pallas_call(
        update_kernel,
        grid_spec=pltpu.PrefetchScalarGridSpec(
            num_scalar_prefetch=1,
            grid=(blocks,),
            in_specs=[
                pl.BlockSpec(norm_tile.shape, lambda j, m: (0, 0)),
                pl.BlockSpec((inner, block), lambda j, m: (0, j)),
                pl.BlockSpec((outer, gout.shape[1]), lambda j, m: (j, 0)),
                pl.BlockSpec(small.shape, lambda j, m: (0, 0)),
                through,
                through,
            ]
            + [weight(shape, ordinal) for ordinal, shape in enumerate(shapes)]
            + shards
            + shards,
            out_specs=[shards[ordinal] for ordinal in range(10) for _ in range(3)]
            + [through, through, pl.BlockSpec((1, 1), lambda j, m: (0, 0))],
        ),
        out_shape=[
            jax.ShapeDtypeStruct(shapes[ordinal], jnp.float32)
            for ordinal in range(10)
            for _ in range(3)
        ]
        + [jax.ShapeDtypeStruct(array.shape, array.dtype) for array in passed]
        + [jax.ShapeDtypeStruct((1, 1), jnp.float32)],
        compiler_params=pltpu.CompilerParams(vmem_limit_bytes=63 * 2**20),
        name="update",
    )(member, norm_tile, gin, gout, small, *passed, *weights, *moments, *averages)
    return outs[30:], [
        out.reshape(-1) if index // 3 in flat else out.T if index // 3 == 4 else out
        for index, out in enumerate(outs[:30])
    ]


def local(
    tokens,
    cotangent,
    doc_lengths,
    norm_gain,
    in_proj,
    conv_weight,
    conv_bias,
    x_proj,
    dt_proj,
    dt_bias,
    a_log,
    d_skip,
    out_proj,
    moment_norm_gain,
    moment_in_proj,
    moment_conv_weight,
    moment_conv_bias,
    moment_x_proj,
    moment_dt_proj,
    moment_dt_bias,
    moment_a_log,
    moment_d_skip,
    moment_out_proj,
    average_norm_gain,
    average_in_proj,
    average_conv_weight,
    average_conv_bias,
    average_x_proj,
    average_dt_proj,
    average_dt_bias,
    average_a_log,
    average_d_skip,
    average_out_proj,
):
    devices = lax.axis_size("seq")
    member_id = lax.axis_index("seq")
    channels = E // devices
    begin = member_id * channels
    stream = tokens[0].astype(jnp.float32)
    steps = stream.shape[0]
    length = steps * devices
    cot_low = cotangent[0]
    nrows = lax.axis_size("rows")
    direct = devices == 2 * nrows and nrows == 4 and E == nrows * 4 * LANES
    member_word = jnp.reshape(member_id, (1,)).astype(jnp.int32)
    moments = (
        moment_norm_gain,
        moment_in_proj,
        moment_conv_weight,
        moment_conv_bias,
        moment_x_proj,
        moment_dt_proj,
        moment_dt_bias,
        moment_a_log,
        moment_d_skip,
        moment_out_proj,
    )
    averages = (
        average_norm_gain,
        average_in_proj,
        average_conv_weight,
        average_conv_bias,
        average_x_proj,
        average_dt_proj,
        average_dt_bias,
        average_a_log,
        average_d_skip,
        average_out_proj,
    )
    if direct:
        weights = (
            norm_gain,
            in_proj,
            conv_weight,
            conv_bias,
            x_proj,
            dt_proj,
            dt_bias,
            a_log,
            d_skip,
            out_proj,
        )
        block_output, input_grad, gin_share, gout_share, small, norm_tile = block_of(
            (
                doc_lengths,
                tokens[0],
                cot_low,
                norm_gain[None],
                in_proj,
                out_proj,
                conv_weight,
                conv_bias[None],
                x_proj.T,
                dt_proj,
                dt_bias[None],
                a_log,
                d_skip[None],
            ),
            nrows,
            devices,
        )
        (block_output, input_grad, grad_norm), updated = update_of(
            member_word,
            norm_tile,
            gin_share,
            gout_share,
            small,
            (block_output, input_grad),
            weights,
            moments,
            averages,
        )
        return (block_output[None], input_grad[None], grad_norm.reshape(()), *updated)
    inverse = lax.rsqrt(jnp.mean(stream * stream, axis=1, keepdims=True) + EPS)
    rates = -jnp.exp(a_log)
    scaled_rates = rates * (1.0 / math.log(2.0))
    lengths = doc_lengths[0]
    starts = (jnp.cumsum(lengths) - lengths).astype(jnp.int32)
    (
        normed,
        inner_low,
        gates_low,
        back_gated,
        pre_act,
        delta_pre,
        ddec,
        drive,
        grady_rows,
        rank_low,
        inb,
        outb,
        everyone,
        all_sums,
    ) = front_of(
        starts,
        tokens[0],
        cot_low,
        norm_gain[None],
        in_proj,
        out_proj,
        conv_weight,
        conv_bias[None],
        x_proj.T,
        dt_proj,
        dt_bias[None],
        scaled_rates,
        devices,
        1,
    )
    cot_all = lax.all_gather(cot_low, "seq", axis=0, tiled=True)
    normed_all = lax.all_gather(normed[0], "seq", axis=0, tiled=True)
    positions = member_id * steps + jnp.arange(-8, steps + 8, dtype=jnp.int32)
    docid, starting = doc_tables(doc_lengths[0], positions)
    masks = []
    for offset in range(K):
        linked = (docid[8:] == docid[8 - offset : steps + 16 - offset]) & (
            positions[8 - offset : steps + 16 - offset] >= 0
        )
        masks.append((linked & (positions[8:] < length)).astype(jnp.float32)[:, None])

    def flat(values):
        return jnp.transpose(values, (1, 0, 2)).reshape(steps, E)

    pre_act, delta_pre = flat(pre_act), flat(delta_pre)
    padded = inner_low[8:].astype(jnp.float32)
    gates = gates_low.astype(jnp.float32)
    act = silu(pre_act)
    act_low = act.astype(jnp.bfloat16)
    delta = jax.nn.softplus(delta_pre)
    silu_gate = silu(gates)
    chan_back = back_gated.astype(jnp.float32)
    grad_y = chan_back * silu_gate
    scanned, along_in, pulled_sum, gin, gout, grad_rates = scan_of(
        member_word, ddec, drive, grady_rows, inb, outb, scaled_rates, everyone, all_sums, 512
    )
    scanned, along_in, pulled_sum = flat(scanned), flat(along_in), flat(pulled_sum)
    y_full = scanned + d_skip[None, :] * act
    gated = (y_full * silu_gate).astype(jnp.bfloat16)
    block_output = (
        stream + jnp.dot(gated, out_proj, preferred_element_type=jnp.float32)
    )[None]
    grad_gates = chan_back * y_full * silu_slope(gates)
    grad_dskip = jnp.sum(grad_y * act, axis=0)
    grad_in_mat = jnp.sum(gin, axis=2)
    grad_out_mat = jnp.sum(gout, axis=2)
    grad_delta = along_in * act + pulled_sum * math.log(2.0)
    grad_alog = grad_rates * rates
    grad_pre = (grad_delta * jax.nn.sigmoid(delta_pre)).astype(jnp.bfloat16)
    grad_dtbias = jnp.sum(grad_pre.astype(jnp.float32), axis=0)
    grad_dtproj = lax.dot_general(
        rank_low, grad_pre, (((0,), (0,)), ((), ())), preferred_element_type=jnp.float32
    )
    rank_back = lax.dot_general(
        grad_pre, dt_proj, (((1,), (1,)), ((), ())), preferred_element_type=jnp.float32
    )
    proj_back = jnp.concatenate([rank_back, grad_in_mat, grad_out_mat], axis=1).astype(jnp.bfloat16)
    grad_xproj = lax.dot_general(
        act_low, proj_back, (((0,), (0,)), ((), ())), preferred_element_type=jnp.float32
    )
    grad_act = (
        grad_y * d_skip[None, :]
        + along_in * delta
        + lax.dot_general(
            proj_back, x_proj, (((1,), (1,)), ((), ())), preferred_element_type=jnp.float32
        )
    )
    grad_pre_act = grad_act * silu_slope(pre_act)
    ahead = lax.ppermute(
        grad_pre_act[:8], "seq", [(i + 1, i) for i in range(devices - 1)]
    )
    extended = jnp.concatenate([grad_pre_act, ahead], axis=0)
    grad_conv_bias = jnp.sum(grad_pre_act, axis=0)
    grad_inner = jnp.zeros_like(gates)
    conv_rows = []
    for offset in range(K):
        masked = extended * masks[offset]
        conv_rows.append(
            jnp.sum(masked[:steps] * padded[8 - offset : 8 - offset + steps], axis=0)
        )
        grad_inner = grad_inner + conv_weight[offset][None, :] * masked[offset : offset + steps]
    grad_convw = jnp.stack(conv_rows)
    back_xz = jnp.stack([grad_inner, grad_gates]).astype(jnp.bfloat16)
    grad_normed = lax.dot_general(
        back_xz[0], in_proj[:, :E], (((1,), (1,)), ((), ())), preferred_element_type=jnp.float32
    ) + lax.dot_general(
        back_xz[1], in_proj[:, E:], (((1,), (1,)), ((), ())), preferred_element_type=jnp.float32
    )
    grad_gain = jnp.sum(grad_normed * stream * inverse, axis=0)
    scaled = grad_normed * norm_gain[None, :]
    input_grad = (
        cot_low.astype(jnp.float32)
        + inverse * scaled
        - stream * inverse * inverse * inverse * jnp.mean(scaled * stream, axis=1, keepdims=True)
    )
    small = jnp.concatenate(
        [
            grad_dtproj,
            grad_xproj.T,
            grad_alog,
            grad_convw,
            grad_conv_bias[None],
            grad_dtbias[None],
            grad_dskip[None],
            jnp.pad(
                grad_gain.reshape(devices, D // devices),
                ((0, 0), (0, channels - D // devices)),
            ).reshape(1, E),
            jnp.zeros((PACKED_ROWS - sum(PACKED), E), jnp.float32),
        ],
        axis=0,
    )
    gated_mine = lax.all_to_all(gated, "seq", split_axis=1, concat_axis=0, tiled=True)
    back_mine = lax.all_to_all(back_xz, "seq", split_axis=2, concat_axis=1, tiled=True)
    gout_share = lax.psum(
        lax.dot_general(
            gated_mine, cot_all, (((0,), (0,)), ((), ())), preferred_element_type=jnp.float32
        ),
        "rows",
    )
    gin_share = lax.psum(
        jnp.einsum("td,ktc->dkc", normed_all, back_mine, preferred_element_type=jnp.float32),
        "rows",
    )
    gin_share = lax.all_to_all(
        gin_share, "seq", split_axis=0, concat_axis=2, tiled=True
    ).reshape(D // devices, 2 * E)
    small = lax.psum(small, "rows")
    small = lax.psum_scatter(small, "seq", scatter_dimension=1, tiled=True)
    squares = jnp.sum(gin_share * gin_share) + jnp.sum(gout_share * gout_share)
    grad_norm = jnp.sqrt(lax.psum(squares + jnp.sum(small * small), "seq"))
    results = [block_output, input_grad[None], grad_norm]
    parts = [small[low:high] for low, high in packed_rows()]
    owner_grads = (
        parts[7][0, : D // devices],
        gin_share.astype(jnp.float32),
        parts[3],
        parts[4][0],
        parts[1].T,
        parts[0],
        parts[5][0],
        parts[2],
        parts[6][0],
        gout_share.astype(jnp.float32),
    )
    conv_mine = lax.dynamic_slice_in_dim(conv_weight, begin, channels, 1)
    cbias_mine = lax.dynamic_slice_in_dim(conv_bias, begin, channels, 0)
    xproj_mine = lax.dynamic_slice_in_dim(x_proj, begin, channels, 0)
    dtproj_mine = lax.dynamic_slice_in_dim(dt_proj, begin, channels, 1)
    dtbias_mine = lax.dynamic_slice_in_dim(dt_bias, begin, channels, 0)
    alog_mine = lax.dynamic_slice_in_dim(a_log, begin, channels, 1)
    dskip_mine = lax.dynamic_slice_in_dim(d_skip, begin, channels, 0)
    shrink_by = 1.0 / jnp.maximum(grad_norm, 1.0)
    gain_rows = D // devices
    outer_rows = E // devices
    mine_weights = (
        lax.dynamic_slice_in_dim(norm_gain, member_id * gain_rows, gain_rows, 0),
        lax.dynamic_slice_in_dim(in_proj, member_id * gain_rows, gain_rows, 0).astype(jnp.float32),
        conv_mine,
        cbias_mine,
        xproj_mine.astype(jnp.float32),
        dtproj_mine.astype(jnp.float32),
        dtbias_mine,
        alog_mine,
        dskip_mine,
        lax.dynamic_slice_in_dim(out_proj, member_id * outer_rows, outer_rows, 0).astype(
            jnp.float32
        ),
    )
    for ordinal in range(10):
        clipped = owner_grads[ordinal] * shrink_by
        momentum_new = MOMENTUM * moments[ordinal] + clipped
        renewed = mine_weights[ordinal] - RATES[ordinal] * math.sqrt(PARAMS) * (
            clipped + MOMENTUM * momentum_new
        )
        results += [momentum_new, renewed, AVERAGE * averages[ordinal] + (1.0 - AVERAGE) * renewed]
    return tuple(results)


def solution(mesh):
    return jax.shard_map(
        local,
        mesh=mesh,
        in_specs=(
            P("rows", "seq", None),
            P("rows", "seq", None),
            P("rows", None),
            P(),
            P(),
            P(),
            P(),
            P(),
            P(),
            P(),
            P(),
            P(),
            P(),
            P("seq"),
            P("seq", None),
            P(None, "seq"),
            P("seq"),
            P("seq", None),
            P(None, "seq"),
            P("seq"),
            P(None, "seq"),
            P("seq"),
            P("seq", None),
            P("seq"),
            P("seq", None),
            P(None, "seq"),
            P("seq"),
            P("seq", None),
            P(None, "seq"),
            P("seq"),
            P(None, "seq"),
            P("seq"),
            P("seq", None),
        ),
        out_specs=(
            P("rows", "seq", None),
            P("rows", "seq", None),
            P(),
            P("seq"),
            P("seq"),
            P("seq"),
            P("seq", None),
            P("seq", None),
            P("seq", None),
            P(None, "seq"),
            P(None, "seq"),
            P(None, "seq"),
            P("seq"),
            P("seq"),
            P("seq"),
            P("seq", None),
            P("seq", None),
            P("seq", None),
            P(None, "seq"),
            P(None, "seq"),
            P(None, "seq"),
            P("seq"),
            P("seq"),
            P("seq"),
            P(None, "seq"),
            P(None, "seq"),
            P(None, "seq"),
            P("seq"),
            P("seq"),
            P("seq"),
            P("seq", None),
            P("seq", None),
            P("seq", None),
        ),
        check_vma=False,
    )
```

```python
import functools
import math

import jax
import jax.numpy as jnp
from jax import lax
from jax.experimental import pallas as pl
from jax.experimental.pallas import tpu as pltpu
from jax.sharding import PartitionSpec as P

D = 1024
E = 2048
N = 16
R = 64
K = 4
PARAMS = 6667264

LANES = 128
RESET = 1e30
MESH = pl.DeviceIdType.MESH


EPS = 1e-05
MOMENTUM = 0.9
AVERAGE = 0.9
RATES = (0.1, 0.03, 0.1, 0.1, 0.03, 0.03, 0.3, 0.3, 0.1, 0.03)


def silu(values):
    return values * jax.nn.sigmoid(values)


def silu_slope(values):
    sigmoid_of = jax.nn.sigmoid(values)
    return sigmoid_of * (1.0 + values * (1.0 - sigmoid_of))


def doc_tables(lengths_row, positions):
    ends = jnp.cumsum(lengths_row)
    starts = ends - lengths_row
    docid = jnp.sum((positions[None, :] >= starts[:, None]).astype(jnp.int32), axis=0)
    first = jnp.sum((positions[None, :] == starts[:, None]).astype(jnp.int32), axis=0)
    return (docid, first > 0)


def scan_kernel(
    member_ref,
    ddec_ref,
    drive_ref,
    grady_ref,
    inb_ref,
    outb_ref,
    rates_ref,
    all_ref,
    sums_ref,
    scanned_ref,
    along_ref,
    decayed_ref,
    gin_ref,
    gout_ref,
    grates_ref,
    kept,
    first,
    second,
):
    groups, steps = ddec_ref.shape[:2]
    devices = all_ref.shape[0]
    base = pl.program_id(0) * groups
    member = member_ref[0]
    columns = [pl.ds(group * LANES, LANES) for group in range(groups)]
    half = N // 2

    @pl.when(pl.program_id(0) == 0)
    def _():
        gin_ref[...] = jnp.zeros_like(gin_ref)
        gout_ref[...] = jnp.zeros_like(gout_ref)

    def through(device, states):
        new = []
        for group in range(groups):
            total = sums_ref[device, pl.ds(base + group, 1), :]
            factor = jnp.exp2(total * rates_ref[:, columns[group]])
            new.append(
                factor * states[group]
                + all_ref[device, 0, :, columns[group]].astype(jnp.float32)
            )
        return new

    zeros = [jnp.zeros((N, LANES), jnp.float32) for _ in range(groups)]
    reach = devices // 2
    entering = lax.fori_loop(jnp.maximum(member - reach, 0), member, through, zeros)
    last = jnp.minimum(member + reach, devices - 1)
    leaving = lax.fori_loop(0, last - member, lambda d, s: through(last - d, s), zeros)

    def fold(values):
        return values[:half] + values[half:]

    def forward(t, hidden):
        in_row, out_row = inb_ref[t], outb_ref[t]
        new = []
        for group in range(groups):
            here = (group, pl.ds(t, 1))
            decay = jnp.exp2(ddec_ref[here] * rates_ref[:, columns[group]])
            state = decay * hidden[group] + drive_ref[here] * in_row
            kept[t + 1, :, columns[group]] = state
            first[group, pl.ds(pl.multiple_of(t * half, half), half), :] = fold(state * out_row)
            new.append(state)
        return new

    for group in range(groups):
        kept[0, :, columns[group]] = entering[group]
    lax.fori_loop(0, steps, forward, entering, unroll=4)

    def collapse(source, target_ref):
        for group in range(groups):
            total = source[group, pl.ds(0, steps, stride=half), :]
            for place in range(1, half):
                total = total + source[group, pl.ds(place, steps, stride=half), :]
            target_ref[group] = total

    collapse(first, scanned_ref)

    def backward(back, carry):
        later, grates = carry
        t = steps - 1 - back
        in_row, out_row = inb_ref[t], outb_ref[t]
        gin, gout = gin_ref[t], gout_ref[t]
        new = ([], [])
        rows = pl.ds(pl.multiple_of(t * half, half), half)
        for group in range(groups):
            here = (group, pl.ds(t, 1))
            grady = grady_ref[here]
            delta = ddec_ref[here]
            rates = rates_ref[:, columns[group]]
            adjoint = grady * out_row + later[group]
            gout = gout + grady * kept[t + 1, :, columns[group]]
            gin = gin + adjoint * drive_ref[here]
            first[group, rows, :] = fold(adjoint * in_row)
            passed = jnp.exp2(delta * rates) * adjoint
            pulled = passed * kept[t, :, columns[group]]
            second[group, rows, :] = fold(pulled * rates)
            new[0].append(passed)
            new[1].append(grates[group] + pulled * delta)
        gin_ref[t] = gin
        gout_ref[t] = gout
        return new

    _, grates = lax.fori_loop(0, steps, backward, (leaving, zeros), unroll=4)
    collapse(first, along_ref)
    collapse(second, decayed_ref)
    for group in range(groups):
        grates_ref[:, columns[group]] = grates[group]


def scan_of(member, ddec, drive, grady, inb, outb, rates, everyone, sums, block):
    steps = ddec.shape[1]
    devices = everyone.shape[0]
    groups = block // LANES
    wide = pl.BlockSpec((block // LANES, steps, LANES), lambda b: (b, 0, 0))
    whole = pl.BlockSpec((steps, N, LANES), lambda b: (0, 0, 0))
    narrow = pl.BlockSpec((N, block), lambda b: (0, b))
    full = jax.ShapeDtypeStruct((E // LANES, steps, LANES), jnp.float32)
    spread = jax.ShapeDtypeStruct((steps, N, LANES), jnp.float32)
    return pl.pallas_call(
        scan_kernel,
        grid=(E // block,),
        in_specs=[
            pl.BlockSpec(memory_space=pltpu.SMEM),
            wide,
            wide,
            wide,
            whole,
            whole,
            narrow,
            pl.BlockSpec((devices, 1, N, block), lambda b: (0, b, 0, 0)),
            pl.BlockSpec(sums.shape, lambda b: (0, 0, 0)),
        ],
        out_specs=[wide, wide, wide, whole, whole, narrow],
        out_shape=[full, full, full, spread, spread, jax.ShapeDtypeStruct((N, E), jnp.float32)],
        scratch_shapes=[
            pltpu.VMEM((steps + 1, N, block), jnp.float32),
            pltpu.VMEM((groups, steps * N // 2, LANES), jnp.float32),
            pltpu.VMEM((groups, steps * N // 2, LANES), jnp.float32),
        ],
        compiler_params=pltpu.CompilerParams(vmem_limit_bytes=48 * 2**20),
        name="scan",
    )(member, ddec, drive, grady, inb, outb, rates, everyone, sums)


def partner(axis, offset):
    size = lax.axis_size(axis)
    return lax.rem(lax.axis_index(axis) + offset, size)


def greet(counts):
    barrier = pltpu.get_barrier_semaphore()
    total = 0
    for axis, count in counts:
        for offset in range(1, count):
            pl.semaphore_signal(
                barrier, inc=1, device_id={axis: partner(axis, offset)}, device_id_type=MESH
            )
        total += count - 1
    pl.semaphore_wait(barrier, total)


def push(source, target, semaphores, at, axis, offset):
    copy = pltpu.make_async_remote_copy(
        src_ref=source,
        dst_ref=target,
        send_sem=semaphores.at[0, at],
        recv_sem=semaphores.at[1, at],
        device_id={axis: partner(axis, offset)},
        device_id_type=MESH,
    )
    copy.start()
    return copy


def span(index, size):
    return pl.ds(index * size, size)


def softplus(values):
    return jnp.maximum(values, 0.0) + jnp.log1p(jnp.exp(-jnp.abs(values)))


def front_kernel(
    devices,
    nrows,
    starts_ref,
    tokens_ref,
    cot_ref,
    gain_ref,
    in_proj_ref,
    out_proj_ref,
    conv_ref,
    cbias_ref,
    x_proj_ref,
    dt_proj_ref,
    dtbias_ref,
    rates_ref,
    normed_ref,
    inner_ref,
    gates_ref,
    back_ref,
    pre_act_ref,
    delta_pre_ref,
    ddec_ref,
    drive_ref,
    grady_ref,
    rank_ref,
    inb_ref,
    outb_ref,
    ends_out,
    sums_out,
    in_proj_buf,
    out_proj_buf,
    padded,
    docid,
    masks,
    proj,
    ends,
    loads,
    halo_wires,
    wires,
    sum_wires,
    row_wires,
):
    member = lax.axis_index("seq")
    own = lax.axis_index("rows") if nrows > 1 else 0
    steps = tokens_ref.shape[0]
    groups = E // LANES
    chunk = 4 * LANES
    chunks = E // chunk
    reach = devices // 2
    halo = inner_ref.shape[0] - steps
    in_loads = [
        pltpu.make_async_copy(
            in_proj_ref.at[:, span(at, chunk)], in_proj_buf.at[at], loads.at[at]
        )
        for at in range(2 * chunks)
    ]
    out_loads = [
        pltpu.make_async_copy(
            out_proj_ref.at[span(at, chunk), :], out_proj_buf.at[at], loads.at[2 * chunks + at]
        )
        for at in range(chunks)
    ]
    for load in in_loads + out_loads:
        load.start()
    barrier = pltpu.get_barrier_semaphore()
    for axis, count in (("seq", devices), ("rows", nrows)):
        for offset in range(1, count):
            pl.semaphore_signal(
                barrier, inc=1, device_id={axis: partner(axis, offset)}, device_id_type=MESH
            )

    stream = tokens_ref[...].astype(jnp.float32)
    inverse = lax.rsqrt(jnp.mean(stream * stream, axis=1, keepdims=True) + EPS)
    normed_ref[own] = (stream * inverse * gain_ref[...]).astype(jnp.bfloat16)

    places = member * steps - 8 + lax.broadcasted_iota(jnp.int32, docid.shape, 0)
    count = jnp.zeros(docid.shape, jnp.int32)
    first = jnp.zeros(docid.shape, jnp.float32)
    for index in range(starts_ref.shape[0]):
        count = count + jnp.where(places >= starts_ref[index], 1, 0)
        first = jnp.where(places == starts_ref[index], 1.0, first)
    docid[...] = count
    masks[0] = first[8 : 8 + steps]
    for offset in range(1, K):
        masks[offset] = jnp.where(
            docid[8 - offset : 8 - offset + steps, :] == docid[8 : 8 + steps, :], 1.0, 0.0
        )

    def project(at):
        in_loads[at].wait()
        return jnp.dot(
            normed_ref[own], in_proj_buf[at], preferred_element_type=jnp.float32
        ).astype(jnp.bfloat16)

    for at in range(chunks):
        inner_ref[halo:, span(at, chunk)] = project(at)
    pl.semaphore_wait(barrier, devices + nrows - 2)
    halo_copy = pltpu.make_async_remote_copy(
        src_ref=inner_ref.at[steps : steps + halo, :],
        dst_ref=inner_ref.at[0:halo, :],
        send_sem=halo_wires.at[0],
        recv_sem=halo_wires.at[1],
        device_id={"seq": partner("seq", 1)},
        device_id_type=MESH,
    )

    @pl.when(member < devices - 1)
    def _():
        halo_copy.start()

    row_copies = [
        push(normed_ref.at[own], normed_ref.at[own], row_wires, offset - 1, "rows", offset)
        for offset in range(1, nrows)
    ]

    @pl.when(member == 0)
    def _():
        inner_ref[0:halo, :] = jnp.zeros((halo, E), jnp.bfloat16)

    for at in range(chunks):
        gates_ref[:, span(at, chunk)] = project(chunks + at)
    for at in range(chunks):
        out_loads[at].wait()
        back_ref[:, span(at, chunk)] = lax.dot_general(
            cot_ref[...],
            out_proj_buf[at],
            (((1,), (1,)), ((), ())),
            preferred_element_type=jnp.float32,
        ).astype(jnp.bfloat16)

    @pl.when(member < devices - 1)
    def _():
        halo_copy.wait_send()

    @pl.when(member > 0)
    def _():
        halo_copy.wait_recv()

    proj[...] = jnp.zeros_like(proj)
    for at in range(chunks):
        lows = []
        for group in range(4 * at, 4 * at + 4):
            columns = span(group, LANES)
            padded[...] = inner_ref[halo - 8 :, columns].astype(jnp.float32)
            value = cbias_ref[:, columns] + conv_ref[0:1, columns] * padded[8:, :]
            for offset in range(1, K):
                value = (
                    value
                    + conv_ref[offset : offset + 1, columns]
                    * padded[8 - offset : 8 - offset + steps, :]
                    * masks[offset]
                )
            pre_act_ref[group] = value
            act = silu(value)
            drive_ref[group] = act
            lows.append(act.astype(jnp.bfloat16))
        proj[...] += lax.dot_general(
            jnp.concatenate(lows, axis=1),
            x_proj_ref[:, span(at, chunk)],
            (((1,), (1,)), ((), ())),
            preferred_element_type=jnp.float32,
        )
    rank_ref[...] = proj[:, :R].astype(jnp.bfloat16)
    inb_ref[...] = jnp.broadcast_to(proj[:, R : R + N][:, :, None], inb_ref.shape)
    outb_ref[...] = jnp.broadcast_to(proj[:, R + N :][:, :, None], outb_ref.shape)

    def later(distance, at):
        return pltpu.make_async_remote_copy(
            src_ref=ends.at[0, at],
            dst_ref=ends_out.at[member, at],
            send_sem=wires.at[0, 0, at, distance - 1],
            recv_sem=wires.at[0, 1, at, distance - 1],
            device_id={"seq": partner("seq", distance)},
            device_id_type=MESH,
        )

    def earlier(distance, at):
        return pltpu.make_async_remote_copy(
            src_ref=ends.at[1, at],
            dst_ref=ends_out.at[member, at],
            send_sem=wires.at[1, 0, at, distance - 1],
            recv_sem=wires.at[1, 1, at, distance - 1],
            device_id={"seq": partner("seq", devices - distance)},
            device_id_type=MESH,
        )

    def sums_to(distance, side):
        offset = distance if side == 0 else devices - distance
        return pltpu.make_async_remote_copy(
            src_ref=sums_out.at[member],
            dst_ref=sums_out.at[member],
            send_sem=sum_wires.at[side, 0, distance - 1],
            recv_sem=sum_wires.at[side, 1, distance - 1],
            device_id={"seq": partner("seq", offset)},
            device_id_type=MESH,
        )

    for at in range(chunks):
        delta_pre = (
            jnp.dot(
                rank_ref[...], dt_proj_ref[:, span(at, chunk)], preferred_element_type=jnp.float32
            )
            + dtbias_ref[:, span(at, chunk)]
        )
        for place in range(4):
            group = 4 * at + place
            columns = span(group, LANES)
            here = delta_pre[:, place * LANES : (place + 1) * LANES]
            delta = softplus(here)
            delta_pre_ref[group] = here
            drive_ref[group] = drive_ref[group] * delta
            ddec = jnp.where(masks[0] > 0.0, RESET, delta)
            ddec_ref[group] = ddec
            sums_out[member, group : group + 1, :] = jnp.sum(ddec, axis=0, keepdims=True)
            grady_ref[group] = back_ref[:, columns].astype(jnp.float32) * silu(
                gates_ref[:, columns].astype(jnp.float32)
            )

        def step(t, carry):
            hidden, decayed, pulled = carry
            in_row, out_row = inb_ref[t], outb_ref[t]
            new = ([], [], [])
            for place in range(4):
                here = (4 * at + place, pl.ds(t, 1))
                decay = jnp.exp2(ddec_ref[here] * rates_ref[:, span(4 * at + place, LANES)])
                new[0].append(decay * hidden[place] + drive_ref[here] * in_row)
                product = decay * decayed[place]
                new[1].append(product)
                new[2].append(pulled[place] + product * (grady_ref[here] * out_row))
            return new

        zeros = [jnp.zeros((N, LANES), jnp.float32) for _ in range(4)]
        ones = [jnp.ones((N, LANES), jnp.float32) for _ in range(4)]
        hidden, _, pulled = lax.fori_loop(0, steps, step, (zeros, ones, zeros), unroll=4)
        ends[0, at] = jnp.concatenate(hidden, axis=1).astype(jnp.bfloat16)
        ends[1, at] = jnp.concatenate(pulled, axis=1).astype(jnp.bfloat16)
        for distance in range(1, reach + 1):

            @pl.when(member + distance < devices)
            def _():
                later(distance, at).start()

            @pl.when(member >= distance)
            def _():
                earlier(distance, at).start()

    for distance in range(1, reach + 1):

        @pl.when(member + distance < devices)
        def _():
            sums_to(distance, 0).start()

        @pl.when(member >= distance)
        def _():
            sums_to(distance, 1).start()

    for distance in range(1, reach + 1):

        @pl.when(member + distance < devices)
        def _():
            for at in range(chunks):
                later(distance, at).wait_send()
                earlier(distance, at).wait_recv()
            sums_to(distance, 0).wait_send()
            sums_to(distance, 1).wait_recv()

        @pl.when(member >= distance)
        def _():
            for at in range(chunks):
                earlier(distance, at).wait_send()
                later(distance, at).wait_recv()
            sums_to(distance, 1).wait_send()
            sums_to(distance, 0).wait_recv()
    for copy in row_copies:
        copy.wait()


def front_of(starts, tokens, cot, gain, in_proj, out_proj, conv, cbias, x_proj, dt_proj, dtbias, rates, devices, nrows):
    steps = tokens.shape[0]
    groups = E // LANES
    chunk = 4 * LANES
    chunks = E // chunk
    reach = devices // 2
    halo = 16
    low = jnp.bfloat16
    vmem = pl.BlockSpec(memory_space=pltpu.VMEM)
    grouped = jax.ShapeDtypeStruct((groups, steps, LANES), jnp.float32)
    spread = jax.ShapeDtypeStruct((steps, N, LANES), jnp.float32)
    return pl.pallas_call(
        functools.partial(front_kernel, devices, nrows),
        in_specs=[pl.BlockSpec(memory_space=pltpu.SMEM)]
        + [vmem] * 3
        + [pl.BlockSpec(memory_space=pl.ANY)] * 2
        + [vmem] * 6,
        out_specs=[vmem] * 14,
        out_shape=[
            jax.ShapeDtypeStruct((nrows, steps, D), low),
            jax.ShapeDtypeStruct((steps + halo, E), low),
            jax.ShapeDtypeStruct((steps, E), low),
            jax.ShapeDtypeStruct((steps, E), low),
            grouped,
            grouped,
            grouped,
            grouped,
            grouped,
            jax.ShapeDtypeStruct((steps, R), low),
            spread,
            spread,
            jax.ShapeDtypeStruct((devices, chunks, N, chunk), low),
            jax.ShapeDtypeStruct((devices, groups, LANES), jnp.float32),
        ],
        scratch_shapes=[
            pltpu.VMEM((2 * chunks, D, chunk), low),
            pltpu.VMEM((chunks, chunk, D), low),
            pltpu.VMEM((steps + 8, LANES), jnp.float32),
            pltpu.VMEM((steps + 16, LANES), jnp.int32),
            pltpu.VMEM((K, steps, LANES), jnp.float32),
            pltpu.VMEM((steps, R + 2 * N), jnp.float32),
            pltpu.VMEM((2, chunks, N, chunk), low),
            pltpu.SemaphoreType.DMA((3 * chunks,)),
            pltpu.SemaphoreType.DMA((2,)),
            pltpu.SemaphoreType.DMA((2, 2, chunks, reach)),
            pltpu.SemaphoreType.DMA((2, 2, reach)),
            pltpu.SemaphoreType.DMA((2, max(nrows - 1, 1))),
        ],
        compiler_params=pltpu.CompilerParams(
            collective_id=0, has_side_effects=True, vmem_limit_bytes=60 * 2**20
        ),
        name="front",
    )(starts, tokens, cot, gain, in_proj, out_proj, conv, cbias, x_proj, dt_proj, dtbias, rates)


PACKED = (R, R + 2 * N, N, K, 1, 1, 1, 1)
PACKED_ROWS = 192


def packed_rows():
    spans = []
    at = 0
    for count in PACKED:
        spans.append((at, at + count))
        at += count
    return spans


def silu_pair(values):
    sigmoid_of = jax.nn.sigmoid(values)
    return values * sigmoid_of, sigmoid_of * (1.0 + values * (1.0 - sigmoid_of))


def block_kernel(
    nrows,
    devices,
    lengths_ref,
    tokens_ref,
    cot_ref,
    gain_ref,
    in_proj_ref,
    out_proj_ref,
    conv_ref,
    cbias_ref,
    x_proj_ref,
    dt_proj_ref,
    dtbias_ref,
    alog_ref,
    dskip_ref,
    output_ref,
    grad_ref,
    gin_out,
    gout_out,
    small_out,
    norm_out,
    in_proj_buf,
    out_proj_buf,
    rates_ref,
    normed_rows,
    normed_sib,
    cot_half,
    cot_sib,
    inner,
    gates,
    back,
    pre_act,
    delta_pre,
    ddec,
    drive,
    grady,
    proj,
    rank_low,
    inb,
    outb,
    ends,
    ends_all,
    sums_all,
    docid,
    masks,
    padded,
    kept,
    first,
    second,
    gin,
    gout,
    gated,
    back_gates,
    back_inner,
    grad_conv,
    rank_back,
    proj_back,
    gated_got,
    back_got,
    gout_sum,
    gout_low,
    gout_got,
    gin_sum,
    gin_low,
    gin_got,
    gin_pub,
    small,
    small_low,
    small_got,
    small_part,
    small_seq,
    norm_part,
    norm_all,
    loads,
    halo_wires,
    state_wires,
    sum_wires,
    gather_wires,
    sib_wires,
    gated_wires,
    back_wires,
    gout_wires,
    line_wires,
    plane_wires,
    row_wires,
    seq_wires,
    norm_wires,
    local,
):
    row = lax.axis_index("rows")
    member = lax.axis_index("seq")
    level, side = member // 2, lax.rem(member, 2)
    levels = devices // 2
    steps = tokens_ref.shape[0]
    groups = E // LANES
    chunk = 4 * LANES
    chunks = E // chunk
    shard = E // devices
    halo = inner.shape[0] - steps
    reach = devices // 2
    half = N // 2
    low = jnp.bfloat16
    wide = jnp.float32
    spans = packed_rows()
    everyone = nrows * devices

    in_loads = [
        pltpu.make_async_copy(
            in_proj_ref.at[:, span(at, chunk)], in_proj_buf.at[at], loads.at[at]
        )
        for at in range(2 * chunks)
    ]
    out_load = pltpu.make_async_copy(out_proj_ref, out_proj_buf, loads.at[2 * chunks])
    for load in in_loads + [out_load]:
        load.start()

    def share(index, size):
        return pl.ds(pl.multiple_of(index * size, size), size)

    def plane(turn, other):
        return {
            "rows": lax.rem(row + turn, nrows),
            "seq": 2 * level + lax.rem(side + other, 2),
        }

    across = [levels - 1 - level, lax.rem(level + 2, levels), level + 1 - 2 * lax.rem(level, 2)]

    def line(turn):
        return {"seq": 2 * across[turn - 1] + side}

    def remote(source, target, send, recv, device):
        return pltpu.make_async_remote_copy(
            src_ref=source,
            dst_ref=target,
            send_sem=send,
            recv_sem=recv,
            device_id=device,
            device_id_type=MESH,
        )

    def begin(copies):
        for copy in copies:
            copy.start()
        return copies

    def settle(copies):
        for copy in copies:
            copy.wait()

    def other_device(offset):
        return {
            "rows": lax.rem(row + offset // devices, nrows),
            "seq": lax.rem(member + offset % devices, devices),
        }

    barrier = pltpu.get_barrier_semaphore()
    for offset in range(1, everyone):
        pl.semaphore_signal(
            barrier, inc=1, device_id=other_device(offset), device_id_type=MESH
        )

    def column_sum(values):
        return jnp.sum(values, axis=0, keepdims=True)

    stream = tokens_ref[...].astype(wide)
    inverse = lax.rsqrt(jnp.mean(stream * stream, axis=1, keepdims=True) + EPS)
    normed_rows[row] = (stream * inverse * gain_ref[...]).astype(low)
    cot_half[row] = cot_ref[:, share(lax.rem(row, 2), D // 2)]
    rates_ref[...] = jnp.exp(alog_ref[...]) * (-1.0 / math.log(2.0))

    places = member * steps - 8 + lax.broadcasted_iota(jnp.int32, docid.shape, 0)
    count = jnp.zeros(docid.shape, jnp.int32)
    starting = jnp.zeros(docid.shape, wide)
    start = 0
    for index in range(lengths_ref.shape[1]):
        count = count + jnp.where(places >= start, 1, 0)
        starting = jnp.where(places == start, 1.0, starting)
        start = start + lengths_ref[0, index]
    docid[...] = count
    masks[0] = starting[8:]
    for offset in range(1, K):
        masks[offset] = jnp.where(
            docid[8 - offset : 16 - offset + steps, :] == docid[8:, :], 1.0, 0.0
        )

    def project(at):
        in_loads[at].wait()
        return jnp.dot(
            normed_rows[row], in_proj_buf[at], preferred_element_type=wide
        ).astype(low)

    for at in range(chunks):
        inner[halo:, span(at, chunk)] = project(at)
    pl.semaphore_wait(barrier, everyone - 1)
    halo_copy = remote(
        inner.at[steps : steps + halo, :],
        inner.at[0:halo, :],
        halo_wires.at[0, 0],
        halo_wires.at[0, 1],
        {"seq": partner("seq", 1)},
    )

    @pl.when(member < devices - 1)
    def _():
        halo_copy.start()

    @pl.when(member == 0)
    def _():
        inner[0:halo, :] = jnp.zeros((halo, E), low)

    def gather_rows(kind, make, target):
        return begin(
            [
                remote(
                    make(partner("rows", offset)),
                    target.at[row],
                    gather_wires.at[kind, 0, offset - 1],
                    gather_wires.at[kind, 1, offset - 1],
                    {"rows": partner("rows", offset)},
                )
                for offset in range(1, nrows)
            ]
        )

    def to_sibling(kind, source, target):
        return begin(
            [
                remote(
                    source,
                    target,
                    sib_wires.at[kind, 0],
                    sib_wires.at[kind, 1],
                    {"seq": 2 * level + 1 - side},
                )
            ]
        )

    normed_moves = gather_rows(0, lambda other: normed_rows.at[row], normed_rows)
    cot_moves = gather_rows(
        1, lambda other: cot_ref.at[:, share(lax.rem(other, 2), D // 2)], cot_half
    )
    for at in range(chunks):
        gates[:, span(at, chunk)] = project(chunks + at)
    out_load.wait()
    for at in range(chunks):
        back[:, span(at, chunk)] = lax.dot_general(
            cot_ref[...],
            out_proj_buf[span(at, chunk), :],
            (((1,), (1,)), ((), ())),
            preferred_element_type=wide,
        ).astype(low)

    gin[...] = jnp.zeros_like(gin)
    gout[...] = jnp.zeros_like(gout)
    rank_back[...] = jnp.zeros_like(rank_back)
    small[...] = jnp.zeros_like(small)
    norm_part[...] = jnp.zeros_like(norm_part)
    proj[...] = jnp.zeros_like(proj)

    @pl.when(member < devices - 1)
    def _():
        halo_copy.wait_send()

    @pl.when(member > 0)
    def _():
        halo_copy.wait_recv()

    for at in range(chunks):
        lows = []
        for group in range(4 * at, 4 * at + 4):
            columns = span(group, LANES)
            padded[...] = inner[halo - 8 :, columns].astype(wide)
            value = cbias_ref[:, columns] + conv_ref[0:1, columns] * padded[8:, :]
            for offset in range(1, K):
                value = (
                    value
                    + conv_ref[offset : offset + 1, columns]
                    * padded[8 - offset : 8 - offset + steps, :]
                    * masks[offset, :steps, :]
                )
            pre_act[group] = value
            act = silu(value)
            drive[group] = act
            lows.append(act.astype(low))
        proj[...] += lax.dot_general(
            jnp.concatenate(lows, axis=1),
            x_proj_ref[:, span(at, chunk)],
            (((1,), (1,)), ((), ())),
            preferred_element_type=wide,
        )
    rank_low[...] = proj[:, :R].astype(low)
    inb[...] = jnp.broadcast_to(proj[:, R : R + N][:, :, None], inb.shape)
    outb[...] = jnp.broadcast_to(proj[:, R + N :][:, :, None], outb.shape)

    def lanes(at, place):
        return share(4 * at + place, LANES)

    def state_copy(direction, distance, at):
        offset = distance if direction == 0 else devices - distance
        return remote(
            ends.at[direction, at],
            ends_all.at[member, at],
            state_wires.at[direction, 0, at, distance - 1],
            state_wires.at[direction, 1, at, distance - 1],
            {"seq": partner("seq", offset)},
        )

    def sum_copy(direction, distance):
        offset = distance if direction == 0 else devices - distance
        return remote(
            sums_all.at[member],
            sums_all.at[member],
            sum_wires.at[direction, 0, distance - 1],
            sum_wires.at[direction, 1, distance - 1],
            {"seq": partner("seq", offset)},
        )

    def to_neighbours(make):
        for distance in range(reach, 0, -1):

            @pl.when(member + distance < devices)
            def _():
                make(0, distance).start()

            @pl.when(member >= distance)
            def _():
                make(1, distance).start()

    def from_neighbours(make):
        for distance in range(1, reach + 1):

            @pl.when(member + distance < devices)
            def _():
                make(0, distance).wait_send()
                make(1, distance).wait_recv()

            @pl.when(member >= distance)
            def _():
                make(1, distance).wait_send()
                make(0, distance).wait_recv()

    for at in range(chunks):
        pre = (
            jnp.dot(rank_low[...], dt_proj_ref[:, span(at, chunk)], preferred_element_type=wide)
            + dtbias_ref[:, span(at, chunk)]
        )
        for place in range(4):
            group = 4 * at + place
            columns = span(group, LANES)
            here = pre[:, place * LANES : (place + 1) * LANES]
            delta = softplus(here)
            delta_pre[group] = here
            drive[group] = drive[group] * delta
            decaying = jnp.where(masks[0, :steps, :] > 0.0, RESET, delta)
            ddec[group] = decaying
            sums_all[member, group : group + 1, :] = column_sum(decaying)
            grady[group] = back[:, columns].astype(wide) * silu(gates[:, columns].astype(wide))
    to_neighbours(sum_copy)
    zeros = [jnp.zeros((N, LANES), wide) for _ in range(4)]
    ones = [jnp.ones((N, LANES), wide) for _ in range(4)]
    order = [(turn, lax.rem(row + turn, nrows)) for turn in [*range(1, nrows), 0]]
    for _, at in order:

        def step(t, carry):
            hidden, decayed, pulled = carry
            in_row, out_row = inb[t], outb[t]
            new = ([], [], [])
            for place in range(4):
                here = (4 * at + place, pl.ds(t, 1))
                decay = jnp.exp2(ddec[here] * rates_ref[:, lanes(at, place)])
                new[0].append(decay * hidden[place] + drive[here] * in_row)
                product = decay * decayed[place]
                new[1].append(product)
                new[2].append(pulled[place] + product * (grady[here] * out_row))
            return new

        hidden, _, pulled = lax.fori_loop(0, steps, step, (zeros, ones, zeros), unroll=8)
        ends[0, at] = jnp.concatenate(hidden, axis=1).astype(low)
        ends[1, at] = jnp.concatenate(pulled, axis=1).astype(low)
        to_neighbours(lambda direction, distance: state_copy(direction, distance, at))
    from_neighbours(sum_copy)

    def fold(values):
        return values[:half] + values[half:]

    def collapse(source, place):
        total = source[place, pl.ds(0, steps, stride=half), :]
        for index in range(1, half):
            total = total + source[place, pl.ds(index, steps, stride=half), :]
        return total

    def trade(kind, source, at, turn):
        copies = []
        for other in range(2):
            columns = share(2 * at + lax.rem(side + other, 2), shard)
            target = back_got.at[kind, other, row]
            if turn == 0 and other == 0:
                copies.append(
                    pltpu.make_async_copy(source.at[:, columns], target, local.at[kind])
                )
            else:
                copies.append(
                    remote(
                        source.at[:, columns],
                        target,
                        back_wires.at[kind, 0, 2 * turn + other],
                        back_wires.at[kind, 1, 2 * turn + other],
                        plane(turn, other),
                    )
                )
        return begin(copies)

    def trade_gated(at):
        copies = []
        for turn in range(nrows):
            for other in range(2):
                columns = share(
                    4 * at + 2 * lax.rem(side + other, 2) + partner("rows", turn) // 2, LANES
                )
                target = gated_got.at[at, other, row]
                if turn == 0 and other == 0:
                    copies.append(
                        pltpu.make_async_copy(gated.at[:, columns], target, local.at[2 + at])
                    )
                else:
                    copies.append(
                        remote(
                            gated.at[:, columns],
                            target,
                            gated_wires.at[0, at, 2 * turn + other],
                            gated_wires.at[1, at, 2 * turn + other],
                            plane(turn, other),
                        )
                    )
        return begin(copies)

    gate_moves, gated_moves = [], []
    leavings = []
    for slot, (turn, at) in enumerate(order):
        from_neighbours(lambda direction, distance: state_copy(direction, distance, at))

        def through(device, states):
            new = []
            for place in range(4):
                total = sums_all[device, pl.ds(4 * at + place, 1), :]
                factor = jnp.exp2(total * rates_ref[:, lanes(at, place)])
                new.append(
                    factor * states[place]
                    + ends_all[device, at, :, place * LANES : (place + 1) * LANES].astype(wide)
                )
            return new

        def forward(t, hidden):
            in_row, out_row = inb[t], outb[t]
            new = []
            for place in range(4):
                here = (4 * at + place, pl.ds(t, 1))
                decay = jnp.exp2(ddec[here] * rates_ref[:, lanes(at, place)])
                state = decay * hidden[place] + drive[here] * in_row
                kept[slot, t + 1, place] = state.astype(low)
                first[place, share(t, half), :] = fold(state * out_row)
                new.append(state)
            return new

        entering = lax.fori_loop(jnp.maximum(member - reach, 0), member, through, zeros)
        last = jnp.minimum(member + reach, devices - 1)
        leavings.append(lax.fori_loop(0, last - member, lambda d, s: through(last - d, s), zeros))
        for place in range(4):
            kept[slot, 0, place] = entering[place].astype(low)
        lax.fori_loop(0, steps, forward, entering, unroll=8)
        for place in range(4):
            group, columns = 4 * at + place, lanes(at, place)
            act = silu(pre_act[group])
            y_full = collapse(first, place) + dskip_ref[:, columns] * act
            gate, slope = silu_pair(gates[:, columns].astype(wide))
            gated[:, columns] = (y_full * gate).astype(low)
            back_gates[:, columns] = (back[:, columns].astype(wide) * y_full * slope).astype(low)
            small[spans[6][0] : spans[6][1], columns] = column_sum(grady[group] * act)
        gate_moves += trade(1, back_gates, at, turn)


    def in_grads(kind):
        total = None
        for other, normed in ((0, normed_rows), (1, normed_sib)):
            part = lax.dot_general(
                normed[...].reshape(nrows * steps, D),
                back_got[kind, other].reshape(nrows * steps, shard),
                (((0,), (0,)), ((), ())),
                preferred_element_type=wide,
            )
            total = part if total is None else total + part
        gin_sum[kind] = total
        gin_low[kind] = total.astype(low)
        return begin(
            [
                remote(
                    gin_low.at[kind, share(across[turn - 1], D // levels), :],
                    gin_got.at[kind, turn - 1],
                    line_wires.at[kind, 0, turn - 1],
                    line_wires.at[kind, 1, turn - 1],
                    line(turn),
                )
                for turn in range(1, levels)
            ]
        )

    def squares(values):
        return jnp.sum(jnp.sum(values * values, axis=0, keepdims=True), axis=1, keepdims=True)

    def in_share(kind, before=None):
        total = gin_sum[kind, share(level, D // levels), :]
        for turn in range(levels - 1):
            total = total + gin_got[kind, turn].astype(wide)
        gin_pub[kind] = total.astype(low)
        owned = D // devices
        columns = share(kind * devices + 2 * row + side, shard)
        gin_out[:, columns] = gin_pub[kind, share(side, owned), :]
        norm_part[...] += squares(total)
        copies = [] if before is None else before()
        copies += begin(
            [
                remote(
                    gin_pub.at[kind, share(lax.rem(side + other, 2), owned), :],
                    gin_out.at[:, columns],
                    plane_wires.at[kind, 0, 2 * turn + other],
                    plane_wires.at[kind, 1, 2 * turn + other],
                    plane(turn, other),
                )
                for turn in range(nrows)
                for other in range(2)
                if turn + other > 0
            ]
        )
        return copies

    def gout_copy(turn):
        return remote(
            gout_low.at[across[turn - 1]],
            gout_got.at[turn - 1],
            gout_wires.at[0, turn - 1],
            gout_wires.at[1, turn - 1],
            line(turn),
        )

    def out_grads():
        for piece in range(levels):
            total = None
            for other, cots in ((0, cot_half), (1, cot_sib)):
                part = lax.dot_general(
                    gated_got[piece, other].reshape(nrows * steps, LANES),
                    cots[...].reshape(nrows * steps, D // 2),
                    (((0,), (0,)), ((), ())),
                    preferred_element_type=wide,
                )
                total = part if total is None else total + part
            gout_sum[piece] = total
            gout_low[piece] = total.astype(low)

    def out_share():
        total = gout_sum[level]
        for turn in range(levels - 1):
            total = total + gout_got[turn].astype(wide)
        mine = gout_out.at[share(row // 2, LANES), share(lax.rem(row, 2), D // 2)]
        mine[...] = total.astype(low)
        norm_part[...] += squares(total)
        return begin(
            [
                remote(
                    mine,
                    mine,
                    row_wires.at[2, 0, turn - 1],
                    row_wires.at[2, 1, turn - 1],
                    {"rows": partner("rows", turn)},
                )
                for turn in range(1, nrows)
            ]
        )

    for slot, (turn, at) in enumerate(order):

        def backward(back_step, carry):
            later, grates, states = carry
            t = steps - 1 - back_step
            in_row, out_row = inb[t], outb[t]
            gin_row, gout_row = gin[t], gout[t]
            new = ([], [], [])
            for place in range(4):
                here = (4 * at + place, pl.ds(t, 1))
                grad_y = grady[here]
                delta = ddec[here]
                rates = rates_ref[:, lanes(at, place)]
                before = kept[slot, t, place].astype(wide)
                adjoint = grad_y * out_row + later[place]
                gout_row = gout_row + grad_y * states[place]
                gin_row = gin_row + adjoint * drive[here]
                first[place, share(t, half), :] = fold(adjoint * in_row)
                passed = jnp.exp2(delta * rates) * adjoint
                pulled = passed * before
                second[place, share(t, half), :] = fold(pulled * rates)
                new[0].append(passed)
                new[1].append(grates[place] + pulled * delta)
                new[2].append(before)
            gin[t] = gin_row
            gout[t] = gout_row
            return new

        ending = [kept[slot, steps, place].astype(wide) for place in range(4)]
        _, grates, _ = lax.fori_loop(
            0, steps, backward, (leavings[slot], zeros, ending), unroll=8
        )
        lows = []
        for place in range(4):
            group, columns = 4 * at + place, lanes(at, place)
            along = collapse(first, place)
            here = delta_pre[group]
            act = silu(pre_act[group])
            grad_delta = along * act + collapse(second, place) * math.log(2.0)
            pre_low = (grad_delta * jax.nn.sigmoid(here)).astype(low)
            lows.append(pre_low)
            drive[group] = grady[group] * dskip_ref[:, columns] + along * softplus(here)
            small[spans[5][0] : spans[5][1], columns] = column_sum(pre_low.astype(wide))
            small[spans[2][0] : spans[2][1], columns] = (
                grates[place] * rates_ref[:, columns] * math.log(2.0)
            )
        lows = jnp.concatenate(lows, axis=1)
        rank_back[...] += lax.dot_general(
            lows,
            dt_proj_ref[:, share(at, chunk)],
            (((1,), (1,)), ((), ())),
            preferred_element_type=wide,
        )
        small[spans[0][0] : spans[0][1], share(at, chunk)] = lax.dot_general(
            rank_low[...], lows, (((0,), (0,)), ((), ())), preferred_element_type=wide
        )
        if slot == 0:
            settle(normed_moves)
            normed_moves = to_sibling(0, normed_rows, normed_sib)
            settle(cot_moves)
            cot_moves = to_sibling(1, cot_half, cot_sib)
            for _, chunk_at in order:
                gated_moves += trade_gated(chunk_at)
        if slot == chunks - 3:
            settle(normed_moves)
            settle(gate_moves)
            gate_moves = in_grads(1)

    parts = [(0, R // nrows), (R, (PACKED_ROWS - R) // nrows)]

    def scatter_small(part):
        begin_row, few = parts[part]
        rows = pl.ds(begin_row, few * nrows)
        small_low[rows, :] = small[rows, :].astype(low)
        return begin(
            [
                remote(
                    small_low.at[pl.ds(begin_row + partner("rows", turn) * few, few), :],
                    small_got.at[turn - 1, pl.ds(begin_row // nrows, few), :],
                    row_wires.at[part, 0, turn - 1],
                    row_wires.at[part, 1, turn - 1],
                    {"rows": partner("rows", turn)},
                )
                for turn in range(1, nrows)
            ]
        )

    def trade_small(part):
        begin_row, few = parts[part]
        rows = pl.ds(begin_row // nrows, few)
        total = small[pl.ds(pl.multiple_of(begin_row + row * few, few), few), :]
        for turn in range(nrows - 1):
            total = total + small_got[turn, rows, :].astype(wide)
        small_part[rows, :] = total.astype(low)
        return begin(
            [
                remote(
                    small_part.at[rows, share(partner("seq", offset), shard)],
                    small_seq.at[offset - 1, rows, :],
                    seq_wires.at[part, 0, offset - 1],
                    seq_wires.at[part, 1, offset - 1],
                    {"seq": partner("seq", offset)},
                )
                for offset in (4, 3, 5, 2, 6, 1, 7)
            ]
        )

    def share_small(part):
        begin_row, few = parts[part]
        rows = pl.ds(begin_row // nrows, few)
        total = small_part[rows, share(member, shard)].astype(wide)
        for offset in range(devices - 1):
            total = total + small_seq[offset, rows, :].astype(wide)
        mine = pl.ds(pl.multiple_of(begin_row + row * few, few), few)
        small_out[mine, :] = total.astype(low)
        norm_part[...] += squares(total)
        return begin(
            [
                remote(
                    small_out.at[mine, :],
                    small_out.at[mine, :],
                    row_wires.at[3 + part, 0, turn - 1],
                    row_wires.at[3 + part, 1, turn - 1],
                    {"rows": partner("rows", turn)},
                )
                for turn in range(1, nrows)
            ]
        )

    dt_moves = scatter_small(0)
    proj_back[:, :R] = rank_back[...].astype(low)
    proj_back[:, R : R + N] = jnp.sum(gin[...], axis=2).astype(low)
    proj_back[:, R + N :] = jnp.sum(gout[...], axis=2).astype(low)
    for at in range(chunks):
        pulled = jnp.dot(
            proj_back[...], x_proj_ref[:, span(at, chunk)], preferred_element_type=wide
        )
        lows = []
        for place in range(4):
            group = 4 * at + place
            act, slope = silu_pair(pre_act[group])
            lows.append(act.astype(low))
            grad_conv[group, :steps, :] = (
                drive[group] + pulled[:, place * LANES : (place + 1) * LANES]
            ) * slope
        small[spans[1][0] : spans[1][1], span(at, chunk)] = lax.dot_general(
            proj_back[...],
            jnp.concatenate(lows, axis=1),
            (((0,), (0,)), ((), ())),
            preferred_element_type=wide,
        )
    halo_back = remote(
        grad_conv.at[:, 0:8, :],
        grad_conv.at[:, steps : steps + 8, :],
        halo_wires.at[1, 0],
        halo_wires.at[1, 1],
        {"seq": partner("seq", devices - 1)},
    )

    @pl.when(member > 0)
    def _():
        halo_back.start()

    @pl.when(member == devices - 1)
    def _():
        grad_conv[:, steps : steps + 8, :] = jnp.zeros((groups, 8, LANES), wide)

    settle(cot_moves)
    settle(gated_moves)
    out_grads()
    gout_moves = begin([gout_copy(turn) for turn in range(1, levels)])
    output_ref[...] = stream + jnp.dot(
        gated[...], out_proj_buf[...], preferred_element_type=wide
    )
    grad_normed = jnp.zeros((steps, D), wide)
    for at in range(chunks):
        grad_normed = grad_normed + lax.dot_general(
            back_gates[:, span(at, chunk)],
            in_proj_buf[chunks + at],
            (((1,), (1,)), ((), ())),
            preferred_element_type=wide,
        )

    @pl.when(member > 0)
    def _():
        halo_back.wait_send()

    @pl.when(member < devices - 1)
    def _():
        halo_back.wait_recv()

    inner_moves = []
    for turn, at in order:
        for place in range(4):
            group, columns = 4 * at + place, lanes(at, place)
            padded[...] = inner[halo - 8 :, columns].astype(wide)
            here = grad_conv[group, :steps, :]
            pulled = conv_ref[0:1, columns] * here
            small[spans[4][0] : spans[4][1], columns] = column_sum(here)
            at_row = spans[3][0]
            small[at_row : at_row + 1, columns] = column_sum(here * padded[8:, :])
            for offset in range(1, K):
                small[at_row + offset : at_row + offset + 1, columns] = column_sum(
                    here * masks[offset, :steps, :] * padded[8 - offset : 8 - offset + steps, :]
                )
                pulled = pulled + conv_ref[offset : offset + 1, columns] * (
                    grad_conv[group, offset : offset + steps, :]
                    * masks[offset, offset : offset + steps, :]
                )
            back_inner[:, columns] = pulled.astype(low)
        inner_moves += trade(0, back_inner, at, turn)

    for at in range(chunks):
        grad_normed = grad_normed + lax.dot_general(
            back_inner[:, span(at, chunk)],
            in_proj_buf[at],
            (((1,), (1,)), ((), ())),
            preferred_element_type=wide,
        )
    settle(dt_moves)
    dt_moves = trade_small(0)
    inverse = lax.rsqrt(jnp.mean(stream * stream, axis=1, keepdims=True) + EPS)
    grad_gain = column_sum(grad_normed * stream * inverse)
    owned = D // devices
    for index in range(devices):
        small[spans[7][0] : spans[7][1], index * shard : index * shard + owned] = grad_gain[
            :, index * owned : (index + 1) * owned
        ]
    small_moves = scatter_small(1)
    scaled = grad_normed * gain_ref[...]
    grad_ref[...] = (
        cot_ref[...].astype(wide)
        + inverse * scaled
        - stream
        * inverse
        * inverse
        * inverse
        * jnp.mean(scaled * stream, axis=1, keepdims=True)
    )

    settle(gate_moves)
    gate_moves = in_share(1)
    settle(inner_moves)
    inner_moves = in_grads(0)
    settle(small_moves)
    small_moves = trade_small(1)
    settle(gout_moves)
    gout_moves = out_share()
    settle(dt_moves)
    dt_moves = share_small(0)
    settle(small_moves)
    small_moves = share_small(1)

    def spread_norm():
        here = row * devices + member
        norm_all[here] = jnp.broadcast_to(norm_part[...], (8, LANES))
        return begin(
            [
                remote(
                    norm_all.at[here],
                    norm_all.at[here],
                    norm_wires.at[0, offset - 1],
                    norm_wires.at[1, offset - 1],
                    other_device(offset),
                )
                for offset in range(1, everyone)
            ]
        )

    settle(inner_moves)
    inner_moves = in_share(0, spread_norm)
    norm_moves, inner_moves = inner_moves[: everyone - 1], inner_moves[everyone - 1 :]
    settle(norm_moves)
    norm_out[...] = jnp.sqrt(jnp.sum(norm_all[...], axis=0))
    settle(gout_moves)
    settle(gate_moves)
    settle(dt_moves)
    settle(small_moves)
    settle(inner_moves)


def block_of(operands, nrows, devices):
    steps = operands[1].shape[0]
    groups = E // LANES
    chunk = 4 * LANES
    chunks = E // chunk
    levels = devices // 2
    reach = devices // 2
    shard = E // devices
    halo = 16
    low, wide = jnp.bfloat16, jnp.float32
    few = PACKED_ROWS // nrows
    vmem = pl.BlockSpec(memory_space=pltpu.VMEM)
    specs = [vmem] * len(operands)
    specs[0] = pl.BlockSpec(memory_space=pltpu.SMEM)
    specs[4] = specs[5] = pl.BlockSpec(memory_space=pl.ANY)
    dma = pltpu.SemaphoreType.DMA
    grouped = pltpu.VMEM((groups, steps, LANES), wide)
    flat = pltpu.VMEM((steps, E), low)
    spread = pltpu.VMEM((steps, N, LANES), wide)
    gathered = pltpu.VMEM((nrows, steps, D), low)
    folded = pltpu.VMEM((4, steps * N // 2, LANES), wide)
    return pl.pallas_call(
        functools.partial(block_kernel, nrows, devices),
        in_specs=specs,
        out_specs=[vmem] * 6,
        out_shape=[
            jax.ShapeDtypeStruct((steps, D), wide),
            jax.ShapeDtypeStruct((steps, D), wide),
            jax.ShapeDtypeStruct((D // devices, 2 * E), low),
            jax.ShapeDtypeStruct((shard, D), low),
            jax.ShapeDtypeStruct((PACKED_ROWS, shard), low),
            jax.ShapeDtypeStruct((8, LANES), wide),
        ],
        scratch_shapes=[
            pltpu.VMEM((2 * chunks, D, chunk), low),
            pltpu.VMEM((E, D), low),
            pltpu.VMEM((N, E), wide),
            gathered,
            gathered,
            pltpu.VMEM((nrows, steps, D // 2), low),
            pltpu.VMEM((nrows, steps, D // 2), low),
            pltpu.VMEM((steps + halo, E), low),
            flat,
            flat,
            grouped,
            grouped,
            grouped,
            grouped,
            grouped,
            pltpu.VMEM((steps, R + 2 * N), wide),
            pltpu.VMEM((steps, R), low),
            spread,
            spread,
            pltpu.VMEM((2, chunks, N, chunk), low),
            pltpu.VMEM((devices, chunks, N, chunk), low),
            pltpu.VMEM((devices, groups, LANES), wide),
            pltpu.VMEM((steps + 16, LANES), jnp.int32),
            pltpu.VMEM((K, steps + 8, LANES), wide),
            pltpu.VMEM((steps + 8, LANES), wide),
            pltpu.VMEM((chunks, steps + 1, 4, N, LANES), low),
            folded,
            folded,
            spread,
            spread,
            flat,
            flat,
            flat,
            pltpu.VMEM((groups, steps + 8, LANES), wide),
            pltpu.VMEM((steps, R), wide),
            pltpu.VMEM((steps, R + 2 * N), low),
            pltpu.VMEM((levels, 2, nrows, steps, LANES), low),
            pltpu.VMEM((2, 2, nrows, steps, shard), low),
            pltpu.VMEM((levels, LANES, D // 2), wide),
            pltpu.VMEM((levels, LANES, D // 2), low),
            pltpu.VMEM((levels - 1, LANES, D // 2), low),
            pltpu.VMEM((2, D, shard), wide),
            pltpu.VMEM((2, D, shard), low),
            pltpu.VMEM((2, levels - 1, D // levels, shard), low),
            pltpu.VMEM((2, D // levels, shard), low),
            pltpu.VMEM((PACKED_ROWS, E), wide),
            pltpu.VMEM((PACKED_ROWS, E), low),
            pltpu.VMEM((nrows - 1, few, E), low),
            pltpu.VMEM((few, E), low),
            pltpu.VMEM((devices - 1, few, shard), low),
            pltpu.VMEM((1, 1), wide),
            pltpu.VMEM((nrows * devices, 8, LANES), wide),
            dma((2 * chunks + 1,)),
            dma((2, 2)),
            dma((2, 2, chunks, reach)),
            dma((2, 2, reach)),
            dma((2, 2, nrows - 1)),
            dma((2, 2)),
            dma((2, levels, 2 * nrows)),
            dma((2, 2, 2 * nrows)),
            dma((2, levels - 1)),
            dma((2, 2, levels - 1)),
            dma((2, 2, 2 * nrows)),
            dma((5, 2, nrows - 1)),
            dma((2, 2, devices - 1)),
            dma((2, nrows * devices - 1)),
            dma((2 + levels,)),
        ],
        compiler_params=pltpu.CompilerParams(
            collective_id=1, has_side_effects=True, vmem_limit_bytes=63 * 2**20
        ),
        name="block",
    )(*operands)


def update_kernel(member_ref, norm_ref, gin_ref, gout_ref, small_ref, *refs):
    passed, weights, moments, averages, outs = (
        refs[:2],
        refs[2:12],
        refs[12:22],
        refs[22:32],
        refs[32:],
    )
    outs[30][...] = passed[0][...]
    outs[31][...] = passed[1][...]
    outs[32][...] = norm_ref[0:1, 0:1]
    shrink_by = 1.0 / jnp.maximum(norm_ref[0:1, 0:1], 1.0)

    def renew(ordinal, grad, at=Ellipsis):
        clipped = grad * shrink_by
        momentum_new = MOMENTUM * moments[ordinal][at] + clipped
        renewed = weights[ordinal][at].astype(jnp.float32) - RATES[ordinal] * math.sqrt(PARAMS) * (
            clipped + MOMENTUM * momentum_new
        )
        outs[3 * ordinal][at] = momentum_new
        outs[3 * ordinal + 1][at] = renewed
        outs[3 * ordinal + 2][at] = AVERAGE * averages[ordinal][at] + (1.0 - AVERAGE) * renewed

    renew(1, gin_ref[...].astype(jnp.float32))
    renew(9, gout_ref[...].astype(jnp.float32))

    @pl.when(pl.program_id(0) == 0)
    def _():
        spans = packed_rows()

        def part(index):
            return small_ref[spans[index][0] : spans[index][1], :].astype(jnp.float32)

        small = small_ref[...].astype(jnp.float32)
        renew(5, part(0))
        renew(4, part(1))
        renew(7, part(2))
        renew(2, part(3))
        for ordinal, index in ((3, 4), (6, 5), (8, 6)):
            renew(ordinal, small[spans[index][0] : spans[index][1]])
        gain = small[spans[7][0] : spans[7][1], : weights[0].shape[1]]
        renew(0, gain)


def update_of(member, norm_tile, gin, gout, small, passed, weights, moments, averages):
    inner = gin.shape[0]
    channels = gout.shape[0]
    blocks = 2
    outer = channels // blocks
    block = gin.shape[1] // blocks
    flat = (0, 3, 6, 8)

    def rows_of(array, ordinal):
        return array.reshape(1, -1) if ordinal in flat else array.T if ordinal == 4 else array

    def shard(shape, ordinal):
        if ordinal == 1:
            return pl.BlockSpec((inner, block), lambda j, m: (0, j))
        if ordinal == 9:
            return pl.BlockSpec((outer, shape[1]), lambda j, m: (j, 0))
        return pl.BlockSpec(shape, lambda j, m: (0, 0))

    def weight(shape, ordinal):
        if ordinal == 1:
            return pl.BlockSpec((inner, block), lambda j, m: (m[0], j))
        if ordinal == 9:
            return pl.BlockSpec((outer, shape[1]), lambda j, m: (m[0] * blocks + j, 0))
        return pl.BlockSpec(shape, lambda j, m: (0, m[0]))

    weights = [rows_of(array, ordinal) for ordinal, array in enumerate(weights)]
    moments = [rows_of(array, ordinal) for ordinal, array in enumerate(moments)]
    averages = [rows_of(array, ordinal) for ordinal, array in enumerate(averages)]
    shapes = [array.shape for array in moments]
    shards = [shard(shape, ordinal) for ordinal, shape in enumerate(shapes)]
    steps, depth = passed[0].shape
    through = pl.BlockSpec((steps // blocks, depth), lambda j, m: (j, 0))
    outs = pl.pallas_call(
        update_kernel,
        grid_spec=pltpu.PrefetchScalarGridSpec(
            num_scalar_prefetch=1,
            grid=(blocks,),
            in_specs=[
                pl.BlockSpec(norm_tile.shape, lambda j, m: (0, 0)),
                pl.BlockSpec((inner, block), lambda j, m: (0, j)),
                pl.BlockSpec((outer, gout.shape[1]), lambda j, m: (j, 0)),
                pl.BlockSpec(small.shape, lambda j, m: (0, 0)),
                through,
                through,
            ]
            + [weight(shape, ordinal) for ordinal, shape in enumerate(shapes)]
            + shards
            + shards,
            out_specs=[shards[ordinal] for ordinal in range(10) for _ in range(3)]
            + [through, through, pl.BlockSpec((1, 1), lambda j, m: (0, 0))],
        ),
        out_shape=[
            jax.ShapeDtypeStruct(shapes[ordinal], jnp.float32)
            for ordinal in range(10)
            for _ in range(3)
        ]
        + [jax.ShapeDtypeStruct(array.shape, array.dtype) for array in passed]
        + [jax.ShapeDtypeStruct((1, 1), jnp.float32)],
        compiler_params=pltpu.CompilerParams(vmem_limit_bytes=63 * 2**20),
        name="update",
    )(member, norm_tile, gin, gout, small, *passed, *weights, *moments, *averages)
    return outs[30:], [
        out.reshape(-1) if index // 3 in flat else out.T if index // 3 == 4 else out
        for index, out in enumerate(outs[:30])
    ]


def local(
    tokens,
    cotangent,
    doc_lengths,
    norm_gain,
    in_proj,
    conv_weight,
    conv_bias,
    x_proj,
    dt_proj,
    dt_bias,
    a_log,
    d_skip,
    out_proj,
    moment_norm_gain,
    moment_in_proj,
    moment_conv_weight,
    moment_conv_bias,
    moment_x_proj,
    moment_dt_proj,
    moment_dt_bias,
    moment_a_log,
    moment_d_skip,
    moment_out_proj,
    average_norm_gain,
    average_in_proj,
    average_conv_weight,
    average_conv_bias,
    average_x_proj,
    average_dt_proj,
    average_dt_bias,
    average_a_log,
    average_d_skip,
    average_out_proj,
):
    devices = lax.axis_size("seq")
    member_id = lax.axis_index("seq")
    channels = E // devices
    begin = member_id * channels
    stream = tokens[0].astype(jnp.float32)
    steps = stream.shape[0]
    length = steps * devices
    cot_low = cotangent[0]
    nrows = lax.axis_size("rows")
    direct = devices == 2 * nrows and nrows == 4 and E == nrows * 4 * LANES
    member_word = jnp.reshape(member_id, (1,)).astype(jnp.int32)
    moments = (
        moment_norm_gain,
        moment_in_proj,
        moment_conv_weight,
        moment_conv_bias,
        moment_x_proj,
        moment_dt_proj,
        moment_dt_bias,
        moment_a_log,
        moment_d_skip,
        moment_out_proj,
    )
    averages = (
        average_norm_gain,
        average_in_proj,
        average_conv_weight,
        average_conv_bias,
        average_x_proj,
        average_dt_proj,
        average_dt_bias,
        average_a_log,
        average_d_skip,
        average_out_proj,
    )
    if direct:
        weights = (
            norm_gain,
            in_proj,
            conv_weight,
            conv_bias,
            x_proj,
            dt_proj,
            dt_bias,
            a_log,
            d_skip,
            out_proj,
        )
        block_output, input_grad, gin_share, gout_share, small, norm_tile = block_of(
            (
                doc_lengths,
                tokens[0],
                cot_low,
                norm_gain[None],
                in_proj,
                out_proj,
                conv_weight,
                conv_bias[None],
                x_proj.T,
                dt_proj,
                dt_bias[None],
                a_log,
                d_skip[None],
            ),
            nrows,
            devices,
        )
        (block_output, input_grad, grad_norm), updated = update_of(
            member_word,
            norm_tile,
            gin_share,
            gout_share,
            small,
            (block_output, input_grad),
            weights,
            moments,
            averages,
        )
        return (block_output[None], input_grad[None], grad_norm.reshape(()), *updated)
    inverse = lax.rsqrt(jnp.mean(stream * stream, axis=1, keepdims=True) + EPS)
    rates = -jnp.exp(a_log)
    scaled_rates = rates * (1.0 / math.log(2.0))
    lengths = doc_lengths[0]
    starts = (jnp.cumsum(lengths) - lengths).astype(jnp.int32)
    (
        normed,
        inner_low,
        gates_low,
        back_gated,
        pre_act,
        delta_pre,
        ddec,
        drive,
        grady_rows,
        rank_low,
        inb,
        outb,
        everyone,
        all_sums,
    ) = front_of(
        starts,
        tokens[0],
        cot_low,
        norm_gain[None],
        in_proj,
        out_proj,
        conv_weight,
        conv_bias[None],
        x_proj.T,
        dt_proj,
        dt_bias[None],
        scaled_rates,
        devices,
        1,
    )
    cot_all = lax.all_gather(cot_low, "seq", axis=0, tiled=True)
    normed_all = lax.all_gather(normed[0], "seq", axis=0, tiled=True)
    positions = member_id * steps + jnp.arange(-8, steps + 8, dtype=jnp.int32)
    docid, starting = doc_tables(doc_lengths[0], positions)
    masks = []
    for offset in range(K):
        linked = (docid[8:] == docid[8 - offset : steps + 16 - offset]) & (
            positions[8 - offset : steps + 16 - offset] >= 0
        )
        masks.append((linked & (positions[8:] < length)).astype(jnp.float32)[:, None])

    def flat(values):
        return jnp.transpose(values, (1, 0, 2)).reshape(steps, E)

    pre_act, delta_pre = flat(pre_act), flat(delta_pre)
    padded = inner_low[8:].astype(jnp.float32)
    gates = gates_low.astype(jnp.float32)
    act = silu(pre_act)
    act_low = act.astype(jnp.bfloat16)
    delta = jax.nn.softplus(delta_pre)
    silu_gate = silu(gates)
    chan_back = back_gated.astype(jnp.float32)
    grad_y = chan_back * silu_gate
    scanned, along_in, pulled_sum, gin, gout, grad_rates = scan_of(
        member_word, ddec, drive, grady_rows, inb, outb, scaled_rates, everyone, all_sums, 512
    )
    scanned, along_in, pulled_sum = flat(scanned), flat(along_in), flat(pulled_sum)
    y_full = scanned + d_skip[None, :] * act
    gated = (y_full * silu_gate).astype(jnp.bfloat16)
    block_output = (
        stream + jnp.dot(gated, out_proj, preferred_element_type=jnp.float32)
    )[None]
    grad_gates = chan_back * y_full * silu_slope(gates)
    grad_dskip = jnp.sum(grad_y * act, axis=0)
    grad_in_mat = jnp.sum(gin, axis=2)
    grad_out_mat = jnp.sum(gout, axis=2)
    grad_delta = along_in * act + pulled_sum * math.log(2.0)
    grad_alog = grad_rates * rates
    grad_pre = (grad_delta * jax.nn.sigmoid(delta_pre)).astype(jnp.bfloat16)
    grad_dtbias = jnp.sum(grad_pre.astype(jnp.float32), axis=0)
    grad_dtproj = lax.dot_general(
        rank_low, grad_pre, (((0,), (0,)), ((), ())), preferred_element_type=jnp.float32
    )
    rank_back = lax.dot_general(
        grad_pre, dt_proj, (((1,), (1,)), ((), ())), preferred_element_type=jnp.float32
    )
    proj_back = jnp.concatenate([rank_back, grad_in_mat, grad_out_mat], axis=1).astype(jnp.bfloat16)
    grad_xproj = lax.dot_general(
        act_low, proj_back, (((0,), (0,)), ((), ())), preferred_element_type=jnp.float32
    )
    grad_act = (
        grad_y * d_skip[None, :]
        + along_in * delta
        + lax.dot_general(
            proj_back, x_proj, (((1,), (1,)), ((), ())), preferred_element_type=jnp.float32
        )
    )
    grad_pre_act = grad_act * silu_slope(pre_act)
    ahead = lax.ppermute(
        grad_pre_act[:8], "seq", [(i + 1, i) for i in range(devices - 1)]
    )
    extended = jnp.concatenate([grad_pre_act, ahead], axis=0)
    grad_conv_bias = jnp.sum(grad_pre_act, axis=0)
    grad_inner = jnp.zeros_like(gates)
    conv_rows = []
    for offset in range(K):
        masked = extended * masks[offset]
        conv_rows.append(
            jnp.sum(masked[:steps] * padded[8 - offset : 8 - offset + steps], axis=0)
        )
        grad_inner = grad_inner + conv_weight[offset][None, :] * masked[offset : offset + steps]
    grad_convw = jnp.stack(conv_rows)
    back_xz = jnp.stack([grad_inner, grad_gates]).astype(jnp.bfloat16)
    grad_normed = lax.dot_general(
        back_xz[0], in_proj[:, :E], (((1,), (1,)), ((), ())), preferred_element_type=jnp.float32
    ) + lax.dot_general(
        back_xz[1], in_proj[:, E:], (((1,), (1,)), ((), ())), preferred_element_type=jnp.float32
    )
    grad_gain = jnp.sum(grad_normed * stream * inverse, axis=0)
    scaled = grad_normed * norm_gain[None, :]
    input_grad = (
        cot_low.astype(jnp.float32)
        + inverse * scaled
        - stream * inverse * inverse * inverse * jnp.mean(scaled * stream, axis=1, keepdims=True)
    )
    small = jnp.concatenate(
        [
            grad_dtproj,
            grad_xproj.T,
            grad_alog,
            grad_convw,
            grad_conv_bias[None],
            grad_dtbias[None],
            grad_dskip[None],
            jnp.pad(
                grad_gain.reshape(devices, D // devices),
                ((0, 0), (0, channels - D // devices)),
            ).reshape(1, E),
            jnp.zeros((PACKED_ROWS - sum(PACKED), E), jnp.float32),
        ],
        axis=0,
    )
    gated_mine = lax.all_to_all(gated, "seq", split_axis=1, concat_axis=0, tiled=True)
    back_mine = lax.all_to_all(back_xz, "seq", split_axis=2, concat_axis=1, tiled=True)
    gout_share = lax.psum(
        lax.dot_general(
            gated_mine, cot_all, (((0,), (0,)), ((), ())), preferred_element_type=jnp.float32
        ),
        "rows",
    )
    gin_share = lax.psum(
        jnp.einsum("td,ktc->dkc", normed_all, back_mine, preferred_element_type=jnp.float32),
        "rows",
    )
    gin_share = lax.all_to_all(
        gin_share, "seq", split_axis=0, concat_axis=2, tiled=True
    ).reshape(D // devices, 2 * E)
    small = lax.psum(small, "rows")
    small = lax.psum_scatter(small, "seq", scatter_dimension=1, tiled=True)
    squares = jnp.sum(gin_share * gin_share) + jnp.sum(gout_share * gout_share)
    grad_norm = jnp.sqrt(lax.psum(squares + jnp.sum(small * small), "seq"))
    results = [block_output, input_grad[None], grad_norm]
    parts = [small[low:high] for low, high in packed_rows()]
    owner_grads = (
        parts[7][0, : D // devices],
        gin_share.astype(jnp.float32),
        parts[3],
        parts[4][0],
        parts[1].T,
        parts[0],
        parts[5][0],
        parts[2],
        parts[6][0],
        gout_share.astype(jnp.float32),
    )
    conv_mine = lax.dynamic_slice_in_dim(conv_weight, begin, channels, 1)
    cbias_mine = lax.dynamic_slice_in_dim(conv_bias, begin, channels, 0)
    xproj_mine = lax.dynamic_slice_in_dim(x_proj, begin, channels, 0)
    dtproj_mine = lax.dynamic_slice_in_dim(dt_proj, begin, channels, 1)
    dtbias_mine = lax.dynamic_slice_in_dim(dt_bias, begin, channels, 0)
    alog_mine = lax.dynamic_slice_in_dim(a_log, begin, channels, 1)
    dskip_mine = lax.dynamic_slice_in_dim(d_skip, begin, channels, 0)
    shrink_by = 1.0 / jnp.maximum(grad_norm, 1.0)
    gain_rows = D // devices
    outer_rows = E // devices
    mine_weights = (
        lax.dynamic_slice_in_dim(norm_gain, member_id * gain_rows, gain_rows, 0),
        lax.dynamic_slice_in_dim(in_proj, member_id * gain_rows, gain_rows, 0).astype(jnp.float32),
        conv_mine,
        cbias_mine,
        xproj_mine.astype(jnp.float32),
        dtproj_mine.astype(jnp.float32),
        dtbias_mine,
        alog_mine,
        dskip_mine,
        lax.dynamic_slice_in_dim(out_proj, member_id * outer_rows, outer_rows, 0).astype(
            jnp.float32
        ),
    )
    for ordinal in range(10):
        clipped = owner_grads[ordinal] * shrink_by
        momentum_new = MOMENTUM * moments[ordinal] + clipped
        renewed = mine_weights[ordinal] - RATES[ordinal] * math.sqrt(PARAMS) * (
            clipped + MOMENTUM * momentum_new
        )
        results += [momentum_new, renewed, AVERAGE * averages[ordinal] + (1.0 - AVERAGE) * renewed]
    return tuple(results)


def solution(mesh):
    return jax.shard_map(
        local,
        mesh=mesh,
        in_specs=(
            P("rows", "seq", None),
            P("rows", "seq", None),
            P("rows", None),
            P(),
            P(),
            P(),
            P(),
            P(),
            P(),
            P(),
            P(),
            P(),
            P(),
            P("seq"),
            P("seq", None),
            P(None, "seq"),
            P("seq"),
            P("seq", None),
            P(None, "seq"),
            P("seq"),
            P(None, "seq"),
            P("seq"),
            P("seq", None),
            P("seq"),
            P("seq", None),
            P(None, "seq"),
            P("seq"),
            P("seq", None),
            P(None, "seq"),
            P("seq"),
            P(None, "seq"),
            P("seq"),
            P("seq", None),
        ),
        out_specs=(
            P("rows", "seq", None),
            P("rows", "seq", None),
            P(),
            P("seq"),
            P("seq"),
            P("seq"),
            P("seq", None),
            P("seq", None),
            P("seq", None),
            P(None, "seq"),
            P(None, "seq"),
            P(None, "seq"),
            P("seq"),
            P("seq"),
            P("seq"),
            P("seq", None),
            P("seq", None),
            P("seq", None),
            P(None, "seq"),
            P(None, "seq"),
            P(None, "seq"),
            P("seq"),
            P("seq"),
            P("seq"),
            P(None, "seq"),
            P(None, "seq"),
            P(None, "seq"),
            P("seq"),
            P("seq"),
            P("seq"),
            P("seq", None),
            P("seq", None),
            P("seq", None),
        ),
        check_vma=False,
    )
```

```python
import functools
import math

import jax
import jax.numpy as jnp
from jax import lax
from jax.experimental import pallas as pl
from jax.experimental.pallas import tpu as pltpu
from jax.sharding import PartitionSpec as P

D = 1024
E = 2048
N = 16
R = 64
K = 4
PARAMS = 6667264

LANES = 128
RESET = 1e30
MESH = pl.DeviceIdType.MESH


EPS = 1e-05
MOMENTUM = 0.9
AVERAGE = 0.9
RATES = (0.1, 0.03, 0.1, 0.1, 0.03, 0.03, 0.3, 0.3, 0.1, 0.03)


def silu(values):
    return values * jax.nn.sigmoid(values)


def silu_slope(values):
    sigmoid_of = jax.nn.sigmoid(values)
    return sigmoid_of * (1.0 + values * (1.0 - sigmoid_of))


def doc_tables(lengths_row, positions):
    ends = jnp.cumsum(lengths_row)
    starts = ends - lengths_row
    docid = jnp.sum((positions[None, :] >= starts[:, None]).astype(jnp.int32), axis=0)
    first = jnp.sum((positions[None, :] == starts[:, None]).astype(jnp.int32), axis=0)
    return (docid, first > 0)


def scan_kernel(
    member_ref,
    ddec_ref,
    drive_ref,
    grady_ref,
    inb_ref,
    outb_ref,
    rates_ref,
    all_ref,
    sums_ref,
    scanned_ref,
    along_ref,
    decayed_ref,
    gin_ref,
    gout_ref,
    grates_ref,
    kept,
    first,
    second,
):
    groups, steps = ddec_ref.shape[:2]
    devices = all_ref.shape[0]
    base = pl.program_id(0) * groups
    member = member_ref[0]
    columns = [pl.ds(group * LANES, LANES) for group in range(groups)]
    half = N // 2

    @pl.when(pl.program_id(0) == 0)
    def _():
        gin_ref[...] = jnp.zeros_like(gin_ref)
        gout_ref[...] = jnp.zeros_like(gout_ref)

    def through(device, states):
        new = []
        for group in range(groups):
            total = sums_ref[device, pl.ds(base + group, 1), :]
            factor = jnp.exp2(total * rates_ref[:, columns[group]])
            new.append(
                factor * states[group]
                + all_ref[device, 0, :, columns[group]].astype(jnp.float32)
            )
        return new

    zeros = [jnp.zeros((N, LANES), jnp.float32) for _ in range(groups)]
    reach = devices // 2
    entering = lax.fori_loop(jnp.maximum(member - reach, 0), member, through, zeros)
    last = jnp.minimum(member + reach, devices - 1)
    leaving = lax.fori_loop(0, last - member, lambda d, s: through(last - d, s), zeros)

    def fold(values):
        return values[:half] + values[half:]

    def forward(t, hidden):
        in_row, out_row = inb_ref[t], outb_ref[t]
        new = []
        for group in range(groups):
            here = (group, pl.ds(t, 1))
            decay = jnp.exp2(ddec_ref[here] * rates_ref[:, columns[group]])
            state = decay * hidden[group] + drive_ref[here] * in_row
            kept[t + 1, :, columns[group]] = state
            first[group, pl.ds(pl.multiple_of(t * half, half), half), :] = fold(state * out_row)
            new.append(state)
        return new

    for group in range(groups):
        kept[0, :, columns[group]] = entering[group]
    lax.fori_loop(0, steps, forward, entering, unroll=4)

    def collapse(source, target_ref):
        for group in range(groups):
            total = source[group, pl.ds(0, steps, stride=half), :]
            for place in range(1, half):
                total = total + source[group, pl.ds(place, steps, stride=half), :]
            target_ref[group] = total

    collapse(first, scanned_ref)

    def backward(back, carry):
        later, grates = carry
        t = steps - 1 - back
        in_row, out_row = inb_ref[t], outb_ref[t]
        gin, gout = gin_ref[t], gout_ref[t]
        new = ([], [])
        rows = pl.ds(pl.multiple_of(t * half, half), half)
        for group in range(groups):
            here = (group, pl.ds(t, 1))
            grady = grady_ref[here]
            delta = ddec_ref[here]
            rates = rates_ref[:, columns[group]]
            adjoint = grady * out_row + later[group]
            gout = gout + grady * kept[t + 1, :, columns[group]]
            gin = gin + adjoint * drive_ref[here]
            first[group, rows, :] = fold(adjoint * in_row)
            passed = jnp.exp2(delta * rates) * adjoint
            pulled = passed * kept[t, :, columns[group]]
            second[group, rows, :] = fold(pulled * rates)
            new[0].append(passed)
            new[1].append(grates[group] + pulled * delta)
        gin_ref[t] = gin
        gout_ref[t] = gout
        return new

    _, grates = lax.fori_loop(0, steps, backward, (leaving, zeros), unroll=4)
    collapse(first, along_ref)
    collapse(second, decayed_ref)
    for group in range(groups):
        grates_ref[:, columns[group]] = grates[group]


def scan_of(member, ddec, drive, grady, inb, outb, rates, everyone, sums, block):
    steps = ddec.shape[1]
    devices = everyone.shape[0]
    groups = block // LANES
    wide = pl.BlockSpec((block // LANES, steps, LANES), lambda b: (b, 0, 0))
    whole = pl.BlockSpec((steps, N, LANES), lambda b: (0, 0, 0))
    narrow = pl.BlockSpec((N, block), lambda b: (0, b))
    full = jax.ShapeDtypeStruct((E // LANES, steps, LANES), jnp.float32)
    spread = jax.ShapeDtypeStruct((steps, N, LANES), jnp.float32)
    return pl.pallas_call(
        scan_kernel,
        grid=(E // block,),
        in_specs=[
            pl.BlockSpec(memory_space=pltpu.SMEM),
            wide,
            wide,
            wide,
            whole,
            whole,
            narrow,
            pl.BlockSpec((devices, 1, N, block), lambda b: (0, b, 0, 0)),
            pl.BlockSpec(sums.shape, lambda b: (0, 0, 0)),
        ],
        out_specs=[wide, wide, wide, whole, whole, narrow],
        out_shape=[full, full, full, spread, spread, jax.ShapeDtypeStruct((N, E), jnp.float32)],
        scratch_shapes=[
            pltpu.VMEM((steps + 1, N, block), jnp.float32),
            pltpu.VMEM((groups, steps * N // 2, LANES), jnp.float32),
            pltpu.VMEM((groups, steps * N // 2, LANES), jnp.float32),
        ],
        compiler_params=pltpu.CompilerParams(vmem_limit_bytes=48 * 2**20),
        name="scan",
    )(member, ddec, drive, grady, inb, outb, rates, everyone, sums)


def partner(axis, offset):
    size = lax.axis_size(axis)
    return lax.rem(lax.axis_index(axis) + offset, size)


def greet(counts):
    barrier = pltpu.get_barrier_semaphore()
    total = 0
    for axis, count in counts:
        for offset in range(1, count):
            pl.semaphore_signal(
                barrier, inc=1, device_id={axis: partner(axis, offset)}, device_id_type=MESH
            )
        total += count - 1
    pl.semaphore_wait(barrier, total)


def push(source, target, semaphores, at, axis, offset):
    copy = pltpu.make_async_remote_copy(
        src_ref=source,
        dst_ref=target,
        send_sem=semaphores.at[0, at],
        recv_sem=semaphores.at[1, at],
        device_id={axis: partner(axis, offset)},
        device_id_type=MESH,
    )
    copy.start()
    return copy


def span(index, size):
    return pl.ds(index * size, size)


def softplus(values):
    return jnp.maximum(values, 0.0) + jnp.log1p(jnp.exp(-jnp.abs(values)))


def front_kernel(
    devices,
    nrows,
    starts_ref,
    tokens_ref,
    cot_ref,
    gain_ref,
    in_proj_ref,
    out_proj_ref,
    conv_ref,
    cbias_ref,
    x_proj_ref,
    dt_proj_ref,
    dtbias_ref,
    rates_ref,
    normed_ref,
    inner_ref,
    gates_ref,
    back_ref,
    pre_act_ref,
    delta_pre_ref,
    ddec_ref,
    drive_ref,
    grady_ref,
    rank_ref,
    inb_ref,
    outb_ref,
    ends_out,
    sums_out,
    in_proj_buf,
    out_proj_buf,
    padded,
    docid,
    masks,
    proj,
    ends,
    loads,
    halo_wires,
    wires,
    sum_wires,
    row_wires,
):
    member = lax.axis_index("seq")
    own = lax.axis_index("rows") if nrows > 1 else 0
    steps = tokens_ref.shape[0]
    groups = E // LANES
    chunk = 4 * LANES
    chunks = E // chunk
    reach = devices // 2
    halo = inner_ref.shape[0] - steps
    in_loads = [
        pltpu.make_async_copy(
            in_proj_ref.at[:, span(at, chunk)], in_proj_buf.at[at], loads.at[at]
        )
        for at in range(2 * chunks)
    ]
    out_loads = [
        pltpu.make_async_copy(
            out_proj_ref.at[span(at, chunk), :], out_proj_buf.at[at], loads.at[2 * chunks + at]
        )
        for at in range(chunks)
    ]
    for load in in_loads + out_loads:
        load.start()
    barrier = pltpu.get_barrier_semaphore()
    for axis, count in (("seq", devices), ("rows", nrows)):
        for offset in range(1, count):
            pl.semaphore_signal(
                barrier, inc=1, device_id={axis: partner(axis, offset)}, device_id_type=MESH
            )

    stream = tokens_ref[...].astype(jnp.float32)
    inverse = lax.rsqrt(jnp.mean(stream * stream, axis=1, keepdims=True) + EPS)
    normed_ref[own] = (stream * inverse * gain_ref[...]).astype(jnp.bfloat16)

    places = member * steps - 8 + lax.broadcasted_iota(jnp.int32, docid.shape, 0)
    count = jnp.zeros(docid.shape, jnp.int32)
    first = jnp.zeros(docid.shape, jnp.float32)
    for index in range(starts_ref.shape[0]):
        count = count + jnp.where(places >= starts_ref[index], 1, 0)
        first = jnp.where(places == starts_ref[index], 1.0, first)
    docid[...] = count
    masks[0] = first[8 : 8 + steps]
    for offset in range(1, K):
        masks[offset] = jnp.where(
            docid[8 - offset : 8 - offset + steps, :] == docid[8 : 8 + steps, :], 1.0, 0.0
        )

    def project(at):
        in_loads[at].wait()
        return jnp.dot(
            normed_ref[own], in_proj_buf[at], preferred_element_type=jnp.float32
        ).astype(jnp.bfloat16)

    for at in range(chunks):
        inner_ref[halo:, span(at, chunk)] = project(at)
    pl.semaphore_wait(barrier, devices + nrows - 2)
    halo_copy = pltpu.make_async_remote_copy(
        src_ref=inner_ref.at[steps : steps + halo, :],
        dst_ref=inner_ref.at[0:halo, :],
        send_sem=halo_wires.at[0],
        recv_sem=halo_wires.at[1],
        device_id={"seq": partner("seq", 1)},
        device_id_type=MESH,
    )

    @pl.when(member < devices - 1)
    def _():
        halo_copy.start()

    row_copies = [
        push(normed_ref.at[own], normed_ref.at[own], row_wires, offset - 1, "rows", offset)
        for offset in range(1, nrows)
    ]

    @pl.when(member == 0)
    def _():
        inner_ref[0:halo, :] = jnp.zeros((halo, E), jnp.bfloat16)

    for at in range(chunks):
        gates_ref[:, span(at, chunk)] = project(chunks + at)
    for at in range(chunks):
        out_loads[at].wait()
        back_ref[:, span(at, chunk)] = lax.dot_general(
            cot_ref[...],
            out_proj_buf[at],
            (((1,), (1,)), ((), ())),
            preferred_element_type=jnp.float32,
        ).astype(jnp.bfloat16)

    @pl.when(member < devices - 1)
    def _():
        halo_copy.wait_send()

    @pl.when(member > 0)
    def _():
        halo_copy.wait_recv()

    proj[...] = jnp.zeros_like(proj)
    for at in range(chunks):
        lows = []
        for group in range(4 * at, 4 * at + 4):
            columns = span(group, LANES)
            padded[...] = inner_ref[halo - 8 :, columns].astype(jnp.float32)
            value = cbias_ref[:, columns] + conv_ref[0:1, columns] * padded[8:, :]
            for offset in range(1, K):
                value = (
                    value
                    + conv_ref[offset : offset + 1, columns]
                    * padded[8 - offset : 8 - offset + steps, :]
                    * masks[offset]
                )
            pre_act_ref[group] = value
            act = silu(value)
            drive_ref[group] = act
            lows.append(act.astype(jnp.bfloat16))
        proj[...] += lax.dot_general(
            jnp.concatenate(lows, axis=1),
            x_proj_ref[:, span(at, chunk)],
            (((1,), (1,)), ((), ())),
            preferred_element_type=jnp.float32,
        )
    rank_ref[...] = proj[:, :R].astype(jnp.bfloat16)
    inb_ref[...] = jnp.broadcast_to(proj[:, R : R + N][:, :, None], inb_ref.shape)
    outb_ref[...] = jnp.broadcast_to(proj[:, R + N :][:, :, None], outb_ref.shape)

    def later(distance, at):
        return pltpu.make_async_remote_copy(
            src_ref=ends.at[0, at],
            dst_ref=ends_out.at[member, at],
            send_sem=wires.at[0, 0, at, distance - 1],
            recv_sem=wires.at[0, 1, at, distance - 1],
            device_id={"seq": partner("seq", distance)},
            device_id_type=MESH,
        )

    def earlier(distance, at):
        return pltpu.make_async_remote_copy(
            src_ref=ends.at[1, at],
            dst_ref=ends_out.at[member, at],
            send_sem=wires.at[1, 0, at, distance - 1],
            recv_sem=wires.at[1, 1, at, distance - 1],
            device_id={"seq": partner("seq", devices - distance)},
            device_id_type=MESH,
        )

    def sums_to(distance, side):
        offset = distance if side == 0 else devices - distance
        return pltpu.make_async_remote_copy(
            src_ref=sums_out.at[member],
            dst_ref=sums_out.at[member],
            send_sem=sum_wires.at[side, 0, distance - 1],
            recv_sem=sum_wires.at[side, 1, distance - 1],
            device_id={"seq": partner("seq", offset)},
            device_id_type=MESH,
        )

    for at in range(chunks):
        delta_pre = (
            jnp.dot(
                rank_ref[...], dt_proj_ref[:, span(at, chunk)], preferred_element_type=jnp.float32
            )
            + dtbias_ref[:, span(at, chunk)]
        )
        for place in range(4):
            group = 4 * at + place
            columns = span(group, LANES)
            here = delta_pre[:, place * LANES : (place + 1) * LANES]
            delta = softplus(here)
            delta_pre_ref[group] = here
            drive_ref[group] = drive_ref[group] * delta
            ddec = jnp.where(masks[0] > 0.0, RESET, delta)
            ddec_ref[group] = ddec
            sums_out[member, group : group + 1, :] = jnp.sum(ddec, axis=0, keepdims=True)
            grady_ref[group] = back_ref[:, columns].astype(jnp.float32) * silu(
                gates_ref[:, columns].astype(jnp.float32)
            )

        def step(t, carry):
            hidden, decayed, pulled = carry
            in_row, out_row = inb_ref[t], outb_ref[t]
            new = ([], [], [])
            for place in range(4):
                here = (4 * at + place, pl.ds(t, 1))
                decay = jnp.exp2(ddec_ref[here] * rates_ref[:, span(4 * at + place, LANES)])
                new[0].append(decay * hidden[place] + drive_ref[here] * in_row)
                product = decay * decayed[place]
                new[1].append(product)
                new[2].append(pulled[place] + product * (grady_ref[here] * out_row))
            return new

        zeros = [jnp.zeros((N, LANES), jnp.float32) for _ in range(4)]
        ones = [jnp.ones((N, LANES), jnp.float32) for _ in range(4)]
        hidden, _, pulled = lax.fori_loop(0, steps, step, (zeros, ones, zeros), unroll=4)
        ends[0, at] = jnp.concatenate(hidden, axis=1).astype(jnp.bfloat16)
        ends[1, at] = jnp.concatenate(pulled, axis=1).astype(jnp.bfloat16)
        for distance in range(1, reach + 1):

            @pl.when(member + distance < devices)
            def _():
                later(distance, at).start()

            @pl.when(member >= distance)
            def _():
                earlier(distance, at).start()

    for distance in range(1, reach + 1):

        @pl.when(member + distance < devices)
        def _():
            sums_to(distance, 0).start()

        @pl.when(member >= distance)
        def _():
            sums_to(distance, 1).start()

    for distance in range(1, reach + 1):

        @pl.when(member + distance < devices)
        def _():
            for at in range(chunks):
                later(distance, at).wait_send()
                earlier(distance, at).wait_recv()
            sums_to(distance, 0).wait_send()
            sums_to(distance, 1).wait_recv()

        @pl.when(member >= distance)
        def _():
            for at in range(chunks):
                earlier(distance, at).wait_send()
                later(distance, at).wait_recv()
            sums_to(distance, 1).wait_send()
            sums_to(distance, 0).wait_recv()
    for copy in row_copies:
        copy.wait()


def front_of(starts, tokens, cot, gain, in_proj, out_proj, conv, cbias, x_proj, dt_proj, dtbias, rates, devices, nrows):
    steps = tokens.shape[0]
    groups = E // LANES
    chunk = 4 * LANES
    chunks = E // chunk
    reach = devices // 2
    halo = 16
    low = jnp.bfloat16
    vmem = pl.BlockSpec(memory_space=pltpu.VMEM)
    grouped = jax.ShapeDtypeStruct((groups, steps, LANES), jnp.float32)
    spread = jax.ShapeDtypeStruct((steps, N, LANES), jnp.float32)
    return pl.pallas_call(
        functools.partial(front_kernel, devices, nrows),
        in_specs=[pl.BlockSpec(memory_space=pltpu.SMEM)]
        + [vmem] * 3
        + [pl.BlockSpec(memory_space=pl.ANY)] * 2
        + [vmem] * 6,
        out_specs=[vmem] * 14,
        out_shape=[
            jax.ShapeDtypeStruct((nrows, steps, D), low),
            jax.ShapeDtypeStruct((steps + halo, E), low),
            jax.ShapeDtypeStruct((steps, E), low),
            jax.ShapeDtypeStruct((steps, E), low),
            grouped,
            grouped,
            grouped,
            grouped,
            grouped,
            jax.ShapeDtypeStruct((steps, R), low),
            spread,
            spread,
            jax.ShapeDtypeStruct((devices, chunks, N, chunk), low),
            jax.ShapeDtypeStruct((devices, groups, LANES), jnp.float32),
        ],
        scratch_shapes=[
            pltpu.VMEM((2 * chunks, D, chunk), low),
            pltpu.VMEM((chunks, chunk, D), low),
            pltpu.VMEM((steps + 8, LANES), jnp.float32),
            pltpu.VMEM((steps + 16, LANES), jnp.int32),
            pltpu.VMEM((K, steps, LANES), jnp.float32),
            pltpu.VMEM((steps, R + 2 * N), jnp.float32),
            pltpu.VMEM((2, chunks, N, chunk), low),
            pltpu.SemaphoreType.DMA((3 * chunks,)),
            pltpu.SemaphoreType.DMA((2,)),
            pltpu.SemaphoreType.DMA((2, 2, chunks, reach)),
            pltpu.SemaphoreType.DMA((2, 2, reach)),
            pltpu.SemaphoreType.DMA((2, max(nrows - 1, 1))),
        ],
        compiler_params=pltpu.CompilerParams(
            collective_id=0, has_side_effects=True, vmem_limit_bytes=60 * 2**20
        ),
        name="front",
    )(starts, tokens, cot, gain, in_proj, out_proj, conv, cbias, x_proj, dt_proj, dtbias, rates)


PACKED = (R, R + 2 * N, N, K, 1, 1, 1, 1)
PACKED_ROWS = 192


def packed_rows():
    spans = []
    at = 0
    for count in PACKED:
        spans.append((at, at + count))
        at += count
    return spans


def silu_pair(values):
    sigmoid_of = jax.nn.sigmoid(values)
    return values * sigmoid_of, sigmoid_of * (1.0 + values * (1.0 - sigmoid_of))


def block_kernel(
    nrows,
    devices,
    lengths_ref,
    tokens_ref,
    cot_ref,
    gain_ref,
    in_proj_ref,
    out_proj_ref,
    conv_ref,
    cbias_ref,
    x_proj_ref,
    dt_proj_ref,
    dtbias_ref,
    alog_ref,
    dskip_ref,
    output_out,
    grad_out,
    gin_out,
    gout_out,
    small_out,
    norm_out,
    output_ref,
    grad_ref,
    in_proj_buf,
    out_proj_buf,
    rates_ref,
    normed_rows,
    normed_sib,
    cot_half,
    cot_sib,
    inner,
    gates,
    back,
    pre_act,
    delta_pre,
    ddec,
    drive,
    grady,
    proj,
    rank_low,
    inb,
    outb,
    ends,
    ends_all,
    sums_all,
    docid,
    masks,
    padded,
    kept,
    first,
    second,
    gin,
    gout,
    gated,
    back_gates,
    back_inner,
    grad_conv,
    rank_back,
    proj_back,
    gated_got,
    back_got,
    gout_sum,
    gout_low,
    gout_got,
    gin_sum,
    gin_low,
    gin_got,
    gin_pub,
    small,
    small_low,
    small_got,
    small_part,
    small_seq,
    norm_part,
    norm_all,
    loads,
    halo_wires,
    state_wires,
    sum_wires,
    gather_wires,
    sib_wires,
    gated_wires,
    back_wires,
    gout_wires,
    line_wires,
    plane_wires,
    row_wires,
    seq_wires,
    norm_wires,
    local,
):
    row = lax.axis_index("rows")
    member = lax.axis_index("seq")
    level, side = member // 2, lax.rem(member, 2)
    levels = devices // 2
    steps = tokens_ref.shape[0]
    groups = E // LANES
    chunk = 4 * LANES
    chunks = E // chunk
    shard = E // devices
    halo = inner.shape[0] - steps
    reach = devices // 2
    half = N // 2
    low = jnp.bfloat16
    wide = jnp.float32
    spans = packed_rows()
    everyone = nrows * devices

    in_loads = [
        pltpu.make_async_copy(
            in_proj_ref.at[:, span(at, chunk)], in_proj_buf.at[at], loads.at[at]
        )
        for at in range(2 * chunks)
    ]
    out_load = pltpu.make_async_copy(out_proj_ref, out_proj_buf, loads.at[2 * chunks])
    for load in in_loads + [out_load]:
        load.start()

    def share(index, size):
        return pl.ds(pl.multiple_of(index * size, size), size)

    def plane(turn, other):
        return {
            "rows": lax.rem(row + turn, nrows),
            "seq": 2 * level + lax.rem(side + other, 2),
        }

    across = [levels - 1 - level, lax.rem(level + 2, levels), level + 1 - 2 * lax.rem(level, 2)]

    def line(turn):
        return {"seq": 2 * across[turn - 1] + side}

    def remote(source, target, send, recv, device):
        return pltpu.make_async_remote_copy(
            src_ref=source,
            dst_ref=target,
            send_sem=send,
            recv_sem=recv,
            device_id=device,
            device_id_type=MESH,
        )

    def begin(copies):
        for copy in copies:
            copy.start()
        return copies

    def settle(copies):
        for copy in copies:
            copy.wait()

    def other_device(offset):
        return {
            "rows": lax.rem(row + offset // devices, nrows),
            "seq": lax.rem(member + offset % devices, devices),
        }

    barrier = pltpu.get_barrier_semaphore()
    for offset in range(1, everyone):
        pl.semaphore_signal(
            barrier, inc=1, device_id=other_device(offset), device_id_type=MESH
        )

    def column_sum(values):
        return jnp.sum(values, axis=0, keepdims=True)

    stream = tokens_ref[...].astype(wide)
    inverse = lax.rsqrt(jnp.mean(stream * stream, axis=1, keepdims=True) + EPS)
    normed_rows[row] = (stream * inverse * gain_ref[...]).astype(low)
    cot_half[row] = cot_ref[:, share(lax.rem(row, 2), D // 2)]
    rates_ref[...] = jnp.exp(alog_ref[...]) * (-1.0 / math.log(2.0))

    places = member * steps - 8 + lax.broadcasted_iota(jnp.int32, docid.shape, 0)
    count = jnp.zeros(docid.shape, jnp.int32)
    starting = jnp.zeros(docid.shape, wide)
    start = 0
    for index in range(lengths_ref.shape[1]):
        count = count + jnp.where(places >= start, 1, 0)
        starting = jnp.where(places == start, 1.0, starting)
        start = start + lengths_ref[0, index]
    docid[...] = count
    masks[0] = starting[8:]
    for offset in range(1, K):
        masks[offset] = jnp.where(
            docid[8 - offset : 16 - offset + steps, :] == docid[8:, :], 1.0, 0.0
        )

    def project(at):
        in_loads[at].wait()
        return jnp.dot(
            normed_rows[row], in_proj_buf[at], preferred_element_type=wide
        ).astype(low)

    for at in range(chunks):
        inner[halo:, span(at, chunk)] = project(at)
    pl.semaphore_wait(barrier, everyone - 1)
    halo_copy = remote(
        inner.at[steps : steps + halo, :],
        inner.at[0:halo, :],
        halo_wires.at[0, 0],
        halo_wires.at[0, 1],
        {"seq": partner("seq", 1)},
    )

    @pl.when(member < devices - 1)
    def _():
        halo_copy.start()

    @pl.when(member == 0)
    def _():
        inner[0:halo, :] = jnp.zeros((halo, E), low)

    def gather_rows(kind, make, target):
        return begin(
            [
                remote(
                    make(partner("rows", offset)),
                    target.at[row],
                    gather_wires.at[kind, 0, offset - 1],
                    gather_wires.at[kind, 1, offset - 1],
                    {"rows": partner("rows", offset)},
                )
                for offset in range(1, nrows)
            ]
        )

    def to_sibling(kind, source, target):
        return begin(
            [
                remote(
                    source,
                    target,
                    sib_wires.at[kind, 0],
                    sib_wires.at[kind, 1],
                    {"seq": 2 * level + 1 - side},
                )
            ]
        )

    normed_moves = gather_rows(0, lambda other: normed_rows.at[row], normed_rows)
    cot_moves = gather_rows(
        1, lambda other: cot_ref.at[:, share(lax.rem(other, 2), D // 2)], cot_half
    )
    for at in range(chunks):
        gates[:, span(at, chunk)] = project(chunks + at)
    out_load.wait()
    for at in range(chunks):
        back[:, span(at, chunk)] = lax.dot_general(
            cot_ref[...],
            out_proj_buf[span(at, chunk), :],
            (((1,), (1,)), ((), ())),
            preferred_element_type=wide,
        ).astype(low)

    gin[...] = jnp.zeros_like(gin)
    gout[...] = jnp.zeros_like(gout)
    rank_back[...] = jnp.zeros_like(rank_back)
    small[...] = jnp.zeros_like(small)
    norm_part[...] = jnp.zeros_like(norm_part)
    proj[...] = jnp.zeros_like(proj)

    @pl.when(member < devices - 1)
    def _():
        halo_copy.wait_send()

    @pl.when(member > 0)
    def _():
        halo_copy.wait_recv()

    for at in range(chunks):
        lows = []
        for group in range(4 * at, 4 * at + 4):
            columns = span(group, LANES)
            padded[...] = inner[halo - 8 :, columns].astype(wide)
            value = cbias_ref[:, columns] + conv_ref[0:1, columns] * padded[8:, :]
            for offset in range(1, K):
                value = (
                    value
                    + conv_ref[offset : offset + 1, columns]
                    * padded[8 - offset : 8 - offset + steps, :]
                    * masks[offset, :steps, :]
                )
            pre_act[group] = value
            act = silu(value)
            drive[group] = act
            lows.append(act.astype(low))
        proj[...] += lax.dot_general(
            jnp.concatenate(lows, axis=1),
            x_proj_ref[:, span(at, chunk)],
            (((1,), (1,)), ((), ())),
            preferred_element_type=wide,
        )
    rank_low[...] = proj[:, :R].astype(low)
    inb[...] = jnp.broadcast_to(proj[:, R : R + N][:, :, None], inb.shape)
    outb[...] = jnp.broadcast_to(proj[:, R + N :][:, :, None], outb.shape)

    def lanes(at, place):
        return share(4 * at + place, LANES)

    def state_copy(direction, distance, at):
        offset = distance if direction == 0 else devices - distance
        return remote(
            ends.at[direction, at],
            ends_all.at[member, at],
            state_wires.at[direction, 0, at, distance - 1],
            state_wires.at[direction, 1, at, distance - 1],
            {"seq": partner("seq", offset)},
        )

    def sum_copy(direction, distance):
        offset = distance if direction == 0 else devices - distance
        return remote(
            sums_all.at[member],
            sums_all.at[member],
            sum_wires.at[direction, 0, distance - 1],
            sum_wires.at[direction, 1, distance - 1],
            {"seq": partner("seq", offset)},
        )

    def to_neighbours(make):
        for distance in range(reach, 0, -1):

            @pl.when(member + distance < devices)
            def _():
                make(0, distance).start()

            @pl.when(member >= distance)
            def _():
                make(1, distance).start()

    def from_neighbours(make):
        for distance in range(1, reach + 1):

            @pl.when(member + distance < devices)
            def _():
                make(0, distance).wait_send()
                make(1, distance).wait_recv()

            @pl.when(member >= distance)
            def _():
                make(1, distance).wait_send()
                make(0, distance).wait_recv()

    for at in range(chunks):
        pre = (
            jnp.dot(rank_low[...], dt_proj_ref[:, span(at, chunk)], preferred_element_type=wide)
            + dtbias_ref[:, span(at, chunk)]
        )
        for place in range(4):
            group = 4 * at + place
            columns = span(group, LANES)
            here = pre[:, place * LANES : (place + 1) * LANES]
            delta = softplus(here)
            delta_pre[group] = here
            drive[group] = drive[group] * delta
            decaying = jnp.where(masks[0, :steps, :] > 0.0, RESET, delta)
            ddec[group] = decaying
            sums_all[member, group : group + 1, :] = column_sum(decaying)
            grady[group] = back[:, columns].astype(wide) * silu(gates[:, columns].astype(wide))
    to_neighbours(sum_copy)
    zeros = [jnp.zeros((N, LANES), wide) for _ in range(4)]
    ones = [jnp.ones((N, LANES), wide) for _ in range(4)]
    order = [(turn, lax.rem(row + turn, nrows)) for turn in [*range(1, nrows), 0]]
    for _, at in order:

        def step(t, carry):
            hidden, decayed, pulled = carry
            in_row, out_row = inb[t], outb[t]
            new = ([], [], [])
            for place in range(4):
                here = (4 * at + place, pl.ds(t, 1))
                decay = jnp.exp2(ddec[here] * rates_ref[:, lanes(at, place)])
                new[0].append(decay * hidden[place] + drive[here] * in_row)
                product = decay * decayed[place]
                new[1].append(product)
                new[2].append(pulled[place] + product * (grady[here] * out_row))
            return new

        hidden, _, pulled = lax.fori_loop(0, steps, step, (zeros, ones, zeros), unroll=8)
        ends[0, at] = jnp.concatenate(hidden, axis=1).astype(low)
        ends[1, at] = jnp.concatenate(pulled, axis=1).astype(low)
        to_neighbours(lambda direction, distance: state_copy(direction, distance, at))
    from_neighbours(sum_copy)

    def fold(values):
        return values[:half] + values[half:]

    def collapse(source, place):
        total = source[place, pl.ds(0, steps, stride=half), :]
        for index in range(1, half):
            total = total + source[place, pl.ds(index, steps, stride=half), :]
        return total

    def trade(kind, source, at, turn):
        copies = []
        for other in range(2):
            columns = share(2 * at + lax.rem(side + other, 2), shard)
            target = back_got.at[kind, other, row]
            if turn == 0 and other == 0:
                copies.append(
                    pltpu.make_async_copy(source.at[:, columns], target, local.at[kind])
                )
            else:
                copies.append(
                    remote(
                        source.at[:, columns],
                        target,
                        back_wires.at[kind, 0, 2 * turn + other],
                        back_wires.at[kind, 1, 2 * turn + other],
                        plane(turn, other),
                    )
                )
        return begin(copies)

    def trade_gated(at):
        copies = []
        for turn in range(nrows):
            for other in range(2):
                columns = share(
                    4 * at + 2 * lax.rem(side + other, 2) + partner("rows", turn) // 2, LANES
                )
                target = gated_got.at[at, other, row]
                if turn == 0 and other == 0:
                    copies.append(
                        pltpu.make_async_copy(gated.at[:, columns], target, local.at[2 + at])
                    )
                else:
                    copies.append(
                        remote(
                            gated.at[:, columns],
                            target,
                            gated_wires.at[0, at, 2 * turn + other],
                            gated_wires.at[1, at, 2 * turn + other],
                            plane(turn, other),
                        )
                    )
        return begin(copies)

    gate_moves, gated_moves = [], []
    leavings = []
    for slot, (turn, at) in enumerate(order):
        from_neighbours(lambda direction, distance: state_copy(direction, distance, at))

        def through(device, states):
            new = []
            for place in range(4):
                total = sums_all[device, pl.ds(4 * at + place, 1), :]
                factor = jnp.exp2(total * rates_ref[:, lanes(at, place)])
                new.append(
                    factor * states[place]
                    + ends_all[device, at, :, place * LANES : (place + 1) * LANES].astype(wide)
                )
            return new

        def forward(t, hidden):
            in_row, out_row = inb[t], outb[t]
            new = []
            for place in range(4):
                here = (4 * at + place, pl.ds(t, 1))
                decay = jnp.exp2(ddec[here] * rates_ref[:, lanes(at, place)])
                state = decay * hidden[place] + drive[here] * in_row
                kept[slot, t + 1, place] = state.astype(low)
                first[place, share(t, half), :] = fold(state * out_row)
                new.append(state)
            return new

        entering = lax.fori_loop(jnp.maximum(member - reach, 0), member, through, zeros)
        last = jnp.minimum(member + reach, devices - 1)
        leavings.append(lax.fori_loop(0, last - member, lambda d, s: through(last - d, s), zeros))
        for place in range(4):
            kept[slot, 0, place] = entering[place].astype(low)
        lax.fori_loop(0, steps, forward, entering, unroll=8)
        for place in range(4):
            group, columns = 4 * at + place, lanes(at, place)
            act = silu(pre_act[group])
            y_full = collapse(first, place) + dskip_ref[:, columns] * act
            gate, slope = silu_pair(gates[:, columns].astype(wide))
            gated[:, columns] = (y_full * gate).astype(low)
            back_gates[:, columns] = (back[:, columns].astype(wide) * y_full * slope).astype(low)
            small[spans[6][0] : spans[6][1], columns] = column_sum(grady[group] * act)
        gate_moves += trade(1, back_gates, at, turn)


    def in_grads(kind):
        total = None
        for other, normed in ((0, normed_rows), (1, normed_sib)):
            part = lax.dot_general(
                normed[...].reshape(nrows * steps, D),
                back_got[kind, other].reshape(nrows * steps, shard),
                (((0,), (0,)), ((), ())),
                preferred_element_type=wide,
            )
            total = part if total is None else total + part
        gin_sum[kind] = total
        gin_low[kind] = total.astype(low)
        return begin(
            [
                remote(
                    gin_low.at[kind, share(across[turn - 1], D // levels), :],
                    gin_got.at[kind, turn - 1],
                    line_wires.at[kind, 0, turn - 1],
                    line_wires.at[kind, 1, turn - 1],
                    line(turn),
                )
                for turn in range(1, levels)
            ]
        )

    def squares(values):
        return jnp.sum(jnp.sum(values * values, axis=0, keepdims=True), axis=1, keepdims=True)

    def in_share(kind, before=None):
        total = gin_sum[kind, share(level, D // levels), :]
        for turn in range(levels - 1):
            total = total + gin_got[kind, turn].astype(wide)
        gin_pub[kind] = total.astype(low)
        owned = D // devices
        columns = share(kind * devices + 2 * row + side, shard)
        gin_out[:, columns] = gin_pub[kind, share(side, owned), :]
        norm_part[...] += squares(total)
        copies = [] if before is None else before()
        copies += begin(
            [
                remote(
                    gin_pub.at[kind, share(lax.rem(side + other, 2), owned), :],
                    gin_out.at[:, columns],
                    plane_wires.at[kind, 0, 2 * turn + other],
                    plane_wires.at[kind, 1, 2 * turn + other],
                    plane(turn, other),
                )
                for turn in range(nrows)
                for other in range(2)
                if turn + other > 0
            ]
        )
        return copies

    def gout_copy(turn):
        return remote(
            gout_low.at[across[turn - 1]],
            gout_got.at[turn - 1],
            gout_wires.at[0, turn - 1],
            gout_wires.at[1, turn - 1],
            line(turn),
        )

    def out_grads():
        for piece in range(levels):
            total = None
            for other, cots in ((0, cot_half), (1, cot_sib)):
                part = lax.dot_general(
                    gated_got[piece, other].reshape(nrows * steps, LANES),
                    cots[...].reshape(nrows * steps, D // 2),
                    (((0,), (0,)), ((), ())),
                    preferred_element_type=wide,
                )
                total = part if total is None else total + part
            gout_sum[piece] = total
            gout_low[piece] = total.astype(low)

    def out_share():
        total = gout_sum[level]
        for turn in range(levels - 1):
            total = total + gout_got[turn].astype(wide)
        mine = gout_out.at[share(row // 2, LANES), share(lax.rem(row, 2), D // 2)]
        mine[...] = total.astype(low)
        norm_part[...] += squares(total)
        return begin(
            [
                remote(
                    mine,
                    mine,
                    row_wires.at[2, 0, turn - 1],
                    row_wires.at[2, 1, turn - 1],
                    {"rows": partner("rows", turn)},
                )
                for turn in range(1, nrows)
            ]
        )

    for slot, (turn, at) in enumerate(order):

        def backward(back_step, carry):
            later, grates, states = carry
            t = steps - 1 - back_step
            in_row, out_row = inb[t], outb[t]
            gin_row, gout_row = gin[t], gout[t]
            new = ([], [], [])
            for place in range(4):
                here = (4 * at + place, pl.ds(t, 1))
                grad_y = grady[here]
                delta = ddec[here]
                rates = rates_ref[:, lanes(at, place)]
                before = kept[slot, t, place].astype(wide)
                adjoint = grad_y * out_row + later[place]
                gout_row = gout_row + grad_y * states[place]
                gin_row = gin_row + adjoint * drive[here]
                first[place, share(t, half), :] = fold(adjoint * in_row)
                passed = jnp.exp2(delta * rates) * adjoint
                pulled = passed * before
                second[place, share(t, half), :] = fold(pulled * rates)
                new[0].append(passed)
                new[1].append(grates[place] + pulled * delta)
                new[2].append(before)
            gin[t] = gin_row
            gout[t] = gout_row
            return new

        ending = [kept[slot, steps, place].astype(wide) for place in range(4)]
        _, grates, _ = lax.fori_loop(
            0, steps, backward, (leavings[slot], zeros, ending), unroll=8
        )
        lows = []
        for place in range(4):
            group, columns = 4 * at + place, lanes(at, place)
            along = collapse(first, place)
            here = delta_pre[group]
            act = silu(pre_act[group])
            grad_delta = along * act + collapse(second, place) * math.log(2.0)
            pre_low = (grad_delta * jax.nn.sigmoid(here)).astype(low)
            lows.append(pre_low)
            drive[group] = grady[group] * dskip_ref[:, columns] + along * softplus(here)
            small[spans[5][0] : spans[5][1], columns] = column_sum(pre_low.astype(wide))
            small[spans[2][0] : spans[2][1], columns] = (
                grates[place] * rates_ref[:, columns] * math.log(2.0)
            )
        lows = jnp.concatenate(lows, axis=1)
        rank_back[...] += lax.dot_general(
            lows,
            dt_proj_ref[:, share(at, chunk)],
            (((1,), (1,)), ((), ())),
            preferred_element_type=wide,
        )
        small[spans[0][0] : spans[0][1], share(at, chunk)] = lax.dot_general(
            rank_low[...], lows, (((0,), (0,)), ((), ())), preferred_element_type=wide
        )
        if slot == 0:
            settle(normed_moves)
            normed_moves = to_sibling(0, normed_rows, normed_sib)
            settle(cot_moves)
            cot_moves = to_sibling(1, cot_half, cot_sib)
            for _, chunk_at in order:
                gated_moves += trade_gated(chunk_at)
        if slot == chunks - 3:
            settle(normed_moves)
            settle(gate_moves)
            gate_moves = in_grads(1)

    parts = [(0, R // nrows), (R, (PACKED_ROWS - R) // nrows)]

    def scatter_small(part):
        begin_row, few = parts[part]
        rows = pl.ds(begin_row, few * nrows)
        small_low[rows, :] = small[rows, :].astype(low)
        return begin(
            [
                remote(
                    small_low.at[pl.ds(begin_row + partner("rows", turn) * few, few), :],
                    small_got.at[turn - 1, pl.ds(begin_row // nrows, few), :],
                    row_wires.at[part, 0, turn - 1],
                    row_wires.at[part, 1, turn - 1],
                    {"rows": partner("rows", turn)},
                )
                for turn in range(1, nrows)
            ]
        )

    def trade_small(part):
        begin_row, few = parts[part]
        rows = pl.ds(begin_row // nrows, few)
        total = small[pl.ds(pl.multiple_of(begin_row + row * few, few), few), :]
        for turn in range(nrows - 1):
            total = total + small_got[turn, rows, :].astype(wide)
        small_part[rows, :] = total.astype(low)
        return begin(
            [
                remote(
                    small_part.at[rows, share(partner("seq", offset), shard)],
                    small_seq.at[offset - 1, rows, :],
                    seq_wires.at[part, 0, offset - 1],
                    seq_wires.at[part, 1, offset - 1],
                    {"seq": partner("seq", offset)},
                )
                for offset in (4, 3, 5, 2, 6, 1, 7)
            ]
        )

    def share_small(part):
        begin_row, few = parts[part]
        rows = pl.ds(begin_row // nrows, few)
        total = small_part[rows, share(member, shard)].astype(wide)
        for offset in range(devices - 1):
            total = total + small_seq[offset, rows, :].astype(wide)
        mine = pl.ds(pl.multiple_of(begin_row + row * few, few), few)
        small_out[mine, :] = total.astype(low)
        norm_part[...] += squares(total)
        return begin(
            [
                remote(
                    small_out.at[mine, :],
                    small_out.at[mine, :],
                    row_wires.at[3 + part, 0, turn - 1],
                    row_wires.at[3 + part, 1, turn - 1],
                    {"rows": partner("rows", turn)},
                )
                for turn in range(1, nrows)
            ]
        )

    dt_moves = scatter_small(0)
    proj_back[:, :R] = rank_back[...].astype(low)
    proj_back[:, R : R + N] = jnp.sum(gin[...], axis=2).astype(low)
    proj_back[:, R + N :] = jnp.sum(gout[...], axis=2).astype(low)
    for at in range(chunks):
        pulled = jnp.dot(
            proj_back[...], x_proj_ref[:, span(at, chunk)], preferred_element_type=wide
        )
        lows = []
        for place in range(4):
            group = 4 * at + place
            act, slope = silu_pair(pre_act[group])
            lows.append(act.astype(low))
            grad_conv[group, :steps, :] = (
                drive[group] + pulled[:, place * LANES : (place + 1) * LANES]
            ) * slope
        small[spans[1][0] : spans[1][1], span(at, chunk)] = lax.dot_general(
            proj_back[...],
            jnp.concatenate(lows, axis=1),
            (((0,), (0,)), ((), ())),
            preferred_element_type=wide,
        )
    halo_back = remote(
        grad_conv.at[:, 0:8, :],
        grad_conv.at[:, steps : steps + 8, :],
        halo_wires.at[1, 0],
        halo_wires.at[1, 1],
        {"seq": partner("seq", devices - 1)},
    )

    @pl.when(member > 0)
    def _():
        halo_back.start()

    @pl.when(member == devices - 1)
    def _():
        grad_conv[:, steps : steps + 8, :] = jnp.zeros((groups, 8, LANES), wide)

    settle(cot_moves)
    settle(gated_moves)
    out_grads()
    gout_moves = begin([gout_copy(turn) for turn in range(1, levels)])
    output_ref[...] = stream + jnp.dot(
        gated[...], out_proj_buf[...], preferred_element_type=wide
    )
    grad_normed = jnp.zeros((steps, D), wide)
    for at in range(chunks):
        grad_normed = grad_normed + lax.dot_general(
            back_gates[:, span(at, chunk)],
            in_proj_buf[chunks + at],
            (((1,), (1,)), ((), ())),
            preferred_element_type=wide,
        )

    @pl.when(member > 0)
    def _():
        halo_back.wait_send()

    @pl.when(member < devices - 1)
    def _():
        halo_back.wait_recv()

    inner_moves = []
    for turn, at in order:
        for place in range(4):
            group, columns = 4 * at + place, lanes(at, place)
            padded[...] = inner[halo - 8 :, columns].astype(wide)
            here = grad_conv[group, :steps, :]
            pulled = conv_ref[0:1, columns] * here
            small[spans[4][0] : spans[4][1], columns] = column_sum(here)
            at_row = spans[3][0]
            small[at_row : at_row + 1, columns] = column_sum(here * padded[8:, :])
            for offset in range(1, K):
                small[at_row + offset : at_row + offset + 1, columns] = column_sum(
                    here * masks[offset, :steps, :] * padded[8 - offset : 8 - offset + steps, :]
                )
                pulled = pulled + conv_ref[offset : offset + 1, columns] * (
                    grad_conv[group, offset : offset + steps, :]
                    * masks[offset, offset : offset + steps, :]
                )
            back_inner[:, columns] = pulled.astype(low)
        inner_moves += trade(0, back_inner, at, turn)

    for at in range(chunks):
        grad_normed = grad_normed + lax.dot_general(
            back_inner[:, span(at, chunk)],
            in_proj_buf[at],
            (((1,), (1,)), ((), ())),
            preferred_element_type=wide,
        )
    settle(dt_moves)
    dt_moves = trade_small(0)
    inverse = lax.rsqrt(jnp.mean(stream * stream, axis=1, keepdims=True) + EPS)
    grad_gain = column_sum(grad_normed * stream * inverse)
    owned = D // devices
    for index in range(devices):
        small[spans[7][0] : spans[7][1], index * shard : index * shard + owned] = grad_gain[
            :, index * owned : (index + 1) * owned
        ]
    small_moves = scatter_small(1)
    scaled = grad_normed * gain_ref[...]
    grad_ref[...] = (
        cot_ref[...].astype(wide)
        + inverse * scaled
        - stream
        * inverse
        * inverse
        * inverse
        * jnp.mean(scaled * stream, axis=1, keepdims=True)
    )

    settle(gate_moves)
    gate_moves = in_share(1)
    position_moves = begin(
        [
            pltpu.make_async_copy(output_ref, output_out, local.at[2 + levels]),
            pltpu.make_async_copy(grad_ref, grad_out, local.at[3 + levels]),
        ]
    )
    settle(inner_moves)
    inner_moves = in_grads(0)
    settle(small_moves)
    small_moves = trade_small(1)
    settle(gout_moves)
    gout_moves = out_share()
    settle(dt_moves)
    dt_moves = share_small(0)
    settle(small_moves)
    small_moves = share_small(1)

    def spread_norm():
        here = row * devices + member
        norm_all[here] = jnp.broadcast_to(norm_part[...], (8, LANES))
        return begin(
            [
                remote(
                    norm_all.at[here],
                    norm_all.at[here],
                    norm_wires.at[0, offset - 1],
                    norm_wires.at[1, offset - 1],
                    other_device(offset),
                )
                for offset in range(1, everyone)
            ]
        )

    settle(inner_moves)
    inner_moves = in_share(0, spread_norm)
    norm_moves, inner_moves = inner_moves[: everyone - 1], inner_moves[everyone - 1 :]
    settle(position_moves)
    settle(norm_moves)
    norm_out[...] = jnp.sqrt(jnp.sum(norm_all[...], axis=0))
    settle(gout_moves)
    settle(gate_moves)
    settle(dt_moves)
    settle(small_moves)
    settle(inner_moves)


def block_of(operands, nrows, devices):
    steps = operands[1].shape[0]
    groups = E // LANES
    chunk = 4 * LANES
    chunks = E // chunk
    levels = devices // 2
    reach = devices // 2
    shard = E // devices
    halo = 16
    low, wide = jnp.bfloat16, jnp.float32
    few = PACKED_ROWS // nrows
    vmem = pl.BlockSpec(memory_space=pltpu.VMEM)
    specs = [vmem] * len(operands)
    specs[0] = pl.BlockSpec(memory_space=pltpu.SMEM)
    specs[4] = specs[5] = pl.BlockSpec(memory_space=pl.ANY)
    dma = pltpu.SemaphoreType.DMA
    grouped = pltpu.VMEM((groups, steps, LANES), wide)
    flat = pltpu.VMEM((steps, E), low)
    spread = pltpu.VMEM((steps, N, LANES), wide)
    gathered = pltpu.VMEM((nrows, steps, D), low)
    folded = pltpu.VMEM((4, steps * N // 2, LANES), wide)
    return pl.pallas_call(
        functools.partial(block_kernel, nrows, devices),
        in_specs=specs,
        out_specs=[pl.BlockSpec(memory_space=pl.ANY)] * 2 + [vmem] * 4,
        out_shape=[
            jax.ShapeDtypeStruct((steps, D), wide),
            jax.ShapeDtypeStruct((steps, D), wide),
            jax.ShapeDtypeStruct((D // devices, 2 * E), low),
            jax.ShapeDtypeStruct((shard, D), low),
            jax.ShapeDtypeStruct((PACKED_ROWS, shard), low),
            jax.ShapeDtypeStruct((8, LANES), wide),
        ],
        scratch_shapes=[
            pltpu.VMEM((steps, D), wide),
            pltpu.VMEM((steps, D), wide),
            pltpu.VMEM((2 * chunks, D, chunk), low),
            pltpu.VMEM((E, D), low),
            pltpu.VMEM((N, E), wide),
            gathered,
            gathered,
            pltpu.VMEM((nrows, steps, D // 2), low),
            pltpu.VMEM((nrows, steps, D // 2), low),
            pltpu.VMEM((steps + halo, E), low),
            flat,
            flat,
            grouped,
            grouped,
            grouped,
            grouped,
            grouped,
            pltpu.VMEM((steps, R + 2 * N), wide),
            pltpu.VMEM((steps, R), low),
            spread,
            spread,
            pltpu.VMEM((2, chunks, N, chunk), low),
            pltpu.VMEM((devices, chunks, N, chunk), low),
            pltpu.VMEM((devices, groups, LANES), wide),
            pltpu.VMEM((steps + 16, LANES), jnp.int32),
            pltpu.VMEM((K, steps + 8, LANES), wide),
            pltpu.VMEM((steps + 8, LANES), wide),
            pltpu.VMEM((chunks, steps + 1, 4, N, LANES), low),
            folded,
            folded,
            spread,
            spread,
            flat,
            flat,
            flat,
            pltpu.VMEM((groups, steps + 8, LANES), wide),
            pltpu.VMEM((steps, R), wide),
            pltpu.VMEM((steps, R + 2 * N), low),
            pltpu.VMEM((levels, 2, nrows, steps, LANES), low),
            pltpu.VMEM((2, 2, nrows, steps, shard), low),
            pltpu.VMEM((levels, LANES, D // 2), wide),
            pltpu.VMEM((levels, LANES, D // 2), low),
            pltpu.VMEM((levels - 1, LANES, D // 2), low),
            pltpu.VMEM((2, D, shard), wide),
            pltpu.VMEM((2, D, shard), low),
            pltpu.VMEM((2, levels - 1, D // levels, shard), low),
            pltpu.VMEM((2, D // levels, shard), low),
            pltpu.VMEM((PACKED_ROWS, E), wide),
            pltpu.VMEM((PACKED_ROWS, E), low),
            pltpu.VMEM((nrows - 1, few, E), low),
            pltpu.VMEM((few, E), low),
            pltpu.VMEM((devices - 1, few, shard), low),
            pltpu.VMEM((1, 1), wide),
            pltpu.VMEM((nrows * devices, 8, LANES), wide),
            dma((2 * chunks + 1,)),
            dma((2, 2)),
            dma((2, 2, chunks, reach)),
            dma((2, 2, reach)),
            dma((2, 2, nrows - 1)),
            dma((2, 2)),
            dma((2, levels, 2 * nrows)),
            dma((2, 2, 2 * nrows)),
            dma((2, levels - 1)),
            dma((2, 2, levels - 1)),
            dma((2, 2, 2 * nrows)),
            dma((5, 2, nrows - 1)),
            dma((2, 2, devices - 1)),
            dma((2, nrows * devices - 1)),
            dma((4 + levels,)),
        ],
        compiler_params=pltpu.CompilerParams(
            collective_id=1, has_side_effects=True, vmem_limit_bytes=63 * 2**20
        ),
        name="block",
    )(*operands)


def update_kernel(member_ref, norm_ref, gin_ref, gout_ref, small_ref, *refs):
    passed, weights, moments, averages, outs = (
        refs[:2],
        refs[2:12],
        refs[12:22],
        refs[22:32],
        refs[32:],
    )
    outs[30][...] = passed[0][...]
    outs[31][...] = passed[1][...]
    outs[32][...] = norm_ref[0:1, 0:1]
    shrink_by = 1.0 / jnp.maximum(norm_ref[0:1, 0:1], 1.0)

    def renew(ordinal, grad, at=Ellipsis):
        clipped = grad * shrink_by
        momentum_new = MOMENTUM * moments[ordinal][at] + clipped
        renewed = weights[ordinal][at].astype(jnp.float32) - RATES[ordinal] * math.sqrt(PARAMS) * (
            clipped + MOMENTUM * momentum_new
        )
        outs[3 * ordinal][at] = momentum_new
        outs[3 * ordinal + 1][at] = renewed
        outs[3 * ordinal + 2][at] = AVERAGE * averages[ordinal][at] + (1.0 - AVERAGE) * renewed

    renew(1, gin_ref[...].astype(jnp.float32))
    renew(9, gout_ref[...].astype(jnp.float32))

    @pl.when(pl.program_id(0) == 0)
    def _():
        spans = packed_rows()

        def part(index):
            return small_ref[spans[index][0] : spans[index][1], :].astype(jnp.float32)

        small = small_ref[...].astype(jnp.float32)
        renew(5, part(0))
        renew(4, part(1))
        renew(7, part(2))
        renew(2, part(3))
        for ordinal, index in ((3, 4), (6, 5), (8, 6)):
            renew(ordinal, small[spans[index][0] : spans[index][1]])
        gain = small[spans[7][0] : spans[7][1], : weights[0].shape[1]]
        renew(0, gain)


def update_of(member, norm_tile, gin, gout, small, passed, weights, moments, averages):
    inner = gin.shape[0]
    channels = gout.shape[0]
    blocks = 2
    outer = channels // blocks
    block = gin.shape[1] // blocks
    flat = (0, 3, 6, 8)

    def rows_of(array, ordinal):
        return array.reshape(1, -1) if ordinal in flat else array.T if ordinal == 4 else array

    def shard(shape, ordinal):
        if ordinal == 1:
            return pl.BlockSpec((inner, block), lambda j, m: (0, j))
        if ordinal == 9:
            return pl.BlockSpec((outer, shape[1]), lambda j, m: (j, 0))
        return pl.BlockSpec(shape, lambda j, m: (0, 0))

    def weight(shape, ordinal):
        if ordinal == 1:
            return pl.BlockSpec((inner, block), lambda j, m: (m[0], j))
        if ordinal == 9:
            return pl.BlockSpec((outer, shape[1]), lambda j, m: (m[0] * blocks + j, 0))
        return pl.BlockSpec(shape, lambda j, m: (0, m[0]))

    weights = [rows_of(array, ordinal) for ordinal, array in enumerate(weights)]
    moments = [rows_of(array, ordinal) for ordinal, array in enumerate(moments)]
    averages = [rows_of(array, ordinal) for ordinal, array in enumerate(averages)]
    shapes = [array.shape for array in moments]
    shards = [shard(shape, ordinal) for ordinal, shape in enumerate(shapes)]
    steps, depth = passed[0].shape
    through = pl.BlockSpec((steps // blocks, depth), lambda j, m: (j, 0))
    outs = pl.pallas_call(
        update_kernel,
        grid_spec=pltpu.PrefetchScalarGridSpec(
            num_scalar_prefetch=1,
            grid=(blocks,),
            in_specs=[
                pl.BlockSpec(norm_tile.shape, lambda j, m: (0, 0)),
                pl.BlockSpec((inner, block), lambda j, m: (0, j)),
                pl.BlockSpec((outer, gout.shape[1]), lambda j, m: (j, 0)),
                pl.BlockSpec(small.shape, lambda j, m: (0, 0)),
                through,
                through,
            ]
            + [weight(shape, ordinal) for ordinal, shape in enumerate(shapes)]
            + shards
            + shards,
            out_specs=[shards[ordinal] for ordinal in range(10) for _ in range(3)]
            + [through, through, pl.BlockSpec((1, 1), lambda j, m: (0, 0))],
        ),
        out_shape=[
            jax.ShapeDtypeStruct(shapes[ordinal], jnp.float32)
            for ordinal in range(10)
            for _ in range(3)
        ]
        + [jax.ShapeDtypeStruct(array.shape, array.dtype) for array in passed]
        + [jax.ShapeDtypeStruct((1, 1), jnp.float32)],
        compiler_params=pltpu.CompilerParams(vmem_limit_bytes=63 * 2**20),
        name="update",
    )(member, norm_tile, gin, gout, small, *passed, *weights, *moments, *averages)
    return outs[30:], [
        out.reshape(-1) if index // 3 in flat else out.T if index // 3 == 4 else out
        for index, out in enumerate(outs[:30])
    ]


def local(
    tokens,
    cotangent,
    doc_lengths,
    norm_gain,
    in_proj,
    conv_weight,
    conv_bias,
    x_proj,
    dt_proj,
    dt_bias,
    a_log,
    d_skip,
    out_proj,
    moment_norm_gain,
    moment_in_proj,
    moment_conv_weight,
    moment_conv_bias,
    moment_x_proj,
    moment_dt_proj,
    moment_dt_bias,
    moment_a_log,
    moment_d_skip,
    moment_out_proj,
    average_norm_gain,
    average_in_proj,
    average_conv_weight,
    average_conv_bias,
    average_x_proj,
    average_dt_proj,
    average_dt_bias,
    average_a_log,
    average_d_skip,
    average_out_proj,
):
    devices = lax.axis_size("seq")
    member_id = lax.axis_index("seq")
    channels = E // devices
    begin = member_id * channels
    stream = tokens[0].astype(jnp.float32)
    steps = stream.shape[0]
    length = steps * devices
    cot_low = cotangent[0]
    nrows = lax.axis_size("rows")
    direct = devices == 2 * nrows and nrows == 4 and E == nrows * 4 * LANES
    member_word = jnp.reshape(member_id, (1,)).astype(jnp.int32)
    moments = (
        moment_norm_gain,
        moment_in_proj,
        moment_conv_weight,
        moment_conv_bias,
        moment_x_proj,
        moment_dt_proj,
        moment_dt_bias,
        moment_a_log,
        moment_d_skip,
        moment_out_proj,
    )
    averages = (
        average_norm_gain,
        average_in_proj,
        average_conv_weight,
        average_conv_bias,
        average_x_proj,
        average_dt_proj,
        average_dt_bias,
        average_a_log,
        average_d_skip,
        average_out_proj,
    )
    if direct:
        weights = (
            norm_gain,
            in_proj,
            conv_weight,
            conv_bias,
            x_proj,
            dt_proj,
            dt_bias,
            a_log,
            d_skip,
            out_proj,
        )
        block_output, input_grad, gin_share, gout_share, small, norm_tile = block_of(
            (
                doc_lengths,
                tokens[0],
                cot_low,
                norm_gain[None],
                in_proj,
                out_proj,
                conv_weight,
                conv_bias[None],
                x_proj.T,
                dt_proj,
                dt_bias[None],
                a_log,
                d_skip[None],
            ),
            nrows,
            devices,
        )
        (block_output, input_grad, grad_norm), updated = update_of(
            member_word,
            norm_tile,
            gin_share,
            gout_share,
            small,
            (block_output, input_grad),
            weights,
            moments,
            averages,
        )
        return (block_output[None], input_grad[None], grad_norm.reshape(()), *updated)
    inverse = lax.rsqrt(jnp.mean(stream * stream, axis=1, keepdims=True) + EPS)
    rates = -jnp.exp(a_log)
    scaled_rates = rates * (1.0 / math.log(2.0))
    lengths = doc_lengths[0]
    starts = (jnp.cumsum(lengths) - lengths).astype(jnp.int32)
    (
        normed,
        inner_low,
        gates_low,
        back_gated,
        pre_act,
        delta_pre,
        ddec,
        drive,
        grady_rows,
        rank_low,
        inb,
        outb,
        everyone,
        all_sums,
    ) = front_of(
        starts,
        tokens[0],
        cot_low,
        norm_gain[None],
        in_proj,
        out_proj,
        conv_weight,
        conv_bias[None],
        x_proj.T,
        dt_proj,
        dt_bias[None],
        scaled_rates,
        devices,
        1,
    )
    cot_all = lax.all_gather(cot_low, "seq", axis=0, tiled=True)
    normed_all = lax.all_gather(normed[0], "seq", axis=0, tiled=True)
    positions = member_id * steps + jnp.arange(-8, steps + 8, dtype=jnp.int32)
    docid, starting = doc_tables(doc_lengths[0], positions)
    masks = []
    for offset in range(K):
        linked = (docid[8:] == docid[8 - offset : steps + 16 - offset]) & (
            positions[8 - offset : steps + 16 - offset] >= 0
        )
        masks.append((linked & (positions[8:] < length)).astype(jnp.float32)[:, None])

    def flat(values):
        return jnp.transpose(values, (1, 0, 2)).reshape(steps, E)

    pre_act, delta_pre = flat(pre_act), flat(delta_pre)
    padded = inner_low[8:].astype(jnp.float32)
    gates = gates_low.astype(jnp.float32)
    act = silu(pre_act)
    act_low = act.astype(jnp.bfloat16)
    delta = jax.nn.softplus(delta_pre)
    silu_gate = silu(gates)
    chan_back = back_gated.astype(jnp.float32)
    grad_y = chan_back * silu_gate
    scanned, along_in, pulled_sum, gin, gout, grad_rates = scan_of(
        member_word, ddec, drive, grady_rows, inb, outb, scaled_rates, everyone, all_sums, 512
    )
    scanned, along_in, pulled_sum = flat(scanned), flat(along_in), flat(pulled_sum)
    y_full = scanned + d_skip[None, :] * act
    gated = (y_full * silu_gate).astype(jnp.bfloat16)
    block_output = (
        stream + jnp.dot(gated, out_proj, preferred_element_type=jnp.float32)
    )[None]
    grad_gates = chan_back * y_full * silu_slope(gates)
    grad_dskip = jnp.sum(grad_y * act, axis=0)
    grad_in_mat = jnp.sum(gin, axis=2)
    grad_out_mat = jnp.sum(gout, axis=2)
    grad_delta = along_in * act + pulled_sum * math.log(2.0)
    grad_alog = grad_rates * rates
    grad_pre = (grad_delta * jax.nn.sigmoid(delta_pre)).astype(jnp.bfloat16)
    grad_dtbias = jnp.sum(grad_pre.astype(jnp.float32), axis=0)
    grad_dtproj = lax.dot_general(
        rank_low, grad_pre, (((0,), (0,)), ((), ())), preferred_element_type=jnp.float32
    )
    rank_back = lax.dot_general(
        grad_pre, dt_proj, (((1,), (1,)), ((), ())), preferred_element_type=jnp.float32
    )
    proj_back = jnp.concatenate([rank_back, grad_in_mat, grad_out_mat], axis=1).astype(jnp.bfloat16)
    grad_xproj = lax.dot_general(
        act_low, proj_back, (((0,), (0,)), ((), ())), preferred_element_type=jnp.float32
    )
    grad_act = (
        grad_y * d_skip[None, :]
        + along_in * delta
        + lax.dot_general(
            proj_back, x_proj, (((1,), (1,)), ((), ())), preferred_element_type=jnp.float32
        )
    )
    grad_pre_act = grad_act * silu_slope(pre_act)
    ahead = lax.ppermute(
        grad_pre_act[:8], "seq", [(i + 1, i) for i in range(devices - 1)]
    )
    extended = jnp.concatenate([grad_pre_act, ahead], axis=0)
    grad_conv_bias = jnp.sum(grad_pre_act, axis=0)
    grad_inner = jnp.zeros_like(gates)
    conv_rows = []
    for offset in range(K):
        masked = extended * masks[offset]
        conv_rows.append(
            jnp.sum(masked[:steps] * padded[8 - offset : 8 - offset + steps], axis=0)
        )
        grad_inner = grad_inner + conv_weight[offset][None, :] * masked[offset : offset + steps]
    grad_convw = jnp.stack(conv_rows)
    back_xz = jnp.stack([grad_inner, grad_gates]).astype(jnp.bfloat16)
    grad_normed = lax.dot_general(
        back_xz[0], in_proj[:, :E], (((1,), (1,)), ((), ())), preferred_element_type=jnp.float32
    ) + lax.dot_general(
        back_xz[1], in_proj[:, E:], (((1,), (1,)), ((), ())), preferred_element_type=jnp.float32
    )
    grad_gain = jnp.sum(grad_normed * stream * inverse, axis=0)
    scaled = grad_normed * norm_gain[None, :]
    input_grad = (
        cot_low.astype(jnp.float32)
        + inverse * scaled
        - stream * inverse * inverse * inverse * jnp.mean(scaled * stream, axis=1, keepdims=True)
    )
    small = jnp.concatenate(
        [
            grad_dtproj,
            grad_xproj.T,
            grad_alog,
            grad_convw,
            grad_conv_bias[None],
            grad_dtbias[None],
            grad_dskip[None],
            jnp.pad(
                grad_gain.reshape(devices, D // devices),
                ((0, 0), (0, channels - D // devices)),
            ).reshape(1, E),
            jnp.zeros((PACKED_ROWS - sum(PACKED), E), jnp.float32),
        ],
        axis=0,
    )
    gated_mine = lax.all_to_all(gated, "seq", split_axis=1, concat_axis=0, tiled=True)
    back_mine = lax.all_to_all(back_xz, "seq", split_axis=2, concat_axis=1, tiled=True)
    gout_share = lax.psum(
        lax.dot_general(
            gated_mine, cot_all, (((0,), (0,)), ((), ())), preferred_element_type=jnp.float32
        ),
        "rows",
    )
    gin_share = lax.psum(
        jnp.einsum("td,ktc->dkc", normed_all, back_mine, preferred_element_type=jnp.float32),
        "rows",
    )
    gin_share = lax.all_to_all(
        gin_share, "seq", split_axis=0, concat_axis=2, tiled=True
    ).reshape(D // devices, 2 * E)
    small = lax.psum(small, "rows")
    small = lax.psum_scatter(small, "seq", scatter_dimension=1, tiled=True)
    squares = jnp.sum(gin_share * gin_share) + jnp.sum(gout_share * gout_share)
    grad_norm = jnp.sqrt(lax.psum(squares + jnp.sum(small * small), "seq"))
    results = [block_output, input_grad[None], grad_norm]
    parts = [small[low:high] for low, high in packed_rows()]
    owner_grads = (
        parts[7][0, : D // devices],
        gin_share.astype(jnp.float32),
        parts[3],
        parts[4][0],
        parts[1].T,
        parts[0],
        parts[5][0],
        parts[2],
        parts[6][0],
        gout_share.astype(jnp.float32),
    )
    conv_mine = lax.dynamic_slice_in_dim(conv_weight, begin, channels, 1)
    cbias_mine = lax.dynamic_slice_in_dim(conv_bias, begin, channels, 0)
    xproj_mine = lax.dynamic_slice_in_dim(x_proj, begin, channels, 0)
    dtproj_mine = lax.dynamic_slice_in_dim(dt_proj, begin, channels, 1)
    dtbias_mine = lax.dynamic_slice_in_dim(dt_bias, begin, channels, 0)
    alog_mine = lax.dynamic_slice_in_dim(a_log, begin, channels, 1)
    dskip_mine = lax.dynamic_slice_in_dim(d_skip, begin, channels, 0)
    shrink_by = 1.0 / jnp.maximum(grad_norm, 1.0)
    gain_rows = D // devices
    outer_rows = E // devices
    mine_weights = (
        lax.dynamic_slice_in_dim(norm_gain, member_id * gain_rows, gain_rows, 0),
        lax.dynamic_slice_in_dim(in_proj, member_id * gain_rows, gain_rows, 0).astype(jnp.float32),
        conv_mine,
        cbias_mine,
        xproj_mine.astype(jnp.float32),
        dtproj_mine.astype(jnp.float32),
        dtbias_mine,
        alog_mine,
        dskip_mine,
        lax.dynamic_slice_in_dim(out_proj, member_id * outer_rows, outer_rows, 0).astype(
            jnp.float32
        ),
    )
    for ordinal in range(10):
        clipped = owner_grads[ordinal] * shrink_by
        momentum_new = MOMENTUM * moments[ordinal] + clipped
        renewed = mine_weights[ordinal] - RATES[ordinal] * math.sqrt(PARAMS) * (
            clipped + MOMENTUM * momentum_new
        )
        results += [momentum_new, renewed, AVERAGE * averages[ordinal] + (1.0 - AVERAGE) * renewed]
    return tuple(results)


def solution(mesh):
    return jax.shard_map(
        local,
        mesh=mesh,
        in_specs=(
            P("rows", "seq", None),
            P("rows", "seq", None),
            P("rows", None),
            P(),
            P(),
            P(),
            P(),
            P(),
            P(),
            P(),
            P(),
            P(),
            P(),
            P("seq"),
            P("seq", None),
            P(None, "seq"),
            P("seq"),
            P("seq", None),
            P(None, "seq"),
            P("seq"),
            P(None, "seq"),
            P("seq"),
            P("seq", None),
            P("seq"),
            P("seq", None),
            P(None, "seq"),
            P("seq"),
            P("seq", None),
            P(None, "seq"),
            P("seq"),
            P(None, "seq"),
            P("seq"),
            P("seq", None),
        ),
        out_specs=(
            P("rows", "seq", None),
            P("rows", "seq", None),
            P(),
            P("seq"),
            P("seq"),
            P("seq"),
            P("seq", None),
            P("seq", None),
            P("seq", None),
            P(None, "seq"),
            P(None, "seq"),
            P(None, "seq"),
            P("seq"),
            P("seq"),
            P("seq"),
            P("seq", None),
            P("seq", None),
            P("seq", None),
            P(None, "seq"),
            P(None, "seq"),
            P(None, "seq"),
            P("seq"),
            P("seq"),
            P("seq"),
            P(None, "seq"),
            P(None, "seq"),
            P(None, "seq"),
            P("seq"),
            P("seq"),
            P("seq"),
            P("seq", None),
            P("seq", None),
            P("seq", None),
        ),
        check_vma=False,
    )
```
